32 devices in a mesh: section: 2 (over core), seg: 4 (over z), tensor: 4 (over y, x).
Axes of the slice: x: 2, y: 2, z: 4, core: 2. Of those that a mesh axis runs over, the one named last changes fastest.
Arguments:
- inputs: bfloat16 [2, 1024, 768], P(None, 'seg'), may hold values from -6 to 6
- out_grad: bfloat16 [2, 1024, 768], P(None, 'seg'), may hold values from -6 to 6
- item_lengths: int32 [2, 4], replicated, may hold values from 0 to 4, as said below
- norm_gains: float32 [2, 2, 768], P('section'), may hold values from 0.1 to 1.9
- norm_biases: float32 [2, 2, 768], P('section'), may hold values from -4 to 4
- w_attn: bfloat16 [2, 3, 768, 768], P('section', None, None, 'tensor'), may hold values from -0.21875 to 0.21875
- attn_bias: float32 [2, 2, 768], P('section', None, 'tensor'), may hold values from -4 to 4
- w_out: bfloat16 [2, 768, 768], P('section', 'tensor'), may hold values from -2 to 2
- out_biases: float32 [2, 2, 768], P('section'), may hold values from -4 to 4
- w_fc: bfloat16 [2, 768, 3072], P('section', None, 'tensor'), may hold values from -0.21875 to 0.21875
- fc_bias: float32 [2, 3072], P('section', 'tensor'), may hold values from -4 to 4
- w_proj: bfloat16 [2, 3072, 768], P('section', 'tensor'), may hold values from -0.109375 to 0.109375
- w_mem_keys: bfloat16 [2, 2, 768, 384], P('section', None, None, 'tensor'), may hold values from -0.21875 to 0.21875
- w_mem_value: bfloat16 [2, 768, 768], P('section', None, 'tensor'), may hold values from -0.21875 to 0.21875
Outputs:
- input_grad: bfloat16 [2, 1024, 768], P('section', 'seg')
- norm_gains_grad: float32 [2, 2, 768], P('section')
- norm_biases_grad: float32 [2, 2, 768], P('section')
- w_attn_grad: float32 [2, 3, 768, 768], P('section', None, 'seg', 'tensor')
- attn_bias_grad: float32 [2, 2, 768], P('section', None, 'tensor')
- w_out_grad: float32 [2, 768, 768], P('section', 'tensor', 'seg')
- out_biases_grad: float32 [2, 2, 768], P('section')
- w_fc_grad: float32 [2, 768, 3072], P('section', 'seg', 'tensor')
- fc_bias_grad: float32 [2, 3072], P('section', 'tensor')
- w_proj_grad: float32 [2, 3072, 768], P('section', 'tensor', 'seg')
- w_mem_keys_grad: float32 [2, 2, 768, 384], P('section', None, 'seg', 'tensor')
- w_mem_value_grad: float32 [2, 768, 768], P('section', 'seg', 'tensor')
The draws below stay inside these ranges and needn't reach their ends.
Inputs may be any that keep to these rules, and one draw needn't show every extreme that they name: `item_lengths`: each row lists item lengths in segments, nonzero ones first and zeros after them, summing to 4; in one row, drawn from the seed, a single item holds all 4 segments; in the other rows each item has 1 to 4 segments.
All inputs are finite; a program needn't handle non-finite values.
Results may differ from the reference program's by a relative error of at most 0.018.
Values may be sent and summed in bfloat16 or wider, within the bound.
A program may use at most 192 MiB of HBM per device.

```python
from functools import partial
import jax
import jax.numpy as jnp
from jax import lax

D = 768
HEADS = 12
HEAD_DIM = 64
FF = 3072
DK = 384
NU = 3
SEG_LEN = 240
MICRO = 2
PHI = 2304
ROWS = 256
SEGMENTS = 4
TOTAL_ROWS = 1024
N_SECTION = 2


def draw_item_lengths(key, part):
    key = jax.random.fold_in(key, 11)
    pick_key, size_key = jax.random.split(key)
    long_row = jax.random.randint(pick_key, (), 0, MICRO)
    drawn = jax.random.randint(size_key, (MICRO, SEGMENTS), 1, 5)
    item_ends = jnp.minimum(jnp.cumsum(drawn, axis=1), SEGMENTS)
    item_begins = jnp.concatenate([jnp.zeros((MICRO, 1), jnp.int32), item_ends[:, :-1]], axis=1)
    short_items = (item_ends - item_begins).astype(jnp.int32)
    whole_item = jnp.zeros((MICRO, SEGMENTS), jnp.int32).at[:, 0].set(SEGMENTS)
    row_ids = jnp.arange(MICRO, dtype=jnp.int32)[:, None]
    return jnp.where(row_ids == long_row, whole_item, short_items).astype(jnp.int32)


def steps_of(key, extent, pieces, smallest, top_value):
    gain, own = 1.0, jax.random.fold_in(key, 6)
    for position, shards_of in pieces:
        heights = jnp.exp(jax.random.uniform(jax.random.fold_in(own, position), (shards_of,), jnp.float32, smallest / len(pieces), top_value / len(pieces)))
        gain = gain * jnp.repeat(heights, extent[position] // shards_of).reshape([-1 if axis == position else 1 for axis in range(len(extent))])
    return gain


def gaussian(stream_key, dims, scale, most, cuts=(), held_as=jnp.bfloat16):
    values = jax.random.normal(stream_key, dims, jnp.float32) * scale
    if len(cuts) > 0:
        values = steps_of(stream_key, dims, cuts, -0.22, 0.18) * values
    return jnp.clip(values, min=-most, max=most).astype(held_as)


def setup_inputs(seed: int = 0) -> dict:
    key_of = jax.random.split(jax.random.key(seed), 15)
    return {
        "inputs": gaussian(key_of[0], (MICRO, TOTAL_ROWS, D), 1.0, 6.0, ((1, 4),)),
        "out_grad": gaussian(key_of[1], (MICRO, TOTAL_ROWS, D), 1.0, 6.0, ((1, 4),)),
        "item_lengths": draw_item_lengths(jax.random.fold_in(key_of[14], 71), 0),
        "norm_gains": jnp.clip(1.0 + 0.18 * jax.random.normal(key_of[3], (N_SECTION, 2, D), jnp.float32), 0.1, 1.9),
        "norm_biases": gaussian(key_of[4], (N_SECTION, 2, D), 0.3, 4.0, ((0, 2),), jnp.float32),
        "w_attn": gaussian(key_of[5], (N_SECTION, 3, D, D), D ** -0.5, 0.21875, ((0, 2), (3, 4))),
        "attn_bias": gaussian(key_of[6], (N_SECTION, 2, D), 0.3, 4.0, ((0, 2), (2, 4)), jnp.float32),
        "w_out": gaussian(key_of[7], (N_SECTION, D, D), (max(D // 96, 1)) ** -0.5, 2.0, ((0, 2), (1, 4))),
        "out_biases": gaussian(key_of[8], (N_SECTION, 2, D), 0.3, 4.0, ((0, 2),), jnp.float32),
        "w_fc": gaussian(key_of[9], (N_SECTION, D, FF), D ** -0.5, 0.21875, ((0, 2), (2, 4))),
        "fc_bias": gaussian(key_of[10], (N_SECTION, FF), 0.3, 4.0, ((0, 2), (1, 4)), jnp.float32),
        "w_proj": gaussian(key_of[11], (N_SECTION, FF, D), FF ** -0.5, 0.109375, ((0, 2), (1, 4))),
        "w_mem_keys": gaussian(key_of[12], (N_SECTION, 2, D, DK), D ** -0.5, 0.21875, ((0, 2), (3, 4))),
        "w_mem_value": gaussian(key_of[13], (N_SECTION, D, D), D ** -0.5, 0.21875, ((0, 2), (2, 4))),
    }


PRECISE = lax.Precision.HIGHEST
EPSILON = 1e-05

@jax.custom_vjp
def low(v):
    return lax.optimization_barrier(v.astype(jnp.bfloat16)).astype(jnp.float32)

@jax.custom_vjp
def low_back(v):
    return v

def low_keep(v):
    return (low(v), None)

def low_pass(kept, grad):
    return (grad,)

def back_keep(v):
    return (v, None)

def back_low(kept, grad):
    return (low(grad),)
low.defvjp(low_keep, low_pass)
low_back.defvjp(back_keep, back_low)

def matmul(left, right):
    return jnp.dot(left, right, precision=PRECISE)

def layer_norm(hidden, scale_row, shift_row):
    row_mean = lax.optimization_barrier(jnp.mean(hidden, axis=-1, keepdims=True))
    centered = hidden - row_mean
    variance = lax.optimization_barrier(jnp.mean(centered * centered, axis=-1, keepdims=True))
    return centered * lax.rsqrt(variance + EPSILON) * scale_row + shift_row

def feature_map(projected):
    doubled = jnp.concatenate([jax.nn.softplus(projected), jax.nn.softplus(-projected)], axis=-1)
    return jnp.concatenate([doubled * jnp.roll(doubled, shift_by, axis=-1) for shift_by in range(1, NU + 1)], axis=-1)

def item_starts(lengths):
    item_ends = jnp.cumsum(lengths, axis=-1)
    item_begins = item_ends - lengths
    places = jnp.arange(lengths.shape[-1], dtype=jnp.int32)
    matches = (item_begins[:, :, None] == places[None, None, :]) & (lengths[:, :, None] > 0)
    return lax.optimization_barrier(jnp.sum(matches.astype(jnp.int32), axis=1))

def memory_read(memory, totals, phi_query):
    return matmul(phi_query, memory.T) / (matmul(phi_query, totals) + 1.0)[:, None]

def memory_update(memory, totals, phi_key, value_mem):
    recalled = memory_read(memory, totals, phi_key)
    return (memory + matmul((value_mem - recalled).T, phi_key), totals + lax.optimization_barrier(jnp.sum(phi_key, axis=0)))

def segment_step(weights, carry, inputs):
    gains, shifts, w_attn, attn_bias, w_out, out_biases, w_fc, fc_bias, w_proj, w_mem_keys, w_mem_value = weights
    memory, totals = carry
    seg_rows, first_flag = inputs
    memory = jnp.where(first_flag > 0, 0.0, memory)
    totals = jnp.where(first_flag > 0, 0.0, totals)
    mem_rows = seg_rows[SEG_LEN:]
    query_mem = low_back(low(matmul(seg_rows, w_mem_keys[0])))
    key_mem = low_back(low(matmul(mem_rows, w_mem_keys[1])))
    value_mem = low_back(matmul(mem_rows, w_mem_value))
    recall_read = memory_read(memory, totals, feature_map(query_mem))
    hidden = seg_rows + low(recall_read)
    new_carry = memory_update(memory, totals, feature_map(key_mem), value_mem)
    normed = low(layer_norm(hidden, gains[0], shifts[0]))
    queries = low_back(low(matmul(normed, w_attn[0]) + attn_bias[0]))
    key_heads = low_back(low(matmul(normed, w_attn[1])))
    values = low_back(low(matmul(normed, w_attn[2]) + attn_bias[1]))
    shaped = (ROWS, HEADS, HEAD_DIM)
    scores = jnp.einsum('qhd,khd->hqk', queries.reshape(shaped), key_heads.reshape(shaped), precision=PRECISE) * HEAD_DIM ** (-0.5)
    positions = jnp.arange(ROWS)
    causal = positions[:, None] >= positions[None, :]
    scores = low_back(jnp.where(causal[None], scores, -jnp.inf))
    attention_probs = low(jax.nn.softmax(scores, axis=-1))
    mixed_heads = jnp.einsum('hqk,khd->qhd', attention_probs, values.reshape(shaped), precision=PRECISE).reshape(ROWS, D)
    mixed_heads = low_back(low(mixed_heads))
    after_attention = hidden + low_back(matmul(mixed_heads, w_out)) + out_biases[0]
    normed_mlp = low(layer_norm(after_attention, gains[1], shifts[1]))
    pre_activation = low_back(matmul(normed_mlp, w_fc) + fc_bias)
    activation = low(jax.nn.gelu(pre_activation, approximate=True))
    output = after_attention + low_back(matmul(activation, w_proj)) + out_biases[1]
    return (new_carry, output)

def run_layer(segment_rows, first_flags, weights):
    step_function = jax.checkpoint(partial(segment_step, weights))
    initial = (jnp.zeros((D, PHI), jnp.float32), jnp.zeros((PHI,), jnp.float32))
    final_carry, outputs = lax.scan(step_function, initial, (segment_rows, first_flags))
    return outputs

def reference(inputs, out_grad, item_lengths, norm_gains, norm_biases, w_attn, attn_bias, w_out, out_biases, w_fc, fc_bias, w_proj, w_mem_keys, w_mem_value):
    first_flags = item_starts(item_lengths)
    params = tuple((weight.astype(jnp.float32) for weight in (norm_gains, norm_biases, w_attn, attn_bias, w_out, out_biases, w_fc, fc_bias, w_proj, w_mem_keys, w_mem_value)))
    rows_in = inputs.astype(jnp.float32).reshape(MICRO, SEGMENTS, ROWS, D)
    cotangent = out_grad.astype(jnp.float32).reshape(MICRO, SEGMENTS, ROWS, D)

    def forward(rows_in, params):
        results = []
        for micro_index in range(MICRO):
            hidden = rows_in[micro_index]
            for layer_index in range(N_SECTION):
                weights = tuple((weight[layer_index] for weight in params))
                hidden = run_layer(hidden, first_flags[micro_index], weights)
                if layer_index + 1 < N_SECTION:
                    hidden = low_back(low(hidden))
            results.append(hidden)
        return jnp.stack(results)
    outputs, pullback = jax.vjp(forward, rows_in, params)
    rows_grad, param_grads = pullback(cotangent)
    gain_grads, shift_grads, attention_grads, abias_grads, out_grads, obias_grads, fc_grads, fcb_grads, proj_grads, mkey_grads, mvalue_grads = param_grads
    input_grad = rows_grad.reshape(MICRO, SEGMENTS * ROWS, D).astype(jnp.bfloat16)
    return (input_grad, gain_grads, shift_grads, attention_grads, abias_grads, out_grads, obias_grads, fc_grads, fcb_grads, proj_grads, mkey_grads, mvalue_grads)
```

```python
import jax
import jax.numpy as jnp
from jax import lax
from jax.sharding import PartitionSpec as P

HEAD_DIM = 64
NU = 3
MEM = 16
EPSILON = 1e-05
F32 = jnp.float32
BF16 = jnp.bfloat16
GELU_A = 0.7978845608028654
GELU_B = 0.044715


def dot_nn(left, right):
    return lax.dot_general(left, right, (((1,), (0,)), ((), ())), preferred_element_type=F32)


def dot_nt(left, right):
    return lax.dot_general(left, right, (((1,), (1,)), ((), ())), preferred_element_type=F32)


def dot_tn(left, right):
    return lax.dot_general(left, right, (((0,), (0,)), ((), ())), preferred_element_type=F32)


def roll_lanes(values, by):
    return jnp.roll(values, by, axis=1)


def doubled_softplus(projected):
    tail = jnp.log1p(jnp.exp(-jnp.abs(projected)))
    return jnp.concatenate(
        [jnp.maximum(projected, 0.0) + tail, jnp.maximum(-projected, 0.0) + tail], axis=1
    )


def feature_map(projected):
    doubled = doubled_softplus(projected)
    return jnp.concatenate([doubled * roll_lanes(doubled, j) for j in range(1, NU + 1)], axis=1)


def feature_map_back(projected, phi_grad):
    doubled = doubled_softplus(projected)
    width = doubled.shape[1]
    total = jnp.zeros_like(doubled)
    for j in range(1, NU + 1):
        part = phi_grad[:, (j - 1) * width : j * width]
        total = total + part * roll_lanes(doubled, j) + roll_lanes(part * doubled, width - j)
    half = width // 2
    gate = 1.0 / (1.0 + jnp.exp(-projected))
    return total[:, :half] * gate - total[:, half:] * (1.0 - gate)


def norm_rows(hidden):
    centered = hidden - jnp.mean(hidden, axis=1, keepdims=True)
    scale = lax.rsqrt(jnp.mean(centered * centered, axis=1, keepdims=True) + EPSILON)
    return centered * scale, scale


def norm_back(hidden, gain_row, grad):
    unit, scale = norm_rows(hidden)
    unit_grad = grad * gain_row
    mean_grad = jnp.mean(unit_grad, axis=1, keepdims=True)
    mean_both = jnp.mean(unit_grad * unit, axis=1, keepdims=True)
    return (
        scale * (unit_grad - mean_grad - unit * mean_both),
        jnp.sum(grad * unit, axis=0, keepdims=True),
        jnp.sum(grad, axis=0, keepdims=True),
    )


def gelu_and_slope(pre):
    square = pre * pre
    bent = jnp.tanh(GELU_A * (pre + GELU_B * square * pre))
    value = 0.5 * pre * (1.0 + bent)
    slope = 0.5 * (1.0 + bent) + 0.5 * pre * (1.0 - bent * bent) * (
        GELU_A * (1.0 + 3.0 * GELU_B * square)
    )
    return value, slope


def item_ids(lengths):
    item_ends = jnp.cumsum(lengths, axis=-1)
    item_begins = item_ends - lengths
    places = jnp.arange(lengths.shape[-1], dtype=jnp.int32)
    matches = (item_begins[:, :, None] == places[None, None, :]) & (lengths[:, :, None] > 0)
    return jnp.cumsum(jnp.sum(matches.astype(jnp.int32), axis=1), axis=-1)


def reach_mask(lengths):
    ids = item_ids(lengths)
    places = jnp.arange(lengths.shape[-1])
    earlier = places[:, None] > places[None, :]
    same = (ids[:, :, None] == ids[:, None, :]) & earlier[None]
    return jnp.repeat(jnp.repeat(same.astype(F32), MEM, axis=1), MEM, axis=2)


def gather_rows(values, axis):
    return lax.all_gather(values, axis, axis=0, tiled=True)


def scatter_rows(values, axis):
    peers = lax.axis_size(axis)
    pieces = values.astype(BF16).reshape(peers, values.shape[0] // peers, values.shape[1])
    got = lax.all_to_all(pieces, axis, 0, 0, tiled=True)
    return jnp.sum(got.astype(F32), axis=0)


def scatter_columns(values, axis):
    peers = lax.axis_size(axis)
    rows = values.shape[0]
    pieces = values.reshape(rows, peers, -1).transpose(1, 0, 2)
    got = lax.all_to_all(pieces.astype(BF16), axis, 0, 0, tiled=True)
    return jnp.sum(got.astype(F32), axis=0)


def solve_forward(key_dots, key_den, value_mem):
    segments = key_dots.shape[0] // MEM
    solved = value_mem
    for s in range(1, segments):
        rows = slice(s * MEM, (s + 1) * MEM)
        read = dot_nn(key_dots[rows].astype(BF16), solved.astype(BF16)) / key_den[rows]
        solved = solved.at[rows].add(-read)
    return solved


def solve_backward(key_dots, key_den, direct):
    segments = key_dots.shape[0] // MEM
    total = direct
    for s in range(segments - 1, 0, -1):
        rows = slice(s * MEM, (s + 1) * MEM)
        back = -total[rows] / key_den[rows]
        total = total + dot_tn(key_dots[rows].astype(BF16), back.astype(BF16))
    return total


def layer_forward(own_rows, mem_rows, mask, place, params):
    gains, shifts, w_attn, attn_bias, w_out, out_biases, w_fc, fc_bias, w_proj, w_q, w_k, w_v = params
    seg, _ = place
    own_mask = lax.dynamic_slice_in_dim(mask, seg * MEM, 1, 0)
    key_mem = dot_nn(mem_rows, w_k).astype(BF16)
    phi_key = feature_map(key_mem.astype(F32)).astype(BF16)
    key_dots = dot_nt(phi_key, phi_key) * mask
    key_den = 1.0 + jnp.sum(key_dots, axis=1, keepdims=True)
    value_part = dot_nn(mem_rows, w_v)
    solved_part = solve_forward(key_dots, key_den, value_part)
    solved = lax.all_gather(solved_part.astype(BF16), "tensor", axis=1, tiled=True)
    query_mem = dot_nn(own_rows, w_q).astype(BF16)
    phi_query = feature_map(query_mem.astype(F32)).astype(BF16)
    query_dots = dot_nt(phi_query, phi_key) * own_mask
    query_den = 1.0 + jnp.sum(query_dots, axis=1, keepdims=True)
    recall = dot_nn(query_dots.astype(BF16), solved) / query_den
    hidden = own_rows.astype(F32) + recall.astype(BF16).astype(F32)
    unit, _ = norm_rows(hidden)
    normed = gather_rows((unit * gains[0] + shifts[0]).astype(BF16), "tensor")
    queries = (dot_nn(normed, w_attn[0]) + attn_bias[0]).astype(BF16)
    key_heads = dot_nn(normed, w_attn[1]).astype(BF16)
    values = (dot_nn(normed, w_attn[2]) + attn_bias[1]).astype(BF16)
    rows = normed.shape[0]
    causal = jnp.arange(rows)[:, None] >= jnp.arange(rows)[None, :]
    probs, mixed = [], []
    for h in range(queries.shape[1] // HEAD_DIM):
        cols = slice(h * HEAD_DIM, (h + 1) * HEAD_DIM)
        scores = dot_nt(queries[:, cols], key_heads[:, cols]) * HEAD_DIM ** (-0.5)
        scores = jnp.where(causal, scores, -jnp.inf)
        heights = jnp.exp(scores - jnp.max(scores, axis=1, keepdims=True))
        probs.append(heights / jnp.sum(heights, axis=1, keepdims=True))
        mixed.append(dot_nn(probs[-1].astype(BF16), values[:, cols]).astype(BF16))
    mixed = jnp.concatenate(mixed, axis=1)
    after = hidden + scatter_rows(dot_nn(mixed, w_out), "tensor") + out_biases[0]
    unit, _ = norm_rows(after)
    normed_mlp = gather_rows((unit * gains[1] + shifts[1]).astype(BF16), "tensor")
    pre = dot_nn(normed_mlp, w_fc) + fc_bias
    activation, slope = gelu_and_slope(pre)
    activation = activation.astype(BF16)
    output = after + scatter_rows(dot_nn(activation, w_proj), "tensor") + out_biases[1]
    kept = (
        own_rows, mem_rows, key_mem, phi_key, key_dots, key_den, value_part, solved_part, solved, query_mem,
        phi_query, query_dots, query_den, recall, hidden, normed, queries, key_heads, values, probs, mixed,
        after, normed_mlp, slope, activation,
    )
    return output, kept


def layer_backward(own_grad, kept, mask, place, params):
    gains, shifts, w_attn, attn_bias, w_out, out_biases, w_fc, fc_bias, w_proj, w_q, w_k, w_v = params
    (
        own_rows, mem_rows, key_mem, phi_key, key_dots, key_den, value_part, solved_part, solved, query_mem,
        phi_query, query_dots, query_den, recall, hidden, normed, queries, key_heads, values, probs, mixed,
        after, normed_mlp, slope, activation,
    ) = kept
    seg, part = place
    own_mask = lax.dynamic_slice_in_dim(mask, seg * MEM, 1, 0)
    grad_low = gather_rows(own_grad.astype(BF16), "tensor")
    pre_grad = (slope * dot_nt(grad_low, w_proj)).astype(BF16)
    proj_grad = dot_tn(activation, grad_low)
    fc_bias_grad = jnp.sum(pre_grad.astype(F32), axis=0)
    fc_grad = dot_tn(normed_mlp, pre_grad)
    after_part, gain_mlp, shift_mlp = norm_back(
        after, gains[1:2], scatter_rows(dot_nt(pre_grad, w_fc), "tensor")
    )
    after_grad = own_grad + after_part
    after_low = gather_rows(after_grad.astype(BF16), "tensor")
    out_grad = dot_tn(mixed, after_low)
    mixed_grad = dot_nt(after_low, w_out).astype(BF16)
    q_grads, k_grads, v_grads = [], [], []
    for h in range(queries.shape[1] // HEAD_DIM):
        cols = slice(h * HEAD_DIM, (h + 1) * HEAD_DIM)
        probs_grad = dot_nt(mixed_grad[:, cols], values[:, cols])
        delta = jnp.sum(probs_grad * probs[h], axis=1, keepdims=True)
        score_grad = (probs[h] * (probs_grad - delta)).astype(BF16)
        q_grads.append((dot_nn(score_grad, key_heads[:, cols]) * HEAD_DIM ** (-0.5)).astype(BF16))
        k_grads.append((dot_tn(score_grad, queries[:, cols]) * HEAD_DIM ** (-0.5)).astype(BF16))
        v_grads.append(dot_tn(probs[h].astype(BF16), mixed_grad[:, cols]).astype(BF16))
    three = [jnp.concatenate(g, axis=1) for g in (q_grads, k_grads, v_grads)]
    attn_bias_grad = jnp.stack([jnp.sum(three[i].astype(F32), axis=0) for i in (0, 2)])
    attn_grad = jnp.stack([dot_tn(normed, g) for g in three])
    normed_part = sum(dot_nt(g, w_attn[i]) for i, g in enumerate(three))
    hidden_part, gain_attn, shift_attn = norm_back(
        hidden, gains[0:1], scatter_rows(normed_part, "tensor")
    )
    hidden_grad = after_grad + hidden_part
    num_grad = (hidden_grad / query_den).astype(BF16)
    den_grad = -jnp.sum(hidden_grad * recall, axis=1, keepdims=True) / query_den
    dots_grad = ((dot_nt(num_grad, solved) + den_grad) * own_mask).astype(BF16)
    query_grad = feature_map_back(query_mem.astype(F32), dot_nn(dots_grad, phi_key)).astype(BF16)
    solved_direct = dot_tn(query_dots.astype(BF16), num_grad)
    key_direct = feature_map_back(key_mem.astype(F32), dot_tn(dots_grad, phi_query))
    solved_direct = scatter_columns(solved_direct, "tensor")
    solved_direct = jnp.sum(lax.all_gather(solved_direct.astype(BF16), "seg").astype(F32), axis=0)
    value_grad = solve_backward(key_dots, key_den, solved_direct)
    read = value_part - solved_part
    key_den_grad = jnp.sum(value_grad * read, axis=1, keepdims=True) / key_den
    back = (-value_grad / key_den).astype(BF16)
    key_dots_grad = (dot_nt(back, solved_part.astype(BF16)) + key_den_grad) * mask
    both = (key_dots_grad + key_dots_grad.T).astype(BF16)
    key_solve = feature_map_back(key_mem.astype(F32), dot_nn(both, phi_key))
    mine = (jnp.arange(key_solve.shape[0]) // MEM == seg)[:, None]
    key_direct = key_direct + jnp.where(mine, key_solve, 0.0)
    key_direct = scatter_columns(key_direct, "tensor")
    key_grad = jnp.sum(lax.all_gather(key_direct.astype(BF16), "seg").astype(F32), axis=0).astype(BF16)
    value_low = value_grad.astype(BF16)
    mem_width = mem_rows.shape[1] // lax.axis_size("seg")
    mem_cols = lax.dynamic_slice_in_dim(mem_rows, seg * mem_width, mem_width, 1)
    mem_key_grad = dot_tn(mem_cols, key_grad)
    mem_value_grad = dot_tn(mem_cols, value_low)
    return (
        hidden_grad, query_grad, key_grad, value_low,
        (gain_attn, gain_mlp, shift_attn, shift_mlp, jnp.sum(after_grad, axis=0, keepdims=True), jnp.sum(own_grad, axis=0, keepdims=True)),
        (attn_grad, attn_bias_grad, out_grad, fc_grad, fc_bias_grad, proj_grad, mem_key_grad, mem_value_grad),
    )


def per_device(
    inputs, out_grad, item_lengths, norm_gains, norm_biases, w_attn, attn_bias, w_out, out_biases, w_fc, fc_bias,
    w_proj, w_mem_keys, w_mem_value,
):
    section, seg, part = (lax.axis_index(name) for name in ("section", "seg", "tensor"))
    segments, parts = lax.axis_size("seg"), lax.axis_size("tensor")
    layers = lax.axis_size("section")
    mask = reach_mask(item_lengths)[section]
    weights = (norm_gains, norm_biases, w_attn, attn_bias, w_out, out_biases, w_fc, fc_bias, w_proj, w_mem_keys, w_mem_value)
    weights = [lax.all_gather(w, "section", axis=0, tiled=True) for w in weights]
    full_keys = lax.all_gather(weights[9], "tensor", axis=3, tiled=True)
    rows_all, grad_all = inputs[section], out_grad[section]
    chunk = rows_all.shape[0] // parts
    own_rows = lax.dynamic_slice_in_dim(rows_all, part * chunk, chunk, 0)
    place = (seg, part)
    saved, layer_params = [], []
    for layer in range(layers):
        mems = lax.all_gather(own_rows[-MEM:], ("seg", "tensor"), axis=0)
        mem_rows = mems[parts - 1 :: parts].reshape(segments * MEM, -1)
        params = tuple(w[layer] for w in weights[:9]) + (full_keys[layer, 0], full_keys[layer, 1], weights[10][layer])
        output, kept = layer_forward(own_rows, mem_rows, mask, place, params)
        saved.append(kept)
        layer_params.append(params)
        own_rows = output.astype(BF16)
    own_grad = lax.dynamic_slice_in_dim(grad_all, part * chunk, chunk, 0).astype(F32)
    rows_grads, matrix_grads = [None] * layers, [None] * layers
    for layer in reversed(range(layers)):
        params, kept = layer_params[layer], saved[layer]
        hidden_grad, query_grad, key_grad, value_low, rows_grads[layer], grads = layer_backward(own_grad, kept, mask, place, params)
        w_q = params[9]
        keys_here = lax.dynamic_slice_in_dim(key_grad, seg * MEM, MEM, 0)
        values_here = lax.dynamic_slice_in_dim(value_low, seg * MEM, MEM, 0)
        tail = dot_nt(keys_here, weights[9][layer, 1]) + dot_nt(values_here, params[11])
        tail = jnp.sum(lax.all_gather(tail.astype(BF16), "tensor").astype(F32), axis=0)
        tail = jnp.concatenate([jnp.zeros((chunk - MEM, tail.shape[1]), F32), tail], axis=0)
        rows_grad = hidden_grad + dot_nt(query_grad, w_q) + jnp.where(part == parts - 1, tail, 0.0)
        own_grad = rows_grad.astype(BF16).astype(F32)
        rows_full = gather_rows(kept[0], "tensor")
        query_cols = lax.all_to_all(query_grad.reshape(chunk, parts, -1).transpose(1, 0, 2), "tensor", 0, 0, tiled=True)
        query_cols = query_cols.reshape(chunk * parts, -1)
        matrix_grads[layer] = grads + (dot_tn(rows_full, query_cols),)
    input_grad = gather_rows(own_grad.astype(BF16), "tensor")[None]

    def over_layers(values):
        return lax.psum_scatter(jnp.stack(values), "section", scatter_dimension=0, tiled=True)

    rows_sums = lax.psum(over_layers([jnp.concatenate(r, axis=0) for r in rows_grads]), ("seg", "tensor"))

    def spread(index, axis):
        stacked = jnp.stack([g[index] for g in matrix_grads]).astype(BF16)
        pair = lax.all_to_all(stacked, "section", 0, 0, tiled=True)
        both = jnp.sum(pair.astype(F32), axis=0)
        cut = both.astype(BF16).reshape(both.shape[:axis] + (segments, -1) + both.shape[axis + 1 :])
        got = lax.all_to_all(cut, "seg", axis, axis, tiled=True)
        return jnp.sum(got.astype(F32), axis=axis)[None]

    biases = lax.psum(
        (over_layers([g[1] for g in matrix_grads]), over_layers([g[4] for g in matrix_grads])), "seg"
    )
    query_w = spread(8, 0)
    key_w = over_layers([g[6] for g in matrix_grads])
    return (
        input_grad,
        rows_sums[:, 0:2],
        rows_sums[:, 2:4],
        spread(0, 1),
        biases[0],
        spread(2, 1),
        rows_sums[:, 4:6],
        spread(3, 0),
        biases[1],
        spread(5, 1),
        jnp.stack([query_w, key_w], axis=1),
        over_layers([g[7] for g in matrix_grads]),
    )


def solution(mesh):
    return jax.shard_map(
        per_device,
        mesh=mesh,
        in_specs=(
            P(None, "seg", None),
            P(None, "seg", None),
            P(),
            P("section", None, None),
            P("section", None, None),
            P("section", None, None, "tensor"),
            P("section", None, "tensor"),
            P("section", "tensor", None),
            P("section", None, None),
            P("section", None, "tensor"),
            P("section", "tensor"),
            P("section", "tensor", None),
            P("section", None, None, "tensor"),
            P("section", None, "tensor"),
        ),
        out_specs=(
            P("section", "seg", None),
            P("section", None, None),
            P("section", None, None),
            P("section", None, "seg", "tensor"),
            P("section", None, "tensor"),
            P("section", "tensor", "seg"),
            P("section", None, None),
            P("section", "seg", "tensor"),
            P("section", "tensor"),
            P("section", "tensor", "seg"),
            P("section", None, "seg", "tensor"),
            P("section", "seg", "tensor"),
        ),
        check_vma=False,
    )
```

```python
import functools
from types import SimpleNamespace
from typing import Any, NamedTuple

import jax
import jax.numpy as jnp
from jax import lax
from jax.experimental import pallas as pl
from jax.experimental.pallas import tpu as pltpu
from jax.sharding import PartitionSpec as P

HEAD_DIM = 64
NU = 3
MEM = 16
EPSILON = 1e-05
F32 = jnp.float32
BF16 = jnp.bfloat16
GELU_A = 0.7978845608028654
GELU_B = 0.044715
LAYERS = 2
MESH = pl.DeviceIdType.MESH


def dot_nn(left, right):
    return lax.dot_general(left, right, (((1,), (0,)), ((), ())), preferred_element_type=F32)


def dot_nt(left, right):
    return lax.dot_general(left, right, (((1,), (1,)), ((), ())), preferred_element_type=F32)


def dot_tn(left, right):
    return lax.dot_general(left, right, (((0,), (0,)), ((), ())), preferred_element_type=F32)


def doubled_softplus(projected):
    small = jnp.exp(-jnp.abs(projected))
    tail = jnp.where(small < 1e-3, small - 0.5 * small * small, jnp.log1p(small))
    return jnp.concatenate(
        [jnp.maximum(projected, 0.0) + tail, jnp.maximum(-projected, 0.0) + tail], axis=1
    )


def feature_map(projected, roll=pltpu.roll):
    doubled = doubled_softplus(projected)
    return jnp.concatenate([doubled * roll(doubled, j, 1) for j in range(1, NU + 1)], axis=1)


def feature_map_back(projected, phi_grad, roll=pltpu.roll):
    doubled = doubled_softplus(projected)
    width = doubled.shape[1]
    total = jnp.zeros_like(doubled)
    for j in range(1, NU + 1):
        part = phi_grad[:, (j - 1) * width : j * width]
        total = total + part * roll(doubled, j, 1) + roll(part * doubled, width - j, 1)
    half = width // 2
    gate = 1.0 / (1.0 + jnp.exp(-projected))
    return total[:, :half] * gate - total[:, half:] * (1.0 - gate)


def norm_rows(hidden):
    centered = hidden - jnp.mean(hidden, axis=1, keepdims=True)
    scale = lax.rsqrt(jnp.mean(centered * centered, axis=1, keepdims=True) + EPSILON)
    return centered * scale, scale


def norm_back(hidden, gain_row, grad):
    unit, scale = norm_rows(hidden)
    unit_grad = grad * gain_row
    mean_grad = jnp.mean(unit_grad, axis=1, keepdims=True)
    mean_both = jnp.mean(unit_grad * unit, axis=1, keepdims=True)
    return (
        scale * (unit_grad - mean_grad - unit * mean_both),
        jnp.sum(grad * unit, axis=0, keepdims=True),
        jnp.sum(grad, axis=0, keepdims=True),
    )


def gelu_and_slope(pre):
    square = pre * pre
    bent = jnp.tanh(GELU_A * (pre + GELU_B * square * pre))
    value = 0.5 * pre * (1.0 + bent)
    slope = 0.5 * (1.0 + bent) + 0.5 * pre * (1.0 - bent * bent) * (
        GELU_A * (1.0 + 3.0 * GELU_B * square)
    )
    return value, slope


def xor_peer(place, other, count):
    total, bit = 0, 1
    while bit < count:
        mine = lax.rem(lax.div(place, bit), 2)
        total = total + bit * (1 - mine if other & bit else mine)
        bit *= 2
    return total


def split(values):
    high = values.astype(BF16)
    return high, (values - high.astype(F32)).astype(BF16)


class Sizes:
    def __init__(self, mesh, shapes):
        self.segs, self.parts = mesh.shape["seg"], mesh.shape["tensor"]
        inputs, w_attn, w_fc, w_keys = shapes
        self.rows, self.width = inputs[1] // self.segs, inputs[2]
        self.chunk = self.rows // self.parts
        self.mems = self.segs * MEM
        self.heads_w = w_attn[3] // self.parts
        self.heads = self.heads_w // HEAD_DIM
        self.units = w_fc[2] // self.parts
        self.keys = w_keys[3]
        self.keys_w = self.keys // self.parts
        self.phi = 2 * self.keys * NU
        self.val_w = self.width // self.parts
        self.cut = self.width // self.segs
        self.cut_pad = -(-self.cut // 16) * 16
        self.sems = 120 + 48 * self.parts + 2 * self.segs * (self.parts + 16)


def scratch_of(z):
    S, T, R, D, C, M = z.segs, z.parts, z.rows, z.width, z.chunk, z.mems
    bf = lambda *d: pltpu.VMEM(d, BF16)
    fl = lambda *d: pltpu.VMEM(d, F32)
    return dict(
        gains=fl(2, 2, D), shifts=fl(2, 2, D), w_attn=bf(2, 3, z.heads_w, D), attn_bias=fl(2, 2, z.heads_w),
        w_out=bf(2, z.heads_w, D), out_biases=fl(2, 2, D), w_fc=bf(2, D, z.units), fc_bias=fl(2, 1, z.units),
        w_proj=bf(2, z.units, D), w_keys=bf(2, 2, z.keys, D), w_value=bf(2, z.val_w, D),
        xfull=bf(2, R, D), gfull=bf(2, R, D), mem_rows=bf(2, M, D),
        keyb=bf(2, M, z.keys), phik=bf(2, M, z.phi), kdots=fl(2, M, M), vpart=fl(2, M, z.val_w),
        upart=fl(2, M, z.val_w), uall=bf(2, T, M, z.val_w), qmem=bf(2, C, z.keys), phiq=bf(2, C, z.phi),
        qdots=fl(2, C, M), recall=fl(2, C, D), hidden=fl(2, C, D), normed=bf(2, R, D), qkv=bf(2, 3, R, z.heads_w),
        probs=fl(2, z.heads, R, R), mixed=bf(2, R, z.heads_w), after=fl(2, C, D), normed_mlp=bf(2, R, D),
        slope=fl(2, R, z.units), act=bf(2, R, z.units), rs_src=bf(7, R, D), rs_own=fl(R, D), q_src=bf(R, z.keys_w), q_parts=bf(T, C, z.keys_w), k_parts=bf(T, M, z.keys_w), rs_dst=bf(7, T - 1, C, D),
        low2=bf(2, R, D), dpre=bf(R, z.units), dqkv=bf(3, R, z.heads_w),
        x1_src=fl(2, T, M, z.val_w), x1_dst=fl(2, T - 1, M, z.val_w), x1_mid=fl(2, M, z.val_w), x1_far=fl(2, max(S - 1, 1), M, z.val_w),
        x2_src=fl(2, T, M, z.keys_w), x2_dst=fl(2, T - 1, M, z.keys_w), x2_mid=fl(2, M, z.keys_w), x2_far=fl(2, max(S - 1, 1), M, z.keys_w), x4_src=fl(2, T, M, z.keys_w), x4_dst=fl(2, T - 1, M, z.keys_w), ksolve=fl(M, z.keys), dk_direct=fl(M, z.keys_w),
        dq_src=bf(2, T, C, z.keys_w), dq_all=bf(2, R, z.keys_w), dv=bf(M, z.val_w), vgrad=fl(M, z.val_w),
        x3_src=bf(2, MEM, D), x3_dst=bf(2, T - 1, MEM, D), final=bf(R, D), tmp=fl(C, D),
        grad_f=bf(2, S, 2, z.cut_pad, D), grad_a=bf(2, S, 4, z.cut_pad, z.heads_w), grad_q=bf(2, S, z.cut_pad, z.keys_w),
        pair_f=bf(S, 2, z.cut_pad, D), pair_a=bf(S, 4, z.cut_pad, z.heads_w), pair_q=bf(S, z.cut_pad, z.keys_w),
        far_f=bf(max(S - 1, 1), 2, z.cut_pad, D), far_a=bf(max(S - 1, 1), 4, z.cut_pad, z.heads_w), far_q=bf(max(S - 1, 1), z.cut_pad, z.keys_w),
        mem_k=fl(2, D, z.keys_w), mem_v=fl(2, D, z.val_w), pair_k=fl(z.cut, z.keys_w), pair_v=fl(z.cut, z.val_w),
        small=fl(2, 16, D), pair_small=fl(16, D), part_small=fl(T, 8, D), seg_small=fl(S, 16, D),
        send=pltpu.SemaphoreType.DMA((z.sems,)), recv=pltpu.SemaphoreType.DMA((z.sems,)), load=pltpu.SemaphoreType.DMA((14, 2)),
        shard=pltpu.SemaphoreType.DMA((2, 2, T)),
    )


class Outer(NamedTuple):
    inputs: Any
    out_grad: Any
    item_lengths: Any
    norm_gains: Any
    norm_biases: Any
    w_attn_in: Any
    attn_bias_in: Any
    w_out_in: Any
    out_biases_in: Any
    w_fc_in: Any
    fc_bias_in: Any
    w_proj_in: Any
    w_keys_in: Any
    w_value_in: Any
    input_grad: Any
    gain_grads: Any
    shift_grads: Any
    attn_grads: Any
    abias_grads: Any
    out_grads: Any
    obias_grads: Any
    fc_grads: Any
    fcb_grads: Any
    proj_grads: Any
    mkey_grads: Any
    mvalue_grads: Any


def kernel(z, held_names, *refs):
    outer = len(Outer._fields)
    r = SimpleNamespace(**Outer(*refs[:outer])._asdict(), **dict(zip(held_names, refs[outer:])))
    S, T, R, D, C, M = z.segs, z.parts, z.rows, z.width, z.chunk, z.mems
    c, s, t = (lax.axis_index(a) for a in ("section", "seg", "tensor"))
    other = 1 - c
    tpeers = [xor_peer(t, i, T) for i in range(T)]
    to_seg = [lax.rem(s + i, S) for i in range(S)]
    own = pl.ds(pl.multiple_of(t * C, C), C)
    seg_rows = pl.ds(pl.multiple_of(s * MEM, MEM), MEM)
    used = [0]
    sent = []
    owed = {}

    def alloc(count):
        used[0] += count
        assert used[0] <= z.sems
        return used[0] - count

    def owe(copies):
        def wait():
            for copy in copies:
                copy.wait_recv()

        owed[id(copies)] = wait
        return id(copies)

    def wait_bytes(ref, semaphore):
        pltpu.make_async_copy(ref, ref, semaphore).wait()

    def remote(src, dst, index, device, recv=None):
        copy = pltpu.make_async_remote_copy(
            src_ref=src, dst_ref=dst, send_sem=r.send.at[index],
            recv_sem=r.recv.at[index] if recv is None else recv, device_id=device, device_id_type=MESH,
        )
        return copy

    def to_parts(src_of, dst):
        base = alloc(T - 1)
        copies = []
        for i in range(T - 1, 0, -1):
            copy = remote(src_of(tpeers[i]), dst(i), base + i - 1, (c, s, tpeers[i]))
            copy.start()
            copies.append(copy)
        sent.extend((copy, None) for copy in copies)
        return owe(copies)

    def to_segs(src_of, dst):
        base = alloc(S - 1)
        copies = [
            remote(src_of(to_seg[i]), dst(i), base + i - 1, (c, to_seg[i], t)) for i in range(1, S)
        ]
        for copy in copies:
            copy.start()
        sent.extend((copy, None) for copy in copies)
        return owe(copies)

    def arrive(key):
        owed.pop(key)()

    def wait_load(ref, layer):
        arrive((id(ref), layer))

    barrier = pltpu.get_barrier_semaphore()
    greeted = [(other, s, t)] + [(c, to_seg[i], tpeers[j]) for i in range(S) for j in range(T) if i or j]
    for device in greeted:
        pl.semaphore_signal(barrier, inc=1, device_id=device, device_id_type=MESH)

    loads = [
        (r.w_value, r.w_value_in.at[0]), (r.gains, r.norm_gains.at[0]), (r.shifts, r.norm_biases.at[0]),
        (r.attn_bias, r.attn_bias_in.at[0]), (r.out_biases, r.out_biases_in.at[0]), (r.w_attn, r.w_attn_in.at[0]), (r.w_out, r.w_out_in.at[0]), (r.w_fc, r.w_fc_in.at[0]),
        (r.w_proj, r.w_proj_in.at[0]), (r.fc_bias, r.fc_bias_in),
    ]
    input_copy = pltpu.make_async_copy(r.inputs.at[c], r.xfull.at[0], r.load.at[10, 0])
    input_copy.start()
    owed[0] = input_copy.wait
    def shard_rows(part):
        return pl.ds(pl.multiple_of(part * z.keys_w, 16), z.keys_w)

    for which in (0, 1):
        pltpu.make_async_copy(
            r.w_keys_in.at[0, which], r.w_keys.at[c, which, shard_rows(t)], r.shard.at[c, which, 0]
        ).start()
    for kind, (held, source) in enumerate(loads):
        pltpu.make_async_copy(source, held.at[c], r.load.at[kind, c]).start()
        for layer in range(LAYERS):
            owed[id(held), layer] = functools.partial(wait_bytes, held.at[layer], r.load.at[kind, layer])
    grad_copy = pltpu.make_async_copy(r.out_grad.at[c], r.gfull.at[1], r.load.at[11, 0])
    grad_copy.start()
    owed[1] = grad_copy.wait

    pl.semaphore_wait(barrier, len(greeted))

    first_rows = to_segs(
        lambda _: r.inputs.at[c, pl.ds(R - MEM, MEM)], lambda i: r.mem_rows.at[0, seg_rows]
    )

    def shard_wait(layer, which, i):
        wait_bytes(r.w_keys.at[layer, which, pl.ds(0, z.keys_w)], r.shard.at[layer, which, i])

    def peer_shards(core, layer, which):
        @pl.when(c == core)
        def _():
            for i in range(1, T):
                shard_wait(layer, which, i)

    def spread_shard(layer, which):
        base = alloc(T - 1)
        place = r.w_keys.at[layer, which, shard_rows(t)]
        copies = [
            remote(r.w_keys_in.at[0, which], place, base + i - 1, (c, s, tpeers[i]), r.shard.at[layer, which, i])
            for i in range(T - 1, 0, -1)
        ]

        @pl.when(c == layer)
        def _():
            for copy in copies:
                copy.start()

        sent.extend((copy, c == layer) for copy in copies)
        owed[11, layer, which] = functools.partial(peer_shards, layer, layer, which)

    def forward_shard(layer, which):
        arrive((11, layer, which))
        base = alloc(T - 1)
        copies = []
        for i in range(1, T):
            place = r.w_keys.at[layer, which, shard_rows(tpeers[i])]
            copies.append(remote(place, place, base + i - 1, (other, s, t), r.shard.at[layer, which, i]))

        @pl.when(c == layer)
        def _():
            for copy in copies:
                copy.start()

        sent.extend((copy, c == layer) for copy in copies)
        owed[12, layer, which] = functools.partial(peer_shards, 1 - layer, layer, which)

    base = alloc(2)
    for which in (0, 1):
        copy = remote(
            r.w_keys_in.at[0, which], r.w_keys.at[c, which, shard_rows(t)], base + which, (other, s, t), r.shard.at[c, which, 0]
        )
        copy.start()
        sent.append((copy, None))
        for layer in range(LAYERS):
            owed[10, layer, which] = functools.partial(shard_wait, layer, which, 0)
    pair_base = alloc(len(loads))
    for kind, (held, source) in enumerate(loads):
        copy = remote(source, held.at[c], pair_base + kind, (other, s, t), r.load.at[kind, c])
        copy.start()
        sent.append((copy, None))

    row_seg = lax.broadcasted_iota(jnp.int32, (M, 1), 0) // MEM
    col_seg = lax.broadcasted_iota(jnp.int32, (1, M), 1) // MEM
    row_item, col_item, own_item = jnp.zeros((M, 1), jnp.int32), jnp.zeros((1, M), jnp.int32), 0
    begin = 0
    for i in range(r.item_lengths.shape[1]):
        length = r.item_lengths[c, i]
        there = jnp.where(length > 0, begin, S)
        row_item = row_item + (row_seg >= there).astype(jnp.int32)
        col_item = col_item + (col_seg >= there).astype(jnp.int32)
        own_item = own_item + jnp.where(s >= there, 1, 0)
        begin = begin + length
    key_mask = jnp.where((row_item == col_item) & (row_seg > col_seg), 1.0, 0.0)
    row_mask = jnp.where((col_item == own_item) & (col_seg < s), 1.0, 0.0)
    lane_head = lax.broadcasted_iota(jnp.int32, (1, z.heads_w), 1) // HEAD_DIM
    head_rows = [(lane_head == h).astype(F32).astype(BF16) for h in range(z.heads)]
    rs_count = [0]

    def reduce_rows(partial):
        k = rs_count[0]
        rs_count[0] += 1
        r.rs_own[...] = partial
        r.rs_src[k] = partial.astype(BF16)
        copies = to_parts(
            lambda peer: r.rs_src.at[k, pl.ds(pl.multiple_of(peer * C, C), C)], lambda i: r.rs_dst.at[k, i - 1]
        )

        def finish():
            arrive(copies)
            total = r.rs_own[own, :]
            for i in range(T - 1):
                total = total + r.rs_dst[k, i].astype(F32)
            return total

        return finish

    def share_rows(ref, layer):
        return to_parts(lambda _: ref.at[layer, own], lambda i: ref.at[layer, own])

    def forward(l):
        own_shard = shard_rows(t)
        if l == 0:
            arrive(0)
            arrive((10, 0, 0))
            r.q_src[...] = dot_nt(r.xfull[0], r.w_keys[0, 0, own_shard, :]).astype(BF16)
            r.q_parts[t] = r.q_src[own, :]
            query_step = to_parts(
                lambda peer: r.q_src.at[pl.ds(pl.multiple_of(peer * C, C), C)], lambda i: r.q_parts.at[t]
            )
            r.mem_rows[0, seg_rows, :] = r.xfull[0, R - MEM :, :]
            arrive((10, 0, 1))
            arrive(first_rows)
            mems = r.mem_rows[0]
            r.k_parts[t] = dot_nt(mems, r.w_keys[0, 1, own_shard, :]).astype(BF16)
            key_step = to_parts(lambda _: r.k_parts.at[t], lambda i: r.k_parts.at[t])
            arrive(query_step)
            queries_mem = jnp.concatenate([r.q_parts[u] for u in range(T)], axis=1)
        else:
            for which in (0, 1):
                arrive((10, 1, which))
                arrive((12, 1, which))
            queries_mem = dot_nt(r.xfull[1, own, :], r.w_keys[1, 0]).astype(BF16)
        x = r.xfull[l, own, :]
        r.qmem[l] = queries_mem
        phi_query = feature_map(queries_mem.astype(F32)).astype(BF16)
        r.phiq[l] = phi_query
        wait_load(r.w_value, l)
        if l == 1:
            arrive(4)
            mems = r.mem_rows[1]
        value_part = dot_nt(mems, r.w_value[l])
        r.vpart[l] = value_part
        r.upart[l] = value_part
        if l == 0:
            arrive(key_step)
            keys = jnp.concatenate([r.k_parts[u] for u in range(T)], axis=1)
        else:
            keys = dot_nt(mems, r.w_keys[1, 1]).astype(BF16)
        r.keyb[l] = keys
        phi_key = feature_map(keys.astype(F32)).astype(BF16)
        r.phik[l] = phi_key
        key_dots = dot_nt(phi_key, phi_key) * key_mask
        r.kdots[l] = key_dots
        key_den = 1.0 + jnp.sum(key_dots, axis=1, keepdims=True)
        for k in range(1, S):
            rows = slice(k * MEM, (k + 1) * MEM)
            read = dot_nn(key_dots[rows].astype(BF16), r.upart[l].astype(BF16)) / key_den[rows]
            r.upart[l, rows, :] = value_part[rows] - read
        r.uall[l, t] = r.upart[l].astype(BF16)
        solved = to_parts(lambda _: r.uall.at[l, t], lambda i: r.uall.at[l, t])
        if l == 0:
            spread_shard(1, 1)
        else:
            spread_shard(0, 0)
        query_dots = dot_nt(phi_query, phi_key) * row_mask
        r.qdots[l] = query_dots
        query_den = 1.0 + jnp.sum(query_dots, axis=1, keepdims=True)
        for ref in (r.gains, r.shifts, r.attn_bias, r.out_biases):
            wait_load(ref, l)
        arrive(solved)
        high, low = split(query_dots)
        recall = [dot_nn(high, r.uall[l, u]) + dot_nn(low, r.uall[l, u]) for u in range(T)]
        recall = jnp.concatenate(recall, axis=1) / query_den
        r.recall[l] = recall
        hidden = x.astype(F32) + recall.astype(BF16).astype(F32)
        r.hidden[l] = hidden
        unit, _ = norm_rows(hidden)
        r.normed[l, own, :] = (unit * r.gains[l, 0:1] + r.shifts[l, 0:1]).astype(BF16)
        shared = share_rows(r.normed, l)
        wait_load(r.w_attn, l)
        wait_load(r.w_out, l)
        arrive(shared)
        if l == 0:
            spread_shard(1, 0)
            row_step = None
        else:
            spread_shard(0, 1)
            row_step = share_rows(r.xfull, 1)
        normed = r.normed[l]
        queries = (dot_nt(normed, r.w_attn[l, 0]) + r.attn_bias[l, 0:1]).astype(BF16)
        key_heads = dot_nt(normed, r.w_attn[l, 1]).astype(BF16)
        values = (dot_nt(normed, r.w_attn[l, 2]) + r.attn_bias[l, 1:2]).astype(BF16)
        r.qkv[l, 0] = queries
        r.qkv[l, 1] = key_heads
        r.qkv[l, 2] = values
        causal = lax.broadcasted_iota(jnp.int32, (R, R), 0) >= lax.broadcasted_iota(jnp.int32, (R, R), 1)
        mixed = jnp.zeros((R, z.heads_w), F32)
        for h in range(z.heads):
            scores = dot_nt(queries, key_heads * head_rows[h]) * HEAD_DIM ** (-0.5)
            scores = jnp.where(causal, scores, -jnp.inf)
            heights = jnp.exp(scores - jnp.max(scores, axis=1, keepdims=True))
            probs = heights * (1.0 / jnp.sum(heights, axis=1, keepdims=True))
            r.probs[l, h] = probs
            mixed = mixed + dot_nn(probs.astype(BF16), values * head_rows[h])
        mixed = mixed.astype(BF16)
        r.mixed[l] = mixed
        finish = reduce_rows(dot_nn(mixed, r.w_out[l]))
        after = r.hidden[l] + finish() + r.out_biases[l, 0:1]
        r.after[l] = after
        unit, _ = norm_rows(after)
        r.normed_mlp[l, own, :] = (unit * r.gains[l, 1:2] + r.shifts[l, 1:2]).astype(BF16)
        shared = share_rows(r.normed_mlp, l)
        wait_load(r.w_fc, l)
        wait_load(r.fc_bias, l)
        wait_load(r.w_proj, l)
        if l == 0:
            forward_shard(1, 1)
            forward_shard(1, 0)
        arrive(shared)
        pre = dot_nn(r.normed_mlp[l], r.w_fc[l]) + r.fc_bias[l]
        activation, slope = gelu_and_slope(pre)
        activation = activation.astype(BF16)
        r.act[l] = activation
        r.slope[l] = slope
        if l == 0:
            finish = reduce_rows(dot_nn(activation, r.w_proj[l]))
            output = r.after[l] + finish() + r.out_biases[l, 1:2]
            r.xfull[1, own, :] = output.astype(BF16)
            base, places = alloc(S), alloc(S * T)
            last = r.xfull.at[1, pl.ds(R - MEM, MEM)]

            @pl.when(t == T - 1)
            def _():
                r.mem_rows[1, seg_rows, :] = r.xfull[1, R - MEM :, :]
                for i in range(S - 1, -1, -1):
                    for j in range(1 if i == 0 else 0, T):
                        copy = pltpu.make_async_remote_copy(
                            src_ref=last, dst_ref=r.mem_rows.at[1, seg_rows], send_sem=r.send.at[places + i * T + j],
                            recv_sem=r.recv.at[base + i], device_id=(c, to_seg[i], tpeers[j]), device_id_type=MESH,
                        )
                        copy.start()

            def wait_rows(i):
                wait_bytes(r.mem_rows.at[1, pl.ds(0, MEM)], r.recv.at[base + i])

            def wait_all():
                pl.when(t != T - 1)(functools.partial(wait_rows, 0))
                for i in range(1, S):
                    wait_rows(i)

            owed[4] = wait_all

            def drain():
                @pl.when(t == T - 1)
                def _():
                    for i in range(S):
                        for j in range(1 if i == 0 else 0, T):
                            wait_bytes(last, r.send.at[places + i * T + j])

            sent.append((drain, drain))
        return row_step

    fam_f, fam_a, fam_q = (r.grad_f, r.pair_f, r.far_f), (r.grad_a, r.pair_a, r.far_a), (r.grad_q, r.pair_q, r.far_q)

    def blocks_of(first_row, count):
        row, pieces = first_row, []
        while row < first_row + count:
            block, inside = row // z.cut, row % z.cut
            size = min(z.cut - inside, first_row + count - row)
            pieces.append((block, inside, row - first_row, size))
            row += size
        return pieces

    def weight_grad(left, right, store):
        stripe = min(256, D)
        for k in range(0, D, stripe):
            grad = dot_tn(left[:, k : k + stripe], right).astype(BF16)
            for block, inside, row, size in blocks_of(k, stripe):
                store(block, slice(inside, inside + size), grad[row : row + size])

    def pair_send(src, dst):
        index = alloc(1)
        return remote(src, dst, index, (other, s, t))

    def hand_over(l, names):
        copies = [pair_send(grad.at[l], pair) for grad, pair, _ in names]

        @pl.when(c != l)
        def _():
            for copy in copies:
                copy.start()

        sent.extend((copy, c != l) for copy in copies)
        return owe_owner(l, copies)

    def owe_owner(l, copies):
        def wait():
            @pl.when(c == l)
            def _():
                for copy in copies:
                    copy.wait_recv()

        owed[id(copies)] = wait
        return id(copies)

    def add_and_spread(l, names, copies):
        bases = [alloc(S - 1) for _ in names]
        arrive(copies)

        @pl.when(c == l)
        def _():
            for (grad, pair, far), base in zip(names, bases):

                @pl.loop(0, S)
                def _(j):
                    if len(grad.shape) == 4:
                        grad[l, j] = (grad[l, j].astype(F32) + pair[j].astype(F32)).astype(BF16)
                    else:
                        for m in range(grad.shape[2]):
                            grad[l, j, m] = (grad[l, j, m].astype(F32) + pair[j, m].astype(F32)).astype(BF16)

                for i in range(1, S):
                    remote(grad.at[l, to_seg[i]], far.at[i - 1], base + i - 1, (c, to_seg[i], t)).start()

        for (grad, _, far), base in zip(names, bases):
            owed[id(far), l] = functools.partial(far_wait, l, far, base)
            sent.append((functools.partial(far_drain, l, grad, base),) * 2)

    def far_wait(l, far, base):
        @pl.when(c == l)
        def _():
            for i in range(1, S):
                wait_bytes(far.at[i - 1], r.recv.at[base + i - 1])

    def far_drain(l, grad, base):
        @pl.when(c == l)
        def _():
            for i in range(1, S):
                wait_bytes(grad.at[l, 0], r.send.at[base + i - 1])

    def owe_small(l):
        copy = pair_send(r.small.at[l], r.pair_small)
        pl.when(c != l)(copy.start)
        sent.append((copy, c != l))
        return owe_owner(l, [copy])

    def owner_copies(l, copies):
        @pl.when(c == l)
        def _():
            for copy in copies:
                copy.start()

        sent.extend((copy, c == l) for copy in copies)
        return owe_owner(l, copies)

    def small_parts(l, key):
        arrive(key)

        @pl.when(c == l)
        def _():
            r.seg_small[0] = r.small[l] + r.pair_small[...]
            r.part_small[0] = r.seg_small[0, 0:8, :]

        base = alloc(T - 1)
        return owner_copies(
            l, [remote(r.part_small.at[0], r.part_small.at[i], base + i - 1, (c, s, tpeers[i])) for i in range(1, T)]
        )

    def small_segs(l, key):
        arrive(key)

        @pl.when(c == l)
        def _():
            total = r.part_small[0]
            for i in range(1, T):
                total = total + r.part_small[i]
            r.seg_small[0, 0:8, :] = total

        base = alloc(S - 1)
        return owner_copies(
            l, [remote(r.seg_small.at[0], r.seg_small.at[i], base + i - 1, (c, to_seg[i], t)) for i in range(1, S)]
        )

    def backward(l):
        if l == 1:
            arrive(1)
        grad_low = r.gfull[l]
        pre_grad = (r.slope[l] * dot_nt(grad_low, r.w_proj[l])).astype(BF16)
        r.dpre[...] = pre_grad
        finish = reduce_rows(dot_nt(pre_grad, r.w_fc[l]))
        own_grad = r.gfull[l, own, :].astype(F32)

        def store_f(m):
            def store(block, rows, value):
                r.grad_f[l, block, m, rows, :] = value

            return store

        weight_grad(r.normed_mlp.at[l], r.dpre[...], store_f(0))
        weight_grad(r.gfull.at[l], r.act[l], store_f(1))
        r.small[l, 8:9, :] = jnp.sum(r.dpre[...].astype(F32), axis=0, keepdims=True)
        pair_f = hand_over(l, (fam_f,))
        if l == 1:
            forward_shard(0, 0)
            forward_shard(0, 1)
        after_part, gain_mlp, shift_mlp = norm_back(r.after[l], r.gains[l, 1:2], finish())
        after_grad = own_grad + after_part
        r.tmp[...] = after_grad
        r.low2[l, own, :] = after_grad.astype(BF16)
        shared = share_rows(r.low2, l)
        r.small[l, 1:2, :] = gain_mlp
        r.small[l, 3:4, :] = shift_mlp
        r.small[l, 4:5, :] = jnp.sum(after_grad, axis=0, keepdims=True)
        r.small[l, 5:6, :] = jnp.sum(own_grad, axis=0, keepdims=True)
        add_and_spread(l, (fam_f,), pair_f)
        arrive(shared)
        after_low = r.low2[l]
        mixed_grad = dot_nt(after_low, r.w_out[l]).astype(BF16)
        queries, key_heads, values = r.qkv[l, 0], r.qkv[l, 1], r.qkv[l, 2]
        q_grad = k_grad = v_grad = jnp.zeros((R, z.heads_w), F32)
        for h in range(z.heads):
            probs = r.probs[l, h]
            mixed_here = mixed_grad * head_rows[h]
            probs_grad = dot_nt(mixed_here, values)
            delta = jnp.sum(probs_grad * probs, axis=1, keepdims=True)
            score_grad = (probs * (probs_grad - delta)).astype(BF16)
            q_grad = q_grad + dot_nn(score_grad, key_heads * head_rows[h])
            k_grad = k_grad + dot_tn(score_grad, queries * head_rows[h])
            v_grad = v_grad + dot_tn(probs.astype(BF16), mixed_here)
        scale = HEAD_DIM ** (-0.5)
        r.dqkv[0] = (q_grad * scale).astype(BF16)
        r.dqkv[1] = (k_grad * scale).astype(BF16)
        r.dqkv[2] = v_grad.astype(BF16)
        finish = reduce_rows(sum(dot_nn(r.dqkv[i], r.w_attn[l, i]) for i in range(3)))

        def store_a(m):
            def store(block, rows, value):
                r.grad_a[l, block, m, rows, :] = value

            return store

        for i in range(3):
            weight_grad(r.normed.at[l], r.dqkv[i], store_a(i))
        weight_grad(r.low2.at[l], r.mixed[l], store_a(3))
        pair_a = hand_over(l, (fam_a,))
        for row, i in ((9, 0), (10, 2)):
            r.small[l, row : row + 1, : z.heads_w] = jnp.sum(r.dqkv[i].astype(F32), axis=0, keepdims=True)
        hidden_part, gain_attn, shift_attn = norm_back(r.hidden[l], r.gains[l, 0:1], finish())
        hidden_grad = r.tmp[...] + hidden_part
        r.tmp[...] = hidden_grad
        r.small[l, 0:1, :] = gain_attn
        r.small[l, 2:3, :] = shift_attn
        small_key = owe_small(l)
        query_den = 1.0 + jnp.sum(r.qdots[l], axis=1, keepdims=True)
        high, low = split(hidden_grad / query_den)
        den_grad = -jnp.sum((hidden_grad / query_den) * r.recall[l], axis=1, keepdims=True)
        highs = [high[:, u * z.val_w : (u + 1) * z.val_w] for u in range(T)]
        lows = [low[:, u * z.val_w : (u + 1) * z.val_w] for u in range(T)]
        dots_high, dots_low = split(r.qdots[l])
        for u in range(T):
            r.x1_src[l, u] = dot_tn(dots_high, highs[u]) + dot_tn(dots_high, lows[u]) + dot_tn(dots_low, highs[u])
        value_step = to_parts(lambda peer: r.x1_src.at[l, peer], lambda i: r.x1_dst.at[l, i - 1])
        dots_grad = sum(dot_nt(highs[u], r.uall[l, u]) + dot_nt(lows[u], r.uall[l, u]) for u in range(T)) + den_grad
        dots_grad = (dots_grad * row_mask).astype(BF16)
        key_direct = feature_map_back(r.keyb[l].astype(F32), dot_tn(dots_grad, r.phiq[l]))
        for u in range(T):
            r.x2_src[l, u] = key_direct[:, u * z.keys_w : (u + 1) * z.keys_w]
        key_step = to_parts(lambda peer: r.x2_src.at[l, peer], lambda i: r.x2_dst.at[l, i - 1])
        arrive(value_step)
        r.x1_mid[l] = r.x1_src[l, t] + sum(r.x1_dst[l, i] for i in range(T - 1))
        value_step = to_segs(lambda _: r.x1_mid.at[l], lambda i: r.x1_far.at[l, i - 1])
        arrive(key_step)
        r.x2_mid[l] = r.x2_src[l, t] + sum(r.x2_dst[l, i] for i in range(T - 1))
        key_step = to_segs(lambda _: r.x2_mid.at[l], lambda i: r.x2_far.at[l, i - 1])
        query_grad = feature_map_back(r.qmem[l].astype(F32), dot_nn(dots_grad, r.phik[l])).astype(BF16)
        for u in range(T):
            r.dq_src[l, u] = query_grad[:, u * z.keys_w : (u + 1) * z.keys_w]
        r.dq_all[l, own, :] = r.dq_src[l, t]
        query_step = to_parts(lambda peer: r.dq_src.at[l, peer], lambda i: r.dq_all.at[l, own])
        if l == 0:
            arrive((12, 0, 0))
            arrive((12, 0, 1))
        r.tmp[...] += dot_nn(query_grad, r.w_keys[l, 0])
        arrive(value_step)
        direct = r.x1_mid[l] + sum(r.x1_far[l, i] for i in range(S - 1))
        key_dots = r.kdots[l]
        key_den = 1.0 + jnp.sum(key_dots, axis=1, keepdims=True)
        r.vgrad[...] = direct
        for k in range(S - 1, 0, -1):
            rows = slice(k * MEM, (k + 1) * MEM)
            back = -r.vgrad[rows, :] / key_den[rows]
            r.vgrad[...] += dot_tn(key_dots[rows].astype(BF16), back.astype(BF16))
        value_grad = r.vgrad[...]
        read = r.vpart[l] - r.upart[l]
        back = (-value_grad / key_den).astype(BF16)
        key_den_grad = -jnp.sum(back.astype(F32) * read, axis=1, keepdims=True)
        key_dots_grad = (dot_nt(back, r.upart[l].astype(BF16)) + key_den_grad) * key_mask
        both = (key_dots_grad + key_dots_grad.T).astype(BF16)
        key_solve = feature_map_back(r.keyb[l].astype(F32), dot_nn(both, r.phik[l]))
        r.ksolve[...] = key_solve
        r.dv[...] = value_grad.astype(BF16)
        arrive(key_step)
        r.dk_direct[...] = r.x2_mid[l] + sum(r.x2_far[l, i] for i in range(S - 1))
        tail = dot_nn(r.dv[seg_rows, :], r.w_value[l])
        tail = tail + dot_nn(r.dk_direct[seg_rows, :].astype(BF16), r.w_keys[l, 1, shard_rows(t), :])
        tail = tail + dot_nn(r.ksolve[seg_rows, :].astype(BF16), r.w_keys[l, 1])
        r.x3_src[l] = tail.astype(BF16)
        base, place = alloc(T - 1), alloc(1)

        for i in range(1, T):

            @pl.when(tpeers[i] == T - 1)
            def _():
                copy = pltpu.make_async_remote_copy(
                    src_ref=r.x3_src.at[l], dst_ref=r.x3_dst.at[l, i - 1], send_sem=r.send.at[place],
                    recv_sem=r.recv.at[base + i - 1], device_id=(c, s, tpeers[i]), device_id_type=MESH,
                )
                copy.start()

        def drain():
            @pl.when(t != T - 1)
            def _():
                wait_bytes(r.x3_src.at[l], r.send.at[place])

        sent.append((drain, drain))
        for u in range(T):
            r.x4_src[l, u] = key_solve[:, u * z.keys_w : (u + 1) * z.keys_w]
        solve_step = to_parts(lambda peer: r.x4_src.at[l, peer], lambda i: r.x4_dst.at[l, i - 1])
        add_and_spread(l, (fam_a,), pair_a)

        @pl.when(t == T - 1)
        def _():
            total = r.x3_src[l].astype(F32)
            for i in range(T - 1):
                wait_bytes(r.x3_dst.at[l, i], r.recv.at[base + i])
                total = total + r.x3_dst[l, i].astype(F32)
            r.tmp[C - MEM :, :] += total

        target = r.gfull.at[0] if l == 1 else r.final
        target[own, :] = r.tmp[...].astype(BF16)
        rows_step = to_parts(lambda _: target.at[own], lambda i: target.at[own])
        arrive(query_step)
        if l == 1:
            arrive(row_step)
        weight_grad(r.xfull.at[l], r.dq_all[l], lambda block, rows, value: r.grad_q.__setitem__((l, block, rows, slice(None)), value))
        pair_q = hand_over(l, (fam_q,))
        r.mem_v[l] = dot_tn(r.mem_rows[l], r.dv[...])
        arrive(solve_step)
        key_grad = r.dk_direct[...] + r.x4_src[l, t] + sum(r.x4_dst[l, i] for i in range(T - 1))
        r.mem_k[l] = dot_tn(r.mem_rows[l], key_grad.astype(BF16))
        rows = pl.ds(pl.multiple_of(s * z.cut, 8), z.cut)
        mem_copies = [pair_send(r.mem_k.at[l, rows], r.pair_k), pair_send(r.mem_v.at[l, rows], r.pair_v)]

        @pl.when(c != l)
        def _():
            for copy in mem_copies:
                copy.start()

        sent.extend((copy, c != l) for copy in mem_copies)
        mem_key = owe_owner(l, mem_copies)
        small_key = small_parts(l, small_key)
        add_and_spread(l, (fam_q,), pair_q)
        arrive(rows_step)
        return mem_key, small_key

    forward(0)
    row_step = forward(1)
    for l in range(LAYERS):
        r.small[l] = jnp.zeros((16, D), F32)
    mem_key1, small_key1 = backward(1)
    mem_key0, small_key0 = backward(0)

    r.input_grad[0] = r.final[...]
    l = c

    small_key1, small_key0 = small_segs(1, small_key1), small_segs(0, small_key0)
    arrive(mem_key1)
    arrive(mem_key0)
    rows = pl.ds(pl.multiple_of(s * z.cut, 8), z.cut)
    r.mkey_grads[0, 1] = r.mem_k[l, rows, :] + r.pair_k[...]
    r.mvalue_grads[0] = r.mem_v[l, rows, :] + r.pair_v[...]

    families = (fam_f, fam_a, fam_q)

    def far_sum(family, m=None):
        grad, _, far = families[family]
        pick = (slice(0, z.cut), slice(None)) if m is None else (m, slice(0, z.cut), slice(None))
        total = grad[(l, s) + pick].astype(F32)
        for i in range(S - 1):
            total = total + far[(i,) + pick].astype(F32)
        return total

    for family in range(3):

        for layer in range(LAYERS):
            arrive((id(families[family][2]), layer))
        if family == 0:
            r.fc_grads[0] = far_sum(0, 0)
            r.proj_grads[0] = far_sum(0, 1)
        elif family == 1:
            for i in range(3):
                r.attn_grads[0, i] = far_sum(1, i)
            r.out_grads[0] = far_sum(1, 3).T
        else:
            r.mkey_grads[0, 0] = far_sum(2)
    arrive(small_key1)
    arrive(small_key0)
    total = r.seg_small[0]
    for i in range(1, S):
        total = total + r.seg_small[i]
    r.gain_grads[0] = total[0:2]
    r.shift_grads[0] = total[2:4]
    r.obias_grads[0] = total[4:6]
    r.fcb_grads[...] = total[8:9, : z.units]
    r.abias_grads[0] = total[9:11, : z.heads_w]

    assert not owed
    for copy, when in sent:
        if when is copy:
            copy()
        elif when is None:
            copy.wait_send()
        else:
            pl.when(when)(copy.wait_send)


def hand_out(*refs):
    count = len(refs) // 2
    for source, target in zip(refs[:count], refs[count:]):
        target[...] = source[...]


def item_ids(lengths):
    item_ends = jnp.cumsum(lengths, axis=-1)
    item_begins = item_ends - lengths
    places = jnp.arange(lengths.shape[-1], dtype=jnp.int32)
    matches = (item_begins[:, :, None] == places[None, None, :]) & (lengths[:, :, None] > 0)
    return jnp.cumsum(jnp.sum(matches.astype(jnp.int32), axis=1), axis=-1)


def reach_mask(lengths):
    ids = item_ids(lengths)
    places = jnp.arange(lengths.shape[-1])
    earlier = places[:, None] > places[None, :]
    same = (ids[:, :, None] == ids[:, None, :]) & earlier[None]
    return jnp.repeat(jnp.repeat(same.astype(F32), MEM, axis=1), MEM, axis=2)


def gather_rows(values, axis):
    return lax.all_gather(values, axis, axis=0, tiled=True)


def scatter_rows(values, axis):
    peers = lax.axis_size(axis)
    pieces = values.astype(BF16).reshape(peers, values.shape[0] // peers, values.shape[1])
    got = lax.all_to_all(pieces, axis, 0, 0, tiled=True)
    return jnp.sum(got.astype(F32), axis=0)


def scatter_columns(values, axis):
    peers = lax.axis_size(axis)
    rows = values.shape[0]
    pieces = values.reshape(rows, peers, -1).transpose(1, 0, 2)
    got = lax.all_to_all(pieces.astype(BF16), axis, 0, 0, tiled=True)
    return jnp.sum(got.astype(F32), axis=0)


def solve_forward(key_dots, key_den, value_mem):
    segments = key_dots.shape[0] // MEM
    solved = value_mem
    for s in range(1, segments):
        rows = slice(s * MEM, (s + 1) * MEM)
        read = dot_nn(key_dots[rows].astype(BF16), solved.astype(BF16)) / key_den[rows]
        solved = solved.at[rows].add(-read)
    return solved


def solve_backward(key_dots, key_den, direct):
    segments = key_dots.shape[0] // MEM
    total = direct
    for s in range(segments - 1, 0, -1):
        rows = slice(s * MEM, (s + 1) * MEM)
        back = -total[rows] / key_den[rows]
        total = total + dot_tn(key_dots[rows].astype(BF16), back.astype(BF16))
    return total


def layer_forward(own_rows, mem_rows, mask, place, params):
    gains, shifts, w_attn, attn_bias, w_out, out_biases, w_fc, fc_bias, w_proj, w_q, w_k, w_v = params
    seg, _ = place
    own_mask = lax.dynamic_slice_in_dim(mask, seg * MEM, 1, 0)
    key_mem = dot_nn(mem_rows, w_k).astype(BF16)
    phi_key = feature_map(key_mem.astype(F32), jnp.roll).astype(BF16)
    key_dots = dot_nt(phi_key, phi_key) * mask
    key_den = 1.0 + jnp.sum(key_dots, axis=1, keepdims=True)
    value_part = dot_nn(mem_rows, w_v)
    solved_part = solve_forward(key_dots, key_den, value_part)
    solved = lax.all_gather(solved_part.astype(BF16), "tensor", axis=1, tiled=True)
    query_mem = dot_nn(own_rows, w_q).astype(BF16)
    phi_query = feature_map(query_mem.astype(F32), jnp.roll).astype(BF16)
    query_dots = dot_nt(phi_query, phi_key) * own_mask
    query_den = 1.0 + jnp.sum(query_dots, axis=1, keepdims=True)
    recall = dot_nn(query_dots.astype(BF16), solved) / query_den
    hidden = own_rows.astype(F32) + recall.astype(BF16).astype(F32)
    unit, _ = norm_rows(hidden)
    normed = gather_rows((unit * gains[0] + shifts[0]).astype(BF16), "tensor")
    queries = (dot_nn(normed, w_attn[0]) + attn_bias[0]).astype(BF16)
    key_heads = dot_nn(normed, w_attn[1]).astype(BF16)
    values = (dot_nn(normed, w_attn[2]) + attn_bias[1]).astype(BF16)
    rows = normed.shape[0]
    causal = jnp.arange(rows)[:, None] >= jnp.arange(rows)[None, :]
    probs, mixed = [], []
    for h in range(queries.shape[1] // HEAD_DIM):
        cols = slice(h * HEAD_DIM, (h + 1) * HEAD_DIM)
        scores = dot_nt(queries[:, cols], key_heads[:, cols]) * HEAD_DIM ** (-0.5)
        scores = jnp.where(causal, scores, -jnp.inf)
        heights = jnp.exp(scores - jnp.max(scores, axis=1, keepdims=True))
        probs.append(heights / jnp.sum(heights, axis=1, keepdims=True))
        mixed.append(dot_nn(probs[-1].astype(BF16), values[:, cols]).astype(BF16))
    mixed = jnp.concatenate(mixed, axis=1)
    after = hidden + scatter_rows(dot_nn(mixed, w_out), "tensor") + out_biases[0]
    unit, _ = norm_rows(after)
    normed_mlp = gather_rows((unit * gains[1] + shifts[1]).astype(BF16), "tensor")
    pre = dot_nn(normed_mlp, w_fc) + fc_bias
    activation, slope = gelu_and_slope(pre)
    activation = activation.astype(BF16)
    output = after + scatter_rows(dot_nn(activation, w_proj), "tensor") + out_biases[1]
    kept = (
        own_rows, mem_rows, key_mem, phi_key, key_dots, key_den, value_part, solved_part, solved, query_mem,
        phi_query, query_dots, query_den, recall, hidden, normed, queries, key_heads, values, probs, mixed,
        after, normed_mlp, slope, activation,
    )
    return output, kept


def layer_backward(own_grad, kept, mask, place, params):
    gains, shifts, w_attn, attn_bias, w_out, out_biases, w_fc, fc_bias, w_proj, w_q, w_k, w_v = params
    (
        own_rows, mem_rows, key_mem, phi_key, key_dots, key_den, value_part, solved_part, solved, query_mem,
        phi_query, query_dots, query_den, recall, hidden, normed, queries, key_heads, values, probs, mixed,
        after, normed_mlp, slope, activation,
    ) = kept
    seg, part = place
    own_mask = lax.dynamic_slice_in_dim(mask, seg * MEM, 1, 0)
    grad_low = gather_rows(own_grad.astype(BF16), "tensor")
    pre_grad = (slope * dot_nt(grad_low, w_proj)).astype(BF16)
    proj_grad = dot_tn(activation, grad_low)
    fc_bias_grad = jnp.sum(pre_grad.astype(F32), axis=0)
    fc_grad = dot_tn(normed_mlp, pre_grad)
    after_part, gain_mlp, shift_mlp = norm_back(
        after, gains[1:2], scatter_rows(dot_nt(pre_grad, w_fc), "tensor")
    )
    after_grad = own_grad + after_part
    after_low = gather_rows(after_grad.astype(BF16), "tensor")
    out_grad = dot_tn(mixed, after_low)
    mixed_grad = dot_nt(after_low, w_out).astype(BF16)
    q_grads, k_grads, v_grads = [], [], []
    for h in range(queries.shape[1] // HEAD_DIM):
        cols = slice(h * HEAD_DIM, (h + 1) * HEAD_DIM)
        probs_grad = dot_nt(mixed_grad[:, cols], values[:, cols])
        delta = jnp.sum(probs_grad * probs[h], axis=1, keepdims=True)
        score_grad = (probs[h] * (probs_grad - delta)).astype(BF16)
        q_grads.append((dot_nn(score_grad, key_heads[:, cols]) * HEAD_DIM ** (-0.5)).astype(BF16))
        k_grads.append((dot_tn(score_grad, queries[:, cols]) * HEAD_DIM ** (-0.5)).astype(BF16))
        v_grads.append(dot_tn(probs[h].astype(BF16), mixed_grad[:, cols]).astype(BF16))
    three = [jnp.concatenate(g, axis=1) for g in (q_grads, k_grads, v_grads)]
    attn_bias_grad = jnp.stack([jnp.sum(three[i].astype(F32), axis=0) for i in (0, 2)])
    attn_grad = jnp.stack([dot_tn(normed, g) for g in three])
    normed_part = sum(dot_nt(g, w_attn[i]) for i, g in enumerate(three))
    hidden_part, gain_attn, shift_attn = norm_back(
        hidden, gains[0:1], scatter_rows(normed_part, "tensor")
    )
    hidden_grad = after_grad + hidden_part
    num_grad = (hidden_grad / query_den).astype(BF16)
    den_grad = -jnp.sum(hidden_grad * recall, axis=1, keepdims=True) / query_den
    dots_grad = ((dot_nt(num_grad, solved) + den_grad) * own_mask).astype(BF16)
    query_grad = feature_map_back(query_mem.astype(F32), dot_nn(dots_grad, phi_key), jnp.roll).astype(BF16)
    solved_direct = dot_tn(query_dots.astype(BF16), num_grad)
    key_direct = feature_map_back(key_mem.astype(F32), dot_tn(dots_grad, phi_query), jnp.roll)
    solved_direct = scatter_columns(solved_direct, "tensor")
    solved_direct = jnp.sum(lax.all_gather(solved_direct.astype(BF16), "seg").astype(F32), axis=0)
    value_grad = solve_backward(key_dots, key_den, solved_direct)
    read = value_part - solved_part
    key_den_grad = jnp.sum(value_grad * read, axis=1, keepdims=True) / key_den
    back = (-value_grad / key_den).astype(BF16)
    key_dots_grad = (dot_nt(back, solved_part.astype(BF16)) + key_den_grad) * mask
    both = (key_dots_grad + key_dots_grad.T).astype(BF16)
    key_solve = feature_map_back(key_mem.astype(F32), dot_nn(both, phi_key), jnp.roll)
    mine = (jnp.arange(key_solve.shape[0]) // MEM == seg)[:, None]
    key_direct = key_direct + jnp.where(mine, key_solve, 0.0)
    key_direct = scatter_columns(key_direct, "tensor")
    key_grad = jnp.sum(lax.all_gather(key_direct.astype(BF16), "seg").astype(F32), axis=0).astype(BF16)
    value_low = value_grad.astype(BF16)
    mem_width = mem_rows.shape[1] // lax.axis_size("seg")
    mem_cols = lax.dynamic_slice_in_dim(mem_rows, seg * mem_width, mem_width, 1)
    mem_key_grad = dot_tn(mem_cols, key_grad)
    mem_value_grad = dot_tn(mem_cols, value_low)
    return (
        hidden_grad, query_grad, key_grad, value_low,
        (gain_attn, gain_mlp, shift_attn, shift_mlp, jnp.sum(after_grad, axis=0, keepdims=True), jnp.sum(own_grad, axis=0, keepdims=True)),
        (attn_grad, attn_bias_grad, out_grad, fc_grad, fc_bias_grad, proj_grad, mem_key_grad, mem_value_grad),
    )


def general_device(
    inputs, out_grad, item_lengths, norm_gains, norm_biases, w_attn, attn_bias, w_out, out_biases, w_fc, fc_bias,
    w_proj, w_mem_keys, w_mem_value,
):
    section, seg, part = (lax.axis_index(name) for name in ("section", "seg", "tensor"))
    segments, parts = lax.axis_size("seg"), lax.axis_size("tensor")
    layers = lax.axis_size("section")
    mask = reach_mask(item_lengths)[section]
    weights = (norm_gains, norm_biases, w_attn, attn_bias, w_out, out_biases, w_fc, fc_bias, w_proj, w_mem_keys, w_mem_value)
    weights = [lax.all_gather(w, "section", axis=0, tiled=True) for w in weights]
    full_keys = lax.all_gather(weights[9], "tensor", axis=3, tiled=True)
    rows_all, grad_all = inputs[section], out_grad[section]
    chunk = rows_all.shape[0] // parts
    own_rows = lax.dynamic_slice_in_dim(rows_all, part * chunk, chunk, 0)
    place = (seg, part)
    saved, layer_params = [], []
    for layer in range(layers):
        mems = lax.all_gather(own_rows[-MEM:], ("seg", "tensor"), axis=0)
        mem_rows = mems[parts - 1 :: parts].reshape(segments * MEM, -1)
        params = tuple(w[layer] for w in weights[:9]) + (full_keys[layer, 0], full_keys[layer, 1], weights[10][layer])
        output, kept = layer_forward(own_rows, mem_rows, mask, place, params)
        saved.append(kept)
        layer_params.append(params)
        own_rows = output.astype(BF16)
    own_grad = lax.dynamic_slice_in_dim(grad_all, part * chunk, chunk, 0).astype(F32)
    rows_grads, matrix_grads = [None] * layers, [None] * layers
    for layer in reversed(range(layers)):
        params, kept = layer_params[layer], saved[layer]
        hidden_grad, query_grad, key_grad, value_low, rows_grads[layer], grads = layer_backward(own_grad, kept, mask, place, params)
        w_q = params[9]
        keys_here = lax.dynamic_slice_in_dim(key_grad, seg * MEM, MEM, 0)
        values_here = lax.dynamic_slice_in_dim(value_low, seg * MEM, MEM, 0)
        tail = dot_nt(keys_here, weights[9][layer, 1]) + dot_nt(values_here, params[11])
        tail = jnp.sum(lax.all_gather(tail.astype(BF16), "tensor").astype(F32), axis=0)
        tail = jnp.concatenate([jnp.zeros((chunk - MEM, tail.shape[1]), F32), tail], axis=0)
        rows_grad = hidden_grad + dot_nt(query_grad, w_q) + jnp.where(part == parts - 1, tail, 0.0)
        own_grad = rows_grad.astype(BF16).astype(F32)
        rows_full = gather_rows(kept[0], "tensor")
        query_cols = lax.all_to_all(query_grad.reshape(chunk, parts, -1).transpose(1, 0, 2), "tensor", 0, 0, tiled=True)
        query_cols = query_cols.reshape(chunk * parts, -1)
        matrix_grads[layer] = grads + (dot_tn(rows_full, query_cols),)
    input_grad = gather_rows(own_grad.astype(BF16), "tensor")[None]

    def over_layers(values):
        return lax.psum_scatter(jnp.stack(values), "section", scatter_dimension=0, tiled=True)

    rows_sums = lax.psum(over_layers([jnp.concatenate(r, axis=0) for r in rows_grads]), ("seg", "tensor"))

    def spread(index, axis):
        stacked = jnp.stack([g[index] for g in matrix_grads]).astype(BF16)
        pair = lax.all_to_all(stacked, "section", 0, 0, tiled=True)
        both = jnp.sum(pair.astype(F32), axis=0)
        cut = both.astype(BF16).reshape(both.shape[:axis] + (segments, -1) + both.shape[axis + 1 :])
        got = lax.all_to_all(cut, "seg", axis, axis, tiled=True)
        return jnp.sum(got.astype(F32), axis=axis)[None]

    biases = lax.psum(
        (over_layers([g[1] for g in matrix_grads]), over_layers([g[4] for g in matrix_grads])), "seg"
    )
    query_w = spread(8, 0)
    key_w = over_layers([g[6] for g in matrix_grads])
    return (
        input_grad,
        rows_sums[:, 0:2],
        rows_sums[:, 2:4],
        spread(0, 1),
        biases[0],
        spread(2, 1),
        rows_sums[:, 4:6],
        spread(3, 0),
        biases[1],
        spread(5, 1),
        jnp.stack([query_w, key_w], axis=1),
        over_layers([g[7] for g in matrix_grads]),
    )


def solution(mesh):
    def per_device(*args):
        inputs, out_grad, item_lengths = args[:3]
        S, T = mesh.shape["seg"], mesh.shape["tensor"]
        w_attn, w_fc, w_keys = args[5], args[9], args[12]
        z = Sizes(
            mesh,
            (
                (0, inputs.shape[1] * S, inputs.shape[2]), (0, 0, 0, w_attn.shape[3] * T), (0, 0, w_fc.shape[2] * T),
                (0, 0, 0, w_keys.shape[3] * T),
            ),
        )
        scratch = scratch_of(z)
        D = z.width
        outs = dict(
            input_grad=((1, z.rows, D), BF16), gain_grads=((1, 2, D), F32), shift_grads=((1, 2, D), F32),
            attn_grads=((1, 3, z.cut, z.heads_w), F32), abias_grads=((1, 2, z.heads_w), F32),
            out_grads=((1, z.heads_w, z.cut), F32), obias_grads=((1, 2, D), F32), fc_grads=((1, z.cut, z.units), F32),
            fcb_grads=((1, z.units), F32), proj_grads=((1, z.cut, z.units), F32),
            mkey_grads=((1, 2, z.cut, z.keys_w), F32), mvalue_grads=((1, z.cut, z.val_w), F32),
        )
        names = tuple(scratch)
        vmem, anywhere = pl.BlockSpec(memory_space=pltpu.VMEM), pl.BlockSpec(memory_space=pl.ANY)
        shapes = [jax.ShapeDtypeStruct(*shape) for shape in outs.values()]
        flip = lambda w: jnp.swapaxes(w, -1, -2)
        results = pl.pallas_call(
            functools.partial(kernel, z, names),
            out_shape=shapes,
            in_specs=[anywhere, anywhere, pl.BlockSpec(memory_space=pltpu.SMEM)] + [anywhere] * 11,
            out_specs=[vmem] * len(outs),
            scratch_shapes=list(scratch.values()),
            compiler_params=pltpu.CompilerParams(
                collective_id=0, has_side_effects=True, vmem_limit_bytes=63 * 2**20
            ),
            name="two_layers",
        )(*args[:5], flip(w_attn), *args[6:12], flip(w_keys), flip(args[13]))
        results = list(pl.pallas_call(
            hand_out, out_shape=shapes, in_specs=[vmem] * len(outs), out_specs=[vmem] * len(outs), name="hand_out"
        )(*results))
        results[9] = flip(results[9])
        return tuple(results)

    return jax.shard_map(
        per_device if mesh.shape["seg"] * MEM <= 128 else general_device,
        mesh=mesh,
        in_specs=(
            P(None, "seg", None),
            P(None, "seg", None),
            P(),
            P("section", None, None),
            P("section", None, None),
            P("section", None, None, "tensor"),
            P("section", None, "tensor"),
            P("section", "tensor", None),
            P("section", None, None),
            P("section", None, "tensor"),
            P("section", "tensor"),
            P("section", "tensor", None),
            P("section", None, None, "tensor"),
            P("section", None, "tensor"),
        ),
        out_specs=(
            P("section", "seg", None),
            P("section", None, None),
            P("section", None, None),
            P("section", None, "seg", "tensor"),
            P("section", None, "tensor"),
            P("section", "tensor", "seg"),
            P("section", None, None),
            P("section", "seg", "tensor"),
            P("section", "tensor"),
            P("section", "tensor", "seg"),
            P("section", None, "seg", "tensor"),
            P("section", "seg", "tensor"),
        ),
        check_vma=False,
    )
```

```python
import functools
from types import SimpleNamespace
from typing import Any, NamedTuple

import jax
import jax.numpy as jnp
from jax import lax
from jax.experimental import pallas as pl
from jax.experimental.pallas import tpu as pltpu
from jax.sharding import PartitionSpec as P

HEAD_DIM = 64
NU = 3
MEM = 16
EPSILON = 1e-05
F32 = jnp.float32
BF16 = jnp.bfloat16
GELU_A = 0.7978845608028654
GELU_B = 0.044715
LAYERS = 2
MESH = pl.DeviceIdType.MESH


def dot_nn(left, right):
    return lax.dot_general(left, right, (((1,), (0,)), ((), ())), preferred_element_type=F32)


def dot_nt(left, right):
    return lax.dot_general(left, right, (((1,), (1,)), ((), ())), preferred_element_type=F32)


def dot_tn(left, right):
    return lax.dot_general(left, right, (((0,), (0,)), ((), ())), preferred_element_type=F32)


def doubled_softplus(projected):
    small = jnp.exp(-jnp.abs(projected))
    tail = jnp.where(small < 1e-3, small - 0.5 * small * small, jnp.log1p(small))
    return jnp.concatenate(
        [jnp.maximum(projected, 0.0) + tail, jnp.maximum(-projected, 0.0) + tail], axis=1
    )


def feature_map(projected, roll=pltpu.roll):
    doubled = doubled_softplus(projected)
    return jnp.concatenate([doubled * roll(doubled, j, 1) for j in range(1, NU + 1)], axis=1)


def feature_map_back(projected, phi_grad, roll=pltpu.roll):
    doubled = doubled_softplus(projected)
    width = doubled.shape[1]
    total = jnp.zeros_like(doubled)
    for j in range(1, NU + 1):
        part = phi_grad[:, (j - 1) * width : j * width]
        total = total + part * roll(doubled, j, 1) + roll(part * doubled, width - j, 1)
    half = width // 2
    gate = 1.0 / (1.0 + jnp.exp(-projected))
    return total[:, :half] * gate - total[:, half:] * (1.0 - gate)


def norm_rows(hidden):
    centered = hidden - jnp.mean(hidden, axis=1, keepdims=True)
    scale = lax.rsqrt(jnp.mean(centered * centered, axis=1, keepdims=True) + EPSILON)
    return centered * scale, scale


def norm_back(hidden, gain_row, grad):
    unit, scale = norm_rows(hidden)
    unit_grad = grad * gain_row
    mean_grad = jnp.mean(unit_grad, axis=1, keepdims=True)
    mean_both = jnp.mean(unit_grad * unit, axis=1, keepdims=True)
    return (
        scale * (unit_grad - mean_grad - unit * mean_both),
        jnp.sum(grad * unit, axis=0, keepdims=True),
        jnp.sum(grad, axis=0, keepdims=True),
    )


def gelu_and_slope(pre):
    square = pre * pre
    bent = jnp.tanh(GELU_A * (pre + GELU_B * square * pre))
    value = 0.5 * pre * (1.0 + bent)
    slope = 0.5 * (1.0 + bent) + 0.5 * pre * (1.0 - bent * bent) * (
        GELU_A * (1.0 + 3.0 * GELU_B * square)
    )
    return value, slope


def xor_peer(place, other, count):
    total, bit = 0, 1
    while bit < count:
        mine = lax.rem(lax.div(place, bit), 2)
        total = total + bit * (1 - mine if other & bit else mine)
        bit *= 2
    return total


def split(values):
    high = values.astype(BF16)
    return high, (values - high.astype(F32)).astype(BF16)


class Sizes:
    def __init__(self, mesh, shapes):
        self.segs, self.parts = mesh.shape["seg"], mesh.shape["tensor"]
        inputs, w_attn, w_fc, w_keys = shapes
        self.rows, self.width = inputs[1] // self.segs, inputs[2]
        self.chunk = self.rows // self.parts
        self.mems = self.segs * MEM
        self.heads_w = w_attn[3] // self.parts
        self.heads = self.heads_w // HEAD_DIM
        self.units = w_fc[2] // self.parts
        self.keys = w_keys[3]
        self.keys_w = self.keys // self.parts
        self.phi = 2 * self.keys * NU
        self.val_w = self.width // self.parts
        self.cut = self.width // self.segs
        self.cut_pad = -(-self.cut // 16) * 16
        self.pieces = 4 if self.cut_pad % 64 == 0 else 1
        self.sems = 120 + 48 * self.parts + 2 * self.segs * (self.parts + 16)


def scratch_of(z):
    S, T, R, D, C, M = z.segs, z.parts, z.rows, z.width, z.chunk, z.mems
    bf = lambda *d: pltpu.VMEM(d, BF16)
    fl = lambda *d: pltpu.VMEM(d, F32)
    return dict(
        gains=fl(2, 2, D), shifts=fl(2, 2, D), w_attn=bf(2, 3, z.heads_w, D), attn_bias=fl(2, 2, z.heads_w),
        w_out=bf(2, z.heads_w, D), out_biases=fl(2, 2, D), w_fc=bf(2, D, z.units), fc_bias=fl(2, 1, z.units),
        w_proj=bf(2, z.units, D), w_keys=bf(2, 2, z.keys, D), w_value=bf(2, z.val_w, D),
        xfull=bf(2, R, D), gfull=bf(2, R, D), mem_rows=bf(2, M, D),
        keyb=bf(2, M, z.keys), phik=bf(2, M, z.phi), kdots=fl(2, M, M), vpart=fl(2, M, z.val_w),
        upart=fl(2, M, z.val_w), uall=bf(2, T, M, z.val_w), qmem=bf(2, C, z.keys), phiq=bf(2, C, z.phi),
        qdots=fl(2, C, M), recall=fl(2, C, D), hidden=fl(2, C, D), normed=bf(2, R, D), qkv=bf(2, 3, R, z.heads_w),
        probs=fl(2, z.heads, R, R), mixed=bf(2, R, z.heads_w), after=fl(2, C, D), normed_mlp=bf(2, R, D),
        slope=fl(2, R, z.units), act=bf(2, R, z.units), rs_src=bf(7, R, D), rs_own=fl(R, D), q_src=bf(R, z.keys_w), q_parts=bf(T, C, z.keys_w), k_parts=bf(T, M, z.keys_w), rs_dst=bf(7, T - 1, C, D),
        low2=bf(2, R, D), dpre=bf(R, z.units), dqkv=bf(3, R, z.heads_w),
        x1_src=fl(2, T, M, z.val_w), x1_dst=fl(2, T - 1, M, z.val_w), x1_mid=fl(2, M, z.val_w), x1_far=fl(2, max(S - 1, 1), M, z.val_w),
        x2_src=fl(2, T, M, z.keys_w), x2_dst=fl(2, T - 1, M, z.keys_w), x2_mid=fl(2, M, z.keys_w), x2_far=fl(2, max(S - 1, 1), M, z.keys_w), x4_src=fl(2, T, M, z.keys_w), x4_dst=fl(2, T - 1, M, z.keys_w), ksolve=fl(M, z.keys), dk_direct=fl(M, z.keys_w),
        dq_src=bf(2, T, C, z.keys_w), dq_all=bf(2, R, z.keys_w), dv=bf(M, z.val_w), vgrad=fl(M, z.val_w),
        x3_src=bf(2, MEM, D), x3_dst=bf(2, T - 1, MEM, D), final=bf(R, D), tmp=fl(C, D),
        grad_p=bf(2, S, z.cut_pad, z.units), grad_c=bf(2, S, z.cut_pad, z.units), grad_qk=bf(2, S, z.cut_pad, 2 * z.heads_w),
        grad_vo=bf(2, S, z.cut_pad, 2 * z.heads_w), grad_q=bf(2, S, z.cut_pad, z.keys_w),
        pair_f=bf(2, S, z.cut_pad, z.units), pair_a=bf(2, S, z.cut_pad, 2 * z.heads_w), pair_q=bf(2, S, z.cut_pad, z.keys_w),
        far_p=bf(S, z.cut_pad, z.units), far_c=bf(S, z.cut_pad, z.units), far_qk=bf(S, z.cut_pad, 2 * z.heads_w),
        far_vo=bf(S, z.cut_pad, 2 * z.heads_w), far_q=bf(S, z.cut_pad, z.keys_w), dqk=bf(R, 2 * z.heads_w),
        mem_k=fl(2, D, z.keys_w), mem_v=fl(2, D, z.val_w), pair_k=fl(z.cut, z.keys_w), pair_v=fl(z.cut, z.val_w),
        small=fl(2, 16, D), pair_small=fl(16, D), part_small=fl(T, 8, D), seg_small=fl(S, 16, D),
        send=pltpu.SemaphoreType.DMA((z.sems,)), recv=pltpu.SemaphoreType.DMA((z.sems,)), load=pltpu.SemaphoreType.DMA((14, 2)),
        shard=pltpu.SemaphoreType.DMA((2, 2, T)),
    )


class Outer(NamedTuple):
    inputs: Any
    out_grad: Any
    item_lengths: Any
    norm_gains: Any
    norm_biases: Any
    w_attn_in: Any
    attn_bias_in: Any
    w_out_in: Any
    out_biases_in: Any
    w_fc_in: Any
    fc_bias_in: Any
    w_proj_in: Any
    w_keys_in: Any
    w_value_in: Any
    input_grad: Any
    gain_grads: Any
    shift_grads: Any
    attn_grads: Any
    abias_grads: Any
    out_grads: Any
    obias_grads: Any
    fc_grads: Any
    fcb_grads: Any
    proj_grads: Any
    mkey_grads: Any
    mvalue_grads: Any


def kernel(z, held_names, *refs):
    outer = len(Outer._fields)
    r = SimpleNamespace(**Outer(*refs[:outer])._asdict(), **dict(zip(held_names, refs[outer:])))
    S, T, R, D, C, M = z.segs, z.parts, z.rows, z.width, z.chunk, z.mems
    c, s, t = (lax.axis_index(a) for a in ("section", "seg", "tensor"))
    other = 1 - c
    tpeers = [xor_peer(t, i, T) for i in range(T)]
    to_seg = [lax.rem(s + i, S) for i in range(S)]
    own = pl.ds(pl.multiple_of(t * C, C), C)
    seg_rows = pl.ds(pl.multiple_of(s * MEM, MEM), MEM)
    used = [0]
    sent = []
    owed = {}

    def alloc(count):
        used[0] += count
        assert used[0] <= z.sems
        return used[0] - count

    def owe(copies):
        def wait():
            for copy in copies:
                copy.wait_recv()

        owed[id(copies)] = wait
        return id(copies)

    def wait_bytes(ref, semaphore):
        pltpu.make_async_copy(ref, ref, semaphore).wait()

    def remote(src, dst, index, device, recv=None):
        copy = pltpu.make_async_remote_copy(
            src_ref=src, dst_ref=dst, send_sem=r.send.at[index],
            recv_sem=r.recv.at[index] if recv is None else recv, device_id=device, device_id_type=MESH,
        )
        return copy

    def to_parts(src_of, dst):
        base = alloc(T - 1)
        copies = []
        for i in range(T - 1, 0, -1):
            copy = remote(src_of(tpeers[i]), dst(i), base + i - 1, (c, s, tpeers[i]))
            copy.start()
            copies.append(copy)
        sent.extend((copy, None) for copy in copies)
        return owe(copies)

    def to_segs(src_of, dst):
        base = alloc(S - 1)
        copies = [
            remote(src_of(to_seg[i]), dst(i), base + i - 1, (c, to_seg[i], t)) for i in range(1, S)
        ]
        for copy in copies:
            copy.start()
        sent.extend((copy, None) for copy in copies)
        return owe(copies)

    def arrive(key, pieces=0):
        pump(pieces)
        owed.pop(key)()

    queues = [], []

    def pump(pieces):
        for core, queue in enumerate(queues):
            now = queue[:pieces]
            del queue[:pieces]

            def start():
                for copy in now:
                    copy.start()

            if now:
                pl.when(c == core)(start)

    def wait_load(ref, layer):
        arrive((id(ref), layer))

    barrier = pltpu.get_barrier_semaphore()
    greeted = [(other, to_seg[i], t) for i in range(S)] + [(c, to_seg[i], tpeers[j]) for i in range(S) for j in range(T) if i or j]
    for device in greeted:
        pl.semaphore_signal(barrier, inc=1, device_id=device, device_id_type=MESH)

    loads = [
        (r.w_value, r.w_value_in.at[0]), (r.gains, r.norm_gains.at[0]), (r.shifts, r.norm_biases.at[0]),
        (r.attn_bias, r.attn_bias_in.at[0]), (r.out_biases, r.out_biases_in.at[0]), (r.w_attn, r.w_attn_in.at[0]), (r.w_out, r.w_out_in.at[0]), (r.w_fc, r.w_fc_in.at[0]),
        (r.w_proj, r.w_proj_in.at[0]), (r.fc_bias, r.fc_bias_in),
    ]
    input_copy = pltpu.make_async_copy(r.inputs.at[c], r.xfull.at[0], r.load.at[10, 0])
    input_copy.start()
    owed[0] = input_copy.wait
    def shard_rows(part):
        return pl.ds(pl.multiple_of(part * z.keys_w, 16), z.keys_w)

    for which in (0, 1):
        pltpu.make_async_copy(
            r.w_keys_in.at[0, which], r.w_keys.at[c, which, shard_rows(t)], r.shard.at[c, which, 0]
        ).start()
    def load_own(kinds):
        for kind in kinds:
            held, source = loads[kind]
            pltpu.make_async_copy(source, held.at[c], r.load.at[kind, c]).start()

    def load_other(kinds):
        for kind in kinds:
            held, source = loads[kind]
            copy = remote(source, held.at[c], pair_base + kind, (other, s, t), r.load.at[kind, c])
            copy.start()
            sent.append((copy, None))
            for layer in range(LAYERS):
                owed[id(held), layer] = functools.partial(wait_bytes, held.at[layer], r.load.at[kind, layer])

    early, middle = range(0, 5), range(5, 7)
    load_own(range(len(loads)))
    grad_copy = pltpu.make_async_copy(r.out_grad.at[c], r.gfull.at[1], r.load.at[11, 0])
    grad_copy.start()
    owed[1] = grad_copy.wait

    pl.semaphore_wait(barrier, len(greeted))

    first_rows = to_segs(
        lambda _: r.inputs.at[c, pl.ds(R - MEM, MEM)], lambda i: r.mem_rows.at[0, seg_rows]
    )

    def shard_wait(layer, which, i):
        wait_bytes(r.w_keys.at[layer, which, pl.ds(0, z.keys_w)], r.shard.at[layer, which, i])

    def peer_shards(core, layer, which):
        @pl.when(c == core)
        def _():
            for i in range(1, T):
                shard_wait(layer, which, i)

    def spread_shard(layer, which):
        base = alloc(T - 1)
        place = r.w_keys.at[layer, which, shard_rows(t)]
        copies = [
            remote(r.w_keys_in.at[0, which], place, base + i - 1, (c, s, tpeers[i]), r.shard.at[layer, which, i])
            for i in range(T - 1, 0, -1)
        ]

        @pl.when(c == layer)
        def _():
            for copy in copies:
                copy.start()

        sent.extend((copy, c == layer) for copy in copies)
        owed[11, layer, which] = functools.partial(peer_shards, layer, layer, which)

    def forward_shard(layer, which):
        arrive((11, layer, which))
        base = alloc(T - 1)
        copies = []
        for i in range(1, T):
            place = r.w_keys.at[layer, which, shard_rows(tpeers[i])]
            copies.append(remote(place, place, base + i - 1, (other, s, t), r.shard.at[layer, which, i]))

        @pl.when(c == layer)
        def _():
            for copy in copies:
                copy.start()

        sent.extend((copy, c == layer) for copy in copies)
        owed[12, layer, which] = functools.partial(peer_shards, 1 - layer, layer, which)

    base = alloc(2)
    for which in (0, 1):
        copy = remote(
            r.w_keys_in.at[0, which], r.w_keys.at[c, which, shard_rows(t)], base + which, (other, s, t), r.shard.at[c, which, 0]
        )
        copy.start()
        sent.append((copy, None))
        for layer in range(LAYERS):
            owed[10, layer, which] = functools.partial(shard_wait, layer, which, 0)
    pair_base = alloc(len(loads))
    load_other(early)

    row_seg = lax.broadcasted_iota(jnp.int32, (M, 1), 0) // MEM
    col_seg = lax.broadcasted_iota(jnp.int32, (1, M), 1) // MEM
    row_item, col_item, own_item = jnp.zeros((M, 1), jnp.int32), jnp.zeros((1, M), jnp.int32), 0
    begin = 0
    for i in range(r.item_lengths.shape[1]):
        length = r.item_lengths[c, i]
        there = jnp.where(length > 0, begin, S)
        row_item = row_item + (row_seg >= there).astype(jnp.int32)
        col_item = col_item + (col_seg >= there).astype(jnp.int32)
        own_item = own_item + jnp.where(s >= there, 1, 0)
        begin = begin + length
    key_mask = jnp.where((row_item == col_item) & (row_seg > col_seg), 1.0, 0.0)
    row_mask = jnp.where((col_item == own_item) & (col_seg < s), 1.0, 0.0)
    lane_head = lax.broadcasted_iota(jnp.int32, (1, z.heads_w), 1) // HEAD_DIM
    head_rows = [(lane_head == h).astype(F32).astype(BF16) for h in range(z.heads)]
    rs_count = [0]

    def reduce_rows(partial):
        k = rs_count[0]
        rs_count[0] += 1
        r.rs_own[...] = partial
        r.rs_src[k] = partial.astype(BF16)
        copies = to_parts(
            lambda peer: r.rs_src.at[k, pl.ds(pl.multiple_of(peer * C, C), C)], lambda i: r.rs_dst.at[k, i - 1]
        )

        def finish():
            arrive(copies, 2)
            total = r.rs_own[own, :]
            for i in range(T - 1):
                total = total + r.rs_dst[k, i].astype(F32)
            return total

        return finish

    def share_rows(ref, layer):
        return to_parts(lambda _: ref.at[layer, own], lambda i: ref.at[layer, own])

    def forward(l):
        own_shard = shard_rows(t)
        if l == 0:
            arrive(0)
            arrive((10, 0, 0))
            r.q_src[...] = dot_nt(r.xfull[0], r.w_keys[0, 0, own_shard, :]).astype(BF16)
            r.q_parts[t] = r.q_src[own, :]
            query_step = to_parts(
                lambda peer: r.q_src.at[pl.ds(pl.multiple_of(peer * C, C), C)], lambda i: r.q_parts.at[t]
            )
            r.mem_rows[0, seg_rows, :] = r.xfull[0, R - MEM :, :]
            arrive((10, 0, 1))
            arrive(first_rows)
            mems = r.mem_rows[0]
            r.k_parts[t] = dot_nt(mems, r.w_keys[0, 1, own_shard, :]).astype(BF16)
            key_step = to_parts(lambda _: r.k_parts.at[t], lambda i: r.k_parts.at[t])
            load_other(middle)
            arrive(query_step)
            queries_mem = jnp.concatenate([r.q_parts[u] for u in range(T)], axis=1)
        else:
            for which in (0, 1):
                arrive((10, 1, which))
                arrive((12, 1, which))
            queries_mem = dot_nt(r.xfull[1, own, :], r.w_keys[1, 0]).astype(BF16)
        x = r.xfull[l, own, :]
        r.qmem[l] = queries_mem
        phi_query = feature_map(queries_mem.astype(F32)).astype(BF16)
        r.phiq[l] = phi_query
        wait_load(r.w_value, l)
        if l == 1:
            arrive(4)
            mems = r.mem_rows[1]
        value_part = dot_nt(mems, r.w_value[l])
        r.vpart[l] = value_part
        r.upart[l] = value_part
        if l == 0:
            arrive(key_step)
            keys = jnp.concatenate([r.k_parts[u] for u in range(T)], axis=1)
        else:
            keys = dot_nt(mems, r.w_keys[1, 1]).astype(BF16)
        r.keyb[l] = keys
        phi_key = feature_map(keys.astype(F32)).astype(BF16)
        r.phik[l] = phi_key
        key_dots = dot_nt(phi_key, phi_key) * key_mask
        r.kdots[l] = key_dots
        key_den = 1.0 + jnp.sum(key_dots, axis=1, keepdims=True)
        for k in range(1, S):
            rows = slice(k * MEM, (k + 1) * MEM)
            read = dot_nn(key_dots[rows].astype(BF16), r.upart[l].astype(BF16)) / key_den[rows]
            r.upart[l, rows, :] = value_part[rows] - read
        r.uall[l, t] = r.upart[l].astype(BF16)
        solved = to_parts(lambda _: r.uall.at[l, t], lambda i: r.uall.at[l, t])
        if l == 0:
            spread_shard(1, 1)
        else:
            spread_shard(0, 0)
        query_dots = dot_nt(phi_query, phi_key) * row_mask
        r.qdots[l] = query_dots
        query_den = 1.0 + jnp.sum(query_dots, axis=1, keepdims=True)
        for ref in (r.gains, r.shifts, r.attn_bias, r.out_biases):
            wait_load(ref, l)
        arrive(solved)
        high, low = split(query_dots)
        recall = [dot_nn(high, r.uall[l, u]) + dot_nn(low, r.uall[l, u]) for u in range(T)]
        recall = jnp.concatenate(recall, axis=1) / query_den
        r.recall[l] = recall
        hidden = x.astype(F32) + recall.astype(BF16).astype(F32)
        r.hidden[l] = hidden
        unit, _ = norm_rows(hidden)
        r.normed[l, own, :] = (unit * r.gains[l, 0:1] + r.shifts[l, 0:1]).astype(BF16)
        shared = share_rows(r.normed, l)
        if l == 0:
            load_other([9, 7])
        wait_load(r.w_attn, l)
        wait_load(r.w_out, l)
        arrive(shared)
        if l == 0:
            spread_shard(1, 0)
        else:
            spread_shard(0, 1)
        normed = r.normed[l]
        queries = (dot_nt(normed, r.w_attn[l, 0]) + r.attn_bias[l, 0:1]).astype(BF16)
        key_heads = dot_nt(normed, r.w_attn[l, 1]).astype(BF16)
        values = (dot_nt(normed, r.w_attn[l, 2]) + r.attn_bias[l, 1:2]).astype(BF16)
        r.qkv[l, 0] = queries
        r.qkv[l, 1] = key_heads
        r.qkv[l, 2] = values
        causal = lax.broadcasted_iota(jnp.int32, (R, R), 0) >= lax.broadcasted_iota(jnp.int32, (R, R), 1)
        mixed = jnp.zeros((R, z.heads_w), F32)
        for h in range(z.heads):
            scores = dot_nt(queries, key_heads * head_rows[h]) * HEAD_DIM ** (-0.5)
            scores = jnp.where(causal, scores, -jnp.inf)
            heights = jnp.exp(scores - jnp.max(scores, axis=1, keepdims=True))
            probs = heights * (1.0 / jnp.sum(heights, axis=1, keepdims=True))
            r.probs[l, h] = probs
            mixed = mixed + dot_nn(probs.astype(BF16), values * head_rows[h])
        mixed = mixed.astype(BF16)
        r.mixed[l] = mixed
        finish = reduce_rows(dot_nn(mixed, r.w_out[l]))
        if l == 0:
            load_other([8])
        after = r.hidden[l] + finish() + r.out_biases[l, 0:1]
        r.after[l] = after
        unit, _ = norm_rows(after)
        r.normed_mlp[l, own, :] = (unit * r.gains[l, 1:2] + r.shifts[l, 1:2]).astype(BF16)
        shared = share_rows(r.normed_mlp, l)
        wait_load(r.w_fc, l)
        wait_load(r.fc_bias, l)
        wait_load(r.w_proj, l)
        if l == 0:
            forward_shard(1, 1)
            forward_shard(1, 0)
        arrive(shared)
        row_step = share_rows(r.xfull, 1) if l == 1 else None
        pre = dot_nn(r.normed_mlp[l], r.w_fc[l]) + r.fc_bias[l]
        activation, slope = gelu_and_slope(pre)
        activation = activation.astype(BF16)
        r.act[l] = activation
        r.slope[l] = slope
        if l == 0:
            finish = reduce_rows(dot_nn(activation, r.w_proj[l]))
            output = r.after[l] + finish() + r.out_biases[l, 1:2]
            r.xfull[1, own, :] = output.astype(BF16)
            base, places = alloc(S), alloc(S * T)
            last = r.xfull.at[1, pl.ds(R - MEM, MEM)]

            @pl.when(t == T - 1)
            def _():
                r.mem_rows[1, seg_rows, :] = r.xfull[1, R - MEM :, :]
                for i in range(S - 1, -1, -1):
                    for j in range(1 if i == 0 else 0, T):
                        copy = pltpu.make_async_remote_copy(
                            src_ref=last, dst_ref=r.mem_rows.at[1, seg_rows], send_sem=r.send.at[places + i * T + j],
                            recv_sem=r.recv.at[base + i], device_id=(c, to_seg[i], tpeers[j]), device_id_type=MESH,
                        )
                        copy.start()

            def wait_rows(i):
                wait_bytes(r.mem_rows.at[1, pl.ds(0, MEM)], r.recv.at[base + i])

            def wait_all():
                pl.when(t != T - 1)(functools.partial(wait_rows, 0))
                for i in range(1, S):
                    wait_rows(i)

            owed[4] = wait_all

            def drain():
                @pl.when(t == T - 1)
                def _():
                    for i in range(S):
                        for j in range(1 if i == 0 else 0, T):
                            wait_bytes(last, r.send.at[places + i * T + j])

            sent.append((drain, drain))
        return row_step

    fam_p, fam_c = (r.grad_p, r.pair_f, r.far_p, 0), (r.grad_c, r.pair_f, r.far_c, 1)
    fam_qk, fam_vo = (r.grad_qk, r.pair_a, r.far_qk, 0), (r.grad_vo, r.pair_a, r.far_vo, 1)
    fam_q = (r.grad_q, r.pair_q, r.far_q, None)

    def blocks_of(first_row, count):
        row, pieces = first_row, []
        while row < first_row + count:
            block, inside = row // z.cut, row % z.cut
            size = min(z.cut - inside, first_row + count - row)
            pieces.append((block, inside, row - first_row, size))
            row += size
        return pieces

    def weight_grad(l, family, *pairs):
        stripe = min(256, D)
        for k in range(0, D, stripe):
            parts = [dot_tn(left[:, k : k + stripe], right).astype(BF16) for left, right in pairs]
            grad = parts[0] if len(parts) == 1 else jnp.concatenate(parts, axis=1)
            for block, inside, row, size in blocks_of(k, stripe):
                family[0][l, block, inside : inside + size, :] = grad[row : row + size]

    def pair_send(src, dst):
        index = alloc(1)
        return remote(src, dst, index, (other, s, t))

    def adder_of(l, family):
        return l if family[3] is None else family[3]

    def hand_over(l, family):
        grad, pair, _, _ = family
        adder = adder_of(l, family)
        copy = pair_send(grad.at[l], pair.at[l])
        pl.when(c != adder)(copy.start)
        sent.append((copy, c != adder))
        return owe_owner(adder, [copy])

    def owe_owner(l, copies):
        def wait():
            @pl.when(c == l)
            def _():
                for copy in copies:
                    copy.wait_recv()

        owed[id(copies)] = wait
        return id(copies)

    def add_pair(l, family, key):
        grad, pair, _, _ = family
        arrive(key)

        @pl.when(c == adder_of(l, family))
        def _():
            @pl.loop(0, S)
            def _(j):
                grad[l, j] = (grad[l, j].astype(F32) + pair[l, j].astype(F32)).astype(BF16)

    def spread(l, family):
        grad, _, far, _ = family
        adder = adder_of(l, family)
        base = alloc(S)
        near = adder == l

        @pl.when(c == adder)
        def _():
            if near:
                far[0] = grad[l, s]
            else:
                remote(grad.at[l, s], far.at[0], base, (other, s, t)).start()

        size = z.cut_pad if z.cut_pad * grad.shape[3] <= 20000 else z.cut_pad // z.pieces
        for i in range(S - 1, 0, -1):
            for first in range(0, z.cut_pad, size):
                piece = pl.ds(first, size)
                copy = remote(grad.at[l, to_seg[i], piece], far.at[i, piece], base + i, (l, to_seg[i], t))
                queues[adder].append(copy)
        pump(1000)

        def wait():
            @pl.when(c == l)
            def _():
                for i in range(1 if near else 0, S):
                    wait_bytes(far.at[i], r.recv.at[base + i])

        def drain():
            @pl.when(c == adder)
            def _():
                for i in range(1 if near else 0, S):
                    wait_bytes(far.at[i], r.send.at[base + i])

        owed[id(far), l] = wait
        sent.append((drain, drain))

    def owe_small(l):
        copy = pair_send(r.small.at[l], r.pair_small)
        pl.when(c != l)(copy.start)
        sent.append((copy, c != l))
        return owe_owner(l, [copy])

    def owner_copies(l, copies):
        @pl.when(c == l)
        def _():
            for copy in copies:
                copy.start()

        sent.extend((copy, c == l) for copy in copies)
        return owe_owner(l, copies)

    def small_parts(l, key):
        arrive(key)

        @pl.when(c == l)
        def _():
            r.seg_small[0] = r.small[l] + r.pair_small[...]
            r.part_small[0] = r.seg_small[0, 0:8, :]

        base = alloc(T - 1)
        return owner_copies(
            l, [remote(r.part_small.at[0], r.part_small.at[i], base + i - 1, (c, s, tpeers[i])) for i in range(1, T)]
        )

    def small_segs(l, key):
        arrive(key)

        @pl.when(c == l)
        def _():
            total = r.part_small[0]
            for i in range(1, T):
                total = total + r.part_small[i]
            r.seg_small[0, 0:8, :] = total

        base = alloc(S - 1)
        return owner_copies(
            l, [remote(r.seg_small.at[0], r.seg_small.at[i], base + i - 1, (c, to_seg[i], t)) for i in range(1, S)]
        )

    def backward(l):
        if l == 1:
            arrive(1)
        grad_low = r.gfull[l]
        pre_grad = (r.slope[l] * dot_nt(grad_low, r.w_proj[l])).astype(BF16)
        r.dpre[...] = pre_grad
        finish = reduce_rows(dot_nt(pre_grad, r.w_fc[l]))
        own_grad = r.gfull[l, own, :].astype(F32)

        weight_grad(l, fam_p, (r.gfull.at[l], r.act[l]))
        pair_p = hand_over(l, fam_p)
        weight_grad(l, fam_c, (r.normed_mlp.at[l], r.dpre[...]))
        pair_c = hand_over(l, fam_c)
        r.small[l, 8:9, :] = jnp.sum(r.dpre[...].astype(F32), axis=0, keepdims=True)
        if l == 1:
            forward_shard(0, 0)
            forward_shard(0, 1)
        add_pair(l, fam_p, pair_p)
        spread(l, fam_p)
        after_part, gain_mlp, shift_mlp = norm_back(r.after[l], r.gains[l, 1:2], finish())
        after_grad = own_grad + after_part
        r.tmp[...] = after_grad
        r.low2[l, own, :] = after_grad.astype(BF16)
        shared = share_rows(r.low2, l)
        r.small[l, 1:2, :] = gain_mlp
        r.small[l, 3:4, :] = shift_mlp
        r.small[l, 4:5, :] = jnp.sum(after_grad, axis=0, keepdims=True)
        r.small[l, 5:6, :] = jnp.sum(own_grad, axis=0, keepdims=True)
        add_pair(l, fam_c, pair_c)
        if l == 0:
            spread(l, fam_c)
        arrive(shared, 2)
        pump(2)
        after_low = r.low2[l]
        mixed_grad = dot_nt(after_low, r.w_out[l]).astype(BF16)
        queries, key_heads, values = r.qkv[l, 0], r.qkv[l, 1], r.qkv[l, 2]
        q_grad = k_grad = v_grad = jnp.zeros((R, z.heads_w), F32)
        for h in range(z.heads):
            probs = r.probs[l, h]
            mixed_here = mixed_grad * head_rows[h]
            probs_grad = dot_nt(mixed_here, values)
            delta = jnp.sum(probs_grad * probs, axis=1, keepdims=True)
            score_grad = (probs * (probs_grad - delta)).astype(BF16)
            q_grad = q_grad + dot_nn(score_grad, key_heads * head_rows[h])
            k_grad = k_grad + dot_tn(score_grad, queries * head_rows[h])
            v_grad = v_grad + dot_tn(probs.astype(BF16), mixed_here)
        scale = HEAD_DIM ** (-0.5)
        r.dqkv[0] = (q_grad * scale).astype(BF16)
        r.dqkv[1] = (k_grad * scale).astype(BF16)
        r.dqkv[2] = v_grad.astype(BF16)
        r.dqk[...] = jnp.concatenate([r.dqkv[0], r.dqkv[1]], axis=1)
        finish = reduce_rows(sum(dot_nn(r.dqkv[i], r.w_attn[l, i]) for i in range(3)))

        weight_grad(l, fam_qk, (r.normed.at[l], r.dqk[...]))
        pair_qk = hand_over(l, fam_qk)
        weight_grad(l, fam_vo, (r.normed.at[l], r.dqkv[2]), (r.low2.at[l], r.mixed[l]))
        pair_vo = hand_over(l, fam_vo)
        for row, i in ((9, 0), (10, 2)):
            r.small[l, row : row + 1, : z.heads_w] = jnp.sum(r.dqkv[i].astype(F32), axis=0, keepdims=True)
        hidden_part, gain_attn, shift_attn = norm_back(r.hidden[l], r.gains[l, 0:1], finish())
        hidden_grad = r.tmp[...] + hidden_part
        r.tmp[...] = hidden_grad
        r.small[l, 0:1, :] = gain_attn
        r.small[l, 2:3, :] = shift_attn
        small_key = owe_small(l)
        query_den = 1.0 + jnp.sum(r.qdots[l], axis=1, keepdims=True)
        high, low = split(hidden_grad / query_den)
        den_grad = -jnp.sum((hidden_grad / query_den) * r.recall[l], axis=1, keepdims=True)
        highs = [high[:, u * z.val_w : (u + 1) * z.val_w] for u in range(T)]
        lows = [low[:, u * z.val_w : (u + 1) * z.val_w] for u in range(T)]
        dots_high, dots_low = split(r.qdots[l])
        for u in range(T):
            r.x1_src[l, u] = dot_tn(dots_high, highs[u]) + dot_tn(dots_high, lows[u]) + dot_tn(dots_low, highs[u])
        value_step = to_parts(lambda peer: r.x1_src.at[l, peer], lambda i: r.x1_dst.at[l, i - 1])
        dots_grad = sum(dot_nt(highs[u], r.uall[l, u]) + dot_nt(lows[u], r.uall[l, u]) for u in range(T)) + den_grad
        dots_grad = (dots_grad * row_mask).astype(BF16)
        key_direct = feature_map_back(r.keyb[l].astype(F32), dot_tn(dots_grad, r.phiq[l]))
        for u in range(T):
            r.x2_src[l, u] = key_direct[:, u * z.keys_w : (u + 1) * z.keys_w]
        key_step = to_parts(lambda peer: r.x2_src.at[l, peer], lambda i: r.x2_dst.at[l, i - 1])
        add_pair(l, fam_qk, pair_qk)
        add_pair(l, fam_vo, pair_vo)
        arrive(value_step, 2)
        r.x1_mid[l] = r.x1_src[l, t] + sum(r.x1_dst[l, i] for i in range(T - 1))
        value_step = to_segs(lambda _: r.x1_mid.at[l], lambda i: r.x1_far.at[l, i - 1])
        arrive(key_step)
        r.x2_mid[l] = r.x2_src[l, t] + sum(r.x2_dst[l, i] for i in range(T - 1))
        key_step = to_segs(lambda _: r.x2_mid.at[l], lambda i: r.x2_far.at[l, i - 1])
        pump(1)
        query_grad = feature_map_back(r.qmem[l].astype(F32), dot_nn(dots_grad, r.phik[l])).astype(BF16)
        for u in range(T):
            r.dq_src[l, u] = query_grad[:, u * z.keys_w : (u + 1) * z.keys_w]
        r.dq_all[l, own, :] = r.dq_src[l, t]
        query_step = to_parts(lambda peer: r.dq_src.at[l, peer], lambda i: r.dq_all.at[l, own])
        if l == 0:
            arrive((12, 0, 0))
            arrive((12, 0, 1))
        r.tmp[...] += dot_nn(query_grad, r.w_keys[l, 0])
        arrive(value_step, 1)
        direct = r.x1_mid[l] + sum(r.x1_far[l, i] for i in range(S - 1))
        arrive(key_step)
        small_key = small_parts(l, small_key)
        for family in (fam_c, fam_qk, fam_vo) if l == 1 else (fam_qk, fam_vo):
            spread(l, family)
        pump(4)
        key_dots = r.kdots[l]
        key_den = 1.0 + jnp.sum(key_dots, axis=1, keepdims=True)
        r.vgrad[...] = direct
        for k in range(S - 1, 0, -1):
            rows = slice(k * MEM, (k + 1) * MEM)
            back = -r.vgrad[rows, :] / key_den[rows]
            r.vgrad[...] += dot_tn(key_dots[rows].astype(BF16), back.astype(BF16))
        value_grad = r.vgrad[...]
        read = r.vpart[l] - r.upart[l]
        back = (-value_grad / key_den).astype(BF16)
        key_den_grad = -jnp.sum(back.astype(F32) * read, axis=1, keepdims=True)
        key_dots_grad = (dot_nt(back, r.upart[l].astype(BF16)) + key_den_grad) * key_mask
        both = (key_dots_grad + key_dots_grad.T).astype(BF16)
        key_solve = feature_map_back(r.keyb[l].astype(F32), dot_nn(both, r.phik[l]))
        r.ksolve[...] = key_solve
        r.dv[...] = value_grad.astype(BF16)
        r.dk_direct[...] = r.x2_mid[l] + sum(r.x2_far[l, i] for i in range(S - 1))
        tail = dot_nn(r.dv[seg_rows, :], r.w_value[l])
        tail = tail + dot_nn(r.dk_direct[seg_rows, :].astype(BF16), r.w_keys[l, 1, shard_rows(t), :])
        tail = tail + dot_nn(r.ksolve[seg_rows, :].astype(BF16), r.w_keys[l, 1])
        r.x3_src[l] = tail.astype(BF16)
        base, place = alloc(T - 1), alloc(1)

        for i in range(1, T):

            @pl.when(tpeers[i] == T - 1)
            def _():
                copy = pltpu.make_async_remote_copy(
                    src_ref=r.x3_src.at[l], dst_ref=r.x3_dst.at[l, i - 1], send_sem=r.send.at[place],
                    recv_sem=r.recv.at[base + i - 1], device_id=(c, s, tpeers[i]), device_id_type=MESH,
                )
                copy.start()

        def drain():
            @pl.when(t != T - 1)
            def _():
                wait_bytes(r.x3_src.at[l], r.send.at[place])

        sent.append((drain, drain))
        for u in range(T):
            r.x4_src[l, u] = key_solve[:, u * z.keys_w : (u + 1) * z.keys_w]
        solve_step = to_parts(lambda peer: r.x4_src.at[l, peer], lambda i: r.x4_dst.at[l, i - 1])
        pump(2)

        @pl.when(t == T - 1)
        def _():
            total = r.x3_src[l].astype(F32)
            for i in range(T - 1):
                wait_bytes(r.x3_dst.at[l, i], r.recv.at[base + i])
                total = total + r.x3_dst[l, i].astype(F32)
            r.tmp[C - MEM :, :] += total

        target = r.gfull.at[0] if l == 1 else r.final
        target[own, :] = r.tmp[...].astype(BF16)
        rows_step = to_parts(lambda _: target.at[own], lambda i: target.at[own])
        small_key = small_segs(l, small_key)
        pump(4)
        arrive(query_step)
        if l == 1:
            arrive(row_step)
        weight_grad(l, fam_q, (r.xfull.at[l], r.dq_all[l]))
        pair_q = hand_over(l, fam_q)
        r.mem_v[l] = dot_tn(r.mem_rows[l], r.dv[...])
        arrive(solve_step)
        key_grad = r.dk_direct[...] + r.x4_src[l, t] + sum(r.x4_dst[l, i] for i in range(T - 1))
        r.mem_k[l] = dot_tn(r.mem_rows[l], key_grad.astype(BF16))
        rows = pl.ds(pl.multiple_of(s * z.cut, 8), z.cut)
        mem_copies = [pair_send(r.mem_k.at[l, rows], r.pair_k), pair_send(r.mem_v.at[l, rows], r.pair_v)]

        @pl.when(c != l)
        def _():
            for copy in mem_copies:
                copy.start()

        sent.extend((copy, c != l) for copy in mem_copies)
        mem_key = owe_owner(l, mem_copies)
        add_pair(l, fam_q, pair_q)
        spread(l, fam_q)
        if l == 0:
            pump(100)
        arrive(rows_step)
        return mem_key, small_key

    forward(0)
    row_step = forward(1)
    for l in range(LAYERS):
        r.small[l] = jnp.zeros((16, D), F32)
    mem_key1, small_key1 = backward(1)
    mem_key0, small_key0 = backward(0)

    r.input_grad[0] = r.final[...]
    l = c

    arrive(mem_key1)
    arrive(mem_key0)
    rows = pl.ds(pl.multiple_of(s * z.cut, 8), z.cut)
    r.mkey_grads[0, 1] = r.mem_k[l, rows, :] + r.pair_k[...]
    r.mvalue_grads[0] = r.mem_v[l, rows, :] + r.pair_v[...]

    def far_sum(far):
        arrive((id(far), 1))
        arrive((id(far), 0))
        return sum(far[i, : z.cut, :].astype(F32) for i in range(S))

    r.proj_grads[0] = far_sum(r.far_p)
    r.fc_grads[0] = far_sum(r.far_c)
    both = far_sum(r.far_qk)
    r.attn_grads[0, 0] = both[:, : z.heads_w]
    r.attn_grads[0, 1] = both[:, z.heads_w :]
    both = far_sum(r.far_vo)
    r.attn_grads[0, 2] = both[:, : z.heads_w]
    r.out_grads[0] = both[:, z.heads_w :].T
    r.mkey_grads[0, 0] = far_sum(r.far_q)
    arrive(small_key1)
    arrive(small_key0)
    total = r.seg_small[0]
    for i in range(1, S):
        total = total + r.seg_small[i]
    r.gain_grads[0] = total[0:2]
    r.shift_grads[0] = total[2:4]
    r.obias_grads[0] = total[4:6]
    r.fcb_grads[...] = total[8:9, : z.units]
    r.abias_grads[0] = total[9:11, : z.heads_w]

    assert not owed
    for copy, when in sent:
        if when is copy:
            copy()
        elif when is None:
            copy.wait_send()
        else:
            pl.when(when)(copy.wait_send)


def hand_out(*refs):
    count = len(refs) // 2
    for source, target in zip(refs[:count], refs[count:]):
        target[...] = source[...]


def item_ids(lengths):
    item_ends = jnp.cumsum(lengths, axis=-1)
    item_begins = item_ends - lengths
    places = jnp.arange(lengths.shape[-1], dtype=jnp.int32)
    matches = (item_begins[:, :, None] == places[None, None, :]) & (lengths[:, :, None] > 0)
    return jnp.cumsum(jnp.sum(matches.astype(jnp.int32), axis=1), axis=-1)


def reach_mask(lengths):
    ids = item_ids(lengths)
    places = jnp.arange(lengths.shape[-1])
    earlier = places[:, None] > places[None, :]
    same = (ids[:, :, None] == ids[:, None, :]) & earlier[None]
    return jnp.repeat(jnp.repeat(same.astype(F32), MEM, axis=1), MEM, axis=2)


def gather_rows(values, axis):
    return lax.all_gather(values, axis, axis=0, tiled=True)


def scatter_rows(values, axis):
    peers = lax.axis_size(axis)
    pieces = values.astype(BF16).reshape(peers, values.shape[0] // peers, values.shape[1])
    got = lax.all_to_all(pieces, axis, 0, 0, tiled=True)
    return jnp.sum(got.astype(F32), axis=0)


def scatter_columns(values, axis):
    peers = lax.axis_size(axis)
    rows = values.shape[0]
    pieces = values.reshape(rows, peers, -1).transpose(1, 0, 2)
    got = lax.all_to_all(pieces.astype(BF16), axis, 0, 0, tiled=True)
    return jnp.sum(got.astype(F32), axis=0)


def solve_forward(key_dots, key_den, value_mem):
    segments = key_dots.shape[0] // MEM
    solved = value_mem
    for s in range(1, segments):
        rows = slice(s * MEM, (s + 1) * MEM)
        read = dot_nn(key_dots[rows].astype(BF16), solved.astype(BF16)) / key_den[rows]
        solved = solved.at[rows].add(-read)
    return solved


def solve_backward(key_dots, key_den, direct):
    segments = key_dots.shape[0] // MEM
    total = direct
    for s in range(segments - 1, 0, -1):
        rows = slice(s * MEM, (s + 1) * MEM)
        back = -total[rows] / key_den[rows]
        total = total + dot_tn(key_dots[rows].astype(BF16), back.astype(BF16))
    return total


def layer_forward(own_rows, mem_rows, mask, place, params):
    gains, shifts, w_attn, attn_bias, w_out, out_biases, w_fc, fc_bias, w_proj, w_q, w_k, w_v = params
    seg, _ = place
    own_mask = lax.dynamic_slice_in_dim(mask, seg * MEM, 1, 0)
    key_mem = dot_nn(mem_rows, w_k).astype(BF16)
    phi_key = feature_map(key_mem.astype(F32), jnp.roll).astype(BF16)
    key_dots = dot_nt(phi_key, phi_key) * mask
    key_den = 1.0 + jnp.sum(key_dots, axis=1, keepdims=True)
    value_part = dot_nn(mem_rows, w_v)
    solved_part = solve_forward(key_dots, key_den, value_part)
    solved = lax.all_gather(solved_part.astype(BF16), "tensor", axis=1, tiled=True)
    query_mem = dot_nn(own_rows, w_q).astype(BF16)
    phi_query = feature_map(query_mem.astype(F32), jnp.roll).astype(BF16)
    query_dots = dot_nt(phi_query, phi_key) * own_mask
    query_den = 1.0 + jnp.sum(query_dots, axis=1, keepdims=True)
    recall = dot_nn(query_dots.astype(BF16), solved) / query_den
    hidden = own_rows.astype(F32) + recall.astype(BF16).astype(F32)
    unit, _ = norm_rows(hidden)
    normed = gather_rows((unit * gains[0] + shifts[0]).astype(BF16), "tensor")
    queries = (dot_nn(normed, w_attn[0]) + attn_bias[0]).astype(BF16)
    key_heads = dot_nn(normed, w_attn[1]).astype(BF16)
    values = (dot_nn(normed, w_attn[2]) + attn_bias[1]).astype(BF16)
    rows = normed.shape[0]
    causal = jnp.arange(rows)[:, None] >= jnp.arange(rows)[None, :]
    probs, mixed = [], []
    for h in range(queries.shape[1] // HEAD_DIM):
        cols = slice(h * HEAD_DIM, (h + 1) * HEAD_DIM)
        scores = dot_nt(queries[:, cols], key_heads[:, cols]) * HEAD_DIM ** (-0.5)
        scores = jnp.where(causal, scores, -jnp.inf)
        heights = jnp.exp(scores - jnp.max(scores, axis=1, keepdims=True))
        probs.append(heights / jnp.sum(heights, axis=1, keepdims=True))
        mixed.append(dot_nn(probs[-1].astype(BF16), values[:, cols]).astype(BF16))
    mixed = jnp.concatenate(mixed, axis=1)
    after = hidden + scatter_rows(dot_nn(mixed, w_out), "tensor") + out_biases[0]
    unit, _ = norm_rows(after)
    normed_mlp = gather_rows((unit * gains[1] + shifts[1]).astype(BF16), "tensor")
    pre = dot_nn(normed_mlp, w_fc) + fc_bias
    activation, slope = gelu_and_slope(pre)
    activation = activation.astype(BF16)
    output = after + scatter_rows(dot_nn(activation, w_proj), "tensor") + out_biases[1]
    kept = (
        own_rows, mem_rows, key_mem, phi_key, key_dots, key_den, value_part, solved_part, solved, query_mem,
        phi_query, query_dots, query_den, recall, hidden, normed, queries, key_heads, values, probs, mixed,
        after, normed_mlp, slope, activation,
    )
    return output, kept


def layer_backward(own_grad, kept, mask, place, params):
    gains, shifts, w_attn, attn_bias, w_out, out_biases, w_fc, fc_bias, w_proj, w_q, w_k, w_v = params
    (
        own_rows, mem_rows, key_mem, phi_key, key_dots, key_den, value_part, solved_part, solved, query_mem,
        phi_query, query_dots, query_den, recall, hidden, normed, queries, key_heads, values, probs, mixed,
        after, normed_mlp, slope, activation,
    ) = kept
    seg, part = place
    own_mask = lax.dynamic_slice_in_dim(mask, seg * MEM, 1, 0)
    grad_low = gather_rows(own_grad.astype(BF16), "tensor")
    pre_grad = (slope * dot_nt(grad_low, w_proj)).astype(BF16)
    proj_grad = dot_tn(activation, grad_low)
    fc_bias_grad = jnp.sum(pre_grad.astype(F32), axis=0)
    fc_grad = dot_tn(normed_mlp, pre_grad)
    after_part, gain_mlp, shift_mlp = norm_back(
        after, gains[1:2], scatter_rows(dot_nt(pre_grad, w_fc), "tensor")
    )
    after_grad = own_grad + after_part
    after_low = gather_rows(after_grad.astype(BF16), "tensor")
    out_grad = dot_tn(mixed, after_low)
    mixed_grad = dot_nt(after_low, w_out).astype(BF16)
    q_grads, k_grads, v_grads = [], [], []
    for h in range(queries.shape[1] // HEAD_DIM):
        cols = slice(h * HEAD_DIM, (h + 1) * HEAD_DIM)
        probs_grad = dot_nt(mixed_grad[:, cols], values[:, cols])
        delta = jnp.sum(probs_grad * probs[h], axis=1, keepdims=True)
        score_grad = (probs[h] * (probs_grad - delta)).astype(BF16)
        q_grads.append((dot_nn(score_grad, key_heads[:, cols]) * HEAD_DIM ** (-0.5)).astype(BF16))
        k_grads.append((dot_tn(score_grad, queries[:, cols]) * HEAD_DIM ** (-0.5)).astype(BF16))
        v_grads.append(dot_tn(probs[h].astype(BF16), mixed_grad[:, cols]).astype(BF16))
    three = [jnp.concatenate(g, axis=1) for g in (q_grads, k_grads, v_grads)]
    attn_bias_grad = jnp.stack([jnp.sum(three[i].astype(F32), axis=0) for i in (0, 2)])
    attn_grad = jnp.stack([dot_tn(normed, g) for g in three])
    normed_part = sum(dot_nt(g, w_attn[i]) for i, g in enumerate(three))
    hidden_part, gain_attn, shift_attn = norm_back(
        hidden, gains[0:1], scatter_rows(normed_part, "tensor")
    )
    hidden_grad = after_grad + hidden_part
    num_grad = (hidden_grad / query_den).astype(BF16)
    den_grad = -jnp.sum(hidden_grad * recall, axis=1, keepdims=True) / query_den
    dots_grad = ((dot_nt(num_grad, solved) + den_grad) * own_mask).astype(BF16)
    query_grad = feature_map_back(query_mem.astype(F32), dot_nn(dots_grad, phi_key), jnp.roll).astype(BF16)
    solved_direct = dot_tn(query_dots.astype(BF16), num_grad)
    key_direct = feature_map_back(key_mem.astype(F32), dot_tn(dots_grad, phi_query), jnp.roll)
    solved_direct = scatter_columns(solved_direct, "tensor")
    solved_direct = jnp.sum(lax.all_gather(solved_direct.astype(BF16), "seg").astype(F32), axis=0)
    value_grad = solve_backward(key_dots, key_den, solved_direct)
    read = value_part - solved_part
    key_den_grad = jnp.sum(value_grad * read, axis=1, keepdims=True) / key_den
    back = (-value_grad / key_den).astype(BF16)
    key_dots_grad = (dot_nt(back, solved_part.astype(BF16)) + key_den_grad) * mask
    both = (key_dots_grad + key_dots_grad.T).astype(BF16)
    key_solve = feature_map_back(key_mem.astype(F32), dot_nn(both, phi_key), jnp.roll)
    mine = (jnp.arange(key_solve.shape[0]) // MEM == seg)[:, None]
    key_direct = key_direct + jnp.where(mine, key_solve, 0.0)
    key_direct = scatter_columns(key_direct, "tensor")
    key_grad = jnp.sum(lax.all_gather(key_direct.astype(BF16), "seg").astype(F32), axis=0).astype(BF16)
    value_low = value_grad.astype(BF16)
    mem_width = mem_rows.shape[1] // lax.axis_size("seg")
    mem_cols = lax.dynamic_slice_in_dim(mem_rows, seg * mem_width, mem_width, 1)
    mem_key_grad = dot_tn(mem_cols, key_grad)
    mem_value_grad = dot_tn(mem_cols, value_low)
    return (
        hidden_grad, query_grad, key_grad, value_low,
        (gain_attn, gain_mlp, shift_attn, shift_mlp, jnp.sum(after_grad, axis=0, keepdims=True), jnp.sum(own_grad, axis=0, keepdims=True)),
        (attn_grad, attn_bias_grad, out_grad, fc_grad, fc_bias_grad, proj_grad, mem_key_grad, mem_value_grad),
    )


def general_device(
    inputs, out_grad, item_lengths, norm_gains, norm_biases, w_attn, attn_bias, w_out, out_biases, w_fc, fc_bias,
    w_proj, w_mem_keys, w_mem_value,
):
    section, seg, part = (lax.axis_index(name) for name in ("section", "seg", "tensor"))
    segments, parts = lax.axis_size("seg"), lax.axis_size("tensor")
    layers = lax.axis_size("section")
    mask = reach_mask(item_lengths)[section]
    weights = (norm_gains, norm_biases, w_attn, attn_bias, w_out, out_biases, w_fc, fc_bias, w_proj, w_mem_keys, w_mem_value)
    weights = [lax.all_gather(w, "section", axis=0, tiled=True) for w in weights]
    full_keys = lax.all_gather(weights[9], "tensor", axis=3, tiled=True)
    rows_all, grad_all = inputs[section], out_grad[section]
    chunk = rows_all.shape[0] // parts
    own_rows = lax.dynamic_slice_in_dim(rows_all, part * chunk, chunk, 0)
    place = (seg, part)
    saved, layer_params = [], []
    for layer in range(layers):
        mems = lax.all_gather(own_rows[-MEM:], ("seg", "tensor"), axis=0)
        mem_rows = mems[parts - 1 :: parts].reshape(segments * MEM, -1)
        params = tuple(w[layer] for w in weights[:9]) + (full_keys[layer, 0], full_keys[layer, 1], weights[10][layer])
        output, kept = layer_forward(own_rows, mem_rows, mask, place, params)
        saved.append(kept)
        layer_params.append(params)
        own_rows = output.astype(BF16)
    own_grad = lax.dynamic_slice_in_dim(grad_all, part * chunk, chunk, 0).astype(F32)
    rows_grads, matrix_grads = [None] * layers, [None] * layers
    for layer in reversed(range(layers)):
        params, kept = layer_params[layer], saved[layer]
        hidden_grad, query_grad, key_grad, value_low, rows_grads[layer], grads = layer_backward(own_grad, kept, mask, place, params)
        w_q = params[9]
        keys_here = lax.dynamic_slice_in_dim(key_grad, seg * MEM, MEM, 0)
        values_here = lax.dynamic_slice_in_dim(value_low, seg * MEM, MEM, 0)
        tail = dot_nt(keys_here, weights[9][layer, 1]) + dot_nt(values_here, params[11])
        tail = jnp.sum(lax.all_gather(tail.astype(BF16), "tensor").astype(F32), axis=0)
        tail = jnp.concatenate([jnp.zeros((chunk - MEM, tail.shape[1]), F32), tail], axis=0)
        rows_grad = hidden_grad + dot_nt(query_grad, w_q) + jnp.where(part == parts - 1, tail, 0.0)
        own_grad = rows_grad.astype(BF16).astype(F32)
        rows_full = gather_rows(kept[0], "tensor")
        query_cols = lax.all_to_all(query_grad.reshape(chunk, parts, -1).transpose(1, 0, 2), "tensor", 0, 0, tiled=True)
        query_cols = query_cols.reshape(chunk * parts, -1)
        matrix_grads[layer] = grads + (dot_tn(rows_full, query_cols),)
    input_grad = gather_rows(own_grad.astype(BF16), "tensor")[None]

    def over_layers(values):
        return lax.psum_scatter(jnp.stack(values), "section", scatter_dimension=0, tiled=True)

    rows_sums = lax.psum(over_layers([jnp.concatenate(r, axis=0) for r in rows_grads]), ("seg", "tensor"))

    def spread(index, axis):
        stacked = jnp.stack([g[index] for g in matrix_grads]).astype(BF16)
        pair = lax.all_to_all(stacked, "section", 0, 0, tiled=True)
        both = jnp.sum(pair.astype(F32), axis=0)
        cut = both.astype(BF16).reshape(both.shape[:axis] + (segments, -1) + both.shape[axis + 1 :])
        got = lax.all_to_all(cut, "seg", axis, axis, tiled=True)
        return jnp.sum(got.astype(F32), axis=axis)[None]

    biases = lax.psum(
        (over_layers([g[1] for g in matrix_grads]), over_layers([g[4] for g in matrix_grads])), "seg"
    )
    query_w = spread(8, 0)
    key_w = over_layers([g[6] for g in matrix_grads])
    return (
        input_grad,
        rows_sums[:, 0:2],
        rows_sums[:, 2:4],
        spread(0, 1),
        biases[0],
        spread(2, 1),
        rows_sums[:, 4:6],
        spread(3, 0),
        biases[1],
        spread(5, 1),
        jnp.stack([query_w, key_w], axis=1),
        over_layers([g[7] for g in matrix_grads]),
    )


def solution(mesh):
    def per_device(*args):
        inputs, out_grad, item_lengths = args[:3]
        S, T = mesh.shape["seg"], mesh.shape["tensor"]
        w_attn, w_fc, w_keys = args[5], args[9], args[12]
        z = Sizes(
            mesh,
            (
                (0, inputs.shape[1] * S, inputs.shape[2]), (0, 0, 0, w_attn.shape[3] * T), (0, 0, w_fc.shape[2] * T),
                (0, 0, 0, w_keys.shape[3] * T),
            ),
        )
        scratch = scratch_of(z)
        D = z.width
        outs = dict(
            input_grad=((1, z.rows, D), BF16), gain_grads=((1, 2, D), F32), shift_grads=((1, 2, D), F32),
            attn_grads=((1, 3, z.cut, z.heads_w), F32), abias_grads=((1, 2, z.heads_w), F32),
            out_grads=((1, z.heads_w, z.cut), F32), obias_grads=((1, 2, D), F32), fc_grads=((1, z.cut, z.units), F32),
            fcb_grads=((1, z.units), F32), proj_grads=((1, z.cut, z.units), F32),
            mkey_grads=((1, 2, z.cut, z.keys_w), F32), mvalue_grads=((1, z.cut, z.val_w), F32),
        )
        names = tuple(scratch)
        vmem, anywhere = pl.BlockSpec(memory_space=pltpu.VMEM), pl.BlockSpec(memory_space=pl.ANY)
        shapes = [jax.ShapeDtypeStruct(*shape) for shape in outs.values()]
        flip = lambda w: jnp.swapaxes(w, -1, -2)
        results = pl.pallas_call(
            functools.partial(kernel, z, names),
            out_shape=shapes,
            in_specs=[anywhere, anywhere, pl.BlockSpec(memory_space=pltpu.SMEM)] + [anywhere] * 11,
            out_specs=[vmem] * len(outs),
            scratch_shapes=list(scratch.values()),
            compiler_params=pltpu.CompilerParams(
                collective_id=0, has_side_effects=True, vmem_limit_bytes=63 * 2**20
            ),
            name="two_layers",
        )(*args[:5], flip(w_attn), *args[6:12], flip(w_keys), flip(args[13]))
        results = list(pl.pallas_call(
            hand_out, out_shape=shapes, in_specs=[vmem] * len(outs), out_specs=[vmem] * len(outs), name="hand_out"
        )(*results))
        results[9] = flip(results[9])
        return tuple(results)

    return jax.shard_map(
        per_device if mesh.shape["seg"] * MEM <= 128 else general_device,
        mesh=mesh,
        in_specs=(
            P(None, "seg", None),
            P(None, "seg", None),
            P(),
            P("section", None, None),
            P("section", None, None),
            P("section", None, None, "tensor"),
            P("section", None, "tensor"),
            P("section", "tensor", None),
            P("section", None, None),
            P("section", None, "tensor"),
            P("section", "tensor"),
            P("section", "tensor", None),
            P("section", None, None, "tensor"),
            P("section", None, "tensor"),
        ),
        out_specs=(
            P("section", "seg", None),
            P("section", None, None),
            P("section", None, None),
            P("section", None, "seg", "tensor"),
            P("section", None, "tensor"),
            P("section", "tensor", "seg"),
            P("section", None, None),
            P("section", "seg", "tensor"),
            P("section", "tensor"),
            P("section", "tensor", "seg"),
            P("section", None, "seg", "tensor"),
            P("section", "seg", "tensor"),
        ),
        check_vma=False,
    )
```

```python
import functools
from types import SimpleNamespace
from typing import Any, NamedTuple

import jax
import jax.numpy as jnp
from jax import lax
from jax.experimental import pallas as pl
from jax.experimental.pallas import tpu as pltpu
from jax.sharding import PartitionSpec as P

HEAD_DIM = 64
NU = 3
MEM = 16
EPSILON = 1e-05
F32 = jnp.float32
BF16 = jnp.bfloat16
GELU_A = 0.7978845608028654
GELU_B = 0.044715
LAYERS = 2
MESH = pl.DeviceIdType.MESH


def dot_nn(left, right):
    return lax.dot_general(left, right, (((1,), (0,)), ((), ())), preferred_element_type=F32)


def dot_nt(left, right):
    return lax.dot_general(left, right, (((1,), (1,)), ((), ())), preferred_element_type=F32)


def dot_tn(left, right):
    return lax.dot_general(left, right, (((0,), (0,)), ((), ())), preferred_element_type=F32)


def doubled_softplus(projected):
    small = jnp.exp(-jnp.abs(projected))
    tail = jnp.where(small < 1e-3, small - 0.5 * small * small, jnp.log1p(small))
    return jnp.concatenate(
        [jnp.maximum(projected, 0.0) + tail, jnp.maximum(-projected, 0.0) + tail], axis=1
    )


def feature_map(projected, roll=pltpu.roll):
    doubled = doubled_softplus(projected)
    return jnp.concatenate([doubled * roll(doubled, j, 1) for j in range(1, NU + 1)], axis=1)


def feature_map_back(projected, phi_grad, roll=pltpu.roll):
    doubled = doubled_softplus(projected)
    width = doubled.shape[1]
    total = jnp.zeros_like(doubled)
    for j in range(1, NU + 1):
        part = phi_grad[:, (j - 1) * width : j * width]
        total = total + part * roll(doubled, j, 1) + roll(part * doubled, width - j, 1)
    half = width // 2
    gate = 1.0 / (1.0 + jnp.exp(-projected))
    return total[:, :half] * gate - total[:, half:] * (1.0 - gate)


def norm_rows(hidden):
    centered = hidden - jnp.mean(hidden, axis=1, keepdims=True)
    scale = lax.rsqrt(jnp.mean(centered * centered, axis=1, keepdims=True) + EPSILON)
    return centered * scale, scale


def norm_back(hidden, gain_row, grad):
    unit, scale = norm_rows(hidden)
    unit_grad = grad * gain_row
    mean_grad = jnp.mean(unit_grad, axis=1, keepdims=True)
    mean_both = jnp.mean(unit_grad * unit, axis=1, keepdims=True)
    return (
        scale * (unit_grad - mean_grad - unit * mean_both),
        jnp.sum(grad * unit, axis=0, keepdims=True),
        jnp.sum(grad, axis=0, keepdims=True),
    )


def gelu_and_slope(pre):
    square = pre * pre
    bent = jnp.tanh(GELU_A * (pre + GELU_B * square * pre))
    value = 0.5 * pre * (1.0 + bent)
    slope = 0.5 * (1.0 + bent) + 0.5 * pre * (1.0 - bent * bent) * (
        GELU_A * (1.0 + 3.0 * GELU_B * square)
    )
    return value, slope


def xor_peer(place, other, count):
    total, bit = 0, 1
    while bit < count:
        mine = lax.rem(lax.div(place, bit), 2)
        total = total + bit * (1 - mine if other & bit else mine)
        bit *= 2
    return total


def split(values):
    high = values.astype(BF16)
    return high, (values - high.astype(F32)).astype(BF16)


class Sizes:
    def __init__(self, mesh, shapes):
        self.segs, self.parts = mesh.shape["seg"], mesh.shape["tensor"]
        inputs, w_attn, w_fc, w_keys = shapes
        self.rows, self.width = inputs[1] // self.segs, inputs[2]
        self.chunk = self.rows // self.parts
        self.mems = self.segs * MEM
        self.heads_w = w_attn[3] // self.parts
        self.heads = self.heads_w // HEAD_DIM
        self.units = w_fc[2] // self.parts
        self.keys = w_keys[3]
        self.keys_w = self.keys // self.parts
        self.phi = 2 * self.keys * NU
        self.val_w = self.width // self.parts
        self.cut = self.width // self.segs
        self.cut_pad = -(-self.cut // 16) * 16
        self.sems = 120 + 48 * self.parts + 2 * self.segs * (self.parts + 16)


def scratch_of(z):
    S, T, R, D, C, M = z.segs, z.parts, z.rows, z.width, z.chunk, z.mems
    bf = lambda *d: pltpu.VMEM(d, BF16)
    fl = lambda *d: pltpu.VMEM(d, F32)
    return dict(
        gains=fl(2, 2, D), shifts=fl(2, 2, D), w_attn=bf(2, 3, z.heads_w, D), attn_bias=fl(2, 2, z.heads_w),
        w_out=bf(2, z.heads_w, D), out_biases=fl(2, 2, D), w_fc=bf(2, D, z.units), fc_bias=fl(2, 1, z.units),
        w_proj=bf(2, z.units, D), w_keys=bf(2, 2, z.keys, D), w_value=bf(2, z.val_w, D),
        xfull=bf(2, R, D), gfull=bf(2, R, D), mem_rows=bf(2, M, D),
        keyb=bf(2, M, z.keys), phik=bf(2, M, z.phi), kdots=fl(2, M, M), vpart=fl(2, M, z.val_w),
        upart=fl(2, M, z.val_w), uall=bf(2, T, M, z.val_w), qmem=bf(2, C, z.keys), phiq=bf(2, C, z.phi),
        qdots=fl(2, C, M), recall=fl(2, C, D), hidden=fl(2, C, D), normed=bf(2, R, D), qkv=bf(2, 3, R, z.heads_w),
        probs=fl(2, z.heads, R, R), mixed=bf(2, R, z.heads_w), after=fl(2, C, D), normed_mlp=bf(2, R, D),
        slope=fl(2, R, z.units), act=bf(2, R, z.units), rs_src=bf(7, R, D), rs_own=fl(R, D), q_src=bf(R, z.keys_w), q_parts=bf(T, C, z.keys_w), k_parts=bf(T, M, z.keys_w), rs_dst=bf(7, T - 1, C, D),
        low2=bf(2, R, D), dpre=bf(R, z.units), dqkv=bf(3, R, z.heads_w),
        x1_src=fl(2, T, M, z.val_w), x1_dst=fl(2, T - 1, M, z.val_w), x1_mid=fl(2, M, z.val_w), x1_far=fl(2, max(S - 1, 1), M, z.val_w),
        x2_src=fl(2, T, M, z.keys_w), x2_dst=fl(2, T - 1, M, z.keys_w), x2_mid=fl(2, M, z.keys_w), x2_far=fl(2, max(S - 1, 1), M, z.keys_w), x4_src=fl(2, T, M, z.keys_w), x4_dst=fl(2, T - 1, M, z.keys_w), ksolve=fl(M, z.keys), dk_direct=fl(M, z.keys_w),
        dq_src=bf(2, T, C, z.keys_w), dq_all=bf(2, R, z.keys_w), dv=bf(M, z.val_w), vgrad=fl(M, z.val_w),
        x3_src=bf(2, MEM, D), x3_dst=bf(2, T - 1, MEM, D), final=bf(R, D), tmp=fl(C, D),
        grad_p=bf(2, S, z.cut_pad, z.units), grad_c=bf(2, S, z.cut_pad, z.units), grad_qk=bf(2, S, z.cut_pad, 2 * z.heads_w),
        grad_vo=bf(2, S, z.cut_pad, 2 * z.heads_w), grad_q=bf(2, S, z.cut_pad, z.keys_w),
        pair_f=bf(2, S, z.cut_pad, z.units), pair_a=bf(2, S, z.cut_pad, 2 * z.heads_w), pair_q=bf(2, S, z.cut_pad, z.keys_w), relay_f=bf(2, 2, z.cut_pad, z.units), relay_a=bf(2, 2, z.cut_pad, 2 * z.heads_w), relay_q=bf(2, 2, z.cut_pad, z.keys_w),
        far_p=bf(S, z.cut_pad, z.units), far_c=bf(S, z.cut_pad, z.units), far_qk=bf(S, z.cut_pad, 2 * z.heads_w),
        far_vo=bf(S, z.cut_pad, 2 * z.heads_w), far_q=bf(S, z.cut_pad, z.keys_w), dqk=bf(R, 2 * z.heads_w),
        mem_k=fl(2, D, z.keys_w), mem_v=fl(2, D, z.val_w), pair_k=fl(z.cut, z.keys_w), pair_v=fl(z.cut, z.val_w),
        small=fl(2, 16, D), pair_small=fl(16, D), part_small=fl(T, 8, D), seg_small=fl(S, 16, D),
        send=pltpu.SemaphoreType.DMA((z.sems,)), recv=pltpu.SemaphoreType.DMA((z.sems,)), load=pltpu.SemaphoreType.DMA((14, 2)),
        shard=pltpu.SemaphoreType.DMA((2, 2, T)),
    )


class Outer(NamedTuple):
    inputs: Any
    out_grad: Any
    item_lengths: Any
    norm_gains: Any
    norm_biases: Any
    w_attn_in: Any
    attn_bias_in: Any
    w_out_in: Any
    out_biases_in: Any
    w_fc_in: Any
    fc_bias_in: Any
    w_proj_in: Any
    w_keys_in: Any
    w_value_in: Any
    input_grad: Any
    gain_grads: Any
    shift_grads: Any
    attn_grads: Any
    abias_grads: Any
    out_grads: Any
    obias_grads: Any
    fc_grads: Any
    fcb_grads: Any
    proj_grads: Any
    mkey_grads: Any
    mvalue_grads: Any


def kernel(z, held_names, *refs):
    outer = len(Outer._fields)
    r = SimpleNamespace(**Outer(*refs[:outer])._asdict(), **dict(zip(held_names, refs[outer:])))
    S, T, R, D, C, M = z.segs, z.parts, z.rows, z.width, z.chunk, z.mems
    c, s, t = (lax.axis_index(a) for a in ("section", "seg", "tensor"))
    other = 1 - c
    tpeers = [xor_peer(t, i, T) for i in range(T)]
    to_seg = [lax.rem(s + i, S) for i in range(S)]
    own = pl.ds(pl.multiple_of(t * C, C), C)
    seg_rows = pl.ds(pl.multiple_of(s * MEM, MEM), MEM)
    used = [0]
    sent = []
    owed = {}

    def alloc(count):
        used[0] += count
        assert used[0] <= z.sems
        return used[0] - count

    def owe(copies):
        def wait():
            for copy in copies:
                copy.wait_recv()

        owed[id(copies)] = wait
        return id(copies)

    def wait_bytes(ref, semaphore):
        pltpu.make_async_copy(ref, ref, semaphore).wait()

    def remote(src, dst, index, device, recv=None):
        copy = pltpu.make_async_remote_copy(
            src_ref=src, dst_ref=dst, send_sem=r.send.at[index],
            recv_sem=r.recv.at[index] if recv is None else recv, device_id=device, device_id_type=MESH,
        )
        return copy

    def to_parts(src_of, dst):
        base = alloc(T - 1)
        copies = []
        for i in range(T - 1, 0, -1):
            copy = remote(src_of(tpeers[i]), dst(i), base + i - 1, (c, s, tpeers[i]))
            copy.start()
            copies.append(copy)
        sent.extend((copy, None) for copy in copies)
        return owe(copies)

    def to_segs(src_of, dst):
        base = alloc(S - 1)
        copies = [
            remote(src_of(to_seg[i]), dst(i), base + i - 1, (c, to_seg[i], t)) for i in range(1, S)
        ]
        for copy in copies:
            copy.start()
        sent.extend((copy, None) for copy in copies)
        return owe(copies)

    def arrive(key):
        owed.pop(key)()

    def wait_load(ref, layer):
        arrive((id(ref), layer))

    barrier = pltpu.get_barrier_semaphore()
    greeted = [(other, to_seg[i], t) for i in range(S)] + [(c, to_seg[i], tpeers[j]) for i in range(S) for j in range(T) if i or j]
    for device in greeted:
        pl.semaphore_signal(barrier, inc=1, device_id=device, device_id_type=MESH)

    loads = [
        (r.w_value, r.w_value_in.at[0]), (r.gains, r.norm_gains.at[0]), (r.shifts, r.norm_biases.at[0]),
        (r.attn_bias, r.attn_bias_in.at[0]), (r.out_biases, r.out_biases_in.at[0]), (r.w_attn, r.w_attn_in.at[0]), (r.w_out, r.w_out_in.at[0]), (r.w_fc, r.w_fc_in.at[0]),
        (r.w_proj, r.w_proj_in.at[0]), (r.fc_bias, r.fc_bias_in),
    ]
    input_copy = pltpu.make_async_copy(r.inputs.at[c], r.xfull.at[0], r.load.at[10, 0])
    input_copy.start()
    owed[0] = input_copy.wait
    def shard_rows(part):
        return pl.ds(pl.multiple_of(part * z.keys_w, 16), z.keys_w)

    for which in (0, 1):
        pltpu.make_async_copy(
            r.w_keys_in.at[0, which], r.w_keys.at[c, which, shard_rows(t)], r.shard.at[c, which, 0]
        ).start()
    def load_own(kinds):
        for kind in kinds:
            held, source = loads[kind]
            pltpu.make_async_copy(source, held.at[c], r.load.at[kind, c]).start()

    def load_other(kinds):
        for kind in kinds:
            held, source = loads[kind]
            copy = remote(source, held.at[c], pair_base + kind, (other, s, t), r.load.at[kind, c])
            copy.start()
            sent.append((copy, None))
            for layer in range(LAYERS):
                owed[id(held), layer] = functools.partial(wait_bytes, held.at[layer], r.load.at[kind, layer])

    early, middle = range(0, 5), range(5, 7)
    load_own(range(len(loads)))
    grad_copy = pltpu.make_async_copy(r.out_grad.at[c], r.gfull.at[1], r.load.at[11, 0])
    grad_copy.start()
    owed[1] = grad_copy.wait

    pl.semaphore_wait(barrier, len(greeted))

    first_rows = to_segs(
        lambda _: r.inputs.at[c, pl.ds(R - MEM, MEM)], lambda i: r.mem_rows.at[0, seg_rows]
    )

    def shard_wait(layer, which, i):
        wait_bytes(r.w_keys.at[layer, which, pl.ds(0, z.keys_w)], r.shard.at[layer, which, i])

    def peer_shards(core, layer, which):
        @pl.when(c == core)
        def _():
            for i in range(1, T):
                shard_wait(layer, which, i)

    def spread_shard(layer, which):
        base = alloc(T - 1)
        place = r.w_keys.at[layer, which, shard_rows(t)]
        copies = [
            remote(r.w_keys_in.at[0, which], place, base + i - 1, (c, s, tpeers[i]), r.shard.at[layer, which, i])
            for i in range(T - 1, 0, -1)
        ]

        @pl.when(c == layer)
        def _():
            for copy in copies:
                copy.start()

        sent.extend((copy, c == layer) for copy in copies)
        owed[11, layer, which] = functools.partial(peer_shards, layer, layer, which)

    def forward_shard(layer, which):
        arrive((11, layer, which))
        base = alloc(T - 1)
        copies = []
        for i in range(1, T):
            place = r.w_keys.at[layer, which, shard_rows(tpeers[i])]
            copies.append(remote(place, place, base + i - 1, (other, s, t), r.shard.at[layer, which, i]))

        @pl.when(c == layer)
        def _():
            for copy in copies:
                copy.start()

        sent.extend((copy, c == layer) for copy in copies)
        owed[12, layer, which] = functools.partial(peer_shards, 1 - layer, layer, which)

    base = alloc(2)
    for which in (0, 1):
        copy = remote(
            r.w_keys_in.at[0, which], r.w_keys.at[c, which, shard_rows(t)], base + which, (other, s, t), r.shard.at[c, which, 0]
        )
        copy.start()
        sent.append((copy, None))
        for layer in range(LAYERS):
            owed[10, layer, which] = functools.partial(shard_wait, layer, which, 0)
    pair_base = alloc(len(loads))
    load_other(early)

    row_seg = lax.broadcasted_iota(jnp.int32, (M, 1), 0) // MEM
    col_seg = lax.broadcasted_iota(jnp.int32, (1, M), 1) // MEM
    row_item, col_item, own_item = jnp.zeros((M, 1), jnp.int32), jnp.zeros((1, M), jnp.int32), 0
    begin = 0
    for i in range(r.item_lengths.shape[1]):
        length = r.item_lengths[c, i]
        there = jnp.where(length > 0, begin, S)
        row_item = row_item + (row_seg >= there).astype(jnp.int32)
        col_item = col_item + (col_seg >= there).astype(jnp.int32)
        own_item = own_item + jnp.where(s >= there, 1, 0)
        begin = begin + length
    key_mask = jnp.where((row_item == col_item) & (row_seg > col_seg), 1.0, 0.0)
    row_mask = jnp.where((col_item == own_item) & (col_seg < s), 1.0, 0.0)
    lane_head = lax.broadcasted_iota(jnp.int32, (1, z.heads_w), 1) // HEAD_DIM
    head_rows = [(lane_head == h).astype(F32).astype(BF16) for h in range(z.heads)]
    rs_count = [0]

    def reduce_rows(partial):
        k = rs_count[0]
        rs_count[0] += 1
        r.rs_own[...] = partial
        r.rs_src[k] = partial.astype(BF16)
        copies = to_parts(
            lambda peer: r.rs_src.at[k, pl.ds(pl.multiple_of(peer * C, C), C)], lambda i: r.rs_dst.at[k, i - 1]
        )

        def finish():
            arrive(copies)
            total = r.rs_own[own, :]
            for i in range(T - 1):
                total = total + r.rs_dst[k, i].astype(F32)
            return total

        return finish

    def share_rows(ref, layer):
        return to_parts(lambda _: ref.at[layer, own], lambda i: ref.at[layer, own])

    def forward(l):
        own_shard = shard_rows(t)
        if l == 0:
            arrive(0)
            arrive((10, 0, 0))
            r.q_src[...] = dot_nt(r.xfull[0], r.w_keys[0, 0, own_shard, :]).astype(BF16)
            r.q_parts[t] = r.q_src[own, :]
            query_step = to_parts(
                lambda peer: r.q_src.at[pl.ds(pl.multiple_of(peer * C, C), C)], lambda i: r.q_parts.at[t]
            )
            r.mem_rows[0, seg_rows, :] = r.xfull[0, R - MEM :, :]
            arrive((10, 0, 1))
            arrive(first_rows)
            mems = r.mem_rows[0]
            r.k_parts[t] = dot_nt(mems, r.w_keys[0, 1, own_shard, :]).astype(BF16)
            key_step = to_parts(lambda _: r.k_parts.at[t], lambda i: r.k_parts.at[t])
            load_other(middle)
            arrive(query_step)
            queries_mem = jnp.concatenate([r.q_parts[u] for u in range(T)], axis=1)
        else:
            for which in (0, 1):
                arrive((10, 1, which))
                arrive((12, 1, which))
            queries_mem = dot_nt(r.xfull[1, own, :], r.w_keys[1, 0]).astype(BF16)
        x = r.xfull[l, own, :]
        r.qmem[l] = queries_mem
        phi_query = feature_map(queries_mem.astype(F32)).astype(BF16)
        r.phiq[l] = phi_query
        wait_load(r.w_value, l)
        if l == 1:
            arrive(4)
            mems = r.mem_rows[1]
        value_part = dot_nt(mems, r.w_value[l])
        r.vpart[l] = value_part
        r.upart[l] = value_part
        if l == 0:
            arrive(key_step)
            keys = jnp.concatenate([r.k_parts[u] for u in range(T)], axis=1)
        else:
            keys = dot_nt(mems, r.w_keys[1, 1]).astype(BF16)
        r.keyb[l] = keys
        phi_key = feature_map(keys.astype(F32)).astype(BF16)
        r.phik[l] = phi_key
        key_dots = dot_nt(phi_key, phi_key) * key_mask
        r.kdots[l] = key_dots
        key_den = 1.0 + jnp.sum(key_dots, axis=1, keepdims=True)
        for k in range(1, S):
            rows = slice(k * MEM, (k + 1) * MEM)
            read = dot_nn(key_dots[rows].astype(BF16), r.upart[l].astype(BF16)) / key_den[rows]
            r.upart[l, rows, :] = value_part[rows] - read
        r.uall[l, t] = r.upart[l].astype(BF16)
        solved = to_parts(lambda _: r.uall.at[l, t], lambda i: r.uall.at[l, t])
        if l == 0:
            spread_shard(1, 1)
        else:
            spread_shard(0, 0)
        query_dots = dot_nt(phi_query, phi_key) * row_mask
        r.qdots[l] = query_dots
        query_den = 1.0 + jnp.sum(query_dots, axis=1, keepdims=True)
        for ref in (r.gains, r.shifts, r.attn_bias, r.out_biases):
            wait_load(ref, l)
        arrive(solved)
        high, low = split(query_dots)
        recall = [dot_nn(high, r.uall[l, u]) + dot_nn(low, r.uall[l, u]) for u in range(T)]
        recall = jnp.concatenate(recall, axis=1) / query_den
        r.recall[l] = recall
        hidden = x.astype(F32) + recall.astype(BF16).astype(F32)
        r.hidden[l] = hidden
        unit, _ = norm_rows(hidden)
        r.normed[l, own, :] = (unit * r.gains[l, 0:1] + r.shifts[l, 0:1]).astype(BF16)
        shared = share_rows(r.normed, l)
        if l == 0:
            load_other([9, 7])
        wait_load(r.w_attn, l)
        wait_load(r.w_out, l)
        arrive(shared)
        if l == 0:
            spread_shard(1, 0)
        else:
            spread_shard(0, 1)
        normed = r.normed[l]
        queries = (dot_nt(normed, r.w_attn[l, 0]) + r.attn_bias[l, 0:1]).astype(BF16)
        key_heads = dot_nt(normed, r.w_attn[l, 1]).astype(BF16)
        values = (dot_nt(normed, r.w_attn[l, 2]) + r.attn_bias[l, 1:2]).astype(BF16)
        r.qkv[l, 0] = queries
        r.qkv[l, 1] = key_heads
        r.qkv[l, 2] = values
        causal = lax.broadcasted_iota(jnp.int32, (R, R), 0) >= lax.broadcasted_iota(jnp.int32, (R, R), 1)
        mixed = jnp.zeros((R, z.heads_w), F32)
        for h in range(z.heads):
            scores = dot_nt(queries, key_heads * head_rows[h]) * HEAD_DIM ** (-0.5)
            scores = jnp.where(causal, scores, -jnp.inf)
            heights = jnp.exp(scores - jnp.max(scores, axis=1, keepdims=True))
            probs = heights * (1.0 / jnp.sum(heights, axis=1, keepdims=True))
            r.probs[l, h] = probs
            mixed = mixed + dot_nn(probs.astype(BF16), values * head_rows[h])
        mixed = mixed.astype(BF16)
        r.mixed[l] = mixed
        finish = reduce_rows(dot_nn(mixed, r.w_out[l]))
        if l == 0:
            load_other([8])
        after = r.hidden[l] + finish() + r.out_biases[l, 0:1]
        r.after[l] = after
        unit, _ = norm_rows(after)
        r.normed_mlp[l, own, :] = (unit * r.gains[l, 1:2] + r.shifts[l, 1:2]).astype(BF16)
        shared = share_rows(r.normed_mlp, l)
        wait_load(r.w_fc, l)
        wait_load(r.fc_bias, l)
        wait_load(r.w_proj, l)
        if l == 0:
            forward_shard(1, 1)
            forward_shard(1, 0)
        arrive(shared)
        row_step = share_rows(r.xfull, 1) if l == 1 else None
        pre = dot_nn(r.normed_mlp[l], r.w_fc[l]) + r.fc_bias[l]
        activation, slope = gelu_and_slope(pre)
        activation = activation.astype(BF16)
        r.act[l] = activation
        r.slope[l] = slope
        if l == 0:
            finish = reduce_rows(dot_nn(activation, r.w_proj[l]))
            output = r.after[l] + finish() + r.out_biases[l, 1:2]
            r.xfull[1, own, :] = output.astype(BF16)
            base, places = alloc(S), alloc(S * T)
            last = r.xfull.at[1, pl.ds(R - MEM, MEM)]

            @pl.when(t == T - 1)
            def _():
                r.mem_rows[1, seg_rows, :] = r.xfull[1, R - MEM :, :]
                for i in range(S - 1, -1, -1):
                    for j in range(1 if i == 0 else 0, T):
                        copy = pltpu.make_async_remote_copy(
                            src_ref=last, dst_ref=r.mem_rows.at[1, seg_rows], send_sem=r.send.at[places + i * T + j],
                            recv_sem=r.recv.at[base + i], device_id=(c, to_seg[i], tpeers[j]), device_id_type=MESH,
                        )
                        copy.start()

            def wait_rows(i):
                wait_bytes(r.mem_rows.at[1, pl.ds(0, MEM)], r.recv.at[base + i])

            def wait_all():
                pl.when(t != T - 1)(functools.partial(wait_rows, 0))
                for i in range(1, S):
                    wait_rows(i)

            owed[4] = wait_all

            def drain():
                @pl.when(t == T - 1)
                def _():
                    for i in range(S):
                        for j in range(1 if i == 0 else 0, T):
                            wait_bytes(last, r.send.at[places + i * T + j])

            sent.append((drain, drain))
        return row_step

    fam_p, fam_c = (r.grad_p, r.pair_f, r.far_p, 0, r.relay_f), (r.grad_c, r.pair_f, r.far_c, 1, r.relay_f)
    fam_qk, fam_vo = (r.grad_qk, r.pair_a, r.far_qk, 0, r.relay_a), (r.grad_vo, r.pair_a, r.far_vo, 1, r.relay_a)
    fam_q = (r.grad_q, r.pair_q, r.far_q, None, r.relay_q)
    on_line = S == 4
    partner = s + 1 - 2 * lax.rem(s, 2)
    across = 2 - 2 * lax.div(s, 2)
    outer = jnp.logical_or(s == 0, s == 3)
    relays = {}

    def blocks_of(first_row, count):
        row, pieces = first_row, []
        while row < first_row + count:
            block, inside = row // z.cut, row % z.cut
            size = min(z.cut - inside, first_row + count - row)
            pieces.append((block, inside, row - first_row, size))
            row += size
        return pieces

    def weight_grad(l, family, *pairs):
        stripe = min(256, D)
        for k in range(0, D, stripe):
            parts = [dot_tn(left[:, k : k + stripe], right).astype(BF16) for left, right in pairs]
            grad = parts[0] if len(parts) == 1 else jnp.concatenate(parts, axis=1)
            for block, inside, row, size in blocks_of(k, stripe):
                family[0][l, block, inside : inside + size, :] = grad[row : row + size]

    def pair_send(src, dst):
        index = alloc(1)
        return remote(src, dst, index, (other, s, t))

    def adder_of(l, family):
        return l if family[3] is None else family[3]

    def hand_over(l, family):
        grad, pair, _, _, _ = family
        adder = adder_of(l, family)
        copy = pair_send(grad.at[l], pair.at[l])
        pl.when(c != adder)(copy.start)
        sent.append((copy, c != adder))
        return owe_owner(adder, [copy])

    def owe_owner(l, copies):
        def wait():
            @pl.when(c == l)
            def _():
                for copy in copies:
                    copy.wait_recv()

        owed[id(copies)] = wait
        return id(copies)

    def add_pair(l, family, key):
        grad, pair, _, _, _ = family
        arrive(key)

        @pl.when(c == adder_of(l, family))
        def _():
            @pl.loop(0, S)
            def _(j):
                grad[l, j] = (grad[l, j].astype(F32) + pair[l, j].astype(F32)).astype(BF16)

    def spread(l, family, direct):
        grad, _, far, _, relay = family
        adder = adder_of(l, family)
        near = adder == l
        direct = direct or not on_line
        base = alloc(S if direct else 5)
        steps = range(1, S) if direct else (1, 2)

        @pl.when(c == adder)
        def _():
            if direct:
                for i in range(S - 1, 0, -1):
                    remote(grad.at[l, to_seg[i]], far.at[i], base + i, (l, to_seg[i], t)).start()
            else:

                @pl.when(outer)
                def _():
                    for k in range(2):
                        remote(grad.at[l, across + k], relay.at[l, k], base + 3 + k, (c, partner, t)).start()

                remote(grad.at[l, partner], far.at[1], base + 1, (l, partner, t)).start()
            if near:
                far[0] = grad[l, s]
            else:
                remote(grad.at[l, s], far.at[0], base, (other, s, t)).start()

        if not direct:

            @pl.when(c == l)
            def _():
                for i in range(3, S):
                    far[i] = jnp.zeros(far.shape[1:], BF16)

            def pass_on():
                @pl.when(jnp.logical_and(c == adder, jnp.logical_not(outer)))
                def _():
                    for k in range(2):
                        wait_bytes(relay.at[l, k], r.recv.at[base + 3 + k])
                        place = across + k
                        grad[l, place] = (grad[l, place].astype(F32) + relay[l, k].astype(F32)).astype(BF16)
                        remote(grad.at[l, place], far.at[2], base + 3 + k, (l, place, t), r.recv.at[base + 2]).start()

            relays[id(far), l] = pass_on

        def wait():
            @pl.when(c == l)
            def _():
                for i in steps if near else (0, *steps):
                    wait_bytes(far.at[i], r.recv.at[base + i])

        def drain():
            @pl.when(c == adder)
            def _():
                ends = tuple(steps) if direct else (1, 3, 4)
                for i in ends if near else (0, *ends):
                    wait_bytes(far.at[0], r.send.at[base + i])

        owed[id(far), l] = wait
        sent.append((drain, drain))

    def pass_on(l, family):
        if (id(family[2]), l) in relays:
            relays.pop((id(family[2]), l))()

    def owe_small(l):
        copy = pair_send(r.small.at[l], r.pair_small)
        pl.when(c != l)(copy.start)
        sent.append((copy, c != l))
        return owe_owner(l, [copy])

    def owner_copies(l, copies):
        @pl.when(c == l)
        def _():
            for copy in copies:
                copy.start()

        sent.extend((copy, c == l) for copy in copies)
        return owe_owner(l, copies)

    def small_parts(l, key):
        arrive(key)

        @pl.when(c == l)
        def _():
            r.seg_small[0] = r.small[l] + r.pair_small[...]
            r.part_small[0] = r.seg_small[0, 0:8, :]

        base = alloc(T - 1)
        return owner_copies(
            l, [remote(r.part_small.at[0], r.part_small.at[i], base + i - 1, (c, s, tpeers[i])) for i in range(1, T)]
        )

    def small_segs(l, key):
        arrive(key)

        @pl.when(c == l)
        def _():
            total = r.part_small[0]
            for i in range(1, T):
                total = total + r.part_small[i]
            r.seg_small[0, 0:8, :] = total

        base = alloc(S - 1)
        return owner_copies(
            l, [remote(r.seg_small.at[0], r.seg_small.at[i], base + i - 1, (c, to_seg[i], t)) for i in range(1, S)]
        )

    def backward(l):
        if l == 1:
            arrive(1)
        grad_low = r.gfull[l]
        pre_grad = (r.slope[l] * dot_nt(grad_low, r.w_proj[l])).astype(BF16)
        r.dpre[...] = pre_grad
        finish = reduce_rows(dot_nt(pre_grad, r.w_fc[l]))
        own_grad = r.gfull[l, own, :].astype(F32)

        weight_grad(l, fam_p, (r.gfull.at[l], r.act[l]))
        pair_p = hand_over(l, fam_p)
        weight_grad(l, fam_c, (r.normed_mlp.at[l], r.dpre[...]))
        pair_c = hand_over(l, fam_c)
        r.small[l, 8:9, :] = jnp.sum(r.dpre[...].astype(F32), axis=0, keepdims=True)
        if l == 1:
            forward_shard(0, 0)
            forward_shard(0, 1)
        if l == 0:
            pass_on(1, fam_c)
            pass_on(1, fam_qk)
        add_pair(l, fam_p, pair_p)
        spread(l, fam_p, False)
        after_part, gain_mlp, shift_mlp = norm_back(r.after[l], r.gains[l, 1:2], finish())
        after_grad = own_grad + after_part
        r.tmp[...] = after_grad
        r.low2[l, own, :] = after_grad.astype(BF16)
        shared = share_rows(r.low2, l)
        r.small[l, 1:2, :] = gain_mlp
        r.small[l, 3:4, :] = shift_mlp
        r.small[l, 4:5, :] = jnp.sum(after_grad, axis=0, keepdims=True)
        r.small[l, 5:6, :] = jnp.sum(own_grad, axis=0, keepdims=True)
        add_pair(l, fam_c, pair_c)
        if l == 0:
            spread(l, fam_c, False)
            pass_on(1, fam_vo)
            pass_on(1, fam_q)
        arrive(shared)
        after_low = r.low2[l]
        mixed_grad = dot_nt(after_low, r.w_out[l]).astype(BF16)
        queries, key_heads, values = r.qkv[l, 0], r.qkv[l, 1], r.qkv[l, 2]
        q_grad = k_grad = v_grad = jnp.zeros((R, z.heads_w), F32)
        for h in range(z.heads):
            probs = r.probs[l, h]
            mixed_here = mixed_grad * head_rows[h]
            probs_grad = dot_nt(mixed_here, values)
            delta = jnp.sum(probs_grad * probs, axis=1, keepdims=True)
            score_grad = (probs * (probs_grad - delta)).astype(BF16)
            q_grad = q_grad + dot_nn(score_grad, key_heads * head_rows[h])
            k_grad = k_grad + dot_tn(score_grad, queries * head_rows[h])
            v_grad = v_grad + dot_tn(probs.astype(BF16), mixed_here)
        scale = HEAD_DIM ** (-0.5)
        r.dqkv[0] = (q_grad * scale).astype(BF16)
        r.dqkv[1] = (k_grad * scale).astype(BF16)
        r.dqkv[2] = v_grad.astype(BF16)
        r.dqk[...] = jnp.concatenate([r.dqkv[0], r.dqkv[1]], axis=1)
        finish = reduce_rows(sum(dot_nn(r.dqkv[i], r.w_attn[l, i]) for i in range(3)))

        weight_grad(l, fam_qk, (r.normed.at[l], r.dqk[...]))
        pair_qk = hand_over(l, fam_qk)
        weight_grad(l, fam_vo, (r.normed.at[l], r.dqkv[2]), (r.low2.at[l], r.mixed[l]))
        pair_vo = hand_over(l, fam_vo)
        for row, i in ((9, 0), (10, 2)):
            r.small[l, row : row + 1, : z.heads_w] = jnp.sum(r.dqkv[i].astype(F32), axis=0, keepdims=True)
        hidden_part, gain_attn, shift_attn = norm_back(r.hidden[l], r.gains[l, 0:1], finish())
        hidden_grad = r.tmp[...] + hidden_part
        r.tmp[...] = hidden_grad
        r.small[l, 0:1, :] = gain_attn
        r.small[l, 2:3, :] = shift_attn
        small_key = owe_small(l)
        query_den = 1.0 + jnp.sum(r.qdots[l], axis=1, keepdims=True)
        high, low = split(hidden_grad / query_den)
        den_grad = -jnp.sum((hidden_grad / query_den) * r.recall[l], axis=1, keepdims=True)
        highs = [high[:, u * z.val_w : (u + 1) * z.val_w] for u in range(T)]
        lows = [low[:, u * z.val_w : (u + 1) * z.val_w] for u in range(T)]
        dots_high, dots_low = split(r.qdots[l])
        for u in range(T):
            r.x1_src[l, u] = dot_tn(dots_high, highs[u]) + dot_tn(dots_high, lows[u]) + dot_tn(dots_low, highs[u])
        value_step = to_parts(lambda peer: r.x1_src.at[l, peer], lambda i: r.x1_dst.at[l, i - 1])
        dots_grad = sum(dot_nt(highs[u], r.uall[l, u]) + dot_nt(lows[u], r.uall[l, u]) for u in range(T)) + den_grad
        dots_grad = (dots_grad * row_mask).astype(BF16)
        key_direct = feature_map_back(r.keyb[l].astype(F32), dot_tn(dots_grad, r.phiq[l]))
        for u in range(T):
            r.x2_src[l, u] = key_direct[:, u * z.keys_w : (u + 1) * z.keys_w]
        key_step = to_parts(lambda peer: r.x2_src.at[l, peer], lambda i: r.x2_dst.at[l, i - 1])
        add_pair(l, fam_qk, pair_qk)
        add_pair(l, fam_vo, pair_vo)
        pass_on(l, fam_p)
        arrive(value_step)
        r.x1_mid[l] = r.x1_src[l, t] + sum(r.x1_dst[l, i] for i in range(T - 1))
        value_step = to_segs(lambda _: r.x1_mid.at[l], lambda i: r.x1_far.at[l, i - 1])
        arrive(key_step)
        r.x2_mid[l] = r.x2_src[l, t] + sum(r.x2_dst[l, i] for i in range(T - 1))
        key_step = to_segs(lambda _: r.x2_mid.at[l], lambda i: r.x2_far.at[l, i - 1])
        query_grad = feature_map_back(r.qmem[l].astype(F32), dot_nn(dots_grad, r.phik[l])).astype(BF16)
        for u in range(T):
            r.dq_src[l, u] = query_grad[:, u * z.keys_w : (u + 1) * z.keys_w]
        r.dq_all[l, own, :] = r.dq_src[l, t]
        query_step = to_parts(lambda peer: r.dq_src.at[l, peer], lambda i: r.dq_all.at[l, own])
        if l == 0:
            arrive((12, 0, 0))
            arrive((12, 0, 1))
        r.tmp[...] += dot_nn(query_grad, r.w_keys[l, 0])
        arrive(value_step)
        direct = r.x1_mid[l] + sum(r.x1_far[l, i] for i in range(S - 1))
        arrive(key_step)
        small_key = small_parts(l, small_key)
        for family in (fam_c, fam_qk, fam_vo) if l == 1 else (fam_qk, fam_vo):
            spread(l, family, False)
        key_dots = r.kdots[l]
        key_den = 1.0 + jnp.sum(key_dots, axis=1, keepdims=True)
        r.vgrad[...] = direct
        for k in range(S - 1, 0, -1):
            rows = slice(k * MEM, (k + 1) * MEM)
            back = -r.vgrad[rows, :] / key_den[rows]
            r.vgrad[...] += dot_tn(key_dots[rows].astype(BF16), back.astype(BF16))
        value_grad = r.vgrad[...]
        read = r.vpart[l] - r.upart[l]
        back = (-value_grad / key_den).astype(BF16)
        key_den_grad = -jnp.sum(back.astype(F32) * read, axis=1, keepdims=True)
        key_dots_grad = (dot_nt(back, r.upart[l].astype(BF16)) + key_den_grad) * key_mask
        both = (key_dots_grad + key_dots_grad.T).astype(BF16)
        key_solve = feature_map_back(r.keyb[l].astype(F32), dot_nn(both, r.phik[l]))
        r.ksolve[...] = key_solve
        r.dv[...] = value_grad.astype(BF16)
        r.dk_direct[...] = r.x2_mid[l] + sum(r.x2_far[l, i] for i in range(S - 1))
        tail = dot_nn(r.dv[seg_rows, :], r.w_value[l])
        tail = tail + dot_nn(r.dk_direct[seg_rows, :].astype(BF16), r.w_keys[l, 1, shard_rows(t), :])
        tail = tail + dot_nn(r.ksolve[seg_rows, :].astype(BF16), r.w_keys[l, 1])
        r.x3_src[l] = tail.astype(BF16)
        base, place = alloc(T - 1), alloc(1)

        for i in range(1, T):

            @pl.when(tpeers[i] == T - 1)
            def _():
                copy = pltpu.make_async_remote_copy(
                    src_ref=r.x3_src.at[l], dst_ref=r.x3_dst.at[l, i - 1], send_sem=r.send.at[place],
                    recv_sem=r.recv.at[base + i - 1], device_id=(c, s, tpeers[i]), device_id_type=MESH,
                )
                copy.start()

        def drain():
            @pl.when(t != T - 1)
            def _():
                wait_bytes(r.x3_src.at[l], r.send.at[place])

        sent.append((drain, drain))
        for u in range(T):
            r.x4_src[l, u] = key_solve[:, u * z.keys_w : (u + 1) * z.keys_w]
        solve_step = to_parts(lambda peer: r.x4_src.at[l, peer], lambda i: r.x4_dst.at[l, i - 1])

        @pl.when(t == T - 1)
        def _():
            total = r.x3_src[l].astype(F32)
            for i in range(T - 1):
                wait_bytes(r.x3_dst.at[l, i], r.recv.at[base + i])
                total = total + r.x3_dst[l, i].astype(F32)
            r.tmp[C - MEM :, :] += total

        target = r.gfull.at[0] if l == 1 else r.final
        target[own, :] = r.tmp[...].astype(BF16)
        rows_step = to_parts(lambda _: target.at[own], lambda i: target.at[own])
        small_key = small_segs(l, small_key)
        arrive(query_step)
        if l == 1:
            arrive(row_step)
        weight_grad(l, fam_q, (r.xfull.at[l], r.dq_all[l]))
        pair_q = hand_over(l, fam_q)
        r.mem_v[l] = dot_tn(r.mem_rows[l], r.dv[...])
        arrive(solve_step)
        key_grad = r.dk_direct[...] + r.x4_src[l, t] + sum(r.x4_dst[l, i] for i in range(T - 1))
        r.mem_k[l] = dot_tn(r.mem_rows[l], key_grad.astype(BF16))
        rows = pl.ds(pl.multiple_of(s * z.cut, 8), z.cut)
        mem_copies = [pair_send(r.mem_k.at[l, rows], r.pair_k), pair_send(r.mem_v.at[l, rows], r.pair_v)]

        @pl.when(c != l)
        def _():
            for copy in mem_copies:
                copy.start()

        sent.extend((copy, c != l) for copy in mem_copies)
        mem_key = owe_owner(l, mem_copies)
        add_pair(l, fam_q, pair_q)
        spread(l, fam_q, False)
        if l == 0:
            pass_on(l, fam_c)
            pass_on(l, fam_qk)
            pass_on(l, fam_vo)
            pass_on(l, fam_q)
        arrive(rows_step)
        return mem_key, small_key

    forward(0)
    row_step = forward(1)
    for l in range(LAYERS):
        r.small[l] = jnp.zeros((16, D), F32)
    mem_key1, small_key1 = backward(1)
    mem_key0, small_key0 = backward(0)

    r.input_grad[0] = r.final[...]
    l = c

    arrive(mem_key1)
    arrive(mem_key0)
    rows = pl.ds(pl.multiple_of(s * z.cut, 8), z.cut)
    r.mkey_grads[0, 1] = r.mem_k[l, rows, :] + r.pair_k[...]
    r.mvalue_grads[0] = r.mem_v[l, rows, :] + r.pair_v[...]

    def far_sum(far):
        arrive((id(far), 1))
        arrive((id(far), 0))
        return sum(far[i, : z.cut, :].astype(F32) for i in range(S))

    r.proj_grads[0] = far_sum(r.far_p)
    r.fc_grads[0] = far_sum(r.far_c)
    both = far_sum(r.far_qk)
    r.attn_grads[0, 0] = both[:, : z.heads_w]
    r.attn_grads[0, 1] = both[:, z.heads_w :]
    both = far_sum(r.far_vo)
    r.attn_grads[0, 2] = both[:, : z.heads_w]
    r.out_grads[0] = both[:, z.heads_w :].T
    r.mkey_grads[0, 0] = far_sum(r.far_q)
    arrive(small_key1)
    arrive(small_key0)
    total = r.seg_small[0]
    for i in range(1, S):
        total = total + r.seg_small[i]
    r.gain_grads[0] = total[0:2]
    r.shift_grads[0] = total[2:4]
    r.obias_grads[0] = total[4:6]
    r.fcb_grads[...] = total[8:9, : z.units]
    r.abias_grads[0] = total[9:11, : z.heads_w]

    assert not owed and not relays
    for copy, when in sent:
        if when is copy:
            copy()
        elif when is None:
            copy.wait_send()
        else:
            pl.when(when)(copy.wait_send)


def hand_out(*refs):
    count = len(refs) // 2
    for source, target in zip(refs[:count], refs[count:]):
        target[...] = source[...]


def item_ids(lengths):
    item_ends = jnp.cumsum(lengths, axis=-1)
    item_begins = item_ends - lengths
    places = jnp.arange(lengths.shape[-1], dtype=jnp.int32)
    matches = (item_begins[:, :, None] == places[None, None, :]) & (lengths[:, :, None] > 0)
    return jnp.cumsum(jnp.sum(matches.astype(jnp.int32), axis=1), axis=-1)


def reach_mask(lengths):
    ids = item_ids(lengths)
    places = jnp.arange(lengths.shape[-1])
    earlier = places[:, None] > places[None, :]
    same = (ids[:, :, None] == ids[:, None, :]) & earlier[None]
    return jnp.repeat(jnp.repeat(same.astype(F32), MEM, axis=1), MEM, axis=2)


def gather_rows(values, axis):
    return lax.all_gather(values, axis, axis=0, tiled=True)


def scatter_rows(values, axis):
    peers = lax.axis_size(axis)
    pieces = values.astype(BF16).reshape(peers, values.shape[0] // peers, values.shape[1])
    got = lax.all_to_all(pieces, axis, 0, 0, tiled=True)
    return jnp.sum(got.astype(F32), axis=0)


def scatter_columns(values, axis):
    peers = lax.axis_size(axis)
    rows = values.shape[0]
    pieces = values.reshape(rows, peers, -1).transpose(1, 0, 2)
    got = lax.all_to_all(pieces.astype(BF16), axis, 0, 0, tiled=True)
    return jnp.sum(got.astype(F32), axis=0)


def solve_forward(key_dots, key_den, value_mem):
    segments = key_dots.shape[0] // MEM
    solved = value_mem
    for s in range(1, segments):
        rows = slice(s * MEM, (s + 1) * MEM)
        read = dot_nn(key_dots[rows].astype(BF16), solved.astype(BF16)) / key_den[rows]
        solved = solved.at[rows].add(-read)
    return solved


def solve_backward(key_dots, key_den, direct):
    segments = key_dots.shape[0] // MEM
    total = direct
    for s in range(segments - 1, 0, -1):
        rows = slice(s * MEM, (s + 1) * MEM)
        back = -total[rows] / key_den[rows]
        total = total + dot_tn(key_dots[rows].astype(BF16), back.astype(BF16))
    return total


def layer_forward(own_rows, mem_rows, mask, place, params):
    gains, shifts, w_attn, attn_bias, w_out, out_biases, w_fc, fc_bias, w_proj, w_q, w_k, w_v = params
    seg, _ = place
    own_mask = lax.dynamic_slice_in_dim(mask, seg * MEM, 1, 0)
    key_mem = dot_nn(mem_rows, w_k).astype(BF16)
    phi_key = feature_map(key_mem.astype(F32), jnp.roll).astype(BF16)
    key_dots = dot_nt(phi_key, phi_key) * mask
    key_den = 1.0 + jnp.sum(key_dots, axis=1, keepdims=True)
    value_part = dot_nn(mem_rows, w_v)
    solved_part = solve_forward(key_dots, key_den, value_part)
    solved = lax.all_gather(solved_part.astype(BF16), "tensor", axis=1, tiled=True)
    query_mem = dot_nn(own_rows, w_q).astype(BF16)
    phi_query = feature_map(query_mem.astype(F32), jnp.roll).astype(BF16)
    query_dots = dot_nt(phi_query, phi_key) * own_mask
    query_den = 1.0 + jnp.sum(query_dots, axis=1, keepdims=True)
    recall = dot_nn(query_dots.astype(BF16), solved) / query_den
    hidden = own_rows.astype(F32) + recall.astype(BF16).astype(F32)
    unit, _ = norm_rows(hidden)
    normed = gather_rows((unit * gains[0] + shifts[0]).astype(BF16), "tensor")
    queries = (dot_nn(normed, w_attn[0]) + attn_bias[0]).astype(BF16)
    key_heads = dot_nn(normed, w_attn[1]).astype(BF16)
    values = (dot_nn(normed, w_attn[2]) + attn_bias[1]).astype(BF16)
    rows = normed.shape[0]
    causal = jnp.arange(rows)[:, None] >= jnp.arange(rows)[None, :]
    probs, mixed = [], []
    for h in range(queries.shape[1] // HEAD_DIM):
        cols = slice(h * HEAD_DIM, (h + 1) * HEAD_DIM)
        scores = dot_nt(queries[:, cols], key_heads[:, cols]) * HEAD_DIM ** (-0.5)
        scores = jnp.where(causal, scores, -jnp.inf)
        heights = jnp.exp(scores - jnp.max(scores, axis=1, keepdims=True))
        probs.append(heights / jnp.sum(heights, axis=1, keepdims=True))
        mixed.append(dot_nn(probs[-1].astype(BF16), values[:, cols]).astype(BF16))
    mixed = jnp.concatenate(mixed, axis=1)
    after = hidden + scatter_rows(dot_nn(mixed, w_out), "tensor") + out_biases[0]
    unit, _ = norm_rows(after)
    normed_mlp = gather_rows((unit * gains[1] + shifts[1]).astype(BF16), "tensor")
    pre = dot_nn(normed_mlp, w_fc) + fc_bias
    activation, slope = gelu_and_slope(pre)
    activation = activation.astype(BF16)
    output = after + scatter_rows(dot_nn(activation, w_proj), "tensor") + out_biases[1]
    kept = (
        own_rows, mem_rows, key_mem, phi_key, key_dots, key_den, value_part, solved_part, solved, query_mem,
        phi_query, query_dots, query_den, recall, hidden, normed, queries, key_heads, values, probs, mixed,
        after, normed_mlp, slope, activation,
    )
    return output, kept


def layer_backward(own_grad, kept, mask, place, params):
    gains, shifts, w_attn, attn_bias, w_out, out_biases, w_fc, fc_bias, w_proj, w_q, w_k, w_v = params
    (
        own_rows, mem_rows, key_mem, phi_key, key_dots, key_den, value_part, solved_part, solved, query_mem,
        phi_query, query_dots, query_den, recall, hidden, normed, queries, key_heads, values, probs, mixed,
        after, normed_mlp, slope, activation,
    ) = kept
    seg, part = place
    own_mask = lax.dynamic_slice_in_dim(mask, seg * MEM, 1, 0)
    grad_low = gather_rows(own_grad.astype(BF16), "tensor")
    pre_grad = (slope * dot_nt(grad_low, w_proj)).astype(BF16)
    proj_grad = dot_tn(activation, grad_low)
    fc_bias_grad = jnp.sum(pre_grad.astype(F32), axis=0)
    fc_grad = dot_tn(normed_mlp, pre_grad)
    after_part, gain_mlp, shift_mlp = norm_back(
        after, gains[1:2], scatter_rows(dot_nt(pre_grad, w_fc), "tensor")
    )
    after_grad = own_grad + after_part
    after_low = gather_rows(after_grad.astype(BF16), "tensor")
    out_grad = dot_tn(mixed, after_low)
    mixed_grad = dot_nt(after_low, w_out).astype(BF16)
    q_grads, k_grads, v_grads = [], [], []
    for h in range(queries.shape[1] // HEAD_DIM):
        cols = slice(h * HEAD_DIM, (h + 1) * HEAD_DIM)
        probs_grad = dot_nt(mixed_grad[:, cols], values[:, cols])
        delta = jnp.sum(probs_grad * probs[h], axis=1, keepdims=True)
        score_grad = (probs[h] * (probs_grad - delta)).astype(BF16)
        q_grads.append((dot_nn(score_grad, key_heads[:, cols]) * HEAD_DIM ** (-0.5)).astype(BF16))
        k_grads.append((dot_tn(score_grad, queries[:, cols]) * HEAD_DIM ** (-0.5)).astype(BF16))
        v_grads.append(dot_tn(probs[h].astype(BF16), mixed_grad[:, cols]).astype(BF16))
    three = [jnp.concatenate(g, axis=1) for g in (q_grads, k_grads, v_grads)]
    attn_bias_grad = jnp.stack([jnp.sum(three[i].astype(F32), axis=0) for i in (0, 2)])
    attn_grad = jnp.stack([dot_tn(normed, g) for g in three])
    normed_part = sum(dot_nt(g, w_attn[i]) for i, g in enumerate(three))
    hidden_part, gain_attn, shift_attn = norm_back(
        hidden, gains[0:1], scatter_rows(normed_part, "tensor")
    )
    hidden_grad = after_grad + hidden_part
    num_grad = (hidden_grad / query_den).astype(BF16)
    den_grad = -jnp.sum(hidden_grad * recall, axis=1, keepdims=True) / query_den
    dots_grad = ((dot_nt(num_grad, solved) + den_grad) * own_mask).astype(BF16)
    query_grad = feature_map_back(query_mem.astype(F32), dot_nn(dots_grad, phi_key), jnp.roll).astype(BF16)
    solved_direct = dot_tn(query_dots.astype(BF16), num_grad)
    key_direct = feature_map_back(key_mem.astype(F32), dot_tn(dots_grad, phi_query), jnp.roll)
    solved_direct = scatter_columns(solved_direct, "tensor")
    solved_direct = jnp.sum(lax.all_gather(solved_direct.astype(BF16), "seg").astype(F32), axis=0)
    value_grad = solve_backward(key_dots, key_den, solved_direct)
    read = value_part - solved_part
    key_den_grad = jnp.sum(value_grad * read, axis=1, keepdims=True) / key_den
    back = (-value_grad / key_den).astype(BF16)
    key_dots_grad = (dot_nt(back, solved_part.astype(BF16)) + key_den_grad) * mask
    both = (key_dots_grad + key_dots_grad.T).astype(BF16)
    key_solve = feature_map_back(key_mem.astype(F32), dot_nn(both, phi_key), jnp.roll)
    mine = (jnp.arange(key_solve.shape[0]) // MEM == seg)[:, None]
    key_direct = key_direct + jnp.where(mine, key_solve, 0.0)
    key_direct = scatter_columns(key_direct, "tensor")
    key_grad = jnp.sum(lax.all_gather(key_direct.astype(BF16), "seg").astype(F32), axis=0).astype(BF16)
    value_low = value_grad.astype(BF16)
    mem_width = mem_rows.shape[1] // lax.axis_size("seg")
    mem_cols = lax.dynamic_slice_in_dim(mem_rows, seg * mem_width, mem_width, 1)
    mem_key_grad = dot_tn(mem_cols, key_grad)
    mem_value_grad = dot_tn(mem_cols, value_low)
    return (
        hidden_grad, query_grad, key_grad, value_low,
        (gain_attn, gain_mlp, shift_attn, shift_mlp, jnp.sum(after_grad, axis=0, keepdims=True), jnp.sum(own_grad, axis=0, keepdims=True)),
        (attn_grad, attn_bias_grad, out_grad, fc_grad, fc_bias_grad, proj_grad, mem_key_grad, mem_value_grad),
    )


def general_device(
    inputs, out_grad, item_lengths, norm_gains, norm_biases, w_attn, attn_bias, w_out, out_biases, w_fc, fc_bias,
    w_proj, w_mem_keys, w_mem_value,
):
    section, seg, part = (lax.axis_index(name) for name in ("section", "seg", "tensor"))
    segments, parts = lax.axis_size("seg"), lax.axis_size("tensor")
    layers = lax.axis_size("section")
    mask = reach_mask(item_lengths)[section]
    weights = (norm_gains, norm_biases, w_attn, attn_bias, w_out, out_biases, w_fc, fc_bias, w_proj, w_mem_keys, w_mem_value)
    weights = [lax.all_gather(w, "section", axis=0, tiled=True) for w in weights]
    full_keys = lax.all_gather(weights[9], "tensor", axis=3, tiled=True)
    rows_all, grad_all = inputs[section], out_grad[section]
    chunk = rows_all.shape[0] // parts
    own_rows = lax.dynamic_slice_in_dim(rows_all, part * chunk, chunk, 0)
    place = (seg, part)
    saved, layer_params = [], []
    for layer in range(layers):
        mems = lax.all_gather(own_rows[-MEM:], ("seg", "tensor"), axis=0)
        mem_rows = mems[parts - 1 :: parts].reshape(segments * MEM, -1)
        params = tuple(w[layer] for w in weights[:9]) + (full_keys[layer, 0], full_keys[layer, 1], weights[10][layer])
        output, kept = layer_forward(own_rows, mem_rows, mask, place, params)
        saved.append(kept)
        layer_params.append(params)
        own_rows = output.astype(BF16)
    own_grad = lax.dynamic_slice_in_dim(grad_all, part * chunk, chunk, 0).astype(F32)
    rows_grads, matrix_grads = [None] * layers, [None] * layers
    for layer in reversed(range(layers)):
        params, kept = layer_params[layer], saved[layer]
        hidden_grad, query_grad, key_grad, value_low, rows_grads[layer], grads = layer_backward(own_grad, kept, mask, place, params)
        w_q = params[9]
        keys_here = lax.dynamic_slice_in_dim(key_grad, seg * MEM, MEM, 0)
        values_here = lax.dynamic_slice_in_dim(value_low, seg * MEM, MEM, 0)
        tail = dot_nt(keys_here, weights[9][layer, 1]) + dot_nt(values_here, params[11])
        tail = jnp.sum(lax.all_gather(tail.astype(BF16), "tensor").astype(F32), axis=0)
        tail = jnp.concatenate([jnp.zeros((chunk - MEM, tail.shape[1]), F32), tail], axis=0)
        rows_grad = hidden_grad + dot_nt(query_grad, w_q) + jnp.where(part == parts - 1, tail, 0.0)
        own_grad = rows_grad.astype(BF16).astype(F32)
        rows_full = gather_rows(kept[0], "tensor")
        query_cols = lax.all_to_all(query_grad.reshape(chunk, parts, -1).transpose(1, 0, 2), "tensor", 0, 0, tiled=True)
        query_cols = query_cols.reshape(chunk * parts, -1)
        matrix_grads[layer] = grads + (dot_tn(rows_full, query_cols),)
    input_grad = gather_rows(own_grad.astype(BF16), "tensor")[None]

    def over_layers(values):
        return lax.psum_scatter(jnp.stack(values), "section", scatter_dimension=0, tiled=True)

    rows_sums = lax.psum(over_layers([jnp.concatenate(r, axis=0) for r in rows_grads]), ("seg", "tensor"))

    def spread(index, axis):
        stacked = jnp.stack([g[index] for g in matrix_grads]).astype(BF16)
        pair = lax.all_to_all(stacked, "section", 0, 0, tiled=True)
        both = jnp.sum(pair.astype(F32), axis=0)
        cut = both.astype(BF16).reshape(both.shape[:axis] + (segments, -1) + both.shape[axis + 1 :])
        got = lax.all_to_all(cut, "seg", axis, axis, tiled=True)
        return jnp.sum(got.astype(F32), axis=axis)[None]

    biases = lax.psum(
        (over_layers([g[1] for g in matrix_grads]), over_layers([g[4] for g in matrix_grads])), "seg"
    )
    query_w = spread(8, 0)
    key_w = over_layers([g[6] for g in matrix_grads])
    return (
        input_grad,
        rows_sums[:, 0:2],
        rows_sums[:, 2:4],
        spread(0, 1),
        biases[0],
        spread(2, 1),
        rows_sums[:, 4:6],
        spread(3, 0),
        biases[1],
        spread(5, 1),
        jnp.stack([query_w, key_w], axis=1),
        over_layers([g[7] for g in matrix_grads]),
    )


def solution(mesh):
    def per_device(*args):
        inputs, out_grad, item_lengths = args[:3]
        S, T = mesh.shape["seg"], mesh.shape["tensor"]
        w_attn, w_fc, w_keys = args[5], args[9], args[12]
        z = Sizes(
            mesh,
            (
                (0, inputs.shape[1] * S, inputs.shape[2]), (0, 0, 0, w_attn.shape[3] * T), (0, 0, w_fc.shape[2] * T),
                (0, 0, 0, w_keys.shape[3] * T),
            ),
        )
        scratch = scratch_of(z)
        D = z.width
        outs = dict(
            input_grad=((1, z.rows, D), BF16), gain_grads=((1, 2, D), F32), shift_grads=((1, 2, D), F32),
            attn_grads=((1, 3, z.cut, z.heads_w), F32), abias_grads=((1, 2, z.heads_w), F32),
            out_grads=((1, z.heads_w, z.cut), F32), obias_grads=((1, 2, D), F32), fc_grads=((1, z.cut, z.units), F32),
            fcb_grads=((1, z.units), F32), proj_grads=((1, z.cut, z.units), F32),
            mkey_grads=((1, 2, z.cut, z.keys_w), F32), mvalue_grads=((1, z.cut, z.val_w), F32),
        )
        names = tuple(scratch)
        vmem, anywhere = pl.BlockSpec(memory_space=pltpu.VMEM), pl.BlockSpec(memory_space=pl.ANY)
        shapes = [jax.ShapeDtypeStruct(*shape) for shape in outs.values()]
        flip = lambda w: jnp.swapaxes(w, -1, -2)
        results = pl.pallas_call(
            functools.partial(kernel, z, names),
            out_shape=shapes,
            in_specs=[anywhere, anywhere, pl.BlockSpec(memory_space=pltpu.SMEM)] + [anywhere] * 11,
            out_specs=[vmem] * len(outs),
            scratch_shapes=list(scratch.values()),
            compiler_params=pltpu.CompilerParams(
                collective_id=0, has_side_effects=True, vmem_limit_bytes=63 * 2**20
            ),
            name="two_layers",
        )(*args[:5], flip(w_attn), *args[6:12], flip(w_keys), flip(args[13]))
        results = list(pl.pallas_call(
            hand_out, out_shape=shapes, in_specs=[vmem] * len(outs), out_specs=[vmem] * len(outs), name="hand_out"
        )(*results))
        results[9] = flip(results[9])
        return tuple(results)

    return jax.shard_map(
        per_device if mesh.shape["seg"] * MEM <= 128 else general_device,
        mesh=mesh,
        in_specs=(
            P(None, "seg", None),
            P(None, "seg", None),
            P(),
            P("section", None, None),
            P("section", None, None),
            P("section", None, None, "tensor"),
            P("section", None, "tensor"),
            P("section", "tensor", None),
            P("section", None, None),
            P("section", None, "tensor"),
            P("section", "tensor"),
            P("section", "tensor", None),
            P("section", None, None, "tensor"),
            P("section", None, "tensor"),
        ),
        out_specs=(
            P("section", "seg", None),
            P("section", None, None),
            P("section", None, None),
            P("section", None, "seg", "tensor"),
            P("section", None, "tensor"),
            P("section", "tensor", "seg"),
            P("section", None, None),
            P("section", "seg", "tensor"),
            P("section", "tensor"),
            P("section", "tensor", "seg"),
            P("section", None, "seg", "tensor"),
            P("section", "seg", "tensor"),
        ),
        check_vma=False,
    )
```

```python
import functools
from types import SimpleNamespace
from typing import Any, NamedTuple

import jax
import jax.numpy as jnp
from jax import lax
from jax.experimental import pallas as pl
from jax.experimental.pallas import tpu as pltpu
from jax.sharding import PartitionSpec as P

HEAD_DIM = 64
NU = 3
MEM = 16
EPSILON = 1e-05
F32 = jnp.float32
BF16 = jnp.bfloat16
GELU_A = 0.7978845608028654
GELU_B = 0.044715
LAYERS = 2
MESH = pl.DeviceIdType.MESH


def dot_nn(left, right):
    return lax.dot_general(left, right, (((1,), (0,)), ((), ())), preferred_element_type=F32)


def dot_nt(left, right):
    return lax.dot_general(left, right, (((1,), (1,)), ((), ())), preferred_element_type=F32)


def dot_tn(left, right):
    return lax.dot_general(left, right, (((0,), (0,)), ((), ())), preferred_element_type=F32)


def doubled_softplus(projected):
    small = jnp.exp(-jnp.abs(projected))
    tail = jnp.where(small < 1e-3, small - 0.5 * small * small, jnp.log1p(small))
    return jnp.concatenate(
        [jnp.maximum(projected, 0.0) + tail, jnp.maximum(-projected, 0.0) + tail], axis=1
    )


def feature_map(projected, roll=pltpu.roll):
    doubled = doubled_softplus(projected)
    return jnp.concatenate([doubled * roll(doubled, j, 1) for j in range(1, NU + 1)], axis=1)


def feature_map_back(projected, phi_grad, roll=pltpu.roll):
    doubled = doubled_softplus(projected)
    width = doubled.shape[1]
    total = jnp.zeros_like(doubled)
    for j in range(1, NU + 1):
        part = phi_grad[:, (j - 1) * width : j * width]
        total = total + part * roll(doubled, j, 1) + roll(part * doubled, width - j, 1)
    half = width // 2
    gate = 1.0 / (1.0 + jnp.exp(-projected))
    return total[:, :half] * gate - total[:, half:] * (1.0 - gate)


def norm_rows(hidden):
    centered = hidden - jnp.mean(hidden, axis=1, keepdims=True)
    scale = lax.rsqrt(jnp.mean(centered * centered, axis=1, keepdims=True) + EPSILON)
    return centered * scale, scale


def norm_back(hidden, gain_row, grad):
    unit, scale = norm_rows(hidden)
    unit_grad = grad * gain_row
    mean_grad = jnp.mean(unit_grad, axis=1, keepdims=True)
    mean_both = jnp.mean(unit_grad * unit, axis=1, keepdims=True)
    return (
        scale * (unit_grad - mean_grad - unit * mean_both),
        jnp.sum(grad * unit, axis=0, keepdims=True),
        jnp.sum(grad, axis=0, keepdims=True),
    )


def gelu_and_slope(pre):
    square = pre * pre
    bent = jnp.tanh(GELU_A * (pre + GELU_B * square * pre))
    value = 0.5 * pre * (1.0 + bent)
    slope = 0.5 * (1.0 + bent) + 0.5 * pre * (1.0 - bent * bent) * (
        GELU_A * (1.0 + 3.0 * GELU_B * square)
    )
    return value, slope


def xor_peer(place, other, count):
    total, bit = 0, 1
    while bit < count:
        mine = lax.rem(lax.div(place, bit), 2)
        total = total + bit * (1 - mine if other & bit else mine)
        bit *= 2
    return total


def split(values):
    high = values.astype(BF16)
    return high, (values - high.astype(F32)).astype(BF16)


def plus(first, others, count):
    total = first.astype(F32)
    for i in range(count):
        total = total + others[i].astype(F32)
    return total


class Sizes:
    def __init__(self, mesh, shapes):
        self.segs, self.parts = mesh.shape["seg"], mesh.shape["tensor"]
        inputs, w_attn, w_fc, w_keys = shapes
        self.rows, self.width = inputs[1] // self.segs, inputs[2]
        self.chunk = self.rows // self.parts
        self.mems = self.segs * MEM
        self.heads_w = w_attn[3] // self.parts
        self.heads = self.heads_w // HEAD_DIM
        self.units = w_fc[2] // self.parts
        self.keys = w_keys[3]
        self.keys_w = self.keys // self.parts
        self.phi = 2 * self.keys * NU
        self.val_w = self.width // self.parts
        self.cut = self.width // self.segs
        self.cut_pad = -(-self.cut // 16) * 16
        self.sems = 120 + 48 * self.parts + 2 * self.segs * (self.parts + 16)


def scratch_of(z):
    S, T, R, D, C, M = z.segs, z.parts, z.rows, z.width, z.chunk, z.mems
    bf = lambda *d: pltpu.VMEM(d, BF16)
    fl = lambda *d: pltpu.VMEM(d, F32)
    return dict(
        gains=fl(2, 2, D), shifts=fl(2, 2, D), w_attn=bf(2, 3, z.heads_w, D), attn_bias=fl(2, 2, z.heads_w),
        w_out=bf(2, z.heads_w, D), out_biases=fl(2, 2, D), w_fc=bf(2, D, z.units), fc_bias=fl(2, 1, z.units),
        w_proj=bf(2, z.units, D), w_keys=bf(2, 2, z.keys, D), w_value=bf(2, z.val_w, D),
        xfull=bf(2, R, D), gfull=bf(2, R, D), mem_rows=bf(2, M, D),
        keyb=bf(2, M, z.keys), phik=bf(2, M, z.phi), kdots=fl(2, M, M), vpart=fl(2, M, z.val_w),
        upart=fl(2, M, z.val_w), uall=bf(2, T, M, z.val_w), qmem=bf(2, C, z.keys), phiq=bf(2, C, z.phi),
        qdots=fl(2, C, M), recall=fl(2, C, D), hidden=fl(2, C, D), normed=bf(2, R, D), qkv=bf(2, 3, R, z.heads_w),
        probs=fl(2, z.heads, R, R), mixed=bf(2, R, z.heads_w), after=fl(2, C, D), normed_mlp=bf(2, R, D),
        slope=fl(2, R, z.units), act=bf(2, R, z.units), rs_src=bf(7, R, D), rs_own=fl(R, D), q_src=bf(R, z.keys_w), q_parts=bf(T, C, z.keys_w), k_parts=bf(T, M, z.keys_w), rs_dst=bf(7, T - 1, C, D),
        low2=bf(2, R, D), dpre=bf(R, z.units), dqkv=bf(3, R, z.heads_w),
        x1_src=bf(2, T, M, z.val_w), x1_dst=bf(2, T - 1, M, z.val_w), x1_mid=bf(2, M, z.val_w), x1_far=bf(2, max(S - 1, 1), M, z.val_w),
        x2_src=bf(2, T, M, z.keys_w), x2_dst=bf(2, T - 1, M, z.keys_w), x2_mid=bf(2, M, z.keys_w), x2_far=bf(2, max(S - 1, 1), M, z.keys_w), x4_src=bf(2, T, M, z.keys_w), x4_dst=bf(2, T - 1, M, z.keys_w), ksolve=fl(M, z.keys), dk_direct=fl(M, z.keys_w),
        dq_src=bf(2, T, C, z.keys_w), dq_all=bf(2, R, z.keys_w), dv=bf(M, z.val_w), vgrad=fl(M, z.val_w),
        x3_src=bf(2, MEM, D), x3_dst=bf(2, T - 1, MEM, D), final=bf(R, D), tmp=fl(C, D),
        grad_p=bf(2, S, z.cut_pad, z.units), grad_c=bf(2, S, z.cut_pad, z.units), grad_qk=bf(2, S, z.cut_pad, 2 * z.heads_w),
        grad_vo=bf(2, S, z.cut_pad, 2 * z.heads_w), grad_q=bf(2, S, z.cut_pad, z.keys_w),
        pair_f=bf(2, S, z.cut_pad, z.units), pair_a=bf(2, S, z.cut_pad, 2 * z.heads_w), pair_q=bf(2, S, z.cut_pad, z.keys_w), relay_f=bf(2, 2, z.cut_pad, z.units), relay_a=bf(2, 2, z.cut_pad, 2 * z.heads_w), relay_q=bf(2, 2, z.cut_pad, z.keys_w),
        far_p=bf(S, z.cut_pad, z.units), far_c=bf(S, z.cut_pad, z.units), far_qk=bf(S, z.cut_pad, 2 * z.heads_w),
        far_vo=bf(S, z.cut_pad, 2 * z.heads_w), far_q=bf(S, z.cut_pad, z.keys_w), dqk=bf(R, 2 * z.heads_w),
        mem_k=fl(2, D, z.keys_w), mem_v=fl(2, D, z.val_w), pair_k=fl(z.cut, z.keys_w), pair_v=fl(z.cut, z.val_w),
        small=fl(2, 16, D), pair_small=fl(16, D), part_small=fl(T, 8, D), sum_small=fl(16, D), seg_small=bf(S, 16, D),
        send=pltpu.SemaphoreType.DMA((z.sems,)), recv=pltpu.SemaphoreType.DMA((z.sems,)), load=pltpu.SemaphoreType.DMA((14, 2)),
        shard=pltpu.SemaphoreType.DMA((2, 2, T)),
    )


class Outer(NamedTuple):
    inputs: Any
    out_grad: Any
    item_lengths: Any
    norm_gains: Any
    norm_biases: Any
    w_attn_in: Any
    attn_bias_in: Any
    w_out_in: Any
    out_biases_in: Any
    w_fc_in: Any
    fc_bias_in: Any
    w_proj_in: Any
    w_keys_in: Any
    w_value_in: Any
    input_grad: Any
    gain_grads: Any
    shift_grads: Any
    attn_grads: Any
    abias_grads: Any
    out_grads: Any
    obias_grads: Any
    fc_grads: Any
    fcb_grads: Any
    proj_grads: Any
    mkey_grads: Any
    mvalue_grads: Any


def kernel(z, held_names, *refs):
    outer = len(Outer._fields)
    r = SimpleNamespace(**Outer(*refs[:outer])._asdict(), **dict(zip(held_names, refs[outer:])))
    S, T, R, D, C, M = z.segs, z.parts, z.rows, z.width, z.chunk, z.mems
    c, s, t = (lax.axis_index(a) for a in ("section", "seg", "tensor"))
    other = 1 - c
    tpeers = [xor_peer(t, i, T) for i in range(T)]
    to_seg = [lax.rem(s + i, S) for i in range(S)]
    own = pl.ds(pl.multiple_of(t * C, C), C)
    seg_rows = pl.ds(pl.multiple_of(s * MEM, MEM), MEM)
    used = [0]
    sent = []
    owed = {}

    def alloc(count):
        used[0] += count
        assert used[0] <= z.sems
        return used[0] - count

    def owe(copies):
        def wait():
            for copy in copies:
                copy.wait_recv()

        owed[id(copies)] = wait
        return id(copies)

    def wait_bytes(ref, semaphore):
        pltpu.make_async_copy(ref, ref, semaphore).wait()

    def remote(src, dst, index, device, recv=None):
        copy = pltpu.make_async_remote_copy(
            src_ref=src, dst_ref=dst, send_sem=r.send.at[index],
            recv_sem=r.recv.at[index] if recv is None else recv, device_id=device, device_id_type=MESH,
        )
        return copy

    def to_parts(src_of, dst):
        base = alloc(T - 1)
        copies = []
        for i in range(T - 1, 0, -1):
            copy = remote(src_of(tpeers[i]), dst(i), base + i - 1, (c, s, tpeers[i]))
            copy.start()
            copies.append(copy)
        sent.extend((copy, None) for copy in copies)
        return owe(copies)

    def to_segs(src_of, dst):
        base = alloc(S - 1)
        copies = [
            remote(src_of(to_seg[i]), dst(i), base + i - 1, (c, to_seg[i], t)) for i in range(1, S)
        ]
        for copy in copies:
            copy.start()
        sent.extend((copy, None) for copy in copies)
        return owe(copies)

    def arrive(key):
        owed.pop(key)()

    def wait_load(ref, layer):
        arrive((id(ref), layer))

    barrier = pltpu.get_barrier_semaphore()
    greeted = [(other, to_seg[i], t) for i in range(S)] + [(c, to_seg[i], tpeers[j]) for i in range(S) for j in range(T) if i or j]
    for device in greeted:
        pl.semaphore_signal(barrier, inc=1, device_id=device, device_id_type=MESH)

    loads = [
        (r.w_value, r.w_value_in.at[0]), (r.gains, r.norm_gains.at[0]), (r.shifts, r.norm_biases.at[0]),
        (r.attn_bias, r.attn_bias_in.at[0]), (r.out_biases, r.out_biases_in.at[0]), (r.w_attn, r.w_attn_in.at[0]), (r.w_out, r.w_out_in.at[0]), (r.w_fc, r.w_fc_in.at[0]),
        (r.w_proj, r.w_proj_in.at[0]), (r.fc_bias, r.fc_bias_in),
    ]
    input_copy = pltpu.make_async_copy(r.inputs.at[c], r.xfull.at[0], r.load.at[10, 0])
    input_copy.start()
    owed[0] = input_copy.wait
    def shard_rows(part):
        return pl.ds(pl.multiple_of(part * z.keys_w, 16), z.keys_w)

    for which in (0, 1):
        pltpu.make_async_copy(
            r.w_keys_in.at[0, which], r.w_keys.at[c, which, shard_rows(t)], r.shard.at[c, which, 0]
        ).start()
    def load_own(kinds):
        for kind in kinds:
            held, source = loads[kind]
            pltpu.make_async_copy(source, held.at[c], r.load.at[kind, c]).start()

    def load_other(kinds):
        for kind in kinds:
            held, source = loads[kind]
            copy = remote(source, held.at[c], pair_base + kind, (other, s, t), r.load.at[kind, c])
            copy.start()
            sent.append((copy, None))
            for layer in range(LAYERS):
                owed[id(held), layer] = functools.partial(wait_bytes, held.at[layer], r.load.at[kind, layer])

    early, middle = range(0, 5), range(5, 7)
    load_own(range(len(loads)))
    grad_copy = pltpu.make_async_copy(r.out_grad.at[c], r.gfull.at[1], r.load.at[11, 0])
    grad_copy.start()
    owed[1] = grad_copy.wait

    pl.semaphore_wait(barrier, len(greeted))

    first_rows = to_segs(
        lambda _: r.inputs.at[c, pl.ds(R - MEM, MEM)], lambda i: r.mem_rows.at[0, seg_rows]
    )

    def shard_wait(layer, which, i):
        wait_bytes(r.w_keys.at[layer, which, pl.ds(0, z.keys_w)], r.shard.at[layer, which, i])

    def peer_shards(core, layer, which):
        @pl.when(c == core)
        def _():
            for i in range(1, T):
                shard_wait(layer, which, i)

    def spread_shard(layer, which):
        base = alloc(T - 1)
        place = r.w_keys.at[layer, which, shard_rows(t)]
        copies = [
            remote(r.w_keys_in.at[0, which], place, base + i - 1, (c, s, tpeers[i]), r.shard.at[layer, which, i])
            for i in range(T - 1, 0, -1)
        ]

        @pl.when(c == layer)
        def _():
            for copy in copies:
                copy.start()

        sent.extend((copy, c == layer) for copy in copies)
        owed[11, layer, which] = functools.partial(peer_shards, layer, layer, which)

    def forward_shard(layer, which):
        arrive((11, layer, which))
        base = alloc(T - 1)
        copies = []
        for i in range(1, T):
            place = r.w_keys.at[layer, which, shard_rows(tpeers[i])]
            copies.append(remote(place, place, base + i - 1, (other, s, t), r.shard.at[layer, which, i]))

        @pl.when(c == layer)
        def _():
            for copy in copies:
                copy.start()

        sent.extend((copy, c == layer) for copy in copies)
        owed[12, layer, which] = functools.partial(peer_shards, 1 - layer, layer, which)

    base = alloc(2)
    for which in (0, 1):
        copy = remote(
            r.w_keys_in.at[0, which], r.w_keys.at[c, which, shard_rows(t)], base + which, (other, s, t), r.shard.at[c, which, 0]
        )
        copy.start()
        sent.append((copy, None))
        for layer in range(LAYERS):
            owed[10, layer, which] = functools.partial(shard_wait, layer, which, 0)
    pair_base = alloc(len(loads))
    load_other(early)

    row_seg = lax.broadcasted_iota(jnp.int32, (M, 1), 0) // MEM
    col_seg = lax.broadcasted_iota(jnp.int32, (1, M), 1) // MEM
    row_item, col_item, own_item = jnp.zeros((M, 1), jnp.int32), jnp.zeros((1, M), jnp.int32), 0
    begin = 0
    for i in range(r.item_lengths.shape[1]):
        length = r.item_lengths[c, i]
        there = jnp.where(length > 0, begin, S)
        row_item = row_item + (row_seg >= there).astype(jnp.int32)
        col_item = col_item + (col_seg >= there).astype(jnp.int32)
        own_item = own_item + jnp.where(s >= there, 1, 0)
        begin = begin + length
    key_mask = jnp.where((row_item == col_item) & (row_seg > col_seg), 1.0, 0.0)
    row_mask = jnp.where((col_item == own_item) & (col_seg < s), 1.0, 0.0)
    lane_head = lax.broadcasted_iota(jnp.int32, (1, z.heads_w), 1) // HEAD_DIM
    head_rows = [(lane_head == h).astype(F32).astype(BF16) for h in range(z.heads)]
    rs_count = [0]

    def reduce_rows(partial):
        k = rs_count[0]
        rs_count[0] += 1
        r.rs_own[...] = partial
        r.rs_src[k] = partial.astype(BF16)
        copies = to_parts(
            lambda peer: r.rs_src.at[k, pl.ds(pl.multiple_of(peer * C, C), C)], lambda i: r.rs_dst.at[k, i - 1]
        )

        def finish():
            arrive(copies)
            total = r.rs_own[own, :]
            for i in range(T - 1):
                total = total + r.rs_dst[k, i].astype(F32)
            return total

        return finish

    def share_rows(ref, layer):
        return to_parts(lambda _: ref.at[layer, own], lambda i: ref.at[layer, own])

    def forward(l):
        own_shard = shard_rows(t)
        if l == 0:
            arrive(0)
            arrive((10, 0, 0))
            r.q_src[...] = dot_nt(r.xfull[0], r.w_keys[0, 0, own_shard, :]).astype(BF16)
            r.q_parts[t] = r.q_src[own, :]
            query_step = to_parts(
                lambda peer: r.q_src.at[pl.ds(pl.multiple_of(peer * C, C), C)], lambda i: r.q_parts.at[t]
            )
            r.mem_rows[0, seg_rows, :] = r.xfull[0, R - MEM :, :]
            arrive((10, 0, 1))
            arrive(first_rows)
            mems = r.mem_rows[0]
            r.k_parts[t] = dot_nt(mems, r.w_keys[0, 1, own_shard, :]).astype(BF16)
            key_step = to_parts(lambda _: r.k_parts.at[t], lambda i: r.k_parts.at[t])
            load_other(middle)
            arrive(query_step)
            queries_mem = jnp.concatenate([r.q_parts[u] for u in range(T)], axis=1)
        else:
            for which in (0, 1):
                arrive((10, 1, which))
                arrive((12, 1, which))
            queries_mem = dot_nt(r.xfull[1, own, :], r.w_keys[1, 0]).astype(BF16)
        x = r.xfull[l, own, :]
        r.qmem[l] = queries_mem
        phi_query = feature_map(queries_mem.astype(F32)).astype(BF16)
        r.phiq[l] = phi_query
        wait_load(r.w_value, l)
        if l == 1:
            arrive(4)
            mems = r.mem_rows[1]
        value_part = dot_nt(mems, r.w_value[l])
        r.vpart[l] = value_part
        r.upart[l] = value_part
        if l == 0:
            arrive(key_step)
            keys = jnp.concatenate([r.k_parts[u] for u in range(T)], axis=1)
        else:
            keys = dot_nt(mems, r.w_keys[1, 1]).astype(BF16)
        r.keyb[l] = keys
        phi_key = feature_map(keys.astype(F32)).astype(BF16)
        r.phik[l] = phi_key
        key_dots = dot_nt(phi_key, phi_key) * key_mask
        r.kdots[l] = key_dots
        key_den = 1.0 + jnp.sum(key_dots, axis=1, keepdims=True)
        for k in range(1, S):
            rows = slice(k * MEM, (k + 1) * MEM)
            read = dot_nn(key_dots[rows].astype(BF16), r.upart[l].astype(BF16)) / key_den[rows]
            r.upart[l, rows, :] = value_part[rows] - read
        r.uall[l, t] = r.upart[l].astype(BF16)
        solved = to_parts(lambda _: r.uall.at[l, t], lambda i: r.uall.at[l, t])
        if l == 0:
            spread_shard(1, 1)
        else:
            spread_shard(0, 0)
        query_dots = dot_nt(phi_query, phi_key) * row_mask
        r.qdots[l] = query_dots
        query_den = 1.0 + jnp.sum(query_dots, axis=1, keepdims=True)
        for ref in (r.gains, r.shifts, r.attn_bias, r.out_biases):
            wait_load(ref, l)
        arrive(solved)
        high, low = split(query_dots)
        recall = [dot_nn(high, r.uall[l, u]) + dot_nn(low, r.uall[l, u]) for u in range(T)]
        recall = jnp.concatenate(recall, axis=1) / query_den
        r.recall[l] = recall
        hidden = x.astype(F32) + recall.astype(BF16).astype(F32)
        r.hidden[l] = hidden
        unit, _ = norm_rows(hidden)
        r.normed[l, own, :] = (unit * r.gains[l, 0:1] + r.shifts[l, 0:1]).astype(BF16)
        shared = share_rows(r.normed, l)
        if l == 0:
            load_other([9, 7])
        wait_load(r.w_attn, l)
        wait_load(r.w_out, l)
        arrive(shared)
        if l == 0:
            spread_shard(1, 0)
        else:
            spread_shard(0, 1)
        normed = r.normed[l]
        queries = (dot_nt(normed, r.w_attn[l, 0]) + r.attn_bias[l, 0:1]).astype(BF16)
        key_heads = dot_nt(normed, r.w_attn[l, 1]).astype(BF16)
        values = (dot_nt(normed, r.w_attn[l, 2]) + r.attn_bias[l, 1:2]).astype(BF16)
        r.qkv[l, 0] = queries
        r.qkv[l, 1] = key_heads
        r.qkv[l, 2] = values
        causal = lax.broadcasted_iota(jnp.int32, (R, R), 0) >= lax.broadcasted_iota(jnp.int32, (R, R), 1)
        mixed = jnp.zeros((R, z.heads_w), F32)
        for h in range(z.heads):
            scores = dot_nt(queries, key_heads * head_rows[h]) * HEAD_DIM ** (-0.5)
            scores = jnp.where(causal, scores, -jnp.inf)
            heights = jnp.exp(scores - jnp.max(scores, axis=1, keepdims=True))
            probs = heights * (1.0 / jnp.sum(heights, axis=1, keepdims=True))
            r.probs[l, h] = probs
            mixed = mixed + dot_nn(probs.astype(BF16), values * head_rows[h])
        mixed = mixed.astype(BF16)
        r.mixed[l] = mixed
        finish = reduce_rows(dot_nn(mixed, r.w_out[l]))
        if l == 0:
            load_other([8])
        after = r.hidden[l] + finish() + r.out_biases[l, 0:1]
        r.after[l] = after
        unit, _ = norm_rows(after)
        r.normed_mlp[l, own, :] = (unit * r.gains[l, 1:2] + r.shifts[l, 1:2]).astype(BF16)
        shared = share_rows(r.normed_mlp, l)
        wait_load(r.w_fc, l)
        wait_load(r.fc_bias, l)
        wait_load(r.w_proj, l)
        if l == 0:
            forward_shard(1, 1)
            forward_shard(1, 0)
        arrive(shared)
        row_step = share_rows(r.xfull, 1) if l == 1 else None
        pre = dot_nn(r.normed_mlp[l], r.w_fc[l]) + r.fc_bias[l]
        activation, slope = gelu_and_slope(pre)
        activation = activation.astype(BF16)
        r.act[l] = activation
        r.slope[l] = slope
        if l == 0:
            finish = reduce_rows(dot_nn(activation, r.w_proj[l]))
            output = r.after[l] + finish() + r.out_biases[l, 1:2]
            r.xfull[1, own, :] = output.astype(BF16)
            base, places = alloc(S), alloc(S * T)
            last = r.xfull.at[1, pl.ds(R - MEM, MEM)]

            @pl.when(t == T - 1)
            def _():
                r.mem_rows[1, seg_rows, :] = r.xfull[1, R - MEM :, :]
                for i in range(S - 1, -1, -1):
                    for j in range(1 if i == 0 else 0, T):
                        copy = pltpu.make_async_remote_copy(
                            src_ref=last, dst_ref=r.mem_rows.at[1, seg_rows], send_sem=r.send.at[places + i * T + j],
                            recv_sem=r.recv.at[base + i], device_id=(c, to_seg[i], tpeers[j]), device_id_type=MESH,
                        )
                        copy.start()

            def wait_rows(i):
                wait_bytes(r.mem_rows.at[1, pl.ds(0, MEM)], r.recv.at[base + i])

            def wait_all():
                pl.when(t != T - 1)(functools.partial(wait_rows, 0))
                for i in range(1, S):
                    wait_rows(i)

            owed[4] = wait_all

            def drain():
                @pl.when(t == T - 1)
                def _():
                    for i in range(S):
                        for j in range(1 if i == 0 else 0, T):
                            wait_bytes(last, r.send.at[places + i * T + j])

            sent.append((drain, drain))
        return row_step

    fam_p, fam_c = (r.grad_p, r.pair_f, r.far_p, 0, r.relay_f), (r.grad_c, r.pair_f, r.far_c, 1, r.relay_f)
    fam_qk, fam_vo = (r.grad_qk, r.pair_a, r.far_qk, 0, r.relay_a), (r.grad_vo, r.pair_a, r.far_vo, 1, r.relay_a)
    fam_q = (r.grad_q, r.pair_q, r.far_q, None, r.relay_q)
    on_line = S == 4
    partner = s + 1 - 2 * lax.rem(s, 2)
    across = 2 - 2 * lax.div(s, 2)
    outer = jnp.logical_or(s == 0, s == 3)
    relays = {}

    def blocks_of(first_row, count):
        row, pieces = first_row, []
        while row < first_row + count:
            block, inside = row // z.cut, row % z.cut
            size = min(z.cut - inside, first_row + count - row)
            pieces.append((block, inside, row - first_row, size))
            row += size
        return pieces

    def weight_grad(l, family, *pairs):
        stripe = min(256, D)
        for k in range(0, D, stripe):
            parts = [dot_tn(left[:, k : k + stripe], right).astype(BF16) for left, right in pairs]
            grad = parts[0] if len(parts) == 1 else jnp.concatenate(parts, axis=1)
            for block, inside, row, size in blocks_of(k, stripe):
                family[0][l, block, inside : inside + size, :] = grad[row : row + size]

    def pair_send(src, dst):
        index = alloc(1)
        return remote(src, dst, index, (other, s, t))

    def adder_of(l, family):
        return l if family[3] is None else family[3]

    def hand_over(l, family):
        grad, pair, _, _, _ = family
        adder = adder_of(l, family)
        copy = pair_send(grad.at[l], pair.at[l])
        pl.when(c != adder)(copy.start)
        sent.append((copy, c != adder))
        return owe_owner(adder, [copy])

    def owe_owner(l, copies):
        def wait():
            @pl.when(c == l)
            def _():
                for copy in copies:
                    copy.wait_recv()

        owed[id(copies)] = wait
        return id(copies)

    def add_pair(l, family, key):
        grad, pair, _, _, _ = family
        arrive(key)

        @pl.when(c == adder_of(l, family))
        def _():
            @pl.loop(0, S)
            def _(j):
                grad[l, j] = (grad[l, j].astype(F32) + pair[l, j].astype(F32)).astype(BF16)

    def spread(l, family, direct):
        grad, _, far, _, relay = family
        adder = adder_of(l, family)
        near = adder == l
        direct = direct or not on_line
        base = alloc(S if direct else 5)
        steps = range(1, S) if direct else (1, 2)

        @pl.when(c == adder)
        def _():
            if direct:
                for i in range(S - 1, 0, -1):
                    remote(grad.at[l, to_seg[i]], far.at[i], base + i, (l, to_seg[i], t)).start()
            else:

                @pl.when(outer)
                def _():
                    for k in range(2):
                        remote(grad.at[l, across + k], relay.at[l, k], base + 3 + k, (c, partner, t)).start()

                remote(grad.at[l, partner], far.at[1], base + 1, (l, partner, t)).start()
            if near:
                far[0] = grad[l, s]
            else:
                remote(grad.at[l, s], far.at[0], base, (other, s, t)).start()

        if not direct:

            @pl.when(c == l)
            def _():
                for i in range(3, S):
                    far[i] = jnp.zeros(far.shape[1:], BF16)

            def pass_on():
                @pl.when(jnp.logical_and(c == adder, jnp.logical_not(outer)))
                def _():
                    for k in range(2):
                        wait_bytes(relay.at[l, k], r.recv.at[base + 3 + k])
                        place = across + k
                        grad[l, place] = (grad[l, place].astype(F32) + relay[l, k].astype(F32)).astype(BF16)
                        remote(grad.at[l, place], far.at[2], base + 3 + k, (l, place, t), r.recv.at[base + 2]).start()

            relays[id(far), l] = pass_on

        def wait():
            @pl.when(c == l)
            def _():
                for i in steps if near else (0, *steps):
                    wait_bytes(far.at[i], r.recv.at[base + i])

        def drain():
            @pl.when(c == adder)
            def _():
                ends = tuple(steps) if direct else (1, 3, 4)
                for i in ends if near else (0, *ends):
                    wait_bytes(far.at[0], r.send.at[base + i])

        owed[id(far), l] = wait
        sent.append((drain, drain))

    def pass_on(l, family):
        if (id(family[2]), l) in relays:
            relays.pop((id(family[2]), l))()

    def owe_small(l):
        copy = pair_send(r.small.at[l], r.pair_small)
        pl.when(c != l)(copy.start)
        sent.append((copy, c != l))
        return owe_owner(l, [copy])

    def owner_copies(l, copies):
        @pl.when(c == l)
        def _():
            for copy in copies:
                copy.start()

        sent.extend((copy, c == l) for copy in copies)
        return owe_owner(l, copies)

    def small_parts(l, key):
        arrive(key)

        @pl.when(c == l)
        def _():
            r.sum_small[...] = r.small[l] + r.pair_small[...]
            r.part_small[0] = r.sum_small[0:8, :]

        base = alloc(T - 1)
        return owner_copies(
            l, [remote(r.part_small.at[0], r.part_small.at[i], base + i - 1, (c, s, tpeers[i])) for i in range(1, T)]
        )

    def small_segs(l, key):
        arrive(key)

        @pl.when(c == l)
        def _():
            total = r.part_small[0]
            for i in range(1, T):
                total = total + r.part_small[i]
            r.sum_small[0:8, :] = total
            r.seg_small[0] = r.sum_small[...].astype(BF16)

        base = alloc(S - 1)
        return owner_copies(
            l, [remote(r.seg_small.at[0], r.seg_small.at[i], base + i - 1, (c, to_seg[i], t)) for i in range(1, S)]
        )

    def backward(l):
        if l == 1:
            arrive(1)
        grad_low = r.gfull[l]
        pre_grad = (r.slope[l] * dot_nt(grad_low, r.w_proj[l])).astype(BF16)
        r.dpre[...] = pre_grad
        finish = reduce_rows(dot_nt(pre_grad, r.w_fc[l]))
        own_grad = r.gfull[l, own, :].astype(F32)

        weight_grad(l, fam_p, (r.gfull.at[l], r.act[l]))
        pair_p = hand_over(l, fam_p)
        weight_grad(l, fam_c, (r.normed_mlp.at[l], r.dpre[...]))
        pair_c = hand_over(l, fam_c)
        r.small[l, 8:9, :] = jnp.sum(r.dpre[...].astype(F32), axis=0, keepdims=True)
        if l == 1:
            forward_shard(0, 0)
            forward_shard(0, 1)
        if l == 0:
            pass_on(1, fam_c)
            pass_on(1, fam_qk)
        add_pair(l, fam_p, pair_p)
        spread(l, fam_p, False)
        after_part, gain_mlp, shift_mlp = norm_back(r.after[l], r.gains[l, 1:2], finish())
        after_grad = own_grad + after_part
        r.tmp[...] = after_grad
        r.low2[l, own, :] = after_grad.astype(BF16)
        shared = share_rows(r.low2, l)
        r.small[l, 1:2, :] = gain_mlp
        r.small[l, 3:4, :] = shift_mlp
        r.small[l, 4:5, :] = jnp.sum(after_grad, axis=0, keepdims=True)
        r.small[l, 5:6, :] = jnp.sum(own_grad, axis=0, keepdims=True)
        add_pair(l, fam_c, pair_c)
        if l == 0:
            spread(l, fam_c, False)
            pass_on(1, fam_vo)
            pass_on(1, fam_q)
        arrive(shared)
        after_low = r.low2[l]
        mixed_grad = dot_nt(after_low, r.w_out[l]).astype(BF16)
        queries, key_heads, values = r.qkv[l, 0], r.qkv[l, 1], r.qkv[l, 2]
        q_grad = k_grad = v_grad = jnp.zeros((R, z.heads_w), F32)
        for h in range(z.heads):
            probs = r.probs[l, h]
            mixed_here = mixed_grad * head_rows[h]
            probs_grad = dot_nt(mixed_here, values)
            delta = jnp.sum(probs_grad * probs, axis=1, keepdims=True)
            score_grad = (probs * (probs_grad - delta)).astype(BF16)
            q_grad = q_grad + dot_nn(score_grad, key_heads * head_rows[h])
            k_grad = k_grad + dot_tn(score_grad, queries * head_rows[h])
            v_grad = v_grad + dot_tn(probs.astype(BF16), mixed_here)
        scale = HEAD_DIM ** (-0.5)
        r.dqkv[0] = (q_grad * scale).astype(BF16)
        r.dqkv[1] = (k_grad * scale).astype(BF16)
        r.dqkv[2] = v_grad.astype(BF16)
        r.dqk[...] = jnp.concatenate([r.dqkv[0], r.dqkv[1]], axis=1)
        finish = reduce_rows(sum(dot_nn(r.dqkv[i], r.w_attn[l, i]) for i in range(3)))

        weight_grad(l, fam_qk, (r.normed.at[l], r.dqk[...]))
        pair_qk = hand_over(l, fam_qk)
        weight_grad(l, fam_vo, (r.normed.at[l], r.dqkv[2]), (r.low2.at[l], r.mixed[l]))
        pair_vo = hand_over(l, fam_vo)
        for row, i in ((9, 0), (10, 2)):
            r.small[l, row : row + 1, : z.heads_w] = jnp.sum(r.dqkv[i].astype(F32), axis=0, keepdims=True)
        hidden_part, gain_attn, shift_attn = norm_back(r.hidden[l], r.gains[l, 0:1], finish())
        hidden_grad = r.tmp[...] + hidden_part
        r.tmp[...] = hidden_grad
        r.small[l, 0:1, :] = gain_attn
        r.small[l, 2:3, :] = shift_attn
        small_key = owe_small(l)
        query_den = 1.0 + jnp.sum(r.qdots[l], axis=1, keepdims=True)
        high, low = split(hidden_grad / query_den)
        den_grad = -jnp.sum((hidden_grad / query_den) * r.recall[l], axis=1, keepdims=True)
        highs = [high[:, u * z.val_w : (u + 1) * z.val_w] for u in range(T)]
        lows = [low[:, u * z.val_w : (u + 1) * z.val_w] for u in range(T)]
        dots_high, dots_low = split(r.qdots[l])
        for u in range(T):
            grad = dot_tn(dots_high, highs[u]) + dot_tn(dots_high, lows[u]) + dot_tn(dots_low, highs[u])
            r.x1_src[l, u] = grad.astype(BF16)
        value_step = to_parts(lambda peer: r.x1_src.at[l, peer], lambda i: r.x1_dst.at[l, i - 1])
        dots_grad = sum(dot_nt(highs[u], r.uall[l, u]) + dot_nt(lows[u], r.uall[l, u]) for u in range(T)) + den_grad
        dots_grad = (dots_grad * row_mask).astype(BF16)
        key_direct = feature_map_back(r.keyb[l].astype(F32), dot_tn(dots_grad, r.phiq[l]))
        for u in range(T):
            r.x2_src[l, u] = key_direct[:, u * z.keys_w : (u + 1) * z.keys_w].astype(BF16)
        key_step = to_parts(lambda peer: r.x2_src.at[l, peer], lambda i: r.x2_dst.at[l, i - 1])
        add_pair(l, fam_qk, pair_qk)
        add_pair(l, fam_vo, pair_vo)
        pass_on(l, fam_p)
        arrive(value_step)
        value_part = plus(r.x1_src[l, t], r.x1_dst.at[l], T - 1)
        r.x1_mid[l] = value_part.astype(BF16)
        value_step = to_segs(lambda _: r.x1_mid.at[l], lambda i: r.x1_far.at[l, i - 1])
        arrive(key_step)
        key_part = plus(r.x2_src[l, t], r.x2_dst.at[l], T - 1)
        r.x2_mid[l] = key_part.astype(BF16)
        key_step = to_segs(lambda _: r.x2_mid.at[l], lambda i: r.x2_far.at[l, i - 1])
        query_grad = feature_map_back(r.qmem[l].astype(F32), dot_nn(dots_grad, r.phik[l])).astype(BF16)
        for u in range(T):
            r.dq_src[l, u] = query_grad[:, u * z.keys_w : (u + 1) * z.keys_w]
        r.dq_all[l, own, :] = r.dq_src[l, t]
        query_step = to_parts(lambda peer: r.dq_src.at[l, peer], lambda i: r.dq_all.at[l, own])
        if l == 0:
            arrive((12, 0, 0))
            arrive((12, 0, 1))
        r.tmp[...] += dot_nn(query_grad, r.w_keys[l, 0])
        arrive(value_step)
        direct = plus(value_part, r.x1_far.at[l], S - 1)
        arrive(key_step)
        small_key = small_parts(l, small_key)
        for family in (fam_c, fam_qk, fam_vo) if l == 1 else (fam_qk, fam_vo):
            spread(l, family, False)
        key_dots = r.kdots[l]
        key_den = 1.0 + jnp.sum(key_dots, axis=1, keepdims=True)
        r.vgrad[...] = direct
        for k in range(S - 1, 0, -1):
            rows = slice(k * MEM, (k + 1) * MEM)
            back = -r.vgrad[rows, :] / key_den[rows]
            r.vgrad[...] += dot_tn(key_dots[rows].astype(BF16), back.astype(BF16))
        value_grad = r.vgrad[...]
        read = r.vpart[l] - r.upart[l]
        back = (-value_grad / key_den).astype(BF16)
        key_den_grad = -jnp.sum(back.astype(F32) * read, axis=1, keepdims=True)
        key_dots_grad = (dot_nt(back, r.upart[l].astype(BF16)) + key_den_grad) * key_mask
        both = (key_dots_grad + key_dots_grad.T).astype(BF16)
        key_solve = feature_map_back(r.keyb[l].astype(F32), dot_nn(both, r.phik[l]))
        r.ksolve[...] = key_solve
        r.dv[...] = value_grad.astype(BF16)
        r.dk_direct[...] = plus(key_part, r.x2_far.at[l], S - 1)
        tail = dot_nn(r.dv[seg_rows, :], r.w_value[l])
        tail = tail + dot_nn(r.dk_direct[seg_rows, :].astype(BF16), r.w_keys[l, 1, shard_rows(t), :])
        tail = tail + dot_nn(r.ksolve[seg_rows, :].astype(BF16), r.w_keys[l, 1])
        r.x3_src[l] = tail.astype(BF16)
        base, place = alloc(T - 1), alloc(1)

        for i in range(1, T):

            @pl.when(tpeers[i] == T - 1)
            def _():
                copy = pltpu.make_async_remote_copy(
                    src_ref=r.x3_src.at[l], dst_ref=r.x3_dst.at[l, i - 1], send_sem=r.send.at[place],
                    recv_sem=r.recv.at[base + i - 1], device_id=(c, s, tpeers[i]), device_id_type=MESH,
                )
                copy.start()

        def drain():
            @pl.when(t != T - 1)
            def _():
                wait_bytes(r.x3_src.at[l], r.send.at[place])

        sent.append((drain, drain))
        for u in range(T):
            r.x4_src[l, u] = key_solve[:, u * z.keys_w : (u + 1) * z.keys_w].astype(BF16)
        solve_step = to_parts(lambda peer: r.x4_src.at[l, peer], lambda i: r.x4_dst.at[l, i - 1])

        @pl.when(t == T - 1)
        def _():
            total = r.x3_src[l].astype(F32)
            for i in range(T - 1):
                wait_bytes(r.x3_dst.at[l, i], r.recv.at[base + i])
                total = total + r.x3_dst[l, i].astype(F32)
            r.tmp[C - MEM :, :] += total

        target = r.gfull.at[0] if l == 1 else r.final
        target[own, :] = r.tmp[...].astype(BF16)
        rows_step = to_parts(lambda _: target.at[own], lambda i: target.at[own])
        small_key = small_segs(l, small_key)
        arrive(query_step)
        if l == 1:
            arrive(row_step)
        weight_grad(l, fam_q, (r.xfull.at[l], r.dq_all[l]))
        pair_q = hand_over(l, fam_q)
        r.mem_v[l] = dot_tn(r.mem_rows[l], r.dv[...])
        arrive(solve_step)
        key_grad = plus(r.dk_direct[...] + r.x4_src[l, t].astype(F32), r.x4_dst.at[l], T - 1)
        r.mem_k[l] = dot_tn(r.mem_rows[l], key_grad.astype(BF16))
        rows = pl.ds(pl.multiple_of(s * z.cut, 8), z.cut)
        mem_copies = [pair_send(r.mem_k.at[l, rows], r.pair_k), pair_send(r.mem_v.at[l, rows], r.pair_v)]

        @pl.when(c != l)
        def _():
            for copy in mem_copies:
                copy.start()

        sent.extend((copy, c != l) for copy in mem_copies)
        mem_key = owe_owner(l, mem_copies)
        add_pair(l, fam_q, pair_q)
        spread(l, fam_q, False)
        if l == 0:
            pass_on(l, fam_c)
            pass_on(l, fam_qk)
            pass_on(l, fam_vo)
            pass_on(l, fam_q)
        arrive(rows_step)
        return mem_key, small_key

    forward(0)
    row_step = forward(1)
    for l in range(LAYERS):
        r.small[l] = jnp.zeros((16, D), F32)
    mem_key1, small_key1 = backward(1)
    mem_key0, small_key0 = backward(0)

    r.input_grad[0] = r.final[...]
    l = c

    arrive(mem_key1)
    arrive(mem_key0)
    rows = pl.ds(pl.multiple_of(s * z.cut, 8), z.cut)
    r.mkey_grads[0, 1] = r.mem_k[l, rows, :] + r.pair_k[...]
    r.mvalue_grads[0] = r.mem_v[l, rows, :] + r.pair_v[...]

    def far_sum(far):
        arrive((id(far), 1))
        arrive((id(far), 0))
        return sum(far[i, : z.cut, :].astype(F32) for i in range(S))

    r.proj_grads[0] = far_sum(r.far_p)
    r.fc_grads[0] = far_sum(r.far_c)
    both = far_sum(r.far_qk)
    r.attn_grads[0, 0] = both[:, : z.heads_w]
    r.attn_grads[0, 1] = both[:, z.heads_w :]
    both = far_sum(r.far_vo)
    r.attn_grads[0, 2] = both[:, : z.heads_w]
    r.out_grads[0] = both[:, z.heads_w :].T
    r.mkey_grads[0, 0] = far_sum(r.far_q)
    arrive(small_key1)
    arrive(small_key0)
    total = r.sum_small[...]
    for i in range(1, S):
        total = total + r.seg_small[i].astype(F32)
    r.gain_grads[0] = total[0:2]
    r.shift_grads[0] = total[2:4]
    r.obias_grads[0] = total[4:6]
    r.fcb_grads[...] = total[8:9, : z.units]
    r.abias_grads[0] = total[9:11, : z.heads_w]

    assert not owed and not relays
    for copy, when in sent:
        if when is copy:
            copy()
        elif when is None:
            copy.wait_send()
        else:
            pl.when(when)(copy.wait_send)


def hand_out(*refs):
    count = len(refs) // 2
    for source, target in zip(refs[:count], refs[count:]):
        target[...] = source[...]


def item_ids(lengths):
    item_ends = jnp.cumsum(lengths, axis=-1)
    item_begins = item_ends - lengths
    places = jnp.arange(lengths.shape[-1], dtype=jnp.int32)
    matches = (item_begins[:, :, None] == places[None, None, :]) & (lengths[:, :, None] > 0)
    return jnp.cumsum(jnp.sum(matches.astype(jnp.int32), axis=1), axis=-1)


def reach_mask(lengths):
    ids = item_ids(lengths)
    places = jnp.arange(lengths.shape[-1])
    earlier = places[:, None] > places[None, :]
    same = (ids[:, :, None] == ids[:, None, :]) & earlier[None]
    return jnp.repeat(jnp.repeat(same.astype(F32), MEM, axis=1), MEM, axis=2)


def gather_rows(values, axis):
    return lax.all_gather(values, axis, axis=0, tiled=True)


def scatter_rows(values, axis):
    peers = lax.axis_size(axis)
    pieces = values.astype(BF16).reshape(peers, values.shape[0] // peers, values.shape[1])
    got = lax.all_to_all(pieces, axis, 0, 0, tiled=True)
    return jnp.sum(got.astype(F32), axis=0)


def scatter_columns(values, axis):
    peers = lax.axis_size(axis)
    rows = values.shape[0]
    pieces = values.reshape(rows, peers, -1).transpose(1, 0, 2)
    got = lax.all_to_all(pieces.astype(BF16), axis, 0, 0, tiled=True)
    return jnp.sum(got.astype(F32), axis=0)


def solve_forward(key_dots, key_den, value_mem):
    segments = key_dots.shape[0] // MEM
    solved = value_mem
    for s in range(1, segments):
        rows = slice(s * MEM, (s + 1) * MEM)
        read = dot_nn(key_dots[rows].astype(BF16), solved.astype(BF16)) / key_den[rows]
        solved = solved.at[rows].add(-read)
    return solved


def solve_backward(key_dots, key_den, direct):
    segments = key_dots.shape[0] // MEM
    total = direct
    for s in range(segments - 1, 0, -1):
        rows = slice(s * MEM, (s + 1) * MEM)
        back = -total[rows] / key_den[rows]
        total = total + dot_tn(key_dots[rows].astype(BF16), back.astype(BF16))
    return total


def layer_forward(own_rows, mem_rows, mask, place, params):
    gains, shifts, w_attn, attn_bias, w_out, out_biases, w_fc, fc_bias, w_proj, w_q, w_k, w_v = params
    seg, _ = place
    own_mask = lax.dynamic_slice_in_dim(mask, seg * MEM, 1, 0)
    key_mem = dot_nn(mem_rows, w_k).astype(BF16)
    phi_key = feature_map(key_mem.astype(F32), jnp.roll).astype(BF16)
    key_dots = dot_nt(phi_key, phi_key) * mask
    key_den = 1.0 + jnp.sum(key_dots, axis=1, keepdims=True)
    value_part = dot_nn(mem_rows, w_v)
    solved_part = solve_forward(key_dots, key_den, value_part)
    solved = lax.all_gather(solved_part.astype(BF16), "tensor", axis=1, tiled=True)
    query_mem = dot_nn(own_rows, w_q).astype(BF16)
    phi_query = feature_map(query_mem.astype(F32), jnp.roll).astype(BF16)
    query_dots = dot_nt(phi_query, phi_key) * own_mask
    query_den = 1.0 + jnp.sum(query_dots, axis=1, keepdims=True)
    recall = dot_nn(query_dots.astype(BF16), solved) / query_den
    hidden = own_rows.astype(F32) + recall.astype(BF16).astype(F32)
    unit, _ = norm_rows(hidden)
    normed = gather_rows((unit * gains[0] + shifts[0]).astype(BF16), "tensor")
    queries = (dot_nn(normed, w_attn[0]) + attn_bias[0]).astype(BF16)
    key_heads = dot_nn(normed, w_attn[1]).astype(BF16)
    values = (dot_nn(normed, w_attn[2]) + attn_bias[1]).astype(BF16)
    rows = normed.shape[0]
    causal = jnp.arange(rows)[:, None] >= jnp.arange(rows)[None, :]
    probs, mixed = [], []
    for h in range(queries.shape[1] // HEAD_DIM):
        cols = slice(h * HEAD_DIM, (h + 1) * HEAD_DIM)
        scores = dot_nt(queries[:, cols], key_heads[:, cols]) * HEAD_DIM ** (-0.5)
        scores = jnp.where(causal, scores, -jnp.inf)
        heights = jnp.exp(scores - jnp.max(scores, axis=1, keepdims=True))
        probs.append(heights / jnp.sum(heights, axis=1, keepdims=True))
        mixed.append(dot_nn(probs[-1].astype(BF16), values[:, cols]).astype(BF16))
    mixed = jnp.concatenate(mixed, axis=1)
    after = hidden + scatter_rows(dot_nn(mixed, w_out), "tensor") + out_biases[0]
    unit, _ = norm_rows(after)
    normed_mlp = gather_rows((unit * gains[1] + shifts[1]).astype(BF16), "tensor")
    pre = dot_nn(normed_mlp, w_fc) + fc_bias
    activation, slope = gelu_and_slope(pre)
    activation = activation.astype(BF16)
    output = after + scatter_rows(dot_nn(activation, w_proj), "tensor") + out_biases[1]
    kept = (
        own_rows, mem_rows, key_mem, phi_key, key_dots, key_den, value_part, solved_part, solved, query_mem,
        phi_query, query_dots, query_den, recall, hidden, normed, queries, key_heads, values, probs, mixed,
        after, normed_mlp, slope, activation,
    )
    return output, kept


def layer_backward(own_grad, kept, mask, place, params):
    gains, shifts, w_attn, attn_bias, w_out, out_biases, w_fc, fc_bias, w_proj, w_q, w_k, w_v = params
    (
        own_rows, mem_rows, key_mem, phi_key, key_dots, key_den, value_part, solved_part, solved, query_mem,
        phi_query, query_dots, query_den, recall, hidden, normed, queries, key_heads, values, probs, mixed,
        after, normed_mlp, slope, activation,
    ) = kept
    seg, part = place
    own_mask = lax.dynamic_slice_in_dim(mask, seg * MEM, 1, 0)
    grad_low = gather_rows(own_grad.astype(BF16), "tensor")
    pre_grad = (slope * dot_nt(grad_low, w_proj)).astype(BF16)
    proj_grad = dot_tn(activation, grad_low)
    fc_bias_grad = jnp.sum(pre_grad.astype(F32), axis=0)
    fc_grad = dot_tn(normed_mlp, pre_grad)
    after_part, gain_mlp, shift_mlp = norm_back(
        after, gains[1:2], scatter_rows(dot_nt(pre_grad, w_fc), "tensor")
    )
    after_grad = own_grad + after_part
    after_low = gather_rows(after_grad.astype(BF16), "tensor")
    out_grad = dot_tn(mixed, after_low)
    mixed_grad = dot_nt(after_low, w_out).astype(BF16)
    q_grads, k_grads, v_grads = [], [], []
    for h in range(queries.shape[1] // HEAD_DIM):
        cols = slice(h * HEAD_DIM, (h + 1) * HEAD_DIM)
        probs_grad = dot_nt(mixed_grad[:, cols], values[:, cols])
        delta = jnp.sum(probs_grad * probs[h], axis=1, keepdims=True)
        score_grad = (probs[h] * (probs_grad - delta)).astype(BF16)
        q_grads.append((dot_nn(score_grad, key_heads[:, cols]) * HEAD_DIM ** (-0.5)).astype(BF16))
        k_grads.append((dot_tn(score_grad, queries[:, cols]) * HEAD_DIM ** (-0.5)).astype(BF16))
        v_grads.append(dot_tn(probs[h].astype(BF16), mixed_grad[:, cols]).astype(BF16))
    three = [jnp.concatenate(g, axis=1) for g in (q_grads, k_grads, v_grads)]
    attn_bias_grad = jnp.stack([jnp.sum(three[i].astype(F32), axis=0) for i in (0, 2)])
    attn_grad = jnp.stack([dot_tn(normed, g) for g in three])
    normed_part = sum(dot_nt(g, w_attn[i]) for i, g in enumerate(three))
    hidden_part, gain_attn, shift_attn = norm_back(
        hidden, gains[0:1], scatter_rows(normed_part, "tensor")
    )
    hidden_grad = after_grad + hidden_part
    num_grad = (hidden_grad / query_den).astype(BF16)
    den_grad = -jnp.sum(hidden_grad * recall, axis=1, keepdims=True) / query_den
    dots_grad = ((dot_nt(num_grad, solved) + den_grad) * own_mask).astype(BF16)
    query_grad = feature_map_back(query_mem.astype(F32), dot_nn(dots_grad, phi_key), jnp.roll).astype(BF16)
    solved_direct = dot_tn(query_dots.astype(BF16), num_grad)
    key_direct = feature_map_back(key_mem.astype(F32), dot_tn(dots_grad, phi_query), jnp.roll)
    solved_direct = scatter_columns(solved_direct, "tensor")
    solved_direct = jnp.sum(lax.all_gather(solved_direct.astype(BF16), "seg").astype(F32), axis=0)
    value_grad = solve_backward(key_dots, key_den, solved_direct)
    read = value_part - solved_part
    key_den_grad = jnp.sum(value_grad * read, axis=1, keepdims=True) / key_den
    back = (-value_grad / key_den).astype(BF16)
    key_dots_grad = (dot_nt(back, solved_part.astype(BF16)) + key_den_grad) * mask
    both = (key_dots_grad + key_dots_grad.T).astype(BF16)
    key_solve = feature_map_back(key_mem.astype(F32), dot_nn(both, phi_key), jnp.roll)
    mine = (jnp.arange(key_solve.shape[0]) // MEM == seg)[:, None]
    key_direct = key_direct + jnp.where(mine, key_solve, 0.0)
    key_direct = scatter_columns(key_direct, "tensor")
    key_grad = jnp.sum(lax.all_gather(key_direct.astype(BF16), "seg").astype(F32), axis=0).astype(BF16)
    value_low = value_grad.astype(BF16)
    mem_width = mem_rows.shape[1] // lax.axis_size("seg")
    mem_cols = lax.dynamic_slice_in_dim(mem_rows, seg * mem_width, mem_width, 1)
    mem_key_grad = dot_tn(mem_cols, key_grad)
    mem_value_grad = dot_tn(mem_cols, value_low)
    return (
        hidden_grad, query_grad, key_grad, value_low,
        (gain_attn, gain_mlp, shift_attn, shift_mlp, jnp.sum(after_grad, axis=0, keepdims=True), jnp.sum(own_grad, axis=0, keepdims=True)),
        (attn_grad, attn_bias_grad, out_grad, fc_grad, fc_bias_grad, proj_grad, mem_key_grad, mem_value_grad),
    )


def general_device(
    inputs, out_grad, item_lengths, norm_gains, norm_biases, w_attn, attn_bias, w_out, out_biases, w_fc, fc_bias,
    w_proj, w_mem_keys, w_mem_value,
):
    section, seg, part = (lax.axis_index(name) for name in ("section", "seg", "tensor"))
    segments, parts = lax.axis_size("seg"), lax.axis_size("tensor")
    layers = lax.axis_size("section")
    mask = reach_mask(item_lengths)[section]
    weights = (norm_gains, norm_biases, w_attn, attn_bias, w_out, out_biases, w_fc, fc_bias, w_proj, w_mem_keys, w_mem_value)
    weights = [lax.all_gather(w, "section", axis=0, tiled=True) for w in weights]
    full_keys = lax.all_gather(weights[9], "tensor", axis=3, tiled=True)
    rows_all, grad_all = inputs[section], out_grad[section]
    chunk = rows_all.shape[0] // parts
    own_rows = lax.dynamic_slice_in_dim(rows_all, part * chunk, chunk, 0)
    place = (seg, part)
    saved, layer_params = [], []
    for layer in range(layers):
        mems = lax.all_gather(own_rows[-MEM:], ("seg", "tensor"), axis=0)
        mem_rows = mems[parts - 1 :: parts].reshape(segments * MEM, -1)
        params = tuple(w[layer] for w in weights[:9]) + (full_keys[layer, 0], full_keys[layer, 1], weights[10][layer])
        output, kept = layer_forward(own_rows, mem_rows, mask, place, params)
        saved.append(kept)
        layer_params.append(params)
        own_rows = output.astype(BF16)
    own_grad = lax.dynamic_slice_in_dim(grad_all, part * chunk, chunk, 0).astype(F32)
    rows_grads, matrix_grads = [None] * layers, [None] * layers
    for layer in reversed(range(layers)):
        params, kept = layer_params[layer], saved[layer]
        hidden_grad, query_grad, key_grad, value_low, rows_grads[layer], grads = layer_backward(own_grad, kept, mask, place, params)
        w_q = params[9]
        keys_here = lax.dynamic_slice_in_dim(key_grad, seg * MEM, MEM, 0)
        values_here = lax.dynamic_slice_in_dim(value_low, seg * MEM, MEM, 0)
        tail = dot_nt(keys_here, weights[9][layer, 1]) + dot_nt(values_here, params[11])
        tail = jnp.sum(lax.all_gather(tail.astype(BF16), "tensor").astype(F32), axis=0)
        tail = jnp.concatenate([jnp.zeros((chunk - MEM, tail.shape[1]), F32), tail], axis=0)
        rows_grad = hidden_grad + dot_nt(query_grad, w_q) + jnp.where(part == parts - 1, tail, 0.0)
        own_grad = rows_grad.astype(BF16).astype(F32)
        rows_full = gather_rows(kept[0], "tensor")
        query_cols = lax.all_to_all(query_grad.reshape(chunk, parts, -1).transpose(1, 0, 2), "tensor", 0, 0, tiled=True)
        query_cols = query_cols.reshape(chunk * parts, -1)
        matrix_grads[layer] = grads + (dot_tn(rows_full, query_cols),)
    input_grad = gather_rows(own_grad.astype(BF16), "tensor")[None]

    def over_layers(values):
        return lax.psum_scatter(jnp.stack(values), "section", scatter_dimension=0, tiled=True)

    rows_sums = lax.psum(over_layers([jnp.concatenate(r, axis=0) for r in rows_grads]), ("seg", "tensor"))

    def spread(index, axis):
        stacked = jnp.stack([g[index] for g in matrix_grads]).astype(BF16)
        pair = lax.all_to_all(stacked, "section", 0, 0, tiled=True)
        both = jnp.sum(pair.astype(F32), axis=0)
        cut = both.astype(BF16).reshape(both.shape[:axis] + (segments, -1) + both.shape[axis + 1 :])
        got = lax.all_to_all(cut, "seg", axis, axis, tiled=True)
        return jnp.sum(got.astype(F32), axis=axis)[None]

    biases = lax.psum(
        (over_layers([g[1] for g in matrix_grads]), over_layers([g[4] for g in matrix_grads])), "seg"
    )
    query_w = spread(8, 0)
    key_w = over_layers([g[6] for g in matrix_grads])
    return (
        input_grad,
        rows_sums[:, 0:2],
        rows_sums[:, 2:4],
        spread(0, 1),
        biases[0],
        spread(2, 1),
        rows_sums[:, 4:6],
        spread(3, 0),
        biases[1],
        spread(5, 1),
        jnp.stack([query_w, key_w], axis=1),
        over_layers([g[7] for g in matrix_grads]),
    )


def solution(mesh):
    def per_device(*args):
        inputs, out_grad, item_lengths = args[:3]
        S, T = mesh.shape["seg"], mesh.shape["tensor"]
        w_attn, w_fc, w_keys = args[5], args[9], args[12]
        z = Sizes(
            mesh,
            (
                (0, inputs.shape[1] * S, inputs.shape[2]), (0, 0, 0, w_attn.shape[3] * T), (0, 0, w_fc.shape[2] * T),
                (0, 0, 0, w_keys.shape[3] * T),
            ),
        )
        scratch = scratch_of(z)
        D = z.width
        outs = dict(
            input_grad=((1, z.rows, D), BF16), gain_grads=((1, 2, D), F32), shift_grads=((1, 2, D), F32),
            attn_grads=((1, 3, z.cut, z.heads_w), F32), abias_grads=((1, 2, z.heads_w), F32),
            out_grads=((1, z.heads_w, z.cut), F32), obias_grads=((1, 2, D), F32), fc_grads=((1, z.cut, z.units), F32),
            fcb_grads=((1, z.units), F32), proj_grads=((1, z.cut, z.units), F32),
            mkey_grads=((1, 2, z.cut, z.keys_w), F32), mvalue_grads=((1, z.cut, z.val_w), F32),
        )
        names = tuple(scratch)
        vmem, anywhere = pl.BlockSpec(memory_space=pltpu.VMEM), pl.BlockSpec(memory_space=pl.ANY)
        shapes = [jax.ShapeDtypeStruct(*shape) for shape in outs.values()]
        flip = lambda w: jnp.swapaxes(w, -1, -2)
        results = pl.pallas_call(
            functools.partial(kernel, z, names),
            out_shape=shapes,
            in_specs=[anywhere, anywhere, pl.BlockSpec(memory_space=pltpu.SMEM)] + [anywhere] * 11,
            out_specs=[vmem] * len(outs),
            scratch_shapes=list(scratch.values()),
            compiler_params=pltpu.CompilerParams(
                collective_id=0, has_side_effects=True, vmem_limit_bytes=63 * 2**20
            ),
            name="two_layers",
        )(*args[:5], flip(w_attn), *args[6:12], flip(w_keys), flip(args[13]))
        results = list(pl.pallas_call(
            hand_out, out_shape=shapes, in_specs=[vmem] * len(outs), out_specs=[vmem] * len(outs), name="hand_out"
        )(*results))
        results[9] = flip(results[9])
        return tuple(results)

    return jax.shard_map(
        per_device if mesh.shape["seg"] * MEM <= 128 else general_device,
        mesh=mesh,
        in_specs=(
            P(None, "seg", None),
            P(None, "seg", None),
            P(),
            P("section", None, None),
            P("section", None, None),
            P("section", None, None, "tensor"),
            P("section", None, "tensor"),
            P("section", "tensor", None),
            P("section", None, None),
            P("section", None, "tensor"),
            P("section", "tensor"),
            P("section", "tensor", None),
            P("section", None, None, "tensor"),
            P("section", None, "tensor"),
        ),
        out_specs=(
            P("section", "seg", None),
            P("section", None, None),
            P("section", None, None),
            P("section", None, "seg", "tensor"),
            P("section", None, "tensor"),
            P("section", "tensor", "seg"),
            P("section", None, None),
            P("section", "seg", "tensor"),
            P("section", "tensor"),
            P("section", "tensor", "seg"),
            P("section", None, "seg", "tensor"),
            P("section", "seg", "tensor"),
        ),
        check_vma=False,
    )
```

```python
import functools
from types import SimpleNamespace
from typing import Any, NamedTuple

import jax
import jax.numpy as jnp
from jax import lax
from jax.experimental import pallas as pl
from jax.experimental.pallas import tpu as pltpu
from jax.sharding import PartitionSpec as P

HEAD_DIM = 64
NU = 3
MEM = 16
EPSILON = 1e-05
F32 = jnp.float32
BF16 = jnp.bfloat16
GELU_A = 0.7978845608028654
GELU_B = 0.044715
LAYERS = 2
MESH = pl.DeviceIdType.MESH


def dot_nn(left, right):
    return lax.dot_general(left, right, (((1,), (0,)), ((), ())), preferred_element_type=F32)


def dot_nt(left, right):
    return lax.dot_general(left, right, (((1,), (1,)), ((), ())), preferred_element_type=F32)


def dot_tn(left, right):
    return lax.dot_general(left, right, (((0,), (0,)), ((), ())), preferred_element_type=F32)


def doubled_softplus(projected):
    small = jnp.exp(-jnp.abs(projected))
    tail = jnp.where(small < 1e-3, small - 0.5 * small * small, jnp.log1p(small))
    return jnp.concatenate(
        [jnp.maximum(projected, 0.0) + tail, jnp.maximum(-projected, 0.0) + tail], axis=1
    )


def feature_map(projected, roll=pltpu.roll):
    doubled = doubled_softplus(projected)
    return jnp.concatenate([doubled * roll(doubled, j, 1) for j in range(1, NU + 1)], axis=1)


def feature_map_back(projected, phi_grad, roll=pltpu.roll):
    doubled = doubled_softplus(projected)
    width = doubled.shape[1]
    total = jnp.zeros_like(doubled)
    for j in range(1, NU + 1):
        part = phi_grad[:, (j - 1) * width : j * width]
        total = total + part * roll(doubled, j, 1) + roll(part * doubled, width - j, 1)
    half = width // 2
    gate = 1.0 / (1.0 + jnp.exp(-projected))
    return total[:, :half] * gate - total[:, half:] * (1.0 - gate)


def norm_rows(hidden):
    centered = hidden - jnp.mean(hidden, axis=1, keepdims=True)
    scale = lax.rsqrt(jnp.mean(centered * centered, axis=1, keepdims=True) + EPSILON)
    return centered * scale, scale


def norm_back(hidden, gain_row, grad):
    unit, scale = norm_rows(hidden)
    unit_grad = grad * gain_row
    mean_grad = jnp.mean(unit_grad, axis=1, keepdims=True)
    mean_both = jnp.mean(unit_grad * unit, axis=1, keepdims=True)
    return (
        scale * (unit_grad - mean_grad - unit * mean_both),
        jnp.sum(grad * unit, axis=0, keepdims=True),
        jnp.sum(grad, axis=0, keepdims=True),
    )


def gelu_and_slope(pre):
    square = pre * pre
    bent = jnp.tanh(GELU_A * (pre + GELU_B * square * pre))
    value = 0.5 * pre * (1.0 + bent)
    slope = 0.5 * (1.0 + bent) + 0.5 * pre * (1.0 - bent * bent) * (
        GELU_A * (1.0 + 3.0 * GELU_B * square)
    )
    return value, slope


def xor_peer(place, other, count):
    total, bit = 0, 1
    while bit < count:
        mine = lax.rem(lax.div(place, bit), 2)
        total = total + bit * (1 - mine if other & bit else mine)
        bit *= 2
    return total


def split(values):
    high = values.astype(BF16)
    return high, (values - high.astype(F32)).astype(BF16)


def plus(first, others, count):
    total = first.astype(F32)
    for i in range(count):
        total = total + others[i].astype(F32)
    return total


class Sizes:
    def __init__(self, mesh, shapes):
        self.segs, self.parts = mesh.shape["seg"], mesh.shape["tensor"]
        inputs, w_attn, w_fc, w_keys = shapes
        self.rows, self.width = inputs[1] // self.segs, inputs[2]
        self.chunk = self.rows // self.parts
        self.mems = self.segs * MEM
        self.heads_w = w_attn[3] // self.parts
        self.heads = self.heads_w // HEAD_DIM
        self.units = w_fc[2] // self.parts
        self.keys = w_keys[3]
        self.keys_w = self.keys // self.parts
        self.phi = 2 * self.keys * NU
        self.val_w = self.width // self.parts
        self.cut = self.width // self.segs
        self.cut_pad = -(-self.cut // 16) * 16
        self.sems = 120 + 48 * self.parts + 2 * self.segs * (self.parts + 16)


def scratch_of(z):
    S, T, R, D, C, M = z.segs, z.parts, z.rows, z.width, z.chunk, z.mems
    bf = lambda *d: pltpu.VMEM(d, BF16)
    fl = lambda *d: pltpu.VMEM(d, F32)
    return dict(
        gains=fl(2, 2, D), shifts=fl(2, 2, D), w_attn=bf(2, 3, z.heads_w, D), attn_bias=fl(2, 2, z.heads_w),
        w_out=bf(2, z.heads_w, D), out_biases=fl(2, 2, D), w_fc=bf(2, D, z.units), fc_bias=fl(2, 1, z.units),
        w_proj=bf(2, z.units, D), w_keys=bf(2, 2, z.keys, D), w_value=bf(2, z.val_w, D),
        xfull=bf(2, R, D), gfull=bf(2, R, D), mem_rows=bf(2, M, D),
        keyb=bf(2, M, z.keys), phik=bf(2, M, z.phi), kdots=fl(2, M, M), vpart=fl(2, M, z.val_w),
        upart=fl(2, M, z.val_w), uall=bf(2, T, M, z.val_w), qmem=bf(2, C, z.keys), phiq=bf(2, C, z.phi),
        qdots=fl(2, C, M), recall=fl(2, C, D), hidden=fl(2, C, D), normed=bf(2, R, D), qkv=bf(2, 3, R, z.heads_w),
        probs=fl(2, z.heads, R, R), mixed=bf(2, R, z.heads_w), after=fl(2, C, D), normed_mlp=bf(2, R, D),
        slope=fl(2, R, z.units), act=bf(2, R, z.units), rs_src=bf(7, R, D), rs_own=fl(R, D), q_src=bf(R, z.keys_w), q_parts=bf(T, C, z.keys_w), k_parts=bf(T, M, z.keys_w), rs_dst=bf(7, T - 1, C, D),
        low2=bf(2, R, D), dpre=bf(R, z.units), dqkv=bf(3, R, z.heads_w),
        x1_src=bf(2, T, M, z.val_w), x1_dst=bf(2, T - 1, M, z.val_w), x1_mid=bf(2, M, z.val_w), x1_far=bf(2, max(S - 1, 1), M, z.val_w),
        x2_src=bf(2, T, M, z.keys_w), x2_dst=bf(2, T - 1, M, z.keys_w), x2_mid=bf(2, M, z.keys_w), x2_far=bf(2, max(S - 1, 1), M, z.keys_w), x4_src=bf(2, T, M, z.keys_w), x4_dst=bf(2, T - 1, M, z.keys_w), ksolve=fl(M, z.keys), dk_direct=fl(M, z.keys_w),
        dq_src=bf(2, T, C, z.keys_w), dq_all=bf(2, R, z.keys_w), dv=bf(M, z.val_w), vgrad=fl(M, z.val_w),
        x3_src=bf(2, MEM, D), x3_dst=bf(2, T - 1, MEM, D), final=bf(R, D), tmp=fl(C, D),
        grad_p=bf(2, S, z.cut_pad, z.units), grad_c=bf(2, S, z.cut_pad, z.units), grad_qk=bf(2, S, z.cut_pad, 2 * z.heads_w),
        grad_vo=bf(2, S, z.cut_pad, 2 * z.heads_w), grad_q=bf(2, S, z.cut_pad, z.keys_w),
        pair_f=bf(2, S, z.cut_pad, z.units), pair_a=bf(2, S, z.cut_pad, 2 * z.heads_w), pair_q=bf(2, S, z.cut_pad, z.keys_w), relay_f=bf(2, 2, z.cut_pad, z.units), relay_a=bf(2, 2, z.cut_pad, 2 * z.heads_w), relay_q=bf(2, 2, z.cut_pad, z.keys_w),
        far_p=bf(S, z.cut_pad, z.units), far_c=bf(S, z.cut_pad, z.units), far_qk=bf(S, z.cut_pad, 2 * z.heads_w),
        far_vo=bf(S, z.cut_pad, 2 * z.heads_w), far_q=bf(S, z.cut_pad, z.keys_w), dqk=bf(R, 2 * z.heads_w),
        mem_k=fl(2, D, z.keys_w), mem_v=fl(2, D, z.val_w), pair_k=fl(z.cut, z.keys_w), pair_v=fl(z.cut, z.val_w),
        small=fl(2, 16, D), pair_small=fl(16, D), part_small=fl(T, 8, D), sum_small=fl(16, D), seg_small=bf(S, 16, D),
        send=pltpu.SemaphoreType.DMA((z.sems,)), recv=pltpu.SemaphoreType.DMA((z.sems,)), load=pltpu.SemaphoreType.DMA((14, 2)),
        shard=pltpu.SemaphoreType.DMA((2, 2, T)),
    )


class Outer(NamedTuple):
    inputs: Any
    out_grad: Any
    item_lengths: Any
    norm_gains: Any
    norm_biases: Any
    w_attn_in: Any
    attn_bias_in: Any
    w_out_in: Any
    out_biases_in: Any
    w_fc_in: Any
    fc_bias_in: Any
    w_proj_in: Any
    w_keys_in: Any
    w_value_in: Any
    input_grad: Any
    gain_grads: Any
    shift_grads: Any
    attn_grads: Any
    abias_grads: Any
    out_grads: Any
    obias_grads: Any
    fc_grads: Any
    fcb_grads: Any
    proj_grads: Any
    mkey_grads: Any
    mvalue_grads: Any


def kernel(z, held_names, *refs):
    outer = len(Outer._fields)
    r = SimpleNamespace(**Outer(*refs[:outer])._asdict(), **dict(zip(held_names, refs[outer:])))
    S, T, R, D, C, M = z.segs, z.parts, z.rows, z.width, z.chunk, z.mems
    c, s, t = (lax.axis_index(a) for a in ("section", "seg", "tensor"))
    other = 1 - c
    tpeers = [xor_peer(t, i, T) for i in range(T)]
    to_seg = [lax.rem(s + i, S) for i in range(S)]
    own = pl.ds(pl.multiple_of(t * C, C), C)
    seg_rows = pl.ds(pl.multiple_of(s * MEM, MEM), MEM)
    used = [0]
    sent = []
    owed = {}

    def alloc(count):
        used[0] += count
        assert used[0] <= z.sems
        return used[0] - count

    def owe(copies):
        def wait():
            for copy in copies:
                copy.wait_recv()

        owed[id(copies)] = wait
        return id(copies)

    def wait_bytes(ref, semaphore):
        pltpu.make_async_copy(ref, ref, semaphore).wait()

    def remote(src, dst, index, device, recv=None):
        copy = pltpu.make_async_remote_copy(
            src_ref=src, dst_ref=dst, send_sem=r.send.at[index],
            recv_sem=r.recv.at[index] if recv is None else recv, device_id=device, device_id_type=MESH,
        )
        return copy

    def to_parts(src_of, dst):
        base = alloc(T - 1)
        copies = []
        for i in range(T - 1, 0, -1):
            copy = remote(src_of(tpeers[i]), dst(i), base + i - 1, (c, s, tpeers[i]))
            copy.start()
            copies.append(copy)
        sent.extend((copy, None) for copy in copies)
        return owe(copies)

    def to_segs(src_of, dst):
        base = alloc(S - 1)
        copies = [
            remote(src_of(to_seg[i]), dst(i), base + i - 1, (c, to_seg[i], t)) for i in range(1, S)
        ]
        for copy in copies:
            copy.start()
        sent.extend((copy, None) for copy in copies)
        return owe(copies)

    def arrive(key):
        owed.pop(key)()

    def wait_load(ref, layer):
        arrive((id(ref), layer))

    barrier = pltpu.get_barrier_semaphore()
    greeted = [(other, to_seg[i], t) for i in range(S)] + [(c, to_seg[i], tpeers[j]) for i in range(S) for j in range(T) if i or j]
    for device in greeted:
        pl.semaphore_signal(barrier, inc=1, device_id=device, device_id_type=MESH)

    loads = [
        (r.w_value, r.w_value_in.at[0]), (r.gains, r.norm_gains.at[0]), (r.shifts, r.norm_biases.at[0]),
        (r.attn_bias, r.attn_bias_in.at[0]), (r.out_biases, r.out_biases_in.at[0]), (r.w_attn, r.w_attn_in.at[0]), (r.w_out, r.w_out_in.at[0]), (r.w_fc, r.w_fc_in.at[0]),
        (r.w_proj, r.w_proj_in.at[0]), (r.fc_bias, r.fc_bias_in),
    ]
    input_copy = pltpu.make_async_copy(r.inputs.at[c], r.xfull.at[0], r.load.at[10, 0])
    input_copy.start()
    owed[0] = input_copy.wait
    def shard_rows(part):
        return pl.ds(pl.multiple_of(part * z.keys_w, 16), z.keys_w)

    for which in (0, 1):
        pltpu.make_async_copy(
            r.w_keys_in.at[0, which], r.w_keys.at[c, which, shard_rows(t)], r.shard.at[c, which, 0]
        ).start()
    def load_own(kinds):
        for kind in kinds:
            held, source = loads[kind]
            pltpu.make_async_copy(source, held.at[c], r.load.at[kind, c]).start()

    def load_other(kinds):
        for kind in kinds:
            held, source = loads[kind]
            copy = remote(source, held.at[c], pair_base + kind, (other, s, t), r.load.at[kind, c])
            copy.start()
            sent.append((copy, None))
            for layer in range(LAYERS):
                owed[id(held), layer] = functools.partial(wait_bytes, held.at[layer], r.load.at[kind, layer])

    early, middle = range(0, 5), range(5, 7)
    load_own(range(len(loads)))
    grad_copy = pltpu.make_async_copy(r.out_grad.at[c], r.gfull.at[1], r.load.at[11, 0])
    grad_copy.start()
    owed[1] = grad_copy.wait

    pl.semaphore_wait(barrier, len(greeted))

    first_rows = to_segs(
        lambda _: r.inputs.at[c, pl.ds(R - MEM, MEM)], lambda i: r.mem_rows.at[0, seg_rows]
    )

    def shard_wait(layer, which, i):
        wait_bytes(r.w_keys.at[layer, which, pl.ds(0, z.keys_w)], r.shard.at[layer, which, i])

    def peer_shards(core, layer, which):
        @pl.when(c == core)
        def _():
            for i in range(1, T):
                shard_wait(layer, which, i)

    def spread_shard(layer, which):
        base = alloc(T - 1)
        place = r.w_keys.at[layer, which, shard_rows(t)]
        copies = [
            remote(r.w_keys_in.at[0, which], place, base + i - 1, (c, s, tpeers[i]), r.shard.at[layer, which, i])
            for i in range(T - 1, 0, -1)
        ]

        @pl.when(c == layer)
        def _():
            for copy in copies:
                copy.start()

        sent.extend((copy, c == layer) for copy in copies)
        owed[11, layer, which] = functools.partial(peer_shards, layer, layer, which)

    def forward_shard(layer, which):
        arrive((11, layer, which))
        base = alloc(T - 1)
        copies = []
        for i in range(1, T):
            place = r.w_keys.at[layer, which, shard_rows(tpeers[i])]
            copies.append(remote(place, place, base + i - 1, (other, s, t), r.shard.at[layer, which, i]))

        @pl.when(c == layer)
        def _():
            for copy in copies:
                copy.start()

        sent.extend((copy, c == layer) for copy in copies)
        owed[12, layer, which] = functools.partial(peer_shards, 1 - layer, layer, which)

    base = alloc(2)
    for which in (0, 1):
        copy = remote(
            r.w_keys_in.at[0, which], r.w_keys.at[c, which, shard_rows(t)], base + which, (other, s, t), r.shard.at[c, which, 0]
        )
        copy.start()
        sent.append((copy, None))
        for layer in range(LAYERS):
            owed[10, layer, which] = functools.partial(shard_wait, layer, which, 0)
    pair_base = alloc(len(loads))
    load_other(early)

    spread_shard(1, 1)
    row_seg = lax.broadcasted_iota(jnp.int32, (M, 1), 0) // MEM
    col_seg = lax.broadcasted_iota(jnp.int32, (1, M), 1) // MEM
    row_item, col_item, own_item = jnp.zeros((M, 1), jnp.int32), jnp.zeros((1, M), jnp.int32), 0
    begin = 0
    for i in range(r.item_lengths.shape[1]):
        length = r.item_lengths[c, i]
        there = jnp.where(length > 0, begin, S)
        row_item = row_item + (row_seg >= there).astype(jnp.int32)
        col_item = col_item + (col_seg >= there).astype(jnp.int32)
        own_item = own_item + jnp.where(s >= there, 1, 0)
        begin = begin + length
    key_mask = jnp.where((row_item == col_item) & (row_seg > col_seg), 1.0, 0.0)
    row_mask = jnp.where((col_item == own_item) & (col_seg < s), 1.0, 0.0)
    lane_head = lax.broadcasted_iota(jnp.int32, (1, z.heads_w), 1) // HEAD_DIM
    head_rows = [(lane_head == h).astype(F32).astype(BF16) for h in range(z.heads)]
    rs_count = [0]

    def reduce_rows(partial):
        k = rs_count[0]
        rs_count[0] += 1
        r.rs_own[...] = partial
        r.rs_src[k] = partial.astype(BF16)
        copies = to_parts(
            lambda peer: r.rs_src.at[k, pl.ds(pl.multiple_of(peer * C, C), C)], lambda i: r.rs_dst.at[k, i - 1]
        )

        def finish():
            arrive(copies)
            total = r.rs_own[own, :]
            for i in range(T - 1):
                total = total + r.rs_dst[k, i].astype(F32)
            return total

        return finish

    def share_rows(ref, layer):
        return to_parts(lambda _: ref.at[layer, own], lambda i: ref.at[layer, own])

    def forward(l):
        own_shard = shard_rows(t)
        if l == 0:
            arrive(0)
            arrive((10, 0, 0))
            r.q_src[...] = dot_nt(r.xfull[0], r.w_keys[0, 0, own_shard, :]).astype(BF16)
            r.q_parts[t] = r.q_src[own, :]
            query_step = to_parts(
                lambda peer: r.q_src.at[pl.ds(pl.multiple_of(peer * C, C), C)], lambda i: r.q_parts.at[t]
            )
            r.mem_rows[0, seg_rows, :] = r.xfull[0, R - MEM :, :]
            arrive((10, 0, 1))
            arrive(first_rows)
            mems = r.mem_rows[0]
            r.k_parts[t] = dot_nt(mems, r.w_keys[0, 1, own_shard, :]).astype(BF16)
            key_step = to_parts(lambda _: r.k_parts.at[t], lambda i: r.k_parts.at[t])
            load_other(middle)
            arrive(query_step)
            queries_mem = jnp.concatenate([r.q_parts[u] for u in range(T)], axis=1)
        else:
            for which in (0, 1):
                arrive((10, 1, which))
                arrive((12, 1, which))
            queries_mem = dot_nt(r.xfull[1, own, :], r.w_keys[1, 0]).astype(BF16)
        x = r.xfull[l, own, :]
        r.qmem[l] = queries_mem
        phi_query = feature_map(queries_mem.astype(F32)).astype(BF16)
        r.phiq[l] = phi_query
        wait_load(r.w_value, l)
        if l == 1:
            arrive(4)
            mems = r.mem_rows[1]
        value_part = dot_nt(mems, r.w_value[l])
        r.vpart[l] = value_part
        r.upart[l] = value_part
        if l == 0:
            arrive(key_step)
            keys = jnp.concatenate([r.k_parts[u] for u in range(T)], axis=1)
        else:
            keys = dot_nt(mems, r.w_keys[1, 1]).astype(BF16)
        r.keyb[l] = keys
        phi_key = feature_map(keys.astype(F32)).astype(BF16)
        r.phik[l] = phi_key
        key_dots = dot_nt(phi_key, phi_key) * key_mask
        r.kdots[l] = key_dots
        key_den = 1.0 + jnp.sum(key_dots, axis=1, keepdims=True)
        for k in range(1, S):
            rows = slice(k * MEM, (k + 1) * MEM)
            read = dot_nn(key_dots[rows].astype(BF16), r.upart[l].astype(BF16)) / key_den[rows]
            r.upart[l, rows, :] = value_part[rows] - read
        r.uall[l, t] = r.upart[l].astype(BF16)
        solved = to_parts(lambda _: r.uall.at[l, t], lambda i: r.uall.at[l, t])
        if l == 0:
            spread_shard(1, 0)
        query_dots = dot_nt(phi_query, phi_key) * row_mask
        r.qdots[l] = query_dots
        query_den = 1.0 + jnp.sum(query_dots, axis=1, keepdims=True)
        for ref in (r.gains, r.shifts, r.attn_bias, r.out_biases):
            wait_load(ref, l)
        arrive(solved)
        high, low = split(query_dots)
        recall = [dot_nn(high, r.uall[l, u]) + dot_nn(low, r.uall[l, u]) for u in range(T)]
        recall = jnp.concatenate(recall, axis=1) / query_den
        r.recall[l] = recall
        hidden = x.astype(F32) + recall.astype(BF16).astype(F32)
        r.hidden[l] = hidden
        unit, _ = norm_rows(hidden)
        r.normed[l, own, :] = (unit * r.gains[l, 0:1] + r.shifts[l, 0:1]).astype(BF16)
        shared = share_rows(r.normed, l)
        if l == 0:
            load_other([9, 7])
        wait_load(r.w_attn, l)
        wait_load(r.w_out, l)
        arrive(shared)
        normed = r.normed[l]
        queries = (dot_nt(normed, r.w_attn[l, 0]) + r.attn_bias[l, 0:1]).astype(BF16)
        key_heads = dot_nt(normed, r.w_attn[l, 1]).astype(BF16)
        values = (dot_nt(normed, r.w_attn[l, 2]) + r.attn_bias[l, 1:2]).astype(BF16)
        r.qkv[l, 0] = queries
        r.qkv[l, 1] = key_heads
        r.qkv[l, 2] = values
        causal = lax.broadcasted_iota(jnp.int32, (R, R), 0) >= lax.broadcasted_iota(jnp.int32, (R, R), 1)
        mixed = jnp.zeros((R, z.heads_w), F32)
        for h in range(z.heads):
            scores = dot_nt(queries, key_heads * head_rows[h]) * HEAD_DIM ** (-0.5)
            scores = jnp.where(causal, scores, -jnp.inf)
            heights = jnp.exp(scores - jnp.max(scores, axis=1, keepdims=True))
            probs = heights * (1.0 / jnp.sum(heights, axis=1, keepdims=True))
            r.probs[l, h] = probs
            mixed = mixed + dot_nn(probs.astype(BF16), values * head_rows[h])
        mixed = mixed.astype(BF16)
        r.mixed[l] = mixed
        finish = reduce_rows(dot_nn(mixed, r.w_out[l]))
        if l == 0:
            load_other([8])
        after = r.hidden[l] + finish() + r.out_biases[l, 0:1]
        r.after[l] = after
        unit, _ = norm_rows(after)
        r.normed_mlp[l, own, :] = (unit * r.gains[l, 1:2] + r.shifts[l, 1:2]).astype(BF16)
        shared = share_rows(r.normed_mlp, l)
        wait_load(r.w_fc, l)
        wait_load(r.fc_bias, l)
        wait_load(r.w_proj, l)
        if l == 0:
            forward_shard(1, 1)
            forward_shard(1, 0)
        arrive(shared)
        pre = dot_nn(r.normed_mlp[l], r.w_fc[l]) + r.fc_bias[l]
        activation, slope = gelu_and_slope(pre)
        activation = activation.astype(BF16)
        r.act[l] = activation
        r.slope[l] = slope
        if l == 0:
            finish = reduce_rows(dot_nn(activation, r.w_proj[l]))
            output = r.after[l] + finish() + r.out_biases[l, 1:2]
            r.xfull[1, own, :] = output.astype(BF16)
            base, places = alloc(S), alloc(S * T)
            last = r.xfull.at[1, pl.ds(R - MEM, MEM)]

            @pl.when(t == T - 1)
            def _():
                r.mem_rows[1, seg_rows, :] = r.xfull[1, R - MEM :, :]
                for i in range(S - 1, -1, -1):
                    for j in range(1 if i == 0 else 0, T):
                        copy = pltpu.make_async_remote_copy(
                            src_ref=last, dst_ref=r.mem_rows.at[1, seg_rows], send_sem=r.send.at[places + i * T + j],
                            recv_sem=r.recv.at[base + i], device_id=(c, to_seg[i], tpeers[j]), device_id_type=MESH,
                        )
                        copy.start()

            def wait_rows(i):
                wait_bytes(r.mem_rows.at[1, pl.ds(0, MEM)], r.recv.at[base + i])

            def wait_all():
                pl.when(t != T - 1)(functools.partial(wait_rows, 0))
                for i in range(1, S):
                    wait_rows(i)

            owed[4] = wait_all

            def drain():
                @pl.when(t == T - 1)
                def _():
                    for i in range(S):
                        for j in range(1 if i == 0 else 0, T):
                            wait_bytes(last, r.send.at[places + i * T + j])

            sent.append((drain, drain))

    fam_p, fam_c = (r.grad_p, r.pair_f, r.far_p, 0, r.relay_f), (r.grad_c, r.pair_f, r.far_c, 1, r.relay_f)
    fam_qk, fam_vo = (r.grad_qk, r.pair_a, r.far_qk, 0, r.relay_a), (r.grad_vo, r.pair_a, r.far_vo, 1, r.relay_a)
    fam_q = (r.grad_q, r.pair_q, r.far_q, None, r.relay_q)
    on_line = S == 4
    partner = s + 1 - 2 * lax.rem(s, 2)
    across = 2 - 2 * lax.div(s, 2)
    outer = jnp.logical_or(s == 0, s == 3)
    relays = {}

    def blocks_of(first_row, count):
        row, pieces = first_row, []
        while row < first_row + count:
            block, inside = row // z.cut, row % z.cut
            size = min(z.cut - inside, first_row + count - row)
            pieces.append((block, inside, row - first_row, size))
            row += size
        return pieces

    def weight_grad(l, family, *pairs):
        stripe = min(256, D)
        for k in range(0, D, stripe):
            parts = [dot_tn(left[:, k : k + stripe], right).astype(BF16) for left, right in pairs]
            grad = parts[0] if len(parts) == 1 else jnp.concatenate(parts, axis=1)
            for block, inside, row, size in blocks_of(k, stripe):
                family[0][l, block, inside : inside + size, :] = grad[row : row + size]

    def pair_send(src, dst):
        index = alloc(1)
        return remote(src, dst, index, (other, s, t))

    def adder_of(l, family):
        return l if family[3] is None else family[3]

    def hand_over(l, family):
        grad, pair, _, _, _ = family
        adder = adder_of(l, family)
        copy = pair_send(grad.at[l], pair.at[l])
        pl.when(c != adder)(copy.start)
        sent.append((copy, c != adder))
        return owe_owner(adder, [copy])

    def owe_owner(l, copies):
        def wait():
            @pl.when(c == l)
            def _():
                for copy in copies:
                    copy.wait_recv()

        owed[id(copies)] = wait
        return id(copies)

    def add_pair(l, family, key):
        grad, pair, _, _, _ = family
        arrive(key)

        @pl.when(c == adder_of(l, family))
        def _():
            @pl.loop(0, S)
            def _(j):
                grad[l, j] = (grad[l, j].astype(F32) + pair[l, j].astype(F32)).astype(BF16)

    def spread(l, family, direct):
        grad, _, far, _, relay = family
        adder = adder_of(l, family)
        near = adder == l
        direct = direct or not on_line
        base = alloc(S if direct else 5)
        steps = range(1, S) if direct else (1, 2)

        @pl.when(c == adder)
        def _():
            if direct:
                for i in range(S - 1, 0, -1):
                    remote(grad.at[l, to_seg[i]], far.at[i], base + i, (l, to_seg[i], t)).start()
            else:

                @pl.when(outer)
                def _():
                    for k in range(2):
                        remote(grad.at[l, across + k], relay.at[l, k], base + 3 + k, (c, partner, t)).start()

                remote(grad.at[l, partner], far.at[1], base + 1, (l, partner, t)).start()
            if near:
                far[0] = grad[l, s]
            else:
                remote(grad.at[l, s], far.at[0], base, (other, s, t)).start()

        if not direct:

            @pl.when(c == l)
            def _():
                for i in range(3, S):
                    far[i] = jnp.zeros(far.shape[1:], BF16)

            def pass_on():
                @pl.when(jnp.logical_and(c == adder, jnp.logical_not(outer)))
                def _():
                    for k in range(2):
                        wait_bytes(relay.at[l, k], r.recv.at[base + 3 + k])
                        place = across + k
                        grad[l, place] = (grad[l, place].astype(F32) + relay[l, k].astype(F32)).astype(BF16)
                        remote(grad.at[l, place], far.at[2], base + 3 + k, (l, place, t), r.recv.at[base + 2]).start()

            relays[id(far), l] = pass_on

        def wait():
            @pl.when(c == l)
            def _():
                for i in steps if near else (0, *steps):
                    wait_bytes(far.at[i], r.recv.at[base + i])

        def drain():
            @pl.when(c == adder)
            def _():
                ends = tuple(steps) if direct else (1, 3, 4)
                for i in ends if near else (0, *ends):
                    wait_bytes(far.at[0], r.send.at[base + i])

        owed[id(far), l] = wait
        sent.append((drain, drain))

    def pass_on(l, family):
        if (id(family[2]), l) in relays:
            relays.pop((id(family[2]), l))()

    def owe_small(l):
        copy = pair_send(r.small.at[l], r.pair_small)
        pl.when(c != l)(copy.start)
        sent.append((copy, c != l))
        return owe_owner(l, [copy])

    def owner_copies(l, copies):
        @pl.when(c == l)
        def _():
            for copy in copies:
                copy.start()

        sent.extend((copy, c == l) for copy in copies)
        return owe_owner(l, copies)

    def small_parts(l, key):
        arrive(key)

        @pl.when(c == l)
        def _():
            r.sum_small[...] = r.small[l] + r.pair_small[...]
            r.part_small[0] = r.sum_small[0:8, :]

        base = alloc(T - 1)
        return owner_copies(
            l, [remote(r.part_small.at[0], r.part_small.at[i], base + i - 1, (c, s, tpeers[i])) for i in range(1, T)]
        )

    def small_segs(l, key):
        arrive(key)

        @pl.when(c == l)
        def _():
            total = r.part_small[0]
            for i in range(1, T):
                total = total + r.part_small[i]
            r.sum_small[0:8, :] = total
            r.seg_small[0] = r.sum_small[...].astype(BF16)

        base = alloc(S - 1)
        return owner_copies(
            l, [remote(r.seg_small.at[0], r.seg_small.at[i], base + i - 1, (c, to_seg[i], t)) for i in range(1, S)]
        )

    def backward(l):
        if l == 1:
            arrive(1)
        grad_low = r.gfull[l]
        pre_grad = (r.slope[l] * dot_nt(grad_low, r.w_proj[l])).astype(BF16)
        r.dpre[...] = pre_grad
        finish = reduce_rows(dot_nt(pre_grad, r.w_fc[l]))
        own_grad = r.gfull[l, own, :].astype(F32)

        weight_grad(l, fam_p, (r.gfull.at[l], r.act[l]))
        pair_p = hand_over(l, fam_p)
        weight_grad(l, fam_c, (r.normed_mlp.at[l], r.dpre[...]))
        pair_c = hand_over(l, fam_c)
        r.small[l, 8:9, :] = jnp.sum(r.dpre[...].astype(F32), axis=0, keepdims=True)
        if l == 0:
            pass_on(1, fam_c)
            pass_on(1, fam_qk)
        add_pair(l, fam_p, pair_p)
        spread(l, fam_p, False)
        after_part, gain_mlp, shift_mlp = norm_back(r.after[l], r.gains[l, 1:2], finish())
        after_grad = own_grad + after_part
        r.tmp[...] = after_grad
        r.low2[l, own, :] = after_grad.astype(BF16)
        shared = share_rows(r.low2, l)
        r.small[l, 1:2, :] = gain_mlp
        r.small[l, 3:4, :] = shift_mlp
        r.small[l, 4:5, :] = jnp.sum(after_grad, axis=0, keepdims=True)
        r.small[l, 5:6, :] = jnp.sum(own_grad, axis=0, keepdims=True)
        add_pair(l, fam_c, pair_c)
        if l == 0:
            spread(l, fam_c, False)
            pass_on(1, fam_vo)
            pass_on(1, fam_q)
        arrive(shared)
        if l == 0:
            forward_shard(0, 0)
            forward_shard(0, 1)
        after_low = r.low2[l]
        mixed_grad = dot_nt(after_low, r.w_out[l]).astype(BF16)
        queries, key_heads, values = r.qkv[l, 0], r.qkv[l, 1], r.qkv[l, 2]
        q_grad = k_grad = v_grad = jnp.zeros((R, z.heads_w), F32)
        for h in range(z.heads):
            probs = r.probs[l, h]
            mixed_here = mixed_grad * head_rows[h]
            probs_grad = dot_nt(mixed_here, values)
            delta = jnp.sum(probs_grad * probs, axis=1, keepdims=True)
            score_grad = (probs * (probs_grad - delta)).astype(BF16)
            q_grad = q_grad + dot_nn(score_grad, key_heads * head_rows[h])
            k_grad = k_grad + dot_tn(score_grad, queries * head_rows[h])
            v_grad = v_grad + dot_tn(probs.astype(BF16), mixed_here)
        scale = HEAD_DIM ** (-0.5)
        r.dqkv[0] = (q_grad * scale).astype(BF16)
        r.dqkv[1] = (k_grad * scale).astype(BF16)
        r.dqkv[2] = v_grad.astype(BF16)
        r.dqk[...] = jnp.concatenate([r.dqkv[0], r.dqkv[1]], axis=1)
        finish = reduce_rows(sum(dot_nn(r.dqkv[i], r.w_attn[l, i]) for i in range(3)))

        weight_grad(l, fam_qk, (r.normed.at[l], r.dqk[...]))
        pair_qk = hand_over(l, fam_qk)
        weight_grad(l, fam_vo, (r.normed.at[l], r.dqkv[2]), (r.low2.at[l], r.mixed[l]))
        pair_vo = hand_over(l, fam_vo)
        for row, i in ((9, 0), (10, 2)):
            r.small[l, row : row + 1, : z.heads_w] = jnp.sum(r.dqkv[i].astype(F32), axis=0, keepdims=True)
        hidden_part, gain_attn, shift_attn = norm_back(r.hidden[l], r.gains[l, 0:1], finish())
        hidden_grad = r.tmp[...] + hidden_part
        r.tmp[...] = hidden_grad
        r.small[l, 0:1, :] = gain_attn
        r.small[l, 2:3, :] = shift_attn
        small_key = owe_small(l)
        query_den = 1.0 + jnp.sum(r.qdots[l], axis=1, keepdims=True)
        high, low = split(hidden_grad / query_den)
        den_grad = -jnp.sum((hidden_grad / query_den) * r.recall[l], axis=1, keepdims=True)
        highs = [high[:, u * z.val_w : (u + 1) * z.val_w] for u in range(T)]
        lows = [low[:, u * z.val_w : (u + 1) * z.val_w] for u in range(T)]
        dots_high, dots_low = split(r.qdots[l])
        for u in range(T):
            grad = dot_tn(dots_high, highs[u]) + dot_tn(dots_high, lows[u]) + dot_tn(dots_low, highs[u])
            r.x1_src[l, u] = grad.astype(BF16)
        value_step = to_parts(lambda peer: r.x1_src.at[l, peer], lambda i: r.x1_dst.at[l, i - 1])
        dots_grad = sum(dot_nt(highs[u], r.uall[l, u]) + dot_nt(lows[u], r.uall[l, u]) for u in range(T)) + den_grad
        dots_grad = (dots_grad * row_mask).astype(BF16)
        key_direct = feature_map_back(r.keyb[l].astype(F32), dot_tn(dots_grad, r.phiq[l]))
        for u in range(T):
            r.x2_src[l, u] = key_direct[:, u * z.keys_w : (u + 1) * z.keys_w].astype(BF16)
        key_step = to_parts(lambda peer: r.x2_src.at[l, peer], lambda i: r.x2_dst.at[l, i - 1])
        if l == 1:
            row_step = share_rows(r.xfull, 1)
        add_pair(l, fam_qk, pair_qk)
        add_pair(l, fam_vo, pair_vo)
        pass_on(l, fam_p)
        arrive(value_step)
        value_part = plus(r.x1_src[l, t], r.x1_dst.at[l], T - 1)
        r.x1_mid[l] = value_part.astype(BF16)
        value_step = to_segs(lambda _: r.x1_mid.at[l], lambda i: r.x1_far.at[l, i - 1])
        arrive(key_step)
        key_part = plus(r.x2_src[l, t], r.x2_dst.at[l], T - 1)
        r.x2_mid[l] = key_part.astype(BF16)
        key_step = to_segs(lambda _: r.x2_mid.at[l], lambda i: r.x2_far.at[l, i - 1])
        for family in (fam_c, fam_qk, fam_vo) if l == 1 else (fam_qk, fam_vo):
            spread(l, family, False)
        query_grad = feature_map_back(r.qmem[l].astype(F32), dot_nn(dots_grad, r.phik[l])).astype(BF16)
        for u in range(T):
            r.dq_src[l, u] = query_grad[:, u * z.keys_w : (u + 1) * z.keys_w]
        r.dq_all[l, own, :] = r.dq_src[l, t]
        query_step = to_parts(lambda peer: r.dq_src.at[l, peer], lambda i: r.dq_all.at[l, own])
        if l == 0:
            arrive((12, 0, 0))
            arrive((12, 0, 1))
        r.tmp[...] += dot_nn(query_grad, r.w_keys[l, 0])
        target = r.gfull.at[0] if l == 1 else r.final
        first = pl.ds(pl.multiple_of(t * C, 16), C - MEM)
        rest = pl.ds(pl.multiple_of(t * C + C - MEM, 16), MEM)
        target[first, :] = r.tmp[: C - MEM, :].astype(BF16)
        first_step = to_parts(lambda _: target.at[first], lambda i: target.at[first])
        if l == 1:
            spread_shard(0, 0)
        arrive(value_step)
        direct = plus(value_part, r.x1_far.at[l], S - 1)
        arrive(key_step)
        small_key = small_parts(l, small_key)
        key_dots = r.kdots[l]
        key_den = 1.0 + jnp.sum(key_dots, axis=1, keepdims=True)
        r.vgrad[...] = direct
        for k in range(S - 1, 0, -1):
            rows = slice(k * MEM, (k + 1) * MEM)
            back = -r.vgrad[rows, :] / key_den[rows]
            r.vgrad[...] += dot_tn(key_dots[rows].astype(BF16), back.astype(BF16))
        value_grad = r.vgrad[...]
        read = r.vpart[l] - r.upart[l]
        back = (-value_grad / key_den).astype(BF16)
        key_den_grad = -jnp.sum(back.astype(F32) * read, axis=1, keepdims=True)
        key_dots_grad = (dot_nt(back, r.upart[l].astype(BF16)) + key_den_grad) * key_mask
        both = (key_dots_grad + key_dots_grad.T).astype(BF16)
        key_solve = feature_map_back(r.keyb[l].astype(F32), dot_nn(both, r.phik[l]))
        r.ksolve[...] = key_solve
        r.dv[...] = value_grad.astype(BF16)
        r.dk_direct[...] = plus(key_part, r.x2_far.at[l], S - 1)
        tail = dot_nn(r.dv[seg_rows, :], r.w_value[l])
        tail = tail + dot_nn(r.dk_direct[seg_rows, :].astype(BF16), r.w_keys[l, 1, shard_rows(t), :])
        tail = tail + dot_nn(r.ksolve[seg_rows, :].astype(BF16), r.w_keys[l, 1])
        r.x3_src[l] = tail.astype(BF16)
        base, place = alloc(T - 1), alloc(1)

        for i in range(1, T):

            @pl.when(tpeers[i] == T - 1)
            def _():
                copy = pltpu.make_async_remote_copy(
                    src_ref=r.x3_src.at[l], dst_ref=r.x3_dst.at[l, i - 1], send_sem=r.send.at[place],
                    recv_sem=r.recv.at[base + i - 1], device_id=(c, s, tpeers[i]), device_id_type=MESH,
                )
                copy.start()

        def drain():
            @pl.when(t != T - 1)
            def _():
                wait_bytes(r.x3_src.at[l], r.send.at[place])

        sent.append((drain, drain))
        for u in range(T):
            r.x4_src[l, u] = key_solve[:, u * z.keys_w : (u + 1) * z.keys_w].astype(BF16)
        solve_step = to_parts(lambda peer: r.x4_src.at[l, peer], lambda i: r.x4_dst.at[l, i - 1])

        @pl.when(t == T - 1)
        def _():
            total = r.x3_src[l].astype(F32)
            for i in range(T - 1):
                wait_bytes(r.x3_dst.at[l, i], r.recv.at[base + i])
                total = total + r.x3_dst[l, i].astype(F32)
            r.tmp[C - MEM :, :] += total

        target[rest, :] = r.tmp[C - MEM :, :].astype(BF16)
        rest_step = to_parts(lambda _: target.at[rest], lambda i: target.at[rest])
        small_key = small_segs(l, small_key)
        if l == 1:
            spread_shard(0, 1)
        arrive(query_step)
        if l == 1:
            arrive(row_step)
        weight_grad(l, fam_q, (r.xfull.at[l], r.dq_all[l]))
        pair_q = hand_over(l, fam_q)
        r.mem_v[l] = dot_tn(r.mem_rows[l], r.dv[...])
        arrive(solve_step)
        key_grad = plus(r.dk_direct[...] + r.x4_src[l, t].astype(F32), r.x4_dst.at[l], T - 1)
        r.mem_k[l] = dot_tn(r.mem_rows[l], key_grad.astype(BF16))
        rows = pl.ds(pl.multiple_of(s * z.cut, 8), z.cut)
        mem_copies = [pair_send(r.mem_k.at[l, rows], r.pair_k), pair_send(r.mem_v.at[l, rows], r.pair_v)]

        @pl.when(c != l)
        def _():
            for copy in mem_copies:
                copy.start()

        sent.extend((copy, c != l) for copy in mem_copies)
        mem_key = owe_owner(l, mem_copies)
        add_pair(l, fam_q, pair_q)
        spread(l, fam_q, False)
        if l == 0:
            pass_on(l, fam_c)
            pass_on(l, fam_qk)
            pass_on(l, fam_vo)
            pass_on(l, fam_q)
        arrive(first_step)
        arrive(rest_step)
        return mem_key, small_key

    forward(0)
    forward(1)
    for l in range(LAYERS):
        r.small[l] = jnp.zeros((16, D), F32)
    mem_key1, small_key1 = backward(1)
    mem_key0, small_key0 = backward(0)

    r.input_grad[0] = r.final[...]
    l = c

    arrive(mem_key1)
    arrive(mem_key0)
    rows = pl.ds(pl.multiple_of(s * z.cut, 8), z.cut)
    r.mkey_grads[0, 1] = r.mem_k[l, rows, :] + r.pair_k[...]
    r.mvalue_grads[0] = r.mem_v[l, rows, :] + r.pair_v[...]

    def far_sum(far):
        arrive((id(far), 1))
        arrive((id(far), 0))
        return sum(far[i, : z.cut, :].astype(F32) for i in range(S))

    r.proj_grads[0] = far_sum(r.far_p)
    r.fc_grads[0] = far_sum(r.far_c)
    both = far_sum(r.far_qk)
    r.attn_grads[0, 0] = both[:, : z.heads_w]
    r.attn_grads[0, 1] = both[:, z.heads_w :]
    both = far_sum(r.far_vo)
    r.attn_grads[0, 2] = both[:, : z.heads_w]
    r.out_grads[0] = both[:, z.heads_w :].T
    r.mkey_grads[0, 0] = far_sum(r.far_q)
    arrive(small_key1)
    arrive(small_key0)
    total = r.sum_small[...]
    for i in range(1, S):
        total = total + r.seg_small[i].astype(F32)
    r.gain_grads[0] = total[0:2]
    r.shift_grads[0] = total[2:4]
    r.obias_grads[0] = total[4:6]
    r.fcb_grads[...] = total[8:9, : z.units]
    r.abias_grads[0] = total[9:11, : z.heads_w]

    assert not owed and not relays
    for copy, when in sent:
        if when is copy:
            copy()
        elif when is None:
            copy.wait_send()
        else:
            pl.when(when)(copy.wait_send)


def hand_out(*refs):
    count = len(refs) // 2
    for source, target in zip(refs[:count], refs[count:]):
        target[...] = source[...]


def item_ids(lengths):
    item_ends = jnp.cumsum(lengths, axis=-1)
    item_begins = item_ends - lengths
    places = jnp.arange(lengths.shape[-1], dtype=jnp.int32)
    matches = (item_begins[:, :, None] == places[None, None, :]) & (lengths[:, :, None] > 0)
    return jnp.cumsum(jnp.sum(matches.astype(jnp.int32), axis=1), axis=-1)


def reach_mask(lengths):
    ids = item_ids(lengths)
    places = jnp.arange(lengths.shape[-1])
    earlier = places[:, None] > places[None, :]
    same = (ids[:, :, None] == ids[:, None, :]) & earlier[None]
    return jnp.repeat(jnp.repeat(same.astype(F32), MEM, axis=1), MEM, axis=2)


def gather_rows(values, axis):
    return lax.all_gather(values, axis, axis=0, tiled=True)


def scatter_rows(values, axis):
    peers = lax.axis_size(axis)
    pieces = values.astype(BF16).reshape(peers, values.shape[0] // peers, values.shape[1])
    got = lax.all_to_all(pieces, axis, 0, 0, tiled=True)
    return jnp.sum(got.astype(F32), axis=0)


def scatter_columns(values, axis):
    peers = lax.axis_size(axis)
    rows = values.shape[0]
    pieces = values.reshape(rows, peers, -1).transpose(1, 0, 2)
    got = lax.all_to_all(pieces.astype(BF16), axis, 0, 0, tiled=True)
    return jnp.sum(got.astype(F32), axis=0)


def solve_forward(key_dots, key_den, value_mem):
    segments = key_dots.shape[0] // MEM
    solved = value_mem
    for s in range(1, segments):
        rows = slice(s * MEM, (s + 1) * MEM)
        read = dot_nn(key_dots[rows].astype(BF16), solved.astype(BF16)) / key_den[rows]
        solved = solved.at[rows].add(-read)
    return solved


def solve_backward(key_dots, key_den, direct):
    segments = key_dots.shape[0] // MEM
    total = direct
    for s in range(segments - 1, 0, -1):
        rows = slice(s * MEM, (s + 1) * MEM)
        back = -total[rows] / key_den[rows]
        total = total + dot_tn(key_dots[rows].astype(BF16), back.astype(BF16))
    return total


def layer_forward(own_rows, mem_rows, mask, place, params):
    gains, shifts, w_attn, attn_bias, w_out, out_biases, w_fc, fc_bias, w_proj, w_q, w_k, w_v = params
    seg, _ = place
    own_mask = lax.dynamic_slice_in_dim(mask, seg * MEM, 1, 0)
    key_mem = dot_nn(mem_rows, w_k).astype(BF16)
    phi_key = feature_map(key_mem.astype(F32), jnp.roll).astype(BF16)
    key_dots = dot_nt(phi_key, phi_key) * mask
    key_den = 1.0 + jnp.sum(key_dots, axis=1, keepdims=True)
    value_part = dot_nn(mem_rows, w_v)
    solved_part = solve_forward(key_dots, key_den, value_part)
    solved = lax.all_gather(solved_part.astype(BF16), "tensor", axis=1, tiled=True)
    query_mem = dot_nn(own_rows, w_q).astype(BF16)
    phi_query = feature_map(query_mem.astype(F32), jnp.roll).astype(BF16)
    query_dots = dot_nt(phi_query, phi_key) * own_mask
    query_den = 1.0 + jnp.sum(query_dots, axis=1, keepdims=True)
    recall = dot_nn(query_dots.astype(BF16), solved) / query_den
    hidden = own_rows.astype(F32) + recall.astype(BF16).astype(F32)
    unit, _ = norm_rows(hidden)
    normed = gather_rows((unit * gains[0] + shifts[0]).astype(BF16), "tensor")
    queries = (dot_nn(normed, w_attn[0]) + attn_bias[0]).astype(BF16)
    key_heads = dot_nn(normed, w_attn[1]).astype(BF16)
    values = (dot_nn(normed, w_attn[2]) + attn_bias[1]).astype(BF16)
    rows = normed.shape[0]
    causal = jnp.arange(rows)[:, None] >= jnp.arange(rows)[None, :]
    probs, mixed = [], []
    for h in range(queries.shape[1] // HEAD_DIM):
        cols = slice(h * HEAD_DIM, (h + 1) * HEAD_DIM)
        scores = dot_nt(queries[:, cols], key_heads[:, cols]) * HEAD_DIM ** (-0.5)
        scores = jnp.where(causal, scores, -jnp.inf)
        heights = jnp.exp(scores - jnp.max(scores, axis=1, keepdims=True))
        probs.append(heights / jnp.sum(heights, axis=1, keepdims=True))
        mixed.append(dot_nn(probs[-1].astype(BF16), values[:, cols]).astype(BF16))
    mixed = jnp.concatenate(mixed, axis=1)
    after = hidden + scatter_rows(dot_nn(mixed, w_out), "tensor") + out_biases[0]
    unit, _ = norm_rows(after)
    normed_mlp = gather_rows((unit * gains[1] + shifts[1]).astype(BF16), "tensor")
    pre = dot_nn(normed_mlp, w_fc) + fc_bias
    activation, slope = gelu_and_slope(pre)
    activation = activation.astype(BF16)
    output = after + scatter_rows(dot_nn(activation, w_proj), "tensor") + out_biases[1]
    kept = (
        own_rows, mem_rows, key_mem, phi_key, key_dots, key_den, value_part, solved_part, solved, query_mem,
        phi_query, query_dots, query_den, recall, hidden, normed, queries, key_heads, values, probs, mixed,
        after, normed_mlp, slope, activation,
    )
    return output, kept


def layer_backward(own_grad, kept, mask, place, params):
    gains, shifts, w_attn, attn_bias, w_out, out_biases, w_fc, fc_bias, w_proj, w_q, w_k, w_v = params
    (
        own_rows, mem_rows, key_mem, phi_key, key_dots, key_den, value_part, solved_part, solved, query_mem,
        phi_query, query_dots, query_den, recall, hidden, normed, queries, key_heads, values, probs, mixed,
        after, normed_mlp, slope, activation,
    ) = kept
    seg, part = place
    own_mask = lax.dynamic_slice_in_dim(mask, seg * MEM, 1, 0)
    grad_low = gather_rows(own_grad.astype(BF16), "tensor")
    pre_grad = (slope * dot_nt(grad_low, w_proj)).astype(BF16)
    proj_grad = dot_tn(activation, grad_low)
    fc_bias_grad = jnp.sum(pre_grad.astype(F32), axis=0)
    fc_grad = dot_tn(normed_mlp, pre_grad)
    after_part, gain_mlp, shift_mlp = norm_back(
        after, gains[1:2], scatter_rows(dot_nt(pre_grad, w_fc), "tensor")
    )
    after_grad = own_grad + after_part
    after_low = gather_rows(after_grad.astype(BF16), "tensor")
    out_grad = dot_tn(mixed, after_low)
    mixed_grad = dot_nt(after_low, w_out).astype(BF16)
    q_grads, k_grads, v_grads = [], [], []
    for h in range(queries.shape[1] // HEAD_DIM):
        cols = slice(h * HEAD_DIM, (h + 1) * HEAD_DIM)
        probs_grad = dot_nt(mixed_grad[:, cols], values[:, cols])
        delta = jnp.sum(probs_grad * probs[h], axis=1, keepdims=True)
        score_grad = (probs[h] * (probs_grad - delta)).astype(BF16)
        q_grads.append((dot_nn(score_grad, key_heads[:, cols]) * HEAD_DIM ** (-0.5)).astype(BF16))
        k_grads.append((dot_tn(score_grad, queries[:, cols]) * HEAD_DIM ** (-0.5)).astype(BF16))
        v_grads.append(dot_tn(probs[h].astype(BF16), mixed_grad[:, cols]).astype(BF16))
    three = [jnp.concatenate(g, axis=1) for g in (q_grads, k_grads, v_grads)]
    attn_bias_grad = jnp.stack([jnp.sum(three[i].astype(F32), axis=0) for i in (0, 2)])
    attn_grad = jnp.stack([dot_tn(normed, g) for g in three])
    normed_part = sum(dot_nt(g, w_attn[i]) for i, g in enumerate(three))
    hidden_part, gain_attn, shift_attn = norm_back(
        hidden, gains[0:1], scatter_rows(normed_part, "tensor")
    )
    hidden_grad = after_grad + hidden_part
    num_grad = (hidden_grad / query_den).astype(BF16)
    den_grad = -jnp.sum(hidden_grad * recall, axis=1, keepdims=True) / query_den
    dots_grad = ((dot_nt(num_grad, solved) + den_grad) * own_mask).astype(BF16)
    query_grad = feature_map_back(query_mem.astype(F32), dot_nn(dots_grad, phi_key), jnp.roll).astype(BF16)
    solved_direct = dot_tn(query_dots.astype(BF16), num_grad)
    key_direct = feature_map_back(key_mem.astype(F32), dot_tn(dots_grad, phi_query), jnp.roll)
    solved_direct = scatter_columns(solved_direct, "tensor")
    solved_direct = jnp.sum(lax.all_gather(solved_direct.astype(BF16), "seg").astype(F32), axis=0)
    value_grad = solve_backward(key_dots, key_den, solved_direct)
    read = value_part - solved_part
    key_den_grad = jnp.sum(value_grad * read, axis=1, keepdims=True) / key_den
    back = (-value_grad / key_den).astype(BF16)
    key_dots_grad = (dot_nt(back, solved_part.astype(BF16)) + key_den_grad) * mask
    both = (key_dots_grad + key_dots_grad.T).astype(BF16)
    key_solve = feature_map_back(key_mem.astype(F32), dot_nn(both, phi_key), jnp.roll)
    mine = (jnp.arange(key_solve.shape[0]) // MEM == seg)[:, None]
    key_direct = key_direct + jnp.where(mine, key_solve, 0.0)
    key_direct = scatter_columns(key_direct, "tensor")
    key_grad = jnp.sum(lax.all_gather(key_direct.astype(BF16), "seg").astype(F32), axis=0).astype(BF16)
    value_low = value_grad.astype(BF16)
    mem_width = mem_rows.shape[1] // lax.axis_size("seg")
    mem_cols = lax.dynamic_slice_in_dim(mem_rows, seg * mem_width, mem_width, 1)
    mem_key_grad = dot_tn(mem_cols, key_grad)
    mem_value_grad = dot_tn(mem_cols, value_low)
    return (
        hidden_grad, query_grad, key_grad, value_low,
        (gain_attn, gain_mlp, shift_attn, shift_mlp, jnp.sum(after_grad, axis=0, keepdims=True), jnp.sum(own_grad, axis=0, keepdims=True)),
        (attn_grad, attn_bias_grad, out_grad, fc_grad, fc_bias_grad, proj_grad, mem_key_grad, mem_value_grad),
    )


def general_device(
    inputs, out_grad, item_lengths, norm_gains, norm_biases, w_attn, attn_bias, w_out, out_biases, w_fc, fc_bias,
    w_proj, w_mem_keys, w_mem_value,
):
    section, seg, part = (lax.axis_index(name) for name in ("section", "seg", "tensor"))
    segments, parts = lax.axis_size("seg"), lax.axis_size("tensor")
    layers = lax.axis_size("section")
    mask = reach_mask(item_lengths)[section]
    weights = (norm_gains, norm_biases, w_attn, attn_bias, w_out, out_biases, w_fc, fc_bias, w_proj, w_mem_keys, w_mem_value)
    weights = [lax.all_gather(w, "section", axis=0, tiled=True) for w in weights]
    full_keys = lax.all_gather(weights[9], "tensor", axis=3, tiled=True)
    rows_all, grad_all = inputs[section], out_grad[section]
    chunk = rows_all.shape[0] // parts
    own_rows = lax.dynamic_slice_in_dim(rows_all, part * chunk, chunk, 0)
    place = (seg, part)
    saved, layer_params = [], []
    for layer in range(layers):
        mems = lax.all_gather(own_rows[-MEM:], ("seg", "tensor"), axis=0)
        mem_rows = mems[parts - 1 :: parts].reshape(segments * MEM, -1)
        params = tuple(w[layer] for w in weights[:9]) + (full_keys[layer, 0], full_keys[layer, 1], weights[10][layer])
        output, kept = layer_forward(own_rows, mem_rows, mask, place, params)
        saved.append(kept)
        layer_params.append(params)
        own_rows = output.astype(BF16)
    own_grad = lax.dynamic_slice_in_dim(grad_all, part * chunk, chunk, 0).astype(F32)
    rows_grads, matrix_grads = [None] * layers, [None] * layers
    for layer in reversed(range(layers)):
        params, kept = layer_params[layer], saved[layer]
        hidden_grad, query_grad, key_grad, value_low, rows_grads[layer], grads = layer_backward(own_grad, kept, mask, place, params)
        w_q = params[9]
        keys_here = lax.dynamic_slice_in_dim(key_grad, seg * MEM, MEM, 0)
        values_here = lax.dynamic_slice_in_dim(value_low, seg * MEM, MEM, 0)
        tail = dot_nt(keys_here, weights[9][layer, 1]) + dot_nt(values_here, params[11])
        tail = jnp.sum(lax.all_gather(tail.astype(BF16), "tensor").astype(F32), axis=0)
        tail = jnp.concatenate([jnp.zeros((chunk - MEM, tail.shape[1]), F32), tail], axis=0)
        rows_grad = hidden_grad + dot_nt(query_grad, w_q) + jnp.where(part == parts - 1, tail, 0.0)
        own_grad = rows_grad.astype(BF16).astype(F32)
        rows_full = gather_rows(kept[0], "tensor")
        query_cols = lax.all_to_all(query_grad.reshape(chunk, parts, -1).transpose(1, 0, 2), "tensor", 0, 0, tiled=True)
        query_cols = query_cols.reshape(chunk * parts, -1)
        matrix_grads[layer] = grads + (dot_tn(rows_full, query_cols),)
    input_grad = gather_rows(own_grad.astype(BF16), "tensor")[None]

    def over_layers(values):
        return lax.psum_scatter(jnp.stack(values), "section", scatter_dimension=0, tiled=True)

    rows_sums = lax.psum(over_layers([jnp.concatenate(r, axis=0) for r in rows_grads]), ("seg", "tensor"))

    def spread(index, axis):
        stacked = jnp.stack([g[index] for g in matrix_grads]).astype(BF16)
        pair = lax.all_to_all(stacked, "section", 0, 0, tiled=True)
        both = jnp.sum(pair.astype(F32), axis=0)
        cut = both.astype(BF16).reshape(both.shape[:axis] + (segments, -1) + both.shape[axis + 1 :])
        got = lax.all_to_all(cut, "seg", axis, axis, tiled=True)
        return jnp.sum(got.astype(F32), axis=axis)[None]

    biases = lax.psum(
        (over_layers([g[1] for g in matrix_grads]), over_layers([g[4] for g in matrix_grads])), "seg"
    )
    query_w = spread(8, 0)
    key_w = over_layers([g[6] for g in matrix_grads])
    return (
        input_grad,
        rows_sums[:, 0:2],
        rows_sums[:, 2:4],
        spread(0, 1),
        biases[0],
        spread(2, 1),
        rows_sums[:, 4:6],
        spread(3, 0),
        biases[1],
        spread(5, 1),
        jnp.stack([query_w, key_w], axis=1),
        over_layers([g[7] for g in matrix_grads]),
    )


def solution(mesh):
    def per_device(*args):
        inputs, out_grad, item_lengths = args[:3]
        S, T = mesh.shape["seg"], mesh.shape["tensor"]
        w_attn, w_fc, w_keys = args[5], args[9], args[12]
        z = Sizes(
            mesh,
            (
                (0, inputs.shape[1] * S, inputs.shape[2]), (0, 0, 0, w_attn.shape[3] * T), (0, 0, w_fc.shape[2] * T),
                (0, 0, 0, w_keys.shape[3] * T),
            ),
        )
        scratch = scratch_of(z)
        D = z.width
        outs = dict(
            input_grad=((1, z.rows, D), BF16), gain_grads=((1, 2, D), F32), shift_grads=((1, 2, D), F32),
            attn_grads=((1, 3, z.cut, z.heads_w), F32), abias_grads=((1, 2, z.heads_w), F32),
            out_grads=((1, z.heads_w, z.cut), F32), obias_grads=((1, 2, D), F32), fc_grads=((1, z.cut, z.units), F32),
            fcb_grads=((1, z.units), F32), proj_grads=((1, z.cut, z.units), F32),
            mkey_grads=((1, 2, z.cut, z.keys_w), F32), mvalue_grads=((1, z.cut, z.val_w), F32),
        )
        names = tuple(scratch)
        vmem, anywhere = pl.BlockSpec(memory_space=pltpu.VMEM), pl.BlockSpec(memory_space=pl.ANY)
        shapes = [jax.ShapeDtypeStruct(*shape) for shape in outs.values()]
        flip = lambda w: jnp.swapaxes(w, -1, -2)
        results = pl.pallas_call(
            functools.partial(kernel, z, names),
            out_shape=shapes,
            in_specs=[anywhere, anywhere, pl.BlockSpec(memory_space=pltpu.SMEM)] + [anywhere] * 11,
            out_specs=[vmem] * len(outs),
            scratch_shapes=list(scratch.values()),
            compiler_params=pltpu.CompilerParams(
                collective_id=0, has_side_effects=True, vmem_limit_bytes=63 * 2**20
            ),
            name="two_layers",
        )(*args[:5], flip(w_attn), *args[6:12], flip(w_keys), flip(args[13]))
        results = list(pl.pallas_call(
            hand_out, out_shape=shapes, in_specs=[vmem] * len(outs), out_specs=[vmem] * len(outs), name="hand_out"
        )(*results))
        results[9] = flip(results[9])
        return tuple(results)

    return jax.shard_map(
        per_device if mesh.shape["seg"] * MEM <= 128 else general_device,
        mesh=mesh,
        in_specs=(
            P(None, "seg", None),
            P(None, "seg", None),
            P(),
            P("section", None, None),
            P("section", None, None),
            P("section", None, None, "tensor"),
            P("section", None, "tensor"),
            P("section", "tensor", None),
            P("section", None, None),
            P("section", None, "tensor"),
            P("section", "tensor"),
            P("section", "tensor", None),
            P("section", None, None, "tensor"),
            P("section", None, "tensor"),
        ),
        out_specs=(
            P("section", "seg", None),
            P("section", None, None),
            P("section", None, None),
            P("section", None, "seg", "tensor"),
            P("section", None, "tensor"),
            P("section", "tensor", "seg"),
            P("section", None, None),
            P("section", "seg", "tensor"),
            P("section", "tensor"),
            P("section", "tensor", "seg"),
            P("section", None, "seg", "tensor"),
            P("section", "seg", "tensor"),
        ),
        check_vma=False,
    )
```

```python
import functools
from types import SimpleNamespace
from typing import Any, NamedTuple

import jax
import jax.numpy as jnp
from jax import lax
from jax.experimental import pallas as pl
from jax.experimental.pallas import tpu as pltpu
from jax.sharding import PartitionSpec as P

HEAD_DIM = 64
NU = 3
MEM = 16
EPSILON = 1e-05
F32 = jnp.float32
BF16 = jnp.bfloat16
GELU_A = 0.7978845608028654
GELU_B = 0.044715
LAYERS = 2
MESH = pl.DeviceIdType.MESH


def dot_nn(left, right):
    return lax.dot_general(left, right, (((1,), (0,)), ((), ())), preferred_element_type=F32)


def dot_nt(left, right):
    return lax.dot_general(left, right, (((1,), (1,)), ((), ())), preferred_element_type=F32)


def dot_tn(left, right):
    return lax.dot_general(left, right, (((0,), (0,)), ((), ())), preferred_element_type=F32)


def doubled_softplus(projected):
    small = jnp.exp(-jnp.abs(projected))
    tail = jnp.where(small < 1e-3, small - 0.5 * small * small, jnp.log1p(small))
    return jnp.concatenate(
        [jnp.maximum(projected, 0.0) + tail, jnp.maximum(-projected, 0.0) + tail], axis=1
    )


def feature_map(projected, roll=pltpu.roll):
    doubled = doubled_softplus(projected)
    return jnp.concatenate([doubled * roll(doubled, j, 1) for j in range(1, NU + 1)], axis=1)


def feature_map_back(projected, phi_grad, roll=pltpu.roll):
    doubled = doubled_softplus(projected)
    width = doubled.shape[1]
    total = jnp.zeros_like(doubled)
    for j in range(1, NU + 1):
        part = phi_grad[:, (j - 1) * width : j * width]
        total = total + part * roll(doubled, j, 1) + roll(part * doubled, width - j, 1)
    half = width // 2
    gate = 1.0 / (1.0 + jnp.exp(-projected))
    return total[:, :half] * gate - total[:, half:] * (1.0 - gate)


def norm_rows(hidden):
    centered = hidden - jnp.mean(hidden, axis=1, keepdims=True)
    scale = lax.rsqrt(jnp.mean(centered * centered, axis=1, keepdims=True) + EPSILON)
    return centered * scale, scale


def norm_back(hidden, gain_row, grad):
    unit, scale = norm_rows(hidden)
    unit_grad = grad * gain_row
    mean_grad = jnp.mean(unit_grad, axis=1, keepdims=True)
    mean_both = jnp.mean(unit_grad * unit, axis=1, keepdims=True)
    return (
        scale * (unit_grad - mean_grad - unit * mean_both),
        jnp.sum(grad * unit, axis=0, keepdims=True),
        jnp.sum(grad, axis=0, keepdims=True),
    )


def gelu_and_slope(pre):
    square = pre * pre
    bent = jnp.tanh(GELU_A * (pre + GELU_B * square * pre))
    value = 0.5 * pre * (1.0 + bent)
    slope = 0.5 * (1.0 + bent) + 0.5 * pre * (1.0 - bent * bent) * (
        GELU_A * (1.0 + 3.0 * GELU_B * square)
    )
    return value, slope


def xor_peer(place, other, count):
    total, bit = 0, 1
    while bit < count:
        mine = lax.rem(lax.div(place, bit), 2)
        total = total + bit * (1 - mine if other & bit else mine)
        bit *= 2
    return total


def split(values):
    high = values.astype(BF16)
    return high, (values - high.astype(F32)).astype(BF16)


def plus(first, others, count):
    total = first.astype(F32)
    for i in range(count):
        total = total + others[i].astype(F32)
    return total


class Sizes:
    def __init__(self, mesh, shapes):
        self.segs, self.parts = mesh.shape["seg"], mesh.shape["tensor"]
        inputs, w_attn, w_fc, w_keys = shapes
        self.rows, self.width = inputs[1] // self.segs, inputs[2]
        self.chunk = self.rows // self.parts
        self.mems = self.segs * MEM
        self.heads_w = w_attn[3] // self.parts
        self.heads = self.heads_w // HEAD_DIM
        self.units = w_fc[2] // self.parts
        self.keys = w_keys[3]
        self.keys_w = self.keys // self.parts
        self.phi = 2 * self.keys * NU
        self.val_w = self.width // self.parts
        self.cut = self.width // self.segs
        self.cut_pad = -(-self.cut // 16) * 16
        self.sems = 120 + 48 * self.parts + 2 * self.segs * (self.parts + 16)


def scratch_of(z):
    S, T, R, D, C, M = z.segs, z.parts, z.rows, z.width, z.chunk, z.mems
    bf = lambda *d: pltpu.VMEM(d, BF16)
    fl = lambda *d: pltpu.VMEM(d, F32)
    return dict(
        gains=fl(2, 2, D), shifts=fl(2, 2, D), w_attn=bf(2, 3, z.heads_w, D), attn_bias=fl(2, 2, z.heads_w),
        w_out=bf(2, z.heads_w, D), out_biases=fl(2, 2, D), w_fc=bf(2, D, z.units), fc_bias=fl(2, 1, z.units),
        w_proj=bf(2, z.units, D), w_keys=bf(2, 2, z.keys, D), w_value=bf(2, z.val_w, D),
        xfull=bf(2, R, D), gfull=bf(2, R, D), mem_rows=bf(2, M, D),
        keyb=bf(2, M, z.keys), phik=bf(2, M, z.phi), kdots=fl(2, M, M), vpart=fl(2, M, z.val_w),
        upart=fl(2, M, z.val_w), uall=bf(2, T, M, z.val_w), qmem=bf(2, C, z.keys), phiq=bf(2, C, z.phi),
        qdots=fl(2, C, M), recall=fl(2, C, D), hidden=fl(2, C, D), normed=bf(2, R, D), qkv=bf(2, 3, R, z.heads_w),
        probs=fl(2, z.heads, R, R), mixed=bf(2, R, z.heads_w), after=fl(2, C, D), normed_mlp=bf(2, R, D),
        slope=fl(2, R, z.units), act=bf(2, R, z.units), rs_src=bf(7, R, D), rs_own=fl(R, D), q_src=bf(R, z.keys_w), q_parts=bf(T, C, z.keys_w), k_parts=bf(T, M, z.keys_w), rs_dst=bf(7, T - 1, C, D),
        low2=bf(2, R, D), dpre=bf(R, z.units), dqkv=bf(3, R, z.heads_w),
        x1_src=bf(2, T, M, z.val_w), x1_dst=bf(2, T - 1, M, z.val_w), x1_mid=bf(2, M, z.val_w), x1_far=bf(2, max(S - 1, 1), M, z.val_w),
        x2_src=bf(2, T, M, z.keys_w), x2_dst=bf(2, T - 1, M, z.keys_w), x2_mid=bf(2, M, z.keys_w), x2_far=bf(2, max(S - 1, 1), M, z.keys_w), x4_src=bf(2, T, M, z.keys_w), x4_dst=bf(2, T - 1, M, z.keys_w), ksolve=fl(M, z.keys), dk_direct=fl(M, z.keys_w),
        dq_src=bf(2, T, C, z.keys_w), dq_all=bf(2, R, z.keys_w), dv=bf(M, z.val_w), vgrad=fl(M, z.val_w),
        x3_src=bf(2, MEM, D), x3_dst=bf(2, T - 1, MEM, D), final=bf(R, D), tmp=fl(C, D),
        grad_p=bf(2, S, z.cut_pad, z.units), grad_c=bf(2, S, z.cut_pad, z.units), grad_qk=bf(2, S, z.cut_pad, 2 * z.heads_w),
        grad_vo=bf(2, S, z.cut_pad, 2 * z.heads_w), grad_q=bf(2, S, z.cut_pad, z.keys_w),
        pair_f=bf(2, S, z.cut_pad, z.units), pair_a=bf(2, S, z.cut_pad, 2 * z.heads_w), pair_q=bf(2, S, z.cut_pad, z.keys_w), relay_f=bf(2, 2, z.cut_pad, z.units), relay_a=bf(2, 2, z.cut_pad, 2 * z.heads_w), relay_q=bf(2, 2, z.cut_pad, z.keys_w),
        far_p=bf(S, z.cut_pad, z.units), far_c=bf(S, z.cut_pad, z.units), far_qk=bf(S, z.cut_pad, 2 * z.heads_w),
        far_vo=bf(S, z.cut_pad, 2 * z.heads_w), far_q=bf(S, z.cut_pad, z.keys_w), dqk=bf(R, 2 * z.heads_w),
        mem_k=fl(2, D, z.keys_w), mem_v=fl(2, D, z.val_w), pair_k=fl(z.cut, z.keys_w), pair_v=fl(z.cut, z.val_w),
        small=fl(2, 16, D), pair_small=fl(16, D), part_small=fl(T, 8, D), sum_small=fl(16, D), seg_small=bf(S, 16, D),
        send=pltpu.SemaphoreType.DMA((z.sems,)), recv=pltpu.SemaphoreType.DMA((z.sems,)), load=pltpu.SemaphoreType.DMA((14, 2)),
        shard=pltpu.SemaphoreType.DMA((2, 2, T)),
    )


class Outer(NamedTuple):
    inputs: Any
    out_grad: Any
    item_lengths: Any
    norm_gains: Any
    norm_biases: Any
    w_attn_in: Any
    attn_bias_in: Any
    w_out_in: Any
    out_biases_in: Any
    w_fc_in: Any
    fc_bias_in: Any
    w_proj_in: Any
    w_keys_in: Any
    w_value_in: Any
    input_grad: Any
    gain_grads: Any
    shift_grads: Any
    attn_grads: Any
    abias_grads: Any
    out_grads: Any
    obias_grads: Any
    fc_grads: Any
    fcb_grads: Any
    proj_grads: Any
    mkey_grads: Any
    mvalue_grads: Any


def kernel(z, held_names, *refs):
    outer = len(Outer._fields)
    r = SimpleNamespace(**Outer(*refs[:outer])._asdict(), **dict(zip(held_names, refs[outer:])))
    S, T, R, D, C, M = z.segs, z.parts, z.rows, z.width, z.chunk, z.mems
    c, s, t = (lax.axis_index(a) for a in ("section", "seg", "tensor"))
    other = 1 - c
    tpeers = [xor_peer(t, i, T) for i in range(T)]
    to_seg = [lax.rem(s + i, S) for i in range(S)]
    own = pl.ds(pl.multiple_of(t * C, C), C)
    seg_rows = pl.ds(pl.multiple_of(s * MEM, MEM), MEM)
    used = [0]
    sent = []
    owed = {}

    def alloc(count):
        used[0] += count
        assert used[0] <= z.sems
        return used[0] - count

    def owe(copies):
        def wait():
            for copy in copies:
                copy.wait_recv()

        owed[id(copies)] = wait
        return id(copies)

    def wait_bytes(ref, semaphore):
        pltpu.make_async_copy(ref, ref, semaphore).wait()

    def remote(src, dst, index, device, recv=None):
        copy = pltpu.make_async_remote_copy(
            src_ref=src, dst_ref=dst, send_sem=r.send.at[index],
            recv_sem=r.recv.at[index] if recv is None else recv, device_id=device, device_id_type=MESH,
        )
        return copy

    def to_parts(src_of, dst):
        base = alloc(T - 1)
        copies = []
        for i in range(T - 1, 0, -1):
            copy = remote(src_of(tpeers[i]), dst(i), base + i - 1, (c, s, tpeers[i]))
            copy.start()
            copies.append(copy)
        sent.extend((copy, None) for copy in copies)
        return owe(copies)

    def to_segs(src_of, dst):
        base = alloc(S - 1)
        copies = [
            remote(src_of(to_seg[i]), dst(i), base + i - 1, (c, to_seg[i], t)) for i in range(1, S)
        ]
        for copy in copies:
            copy.start()
        sent.extend((copy, None) for copy in copies)
        return owe(copies)

    def arrive(key):
        owed.pop(key)()

    def wait_load(ref, layer):
        arrive((id(ref), layer))

    barrier = pltpu.get_barrier_semaphore()
    greeted = [(other, to_seg[i], t) for i in range(S)] + [(c, to_seg[i], tpeers[j]) for i in range(S) for j in range(T) if i or j]
    for device in greeted:
        pl.semaphore_signal(barrier, inc=1, device_id=device, device_id_type=MESH)

    loads = [
        (r.w_value, r.w_value_in.at[0]), (r.gains, r.norm_gains.at[0]), (r.shifts, r.norm_biases.at[0]),
        (r.attn_bias, r.attn_bias_in.at[0]), (r.out_biases, r.out_biases_in.at[0]), (r.w_attn, r.w_attn_in.at[0]), (r.w_out, r.w_out_in.at[0]), (r.w_fc, r.w_fc_in.at[0]),
        (r.w_proj, r.w_proj_in.at[0]), (r.fc_bias, r.fc_bias_in),
    ]
    input_copy = pltpu.make_async_copy(r.inputs.at[c], r.xfull.at[0], r.load.at[10, 0])
    input_copy.start()
    owed[0] = input_copy.wait
    def shard_rows(part):
        return pl.ds(pl.multiple_of(part * z.keys_w, 16), z.keys_w)

    for which in (0, 1):
        pltpu.make_async_copy(
            r.w_keys_in.at[0, which], r.w_keys.at[c, which, shard_rows(t)], r.shard.at[c, which, 0]
        ).start()
    def load_own(kinds):
        for kind in kinds:
            held, source = loads[kind]
            pltpu.make_async_copy(source, held.at[c], r.load.at[kind, c]).start()

    def load_other(kinds):
        for kind in kinds:
            held, source = loads[kind]
            copy = remote(source, held.at[c], pair_base + kind, (other, s, t), r.load.at[kind, c])
            copy.start()
            sent.append((copy, None))
            for layer in range(LAYERS):
                owed[id(held), layer] = functools.partial(wait_bytes, held.at[layer], r.load.at[kind, layer])

    early, middle = range(0, 5), range(5, 7)
    load_own(range(len(loads)))
    grad_copy = pltpu.make_async_copy(r.out_grad.at[c], r.gfull.at[1], r.load.at[11, 0])
    grad_copy.start()
    owed[1] = grad_copy.wait

    pl.semaphore_wait(barrier, len(greeted))

    first_rows = to_segs(
        lambda _: r.inputs.at[c, pl.ds(R - MEM, MEM)], lambda i: r.mem_rows.at[0, seg_rows]
    )

    def shard_wait(layer, which, i):
        wait_bytes(r.w_keys.at[layer, which, pl.ds(0, z.keys_w)], r.shard.at[layer, which, i])

    def peer_shards(core, layer, which):
        @pl.when(c == core)
        def _():
            for i in range(1, T):
                shard_wait(layer, which, i)

    def spread_shard(layer, which):
        base = alloc(T - 1)
        place = r.w_keys.at[layer, which, shard_rows(t)]
        copies = [
            remote(r.w_keys_in.at[0, which], place, base + i - 1, (c, s, tpeers[i]), r.shard.at[layer, which, i])
            for i in range(T - 1, 0, -1)
        ]

        @pl.when(c == layer)
        def _():
            for copy in copies:
                copy.start()

        sent.extend((copy, c == layer) for copy in copies)
        owed[11, layer, which] = functools.partial(peer_shards, layer, layer, which)

    def forward_shard(layer, which):
        arrive((11, layer, which))
        base = alloc(T - 1)
        copies = []
        for i in range(1, T):
            place = r.w_keys.at[layer, which, shard_rows(tpeers[i])]
            copies.append(remote(place, place, base + i - 1, (other, s, t), r.shard.at[layer, which, i]))

        @pl.when(c == layer)
        def _():
            for copy in copies:
                copy.start()

        sent.extend((copy, c == layer) for copy in copies)
        owed[12, layer, which] = functools.partial(peer_shards, 1 - layer, layer, which)

    base = alloc(2)
    for which in (0, 1):
        copy = remote(
            r.w_keys_in.at[0, which], r.w_keys.at[c, which, shard_rows(t)], base + which, (other, s, t), r.shard.at[c, which, 0]
        )
        copy.start()
        sent.append((copy, None))
        for layer in range(LAYERS):
            owed[10, layer, which] = functools.partial(shard_wait, layer, which, 0)
    pair_base = alloc(len(loads))
    load_other(early)

    spread_shard(1, 1)
    row_seg = lax.broadcasted_iota(jnp.int32, (M, 1), 0) // MEM
    col_seg = lax.broadcasted_iota(jnp.int32, (1, M), 1) // MEM
    row_item, col_item, own_item = jnp.zeros((M, 1), jnp.int32), jnp.zeros((1, M), jnp.int32), 0
    begin = 0
    for i in range(r.item_lengths.shape[1]):
        length = r.item_lengths[c, i]
        there = jnp.where(length > 0, begin, S)
        row_item = row_item + (row_seg >= there).astype(jnp.int32)
        col_item = col_item + (col_seg >= there).astype(jnp.int32)
        own_item = own_item + jnp.where(s >= there, 1, 0)
        begin = begin + length
    key_mask = jnp.where((row_item == col_item) & (row_seg > col_seg), 1.0, 0.0)
    row_mask = jnp.where((col_item == own_item) & (col_seg < s), 1.0, 0.0)
    lane_head = lax.broadcasted_iota(jnp.int32, (1, z.heads_w), 1) // HEAD_DIM
    head_rows = [(lane_head == h).astype(F32).astype(BF16) for h in range(z.heads)]
    rs_count = [0]

    def reduce_rows(partial):
        k = rs_count[0]
        rs_count[0] += 1
        r.rs_own[...] = partial
        r.rs_src[k] = partial.astype(BF16)
        copies = to_parts(
            lambda peer: r.rs_src.at[k, pl.ds(pl.multiple_of(peer * C, C), C)], lambda i: r.rs_dst.at[k, i - 1]
        )

        def finish():
            arrive(copies)
            total = r.rs_own[own, :]
            for i in range(T - 1):
                total = total + r.rs_dst[k, i].astype(F32)
            return total

        return finish

    def share_rows(ref, layer):
        return to_parts(lambda _: ref.at[layer, own], lambda i: ref.at[layer, own])

    def forward(l):
        own_shard = shard_rows(t)
        if l == 0:
            arrive(0)
            arrive((10, 0, 0))
            r.q_src[...] = dot_nt(r.xfull[0], r.w_keys[0, 0, own_shard, :]).astype(BF16)
            r.q_parts[t] = r.q_src[own, :]
            query_step = to_parts(
                lambda peer: r.q_src.at[pl.ds(pl.multiple_of(peer * C, C), C)], lambda i: r.q_parts.at[t]
            )
            r.mem_rows[0, seg_rows, :] = r.xfull[0, R - MEM :, :]
            arrive((10, 0, 1))
            arrive(first_rows)
            mems = r.mem_rows[0]
            r.k_parts[t] = dot_nt(mems, r.w_keys[0, 1, own_shard, :]).astype(BF16)
            key_step = to_parts(lambda _: r.k_parts.at[t], lambda i: r.k_parts.at[t])
            load_other(middle)
            arrive(query_step)
            queries_mem = jnp.concatenate([r.q_parts[u] for u in range(T)], axis=1)
        else:
            for which in (0, 1):
                arrive((10, 1, which))
                arrive((12, 1, which))
            queries_mem = dot_nt(r.xfull[1, own, :], r.w_keys[1, 0]).astype(BF16)
        x = r.xfull[l, own, :]
        r.qmem[l] = queries_mem
        phi_query = feature_map(queries_mem.astype(F32)).astype(BF16)
        r.phiq[l] = phi_query
        wait_load(r.w_value, l)
        if l == 1:
            arrive(4)
            mems = r.mem_rows[1]
        value_part = dot_nt(mems, r.w_value[l])
        r.vpart[l] = value_part
        r.upart[l] = value_part
        if l == 0:
            arrive(key_step)
            keys = jnp.concatenate([r.k_parts[u] for u in range(T)], axis=1)
        else:
            keys = dot_nt(mems, r.w_keys[1, 1]).astype(BF16)
        r.keyb[l] = keys
        phi_key = feature_map(keys.astype(F32)).astype(BF16)
        r.phik[l] = phi_key
        key_dots = dot_nt(phi_key, phi_key) * key_mask
        r.kdots[l] = key_dots
        key_den = 1.0 + jnp.sum(key_dots, axis=1, keepdims=True)
        for k in range(1, S):
            rows = slice(k * MEM, (k + 1) * MEM)
            read = dot_nn(key_dots[rows].astype(BF16), r.upart[l].astype(BF16)) / key_den[rows]
            r.upart[l, rows, :] = value_part[rows] - read
        r.uall[l, t] = r.upart[l].astype(BF16)
        solved = to_parts(lambda _: r.uall.at[l, t], lambda i: r.uall.at[l, t])
        if l == 0:
            spread_shard(1, 0)
        query_dots = dot_nt(phi_query, phi_key) * row_mask
        r.qdots[l] = query_dots
        query_den = 1.0 + jnp.sum(query_dots, axis=1, keepdims=True)
        for ref in (r.gains, r.shifts, r.attn_bias, r.out_biases):
            wait_load(ref, l)
        arrive(solved)
        high, low = split(query_dots)
        recall = [dot_nn(high, r.uall[l, u]) + dot_nn(low, r.uall[l, u]) for u in range(T)]
        recall = jnp.concatenate(recall, axis=1) / query_den
        r.recall[l] = recall
        hidden = x.astype(F32) + recall.astype(BF16).astype(F32)
        r.hidden[l] = hidden
        unit, _ = norm_rows(hidden)
        r.normed[l, own, :] = (unit * r.gains[l, 0:1] + r.shifts[l, 0:1]).astype(BF16)
        shared = share_rows(r.normed, l)
        if l == 0:
            load_other([9, 7])
        wait_load(r.w_attn, l)
        wait_load(r.w_out, l)
        arrive(shared)
        normed = r.normed[l]
        queries = (dot_nt(normed, r.w_attn[l, 0]) + r.attn_bias[l, 0:1]).astype(BF16)
        key_heads = dot_nt(normed, r.w_attn[l, 1]).astype(BF16)
        values = (dot_nt(normed, r.w_attn[l, 2]) + r.attn_bias[l, 1:2]).astype(BF16)
        r.qkv[l, 0] = queries
        r.qkv[l, 1] = key_heads
        r.qkv[l, 2] = values
        causal = lax.broadcasted_iota(jnp.int32, (R, R), 0) >= lax.broadcasted_iota(jnp.int32, (R, R), 1)
        mixed = jnp.zeros((R, z.heads_w), F32)
        for h in range(z.heads):
            scores = dot_nt(queries, key_heads * head_rows[h]) * HEAD_DIM ** (-0.5)
            scores = jnp.where(causal, scores, -jnp.inf)
            heights = jnp.exp(scores - jnp.max(scores, axis=1, keepdims=True))
            probs = heights * (1.0 / jnp.sum(heights, axis=1, keepdims=True))
            r.probs[l, h] = probs
            mixed = mixed + dot_nn(probs.astype(BF16), values * head_rows[h])
        mixed = mixed.astype(BF16)
        r.mixed[l] = mixed
        finish = reduce_rows(dot_nn(mixed, r.w_out[l]))
        if l == 0:
            load_other([8])
        after = r.hidden[l] + finish() + r.out_biases[l, 0:1]
        r.after[l] = after
        unit, _ = norm_rows(after)
        r.normed_mlp[l, own, :] = (unit * r.gains[l, 1:2] + r.shifts[l, 1:2]).astype(BF16)
        shared = share_rows(r.normed_mlp, l)
        wait_load(r.w_fc, l)
        wait_load(r.fc_bias, l)
        wait_load(r.w_proj, l)
        if l == 0:
            forward_shard(1, 1)
            forward_shard(1, 0)
        arrive(shared)
        pre = dot_nn(r.normed_mlp[l], r.w_fc[l]) + r.fc_bias[l]
        activation, slope = gelu_and_slope(pre)
        activation = activation.astype(BF16)
        r.act[l] = activation
        r.slope[l] = slope
        if l == 0:
            finish = reduce_rows(dot_nn(activation, r.w_proj[l]))
            output = r.after[l] + finish() + r.out_biases[l, 1:2]
            r.xfull[1, own, :] = output.astype(BF16)
            base, places = alloc(S), alloc(S * T)
            last = r.xfull.at[1, pl.ds(R - MEM, MEM)]

            @pl.when(t == T - 1)
            def _():
                r.mem_rows[1, seg_rows, :] = r.xfull[1, R - MEM :, :]
                for i in range(S - 1, -1, -1):
                    for j in range(1 if i == 0 else 0, T):
                        copy = pltpu.make_async_remote_copy(
                            src_ref=last, dst_ref=r.mem_rows.at[1, seg_rows], send_sem=r.send.at[places + i * T + j],
                            recv_sem=r.recv.at[base + i], device_id=(c, to_seg[i], tpeers[j]), device_id_type=MESH,
                        )
                        copy.start()

            def wait_rows(i):
                wait_bytes(r.mem_rows.at[1, pl.ds(0, MEM)], r.recv.at[base + i])

            def wait_all():
                pl.when(t != T - 1)(functools.partial(wait_rows, 0))
                for i in range(1, S):
                    wait_rows(i)

            owed[4] = wait_all

            def drain():
                @pl.when(t == T - 1)
                def _():
                    for i in range(S):
                        for j in range(1 if i == 0 else 0, T):
                            wait_bytes(last, r.send.at[places + i * T + j])

            sent.append((drain, drain))

    fam_p, fam_c = (r.grad_p, r.pair_f, r.far_p, 0, r.relay_f), (r.grad_c, r.pair_f, r.far_c, 1, r.relay_f)
    fam_qk, fam_vo = (r.grad_qk, r.pair_a, r.far_qk, 0, r.relay_a), (r.grad_vo, r.pair_a, r.far_vo, 1, r.relay_a)
    fam_q = (r.grad_q, r.pair_q, r.far_q, None, r.relay_q)
    on_line = S == 4
    partner = s + 1 - 2 * lax.rem(s, 2)
    across = 2 - 2 * lax.div(s, 2)
    outer = jnp.logical_or(s == 0, s == 3)
    relays = {}

    def blocks_of(first_row, count):
        row, pieces = first_row, []
        while row < first_row + count:
            block, inside = row // z.cut, row % z.cut
            size = min(z.cut - inside, first_row + count - row)
            pieces.append((block, inside, row - first_row, size))
            row += size
        return pieces

    def weight_grad(l, family, *pairs):
        stripe = min(256, D)
        for k in range(0, D, stripe):
            parts = [dot_tn(left[:, k : k + stripe], right).astype(BF16) for left, right in pairs]
            grad = parts[0] if len(parts) == 1 else jnp.concatenate(parts, axis=1)
            for block, inside, row, size in blocks_of(k, stripe):
                family[0][l, block, inside : inside + size, :] = grad[row : row + size]

    def pair_send(src, dst):
        index = alloc(1)
        return remote(src, dst, index, (other, s, t))

    def adder_of(l, family):
        return l if family[3] is None else family[3]

    def hand_over(l, family):
        grad, pair, _, _, _ = family
        adder = adder_of(l, family)
        copy = pair_send(grad.at[l], pair.at[l])
        pl.when(c != adder)(copy.start)
        sent.append((copy, c != adder))
        return owe_owner(adder, [copy])

    def owe_owner(l, copies):
        def wait():
            @pl.when(c == l)
            def _():
                for copy in copies:
                    copy.wait_recv()

        owed[id(copies)] = wait
        return id(copies)

    def add_pair(l, family, key):
        grad, pair, _, _, _ = family
        arrive(key)

        @pl.when(c == adder_of(l, family))
        def _():
            @pl.loop(0, S)
            def _(j):
                grad[l, j] = (grad[l, j].astype(F32) + pair[l, j].astype(F32)).astype(BF16)

    def spread(l, family, direct):
        grad, _, far, _, relay = family
        adder = adder_of(l, family)
        near = adder == l
        direct = direct or not on_line
        base = alloc(S if direct else 5)
        steps = range(1, S) if direct else (1, 2)

        @pl.when(c == adder)
        def _():
            if direct:
                for i in range(S - 1, 0, -1):
                    remote(grad.at[l, to_seg[i]], far.at[i], base + i, (l, to_seg[i], t)).start()
            else:

                @pl.when(outer)
                def _():
                    for k in range(2):
                        remote(grad.at[l, across + k], relay.at[l, k], base + 3 + k, (c, partner, t)).start()

                remote(grad.at[l, partner], far.at[1], base + 1, (l, partner, t)).start()
            if near:
                far[0] = grad[l, s]
            else:
                remote(grad.at[l, s], far.at[0], base, (other, s, t)).start()

        if not direct:

            @pl.when(c == l)
            def _():
                for i in range(3, S):
                    far[i] = jnp.zeros(far.shape[1:], BF16)

            def pass_on():
                @pl.when(jnp.logical_and(c == adder, jnp.logical_not(outer)))
                def _():
                    for k in range(2):
                        wait_bytes(relay.at[l, k], r.recv.at[base + 3 + k])
                        place = across + k
                        grad[l, place] = (grad[l, place].astype(F32) + relay[l, k].astype(F32)).astype(BF16)
                        remote(grad.at[l, place], far.at[2], base + 3 + k, (l, place, t), r.recv.at[base + 2]).start()

            relays[id(far), l] = pass_on

        def wait():
            @pl.when(c == l)
            def _():
                for i in steps if near else (0, *steps):
                    wait_bytes(far.at[i], r.recv.at[base + i])

        def drain():
            @pl.when(c == adder)
            def _():
                ends = tuple(steps) if direct else (1, 3, 4)
                for i in ends if near else (0, *ends):
                    wait_bytes(far.at[0], r.send.at[base + i])

        owed[id(far), l] = wait
        sent.append((drain, drain))

    def pass_on(l, family):
        if (id(family[2]), l) in relays:
            relays.pop((id(family[2]), l))()

    def owe_small(l):
        copy = pair_send(r.small.at[l], r.pair_small)
        pl.when(c != l)(copy.start)
        sent.append((copy, c != l))
        return owe_owner(l, [copy])

    def owner_copies(l, copies):
        @pl.when(c == l)
        def _():
            for copy in copies:
                copy.start()

        sent.extend((copy, c == l) for copy in copies)
        return owe_owner(l, copies)

    def small_parts(l, key):
        arrive(key)

        @pl.when(c == l)
        def _():
            r.sum_small[...] = r.small[l] + r.pair_small[...]
            r.part_small[0] = r.sum_small[0:8, :]

        base = alloc(T - 1)
        return owner_copies(
            l, [remote(r.part_small.at[0], r.part_small.at[i], base + i - 1, (c, s, tpeers[i])) for i in range(1, T)]
        )

    def small_segs(l, key):
        arrive(key)

        @pl.when(c == l)
        def _():
            total = r.part_small[0]
            for i in range(1, T):
                total = total + r.part_small[i]
            r.sum_small[0:8, :] = total
            r.seg_small[0] = r.sum_small[...].astype(BF16)

        base = alloc(S - 1)
        return owner_copies(
            l, [remote(r.seg_small.at[0], r.seg_small.at[i], base + i - 1, (c, to_seg[i], t)) for i in range(1, S)]
        )

    def backward(l):
        if l == 1:
            arrive(1)
        grad_low = r.gfull[l]
        pre_grad = (r.slope[l] * dot_nt(grad_low, r.w_proj[l])).astype(BF16)
        r.dpre[...] = pre_grad
        finish = reduce_rows(dot_nt(pre_grad, r.w_fc[l]))
        own_grad = r.gfull[l, own, :].astype(F32)

        weight_grad(l, fam_p, (r.gfull.at[l], r.act[l]))
        pair_p = hand_over(l, fam_p)
        weight_grad(l, fam_c, (r.normed_mlp.at[l], r.dpre[...]))
        pair_c = hand_over(l, fam_c)
        r.small[l, 8:9, :] = jnp.sum(r.dpre[...].astype(F32), axis=0, keepdims=True)
        if l == 0:
            pass_on(1, fam_c)
            pass_on(1, fam_qk)
        add_pair(l, fam_p, pair_p)
        spread(l, fam_p, False)
        after_part, gain_mlp, shift_mlp = norm_back(r.after[l], r.gains[l, 1:2], finish())
        after_grad = own_grad + after_part
        r.tmp[...] = after_grad
        r.low2[l, own, :] = after_grad.astype(BF16)
        shared = share_rows(r.low2, l)
        r.small[l, 1:2, :] = gain_mlp
        r.small[l, 3:4, :] = shift_mlp
        r.small[l, 4:5, :] = jnp.sum(after_grad, axis=0, keepdims=True)
        r.small[l, 5:6, :] = jnp.sum(own_grad, axis=0, keepdims=True)
        add_pair(l, fam_c, pair_c)
        spread(l, fam_c, False)
        if l == 0:
            pass_on(1, fam_vo)
            pass_on(1, fam_q)
        arrive(shared)
        if l == 0:
            forward_shard(0, 0)
            forward_shard(0, 1)
        after_low = r.low2[l]
        mixed_grad = dot_nt(after_low, r.w_out[l]).astype(BF16)
        queries, key_heads, values = r.qkv[l, 0], r.qkv[l, 1], r.qkv[l, 2]
        q_grad = k_grad = v_grad = jnp.zeros((R, z.heads_w), F32)
        for h in range(z.heads):
            probs = r.probs[l, h]
            mixed_here = mixed_grad * head_rows[h]
            probs_grad = dot_nt(mixed_here, values)
            delta = jnp.sum(probs_grad * probs, axis=1, keepdims=True)
            score_grad = (probs * (probs_grad - delta)).astype(BF16)
            q_grad = q_grad + dot_nn(score_grad, key_heads * head_rows[h])
            k_grad = k_grad + dot_tn(score_grad, queries * head_rows[h])
            v_grad = v_grad + dot_tn(probs.astype(BF16), mixed_here)
        scale = HEAD_DIM ** (-0.5)
        r.dqkv[0] = (q_grad * scale).astype(BF16)
        r.dqkv[1] = (k_grad * scale).astype(BF16)
        r.dqkv[2] = v_grad.astype(BF16)
        r.dqk[...] = jnp.concatenate([r.dqkv[0], r.dqkv[1]], axis=1)
        finish = reduce_rows(sum(dot_nn(r.dqkv[i], r.w_attn[l, i]) for i in range(3)))

        weight_grad(l, fam_qk, (r.normed.at[l], r.dqk[...]))
        pair_qk = hand_over(l, fam_qk)
        weight_grad(l, fam_vo, (r.normed.at[l], r.dqkv[2]), (r.low2.at[l], r.mixed[l]))
        pair_vo = hand_over(l, fam_vo)
        for row, i in ((9, 0), (10, 2)):
            r.small[l, row : row + 1, : z.heads_w] = jnp.sum(r.dqkv[i].astype(F32), axis=0, keepdims=True)
        pass_on(l, fam_p)
        hidden_part, gain_attn, shift_attn = norm_back(r.hidden[l], r.gains[l, 0:1], finish())
        hidden_grad = r.tmp[...] + hidden_part
        r.tmp[...] = hidden_grad
        r.small[l, 0:1, :] = gain_attn
        r.small[l, 2:3, :] = shift_attn
        small_key = owe_small(l)
        query_den = 1.0 + jnp.sum(r.qdots[l], axis=1, keepdims=True)
        high, low = split(hidden_grad / query_den)
        den_grad = -jnp.sum((hidden_grad / query_den) * r.recall[l], axis=1, keepdims=True)
        highs = [high[:, u * z.val_w : (u + 1) * z.val_w] for u in range(T)]
        lows = [low[:, u * z.val_w : (u + 1) * z.val_w] for u in range(T)]
        dots_high, dots_low = split(r.qdots[l])
        for u in range(T):
            grad = dot_tn(dots_high, highs[u]) + dot_tn(dots_high, lows[u]) + dot_tn(dots_low, highs[u])
            r.x1_src[l, u] = grad.astype(BF16)
        value_step = to_parts(lambda peer: r.x1_src.at[l, peer], lambda i: r.x1_dst.at[l, i - 1])
        dots_grad = sum(dot_nt(highs[u], r.uall[l, u]) + dot_nt(lows[u], r.uall[l, u]) for u in range(T)) + den_grad
        dots_grad = (dots_grad * row_mask).astype(BF16)
        key_direct = feature_map_back(r.keyb[l].astype(F32), dot_tn(dots_grad, r.phiq[l]))
        for u in range(T):
            r.x2_src[l, u] = key_direct[:, u * z.keys_w : (u + 1) * z.keys_w].astype(BF16)
        key_step = to_parts(lambda peer: r.x2_src.at[l, peer], lambda i: r.x2_dst.at[l, i - 1])
        if l == 1:
            row_step = share_rows(r.xfull, 1)
        add_pair(l, fam_qk, pair_qk)
        add_pair(l, fam_vo, pair_vo)
        arrive(value_step)
        value_part = plus(r.x1_src[l, t], r.x1_dst.at[l], T - 1)
        r.x1_mid[l] = value_part.astype(BF16)
        value_step = to_segs(lambda _: r.x1_mid.at[l], lambda i: r.x1_far.at[l, i - 1])
        arrive(key_step)
        key_part = plus(r.x2_src[l, t], r.x2_dst.at[l], T - 1)
        r.x2_mid[l] = key_part.astype(BF16)
        key_step = to_segs(lambda _: r.x2_mid.at[l], lambda i: r.x2_far.at[l, i - 1])
        for family in (fam_qk, fam_vo):
            spread(l, family, False)
        query_grad = feature_map_back(r.qmem[l].astype(F32), dot_nn(dots_grad, r.phik[l])).astype(BF16)
        for u in range(T):
            r.dq_src[l, u] = query_grad[:, u * z.keys_w : (u + 1) * z.keys_w]
        r.dq_all[l, own, :] = r.dq_src[l, t]
        query_step = to_parts(lambda peer: r.dq_src.at[l, peer], lambda i: r.dq_all.at[l, own])
        if l == 0:
            arrive((12, 0, 0))
            arrive((12, 0, 1))
        r.tmp[...] += dot_nn(query_grad, r.w_keys[l, 0])
        target = r.gfull.at[0] if l == 1 else r.final
        first = pl.ds(pl.multiple_of(t * C, 16), C - MEM)
        rest = pl.ds(pl.multiple_of(t * C + C - MEM, 16), MEM)
        target[first, :] = r.tmp[: C - MEM, :].astype(BF16)
        first_step = to_parts(lambda _: target.at[first], lambda i: target.at[first])
        if l == 1:
            spread_shard(0, 0)
        if l == 1:
            pass_on(l, fam_c)
        arrive(value_step)
        direct = plus(value_part, r.x1_far.at[l], S - 1)
        arrive(key_step)
        small_key = small_parts(l, small_key)
        key_dots = r.kdots[l]
        key_den = 1.0 + jnp.sum(key_dots, axis=1, keepdims=True)
        r.vgrad[...] = direct
        for k in range(S - 1, 0, -1):
            rows = slice(k * MEM, (k + 1) * MEM)
            back = -r.vgrad[rows, :] / key_den[rows]
            r.vgrad[...] += dot_tn(key_dots[rows].astype(BF16), back.astype(BF16))
        value_grad = r.vgrad[...]
        read = r.vpart[l] - r.upart[l]
        back = (-value_grad / key_den).astype(BF16)
        key_den_grad = -jnp.sum(back.astype(F32) * read, axis=1, keepdims=True)
        key_dots_grad = (dot_nt(back, r.upart[l].astype(BF16)) + key_den_grad) * key_mask
        both = (key_dots_grad + key_dots_grad.T).astype(BF16)
        key_solve = feature_map_back(r.keyb[l].astype(F32), dot_nn(both, r.phik[l]))
        r.ksolve[...] = key_solve
        r.dv[...] = value_grad.astype(BF16)
        r.dk_direct[...] = plus(key_part, r.x2_far.at[l], S - 1)
        tail = dot_nn(r.dv[seg_rows, :], r.w_value[l])
        tail = tail + dot_nn(r.dk_direct[seg_rows, :].astype(BF16), r.w_keys[l, 1, shard_rows(t), :])
        tail = tail + dot_nn(r.ksolve[seg_rows, :].astype(BF16), r.w_keys[l, 1])
        r.x3_src[l] = tail.astype(BF16)
        base, place = alloc(T - 1), alloc(1)

        for i in range(1, T):

            @pl.when(tpeers[i] == T - 1)
            def _():
                copy = pltpu.make_async_remote_copy(
                    src_ref=r.x3_src.at[l], dst_ref=r.x3_dst.at[l, i - 1], send_sem=r.send.at[place],
                    recv_sem=r.recv.at[base + i - 1], device_id=(c, s, tpeers[i]), device_id_type=MESH,
                )
                copy.start()

        def drain():
            @pl.when(t != T - 1)
            def _():
                wait_bytes(r.x3_src.at[l], r.send.at[place])

        sent.append((drain, drain))
        for u in range(T):
            r.x4_src[l, u] = key_solve[:, u * z.keys_w : (u + 1) * z.keys_w].astype(BF16)
        solve_step = to_parts(lambda peer: r.x4_src.at[l, peer], lambda i: r.x4_dst.at[l, i - 1])

        @pl.when(t == T - 1)
        def _():
            total = r.x3_src[l].astype(F32)
            for i in range(T - 1):
                wait_bytes(r.x3_dst.at[l, i], r.recv.at[base + i])
                total = total + r.x3_dst[l, i].astype(F32)
            r.tmp[C - MEM :, :] += total

        target[rest, :] = r.tmp[C - MEM :, :].astype(BF16)
        rest_step = to_parts(lambda _: target.at[rest], lambda i: target.at[rest])
        small_key = small_segs(l, small_key)
        if l == 1:
            spread_shard(0, 1)
        arrive(query_step)
        if l == 1:
            arrive(row_step)
        weight_grad(l, fam_q, (r.xfull.at[l], r.dq_all[l]))
        pair_q = hand_over(l, fam_q)
        r.mem_v[l] = dot_tn(r.mem_rows[l], r.dv[...])
        arrive(solve_step)
        key_grad = plus(r.dk_direct[...] + r.x4_src[l, t].astype(F32), r.x4_dst.at[l], T - 1)
        r.mem_k[l] = dot_tn(r.mem_rows[l], key_grad.astype(BF16))
        rows = pl.ds(pl.multiple_of(s * z.cut, 8), z.cut)
        mem_copies = [pair_send(r.mem_k.at[l, rows], r.pair_k), pair_send(r.mem_v.at[l, rows], r.pair_v)]

        @pl.when(c != l)
        def _():
            for copy in mem_copies:
                copy.start()

        sent.extend((copy, c != l) for copy in mem_copies)
        mem_key = owe_owner(l, mem_copies)
        add_pair(l, fam_q, pair_q)
        spread(l, fam_q, False)
        if l == 0:
            pass_on(l, fam_c)
            pass_on(l, fam_qk)
            pass_on(l, fam_vo)
            pass_on(l, fam_q)
        arrive(first_step)
        arrive(rest_step)
        return mem_key, small_key

    forward(0)
    forward(1)
    for l in range(LAYERS):
        r.small[l] = jnp.zeros((16, D), F32)
    mem_key1, small_key1 = backward(1)
    mem_key0, small_key0 = backward(0)

    r.input_grad[0] = r.final[...]
    l = c

    arrive(mem_key1)
    arrive(mem_key0)
    rows = pl.ds(pl.multiple_of(s * z.cut, 8), z.cut)
    r.mkey_grads[0, 1] = r.mem_k[l, rows, :] + r.pair_k[...]
    r.mvalue_grads[0] = r.mem_v[l, rows, :] + r.pair_v[...]

    def far_sum(far):
        arrive((id(far), 1))
        arrive((id(far), 0))
        return sum(far[i, : z.cut, :].astype(F32) for i in range(S))

    r.proj_grads[0] = far_sum(r.far_p)
    r.fc_grads[0] = far_sum(r.far_c)
    both = far_sum(r.far_qk)
    r.attn_grads[0, 0] = both[:, : z.heads_w]
    r.attn_grads[0, 1] = both[:, z.heads_w :]
    both = far_sum(r.far_vo)
    r.attn_grads[0, 2] = both[:, : z.heads_w]
    r.out_grads[0] = both[:, z.heads_w :].T
    r.mkey_grads[0, 0] = far_sum(r.far_q)
    arrive(small_key1)
    arrive(small_key0)
    total = r.sum_small[...]
    for i in range(1, S):
        total = total + r.seg_small[i].astype(F32)
    r.gain_grads[0] = total[0:2]
    r.shift_grads[0] = total[2:4]
    r.obias_grads[0] = total[4:6]
    r.fcb_grads[...] = total[8:9, : z.units]
    r.abias_grads[0] = total[9:11, : z.heads_w]

    assert not owed and not relays
    for copy, when in sent:
        if when is copy:
            copy()
        elif when is None:
            copy.wait_send()
        else:
            pl.when(when)(copy.wait_send)


def hand_out(*refs):
    count = len(refs) // 2
    for source, target in zip(refs[:count], refs[count:]):
        target[...] = source[...]


def item_ids(lengths):
    item_ends = jnp.cumsum(lengths, axis=-1)
    item_begins = item_ends - lengths
    places = jnp.arange(lengths.shape[-1], dtype=jnp.int32)
    matches = (item_begins[:, :, None] == places[None, None, :]) & (lengths[:, :, None] > 0)
    return jnp.cumsum(jnp.sum(matches.astype(jnp.int32), axis=1), axis=-1)


def reach_mask(lengths):
    ids = item_ids(lengths)
    places = jnp.arange(lengths.shape[-1])
    earlier = places[:, None] > places[None, :]
    same = (ids[:, :, None] == ids[:, None, :]) & earlier[None]
    return jnp.repeat(jnp.repeat(same.astype(F32), MEM, axis=1), MEM, axis=2)


def gather_rows(values, axis):
    return lax.all_gather(values, axis, axis=0, tiled=True)


def scatter_rows(values, axis):
    peers = lax.axis_size(axis)
    pieces = values.astype(BF16).reshape(peers, values.shape[0] // peers, values.shape[1])
    got = lax.all_to_all(pieces, axis, 0, 0, tiled=True)
    return jnp.sum(got.astype(F32), axis=0)


def scatter_columns(values, axis):
    peers = lax.axis_size(axis)
    rows = values.shape[0]
    pieces = values.reshape(rows, peers, -1).transpose(1, 0, 2)
    got = lax.all_to_all(pieces.astype(BF16), axis, 0, 0, tiled=True)
    return jnp.sum(got.astype(F32), axis=0)


def solve_forward(key_dots, key_den, value_mem):
    segments = key_dots.shape[0] // MEM
    solved = value_mem
    for s in range(1, segments):
        rows = slice(s * MEM, (s + 1) * MEM)
        read = dot_nn(key_dots[rows].astype(BF16), solved.astype(BF16)) / key_den[rows]
        solved = solved.at[rows].add(-read)
    return solved


def solve_backward(key_dots, key_den, direct):
    segments = key_dots.shape[0] // MEM
    total = direct
    for s in range(segments - 1, 0, -1):
        rows = slice(s * MEM, (s + 1) * MEM)
        back = -total[rows] / key_den[rows]
        total = total + dot_tn(key_dots[rows].astype(BF16), back.astype(BF16))
    return total


def layer_forward(own_rows, mem_rows, mask, place, params):
    gains, shifts, w_attn, attn_bias, w_out, out_biases, w_fc, fc_bias, w_proj, w_q, w_k, w_v = params
    seg, _ = place
    own_mask = lax.dynamic_slice_in_dim(mask, seg * MEM, 1, 0)
    key_mem = dot_nn(mem_rows, w_k).astype(BF16)
    phi_key = feature_map(key_mem.astype(F32), jnp.roll).astype(BF16)
    key_dots = dot_nt(phi_key, phi_key) * mask
    key_den = 1.0 + jnp.sum(key_dots, axis=1, keepdims=True)
    value_part = dot_nn(mem_rows, w_v)
    solved_part = solve_forward(key_dots, key_den, value_part)
    solved = lax.all_gather(solved_part.astype(BF16), "tensor", axis=1, tiled=True)
    query_mem = dot_nn(own_rows, w_q).astype(BF16)
    phi_query = feature_map(query_mem.astype(F32), jnp.roll).astype(BF16)
    query_dots = dot_nt(phi_query, phi_key) * own_mask
    query_den = 1.0 + jnp.sum(query_dots, axis=1, keepdims=True)
    recall = dot_nn(query_dots.astype(BF16), solved) / query_den
    hidden = own_rows.astype(F32) + recall.astype(BF16).astype(F32)
    unit, _ = norm_rows(hidden)
    normed = gather_rows((unit * gains[0] + shifts[0]).astype(BF16), "tensor")
    queries = (dot_nn(normed, w_attn[0]) + attn_bias[0]).astype(BF16)
    key_heads = dot_nn(normed, w_attn[1]).astype(BF16)
    values = (dot_nn(normed, w_attn[2]) + attn_bias[1]).astype(BF16)
    rows = normed.shape[0]
    causal = jnp.arange(rows)[:, None] >= jnp.arange(rows)[None, :]
    probs, mixed = [], []
    for h in range(queries.shape[1] // HEAD_DIM):
        cols = slice(h * HEAD_DIM, (h + 1) * HEAD_DIM)
        scores = dot_nt(queries[:, cols], key_heads[:, cols]) * HEAD_DIM ** (-0.5)
        scores = jnp.where(causal, scores, -jnp.inf)
        heights = jnp.exp(scores - jnp.max(scores, axis=1, keepdims=True))
        probs.append(heights / jnp.sum(heights, axis=1, keepdims=True))
        mixed.append(dot_nn(probs[-1].astype(BF16), values[:, cols]).astype(BF16))
    mixed = jnp.concatenate(mixed, axis=1)
    after = hidden + scatter_rows(dot_nn(mixed, w_out), "tensor") + out_biases[0]
    unit, _ = norm_rows(after)
    normed_mlp = gather_rows((unit * gains[1] + shifts[1]).astype(BF16), "tensor")
    pre = dot_nn(normed_mlp, w_fc) + fc_bias
    activation, slope = gelu_and_slope(pre)
    activation = activation.astype(BF16)
    output = after + scatter_rows(dot_nn(activation, w_proj), "tensor") + out_biases[1]
    kept = (
        own_rows, mem_rows, key_mem, phi_key, key_dots, key_den, value_part, solved_part, solved, query_mem,
        phi_query, query_dots, query_den, recall, hidden, normed, queries, key_heads, values, probs, mixed,
        after, normed_mlp, slope, activation,
    )
    return output, kept


def layer_backward(own_grad, kept, mask, place, params):
    gains, shifts, w_attn, attn_bias, w_out, out_biases, w_fc, fc_bias, w_proj, w_q, w_k, w_v = params
    (
        own_rows, mem_rows, key_mem, phi_key, key_dots, key_den, value_part, solved_part, solved, query_mem,
        phi_query, query_dots, query_den, recall, hidden, normed, queries, key_heads, values, probs, mixed,
        after, normed_mlp, slope, activation,
    ) = kept
    seg, part = place
    own_mask = lax.dynamic_slice_in_dim(mask, seg * MEM, 1, 0)
    grad_low = gather_rows(own_grad.astype(BF16), "tensor")
    pre_grad = (slope * dot_nt(grad_low, w_proj)).astype(BF16)
    proj_grad = dot_tn(activation, grad_low)
    fc_bias_grad = jnp.sum(pre_grad.astype(F32), axis=0)
    fc_grad = dot_tn(normed_mlp, pre_grad)
    after_part, gain_mlp, shift_mlp = norm_back(
        after, gains[1:2], scatter_rows(dot_nt(pre_grad, w_fc), "tensor")
    )
    after_grad = own_grad + after_part
    after_low = gather_rows(after_grad.astype(BF16), "tensor")
    out_grad = dot_tn(mixed, after_low)
    mixed_grad = dot_nt(after_low, w_out).astype(BF16)
    q_grads, k_grads, v_grads = [], [], []
    for h in range(queries.shape[1] // HEAD_DIM):
        cols = slice(h * HEAD_DIM, (h + 1) * HEAD_DIM)
        probs_grad = dot_nt(mixed_grad[:, cols], values[:, cols])
        delta = jnp.sum(probs_grad * probs[h], axis=1, keepdims=True)
        score_grad = (probs[h] * (probs_grad - delta)).astype(BF16)
        q_grads.append((dot_nn(score_grad, key_heads[:, cols]) * HEAD_DIM ** (-0.5)).astype(BF16))
        k_grads.append((dot_tn(score_grad, queries[:, cols]) * HEAD_DIM ** (-0.5)).astype(BF16))
        v_grads.append(dot_tn(probs[h].astype(BF16), mixed_grad[:, cols]).astype(BF16))
    three = [jnp.concatenate(g, axis=1) for g in (q_grads, k_grads, v_grads)]
    attn_bias_grad = jnp.stack([jnp.sum(three[i].astype(F32), axis=0) for i in (0, 2)])
    attn_grad = jnp.stack([dot_tn(normed, g) for g in three])
    normed_part = sum(dot_nt(g, w_attn[i]) for i, g in enumerate(three))
    hidden_part, gain_attn, shift_attn = norm_back(
        hidden, gains[0:1], scatter_rows(normed_part, "tensor")
    )
    hidden_grad = after_grad + hidden_part
    num_grad = (hidden_grad / query_den).astype(BF16)
    den_grad = -jnp.sum(hidden_grad * recall, axis=1, keepdims=True) / query_den
    dots_grad = ((dot_nt(num_grad, solved) + den_grad) * own_mask).astype(BF16)
    query_grad = feature_map_back(query_mem.astype(F32), dot_nn(dots_grad, phi_key), jnp.roll).astype(BF16)
    solved_direct = dot_tn(query_dots.astype(BF16), num_grad)
    key_direct = feature_map_back(key_mem.astype(F32), dot_tn(dots_grad, phi_query), jnp.roll)
    solved_direct = scatter_columns(solved_direct, "tensor")
    solved_direct = jnp.sum(lax.all_gather(solved_direct.astype(BF16), "seg").astype(F32), axis=0)
    value_grad = solve_backward(key_dots, key_den, solved_direct)
    read = value_part - solved_part
    key_den_grad = jnp.sum(value_grad * read, axis=1, keepdims=True) / key_den
    back = (-value_grad / key_den).astype(BF16)
    key_dots_grad = (dot_nt(back, solved_part.astype(BF16)) + key_den_grad) * mask
    both = (key_dots_grad + key_dots_grad.T).astype(BF16)
    key_solve = feature_map_back(key_mem.astype(F32), dot_nn(both, phi_key), jnp.roll)
    mine = (jnp.arange(key_solve.shape[0]) // MEM == seg)[:, None]
    key_direct = key_direct + jnp.where(mine, key_solve, 0.0)
    key_direct = scatter_columns(key_direct, "tensor")
    key_grad = jnp.sum(lax.all_gather(key_direct.astype(BF16), "seg").astype(F32), axis=0).astype(BF16)
    value_low = value_grad.astype(BF16)
    mem_width = mem_rows.shape[1] // lax.axis_size("seg")
    mem_cols = lax.dynamic_slice_in_dim(mem_rows, seg * mem_width, mem_width, 1)
    mem_key_grad = dot_tn(mem_cols, key_grad)
    mem_value_grad = dot_tn(mem_cols, value_low)
    return (
        hidden_grad, query_grad, key_grad, value_low,
        (gain_attn, gain_mlp, shift_attn, shift_mlp, jnp.sum(after_grad, axis=0, keepdims=True), jnp.sum(own_grad, axis=0, keepdims=True)),
        (attn_grad, attn_bias_grad, out_grad, fc_grad, fc_bias_grad, proj_grad, mem_key_grad, mem_value_grad),
    )


def general_device(
    inputs, out_grad, item_lengths, norm_gains, norm_biases, w_attn, attn_bias, w_out, out_biases, w_fc, fc_bias,
    w_proj, w_mem_keys, w_mem_value,
):
    section, seg, part = (lax.axis_index(name) for name in ("section", "seg", "tensor"))
    segments, parts = lax.axis_size("seg"), lax.axis_size("tensor")
    layers = lax.axis_size("section")
    mask = reach_mask(item_lengths)[section]
    weights = (norm_gains, norm_biases, w_attn, attn_bias, w_out, out_biases, w_fc, fc_bias, w_proj, w_mem_keys, w_mem_value)
    weights = [lax.all_gather(w, "section", axis=0, tiled=True) for w in weights]
    full_keys = lax.all_gather(weights[9], "tensor", axis=3, tiled=True)
    rows_all, grad_all = inputs[section], out_grad[section]
    chunk = rows_all.shape[0] // parts
    own_rows = lax.dynamic_slice_in_dim(rows_all, part * chunk, chunk, 0)
    place = (seg, part)
    saved, layer_params = [], []
    for layer in range(layers):
        mems = lax.all_gather(own_rows[-MEM:], ("seg", "tensor"), axis=0)
        mem_rows = mems[parts - 1 :: parts].reshape(segments * MEM, -1)
        params = tuple(w[layer] for w in weights[:9]) + (full_keys[layer, 0], full_keys[layer, 1], weights[10][layer])
        output, kept = layer_forward(own_rows, mem_rows, mask, place, params)
        saved.append(kept)
        layer_params.append(params)
        own_rows = output.astype(BF16)
    own_grad = lax.dynamic_slice_in_dim(grad_all, part * chunk, chunk, 0).astype(F32)
    rows_grads, matrix_grads = [None] * layers, [None] * layers
    for layer in reversed(range(layers)):
        params, kept = layer_params[layer], saved[layer]
        hidden_grad, query_grad, key_grad, value_low, rows_grads[layer], grads = layer_backward(own_grad, kept, mask, place, params)
        w_q = params[9]
        keys_here = lax.dynamic_slice_in_dim(key_grad, seg * MEM, MEM, 0)
        values_here = lax.dynamic_slice_in_dim(value_low, seg * MEM, MEM, 0)
        tail = dot_nt(keys_here, weights[9][layer, 1]) + dot_nt(values_here, params[11])
        tail = jnp.sum(lax.all_gather(tail.astype(BF16), "tensor").astype(F32), axis=0)
        tail = jnp.concatenate([jnp.zeros((chunk - MEM, tail.shape[1]), F32), tail], axis=0)
        rows_grad = hidden_grad + dot_nt(query_grad, w_q) + jnp.where(part == parts - 1, tail, 0.0)
        own_grad = rows_grad.astype(BF16).astype(F32)
        rows_full = gather_rows(kept[0], "tensor")
        query_cols = lax.all_to_all(query_grad.reshape(chunk, parts, -1).transpose(1, 0, 2), "tensor", 0, 0, tiled=True)
        query_cols = query_cols.reshape(chunk * parts, -1)
        matrix_grads[layer] = grads + (dot_tn(rows_full, query_cols),)
    input_grad = gather_rows(own_grad.astype(BF16), "tensor")[None]

    def over_layers(values):
        return lax.psum_scatter(jnp.stack(values), "section", scatter_dimension=0, tiled=True)

    rows_sums = lax.psum(over_layers([jnp.concatenate(r, axis=0) for r in rows_grads]), ("seg", "tensor"))

    def spread(index, axis):
        stacked = jnp.stack([g[index] for g in matrix_grads]).astype(BF16)
        pair = lax.all_to_all(stacked, "section", 0, 0, tiled=True)
        both = jnp.sum(pair.astype(F32), axis=0)
        cut = both.astype(BF16).reshape(both.shape[:axis] + (segments, -1) + both.shape[axis + 1 :])
        got = lax.all_to_all(cut, "seg", axis, axis, tiled=True)
        return jnp.sum(got.astype(F32), axis=axis)[None]

    biases = lax.psum(
        (over_layers([g[1] for g in matrix_grads]), over_layers([g[4] for g in matrix_grads])), "seg"
    )
    query_w = spread(8, 0)
    key_w = over_layers([g[6] for g in matrix_grads])
    return (
        input_grad,
        rows_sums[:, 0:2],
        rows_sums[:, 2:4],
        spread(0, 1),
        biases[0],
        spread(2, 1),
        rows_sums[:, 4:6],
        spread(3, 0),
        biases[1],
        spread(5, 1),
        jnp.stack([query_w, key_w], axis=1),
        over_layers([g[7] for g in matrix_grads]),
    )


def solution(mesh):
    def per_device(*args):
        inputs, out_grad, item_lengths = args[:3]
        S, T = mesh.shape["seg"], mesh.shape["tensor"]
        w_attn, w_fc, w_keys = args[5], args[9], args[12]
        z = Sizes(
            mesh,
            (
                (0, inputs.shape[1] * S, inputs.shape[2]), (0, 0, 0, w_attn.shape[3] * T), (0, 0, w_fc.shape[2] * T),
                (0, 0, 0, w_keys.shape[3] * T),
            ),
        )
        scratch = scratch_of(z)
        D = z.width
        outs = dict(
            input_grad=((1, z.rows, D), BF16), gain_grads=((1, 2, D), F32), shift_grads=((1, 2, D), F32),
            attn_grads=((1, 3, z.cut, z.heads_w), F32), abias_grads=((1, 2, z.heads_w), F32),
            out_grads=((1, z.heads_w, z.cut), F32), obias_grads=((1, 2, D), F32), fc_grads=((1, z.cut, z.units), F32),
            fcb_grads=((1, z.units), F32), proj_grads=((1, z.cut, z.units), F32),
            mkey_grads=((1, 2, z.cut, z.keys_w), F32), mvalue_grads=((1, z.cut, z.val_w), F32),
        )
        names = tuple(scratch)
        vmem, anywhere = pl.BlockSpec(memory_space=pltpu.VMEM), pl.BlockSpec(memory_space=pl.ANY)
        shapes = [jax.ShapeDtypeStruct(*shape) for shape in outs.values()]
        flip = lambda w: jnp.swapaxes(w, -1, -2)
        results = pl.pallas_call(
            functools.partial(kernel, z, names),
            out_shape=shapes,
            in_specs=[anywhere, anywhere, pl.BlockSpec(memory_space=pltpu.SMEM)] + [anywhere] * 11,
            out_specs=[vmem] * len(outs),
            scratch_shapes=list(scratch.values()),
            compiler_params=pltpu.CompilerParams(
                collective_id=0, has_side_effects=True, vmem_limit_bytes=63 * 2**20
            ),
            name="two_layers",
        )(*args[:5], flip(w_attn), *args[6:12], flip(w_keys), flip(args[13]))
        results = list(pl.pallas_call(
            hand_out, out_shape=shapes, in_specs=[vmem] * len(outs), out_specs=[vmem] * len(outs), name="hand_out"
        )(*results))
        results[9] = flip(results[9])
        return tuple(results)

    return jax.shard_map(
        per_device if mesh.shape["seg"] * MEM <= 128 else general_device,
        mesh=mesh,
        in_specs=(
            P(None, "seg", None),
            P(None, "seg", None),
            P(),
            P("section", None, None),
            P("section", None, None),
            P("section", None, None, "tensor"),
            P("section", None, "tensor"),
            P("section", "tensor", None),
            P("section", None, None),
            P("section", None, "tensor"),
            P("section", "tensor"),
            P("section", "tensor", None),
            P("section", None, None, "tensor"),
            P("section", None, "tensor"),
        ),
        out_specs=(
            P("section", "seg", None),
            P("section", None, None),
            P("section", None, None),
            P("section", None, "seg", "tensor"),
            P("section", None, "tensor"),
            P("section", "tensor", "seg"),
            P("section", None, None),
            P("section", "seg", "tensor"),
            P("section", "tensor"),
            P("section", "tensor", "seg"),
            P("section", None, "seg", "tensor"),
            P("section", "seg", "tensor"),
        ),
        check_vma=False,
    )
```

```python
import functools
from types import SimpleNamespace
from typing import Any, NamedTuple

import jax
import jax.numpy as jnp
from jax import lax
from jax.experimental import pallas as pl
from jax.experimental.pallas import tpu as pltpu
from jax.sharding import PartitionSpec as P

HEAD_DIM = 64
NU = 3
MEM = 16
EPSILON = 1e-05
F32 = jnp.float32
BF16 = jnp.bfloat16
GELU_A = 0.7978845608028654
GELU_B = 0.044715
LAYERS = 2
MESH = pl.DeviceIdType.MESH


def dot_nn(left, right):
    return lax.dot_general(left, right, (((1,), (0,)), ((), ())), preferred_element_type=F32)


def dot_nt(left, right):
    return lax.dot_general(left, right, (((1,), (1,)), ((), ())), preferred_element_type=F32)


def dot_tn(left, right):
    return lax.dot_general(left, right, (((0,), (0,)), ((), ())), preferred_element_type=F32)


def doubled_softplus(projected):
    small = jnp.exp(-jnp.abs(projected))
    tail = jnp.where(small < 1e-3, small - 0.5 * small * small, jnp.log1p(small))
    return jnp.concatenate(
        [jnp.maximum(projected, 0.0) + tail, jnp.maximum(-projected, 0.0) + tail], axis=1
    )


def feature_map(projected, roll=pltpu.roll):
    doubled = doubled_softplus(projected)
    return jnp.concatenate([doubled * roll(doubled, j, 1) for j in range(1, NU + 1)], axis=1)


def feature_map_back(projected, phi_grad, roll=pltpu.roll):
    doubled = doubled_softplus(projected)
    width = doubled.shape[1]
    total = jnp.zeros_like(doubled)
    for j in range(1, NU + 1):
        part = phi_grad[:, (j - 1) * width : j * width]
        total = total + part * roll(doubled, j, 1) + roll(part * doubled, width - j, 1)
    half = width // 2
    gate = 1.0 / (1.0 + jnp.exp(-projected))
    return total[:, :half] * gate - total[:, half:] * (1.0 - gate)


def norm_rows(hidden):
    centered = hidden - jnp.mean(hidden, axis=1, keepdims=True)
    scale = lax.rsqrt(jnp.mean(centered * centered, axis=1, keepdims=True) + EPSILON)
    return centered * scale, scale


def norm_back(hidden, gain_row, grad):
    unit, scale = norm_rows(hidden)
    unit_grad = grad * gain_row
    mean_grad = jnp.mean(unit_grad, axis=1, keepdims=True)
    mean_both = jnp.mean(unit_grad * unit, axis=1, keepdims=True)
    return (
        scale * (unit_grad - mean_grad - unit * mean_both),
        jnp.sum(grad * unit, axis=0, keepdims=True),
        jnp.sum(grad, axis=0, keepdims=True),
    )


def gelu_and_slope(pre):
    square = pre * pre
    bent = jnp.tanh(GELU_A * (pre + GELU_B * square * pre))
    value = 0.5 * pre * (1.0 + bent)
    slope = 0.5 * (1.0 + bent) + 0.5 * pre * (1.0 - bent * bent) * (
        GELU_A * (1.0 + 3.0 * GELU_B * square)
    )
    return value, slope


def xor_peer(place, other, count):
    total, bit = 0, 1
    while bit < count:
        mine = lax.rem(lax.div(place, bit), 2)
        total = total + bit * (1 - mine if other & bit else mine)
        bit *= 2
    return total


def split(values):
    high = values.astype(BF16)
    return high, (values - high.astype(F32)).astype(BF16)


def plus(first, others, count):
    total = first.astype(F32)
    for i in range(count):
        total = total + others[i].astype(F32)
    return total


class Sizes:
    def __init__(self, mesh, shapes):
        self.segs, self.parts = mesh.shape["seg"], mesh.shape["tensor"]
        inputs, w_attn, w_fc, w_keys = shapes
        self.rows, self.width = inputs[1] // self.segs, inputs[2]
        self.chunk = self.rows // self.parts
        self.mems = self.segs * MEM
        self.heads_w = w_attn[3] // self.parts
        self.heads = self.heads_w // HEAD_DIM
        self.units = w_fc[2] // self.parts
        self.keys = w_keys[3]
        self.keys_w = self.keys // self.parts
        self.phi = 2 * self.keys * NU
        self.val_w = self.width // self.parts
        self.cut = self.width // self.segs
        self.cut_pad = -(-self.cut // 16) * 16
        self.sems = 120 + 48 * self.parts + 2 * self.segs * (self.parts + 16)


def scratch_of(z):
    S, T, R, D, C, M = z.segs, z.parts, z.rows, z.width, z.chunk, z.mems
    bf = lambda *d: pltpu.VMEM(d, BF16)
    fl = lambda *d: pltpu.VMEM(d, F32)
    return dict(
        gains=fl(2, 2, D), shifts=fl(2, 2, D), w_attn=bf(2, 3, z.heads_w, D), attn_bias=fl(2, 2, z.heads_w),
        w_out=bf(2, z.heads_w, D), out_biases=fl(2, 2, D), w_fc=bf(2, D, z.units), fc_bias=fl(2, 1, z.units),
        w_proj=bf(2, z.units, D), w_keys=bf(2, 2, z.keys, D), w_value=bf(2, z.val_w, D),
        xfull=bf(2, R, D), gfull=bf(2, R, D), mem_rows=bf(2, M, D),
        keyb=bf(2, M, z.keys), phik=bf(2, M, z.phi), kdots=fl(2, M, M), vpart=fl(2, M, z.val_w),
        upart=fl(2, M, z.val_w), uall=bf(2, T, M, z.val_w), qmem=bf(2, C, z.keys), phiq=bf(2, C, z.phi),
        qdots=fl(2, C, M), recall=fl(2, C, D), hidden=fl(2, C, D), normed=bf(2, R, D), qkv=bf(2, 3, R, z.heads_w),
        probs=fl(2, z.heads, R, R), mixed=bf(2, R, z.heads_w), after=fl(2, C, D), normed_mlp=bf(2, R, D),
        slope=fl(2, R, z.units), act=bf(2, R, z.units), rs_src=bf(7, R, D), rs_own=fl(R, D), q_src=bf(R, z.keys_w), q_parts=bf(T, C, z.keys_w), k_parts=bf(T, M, z.keys_w), rs_dst=bf(7, T - 1, C, D),
        low2=bf(2, R, D), dpre=bf(R, z.units), dqkv=bf(3, R, z.heads_w),
        x1_src=bf(2, T, M - MEM, z.val_w), x1_dst=bf(2, T - 1, M - MEM, z.val_w), x1_mid=bf(2, M - MEM, z.val_w), x1_far=bf(2, max(S - 1, 1), M - MEM, z.val_w),
        x2_src=bf(2, T, M - MEM, z.keys_w), x2_dst=bf(2, T - 1, M - MEM, z.keys_w), x2_mid=bf(2, M - MEM, z.keys_w), x2_far=bf(2, max(S - 1, 1), M - MEM, z.keys_w), x4_src=bf(2, T, M, z.keys_w), x4_dst=bf(2, T - 1, M, z.keys_w), ksolve=fl(M, z.keys), dk_direct=fl(M, z.keys_w),
        dq_src=bf(2, T, C, z.keys_w), dq_all=bf(2, R, z.keys_w), dv=bf(M, z.val_w), vgrad=fl(M, z.val_w),
        x3_src=bf(2, MEM, D), x3_dst=bf(2, T - 1, MEM, D), final=bf(R, D), tmp=fl(C, D),
        grad_p=bf(2, S, z.cut_pad, z.units), grad_c=bf(2, S, z.cut_pad, z.units), grad_qk=bf(2, S, z.cut_pad, 2 * z.heads_w),
        grad_vo=bf(2, S, z.cut_pad, 2 * z.heads_w), grad_q=bf(2, S, z.cut_pad, z.keys_w),
        pair_f=bf(2, S, z.cut_pad, z.units), pair_a=bf(2, S, z.cut_pad, 2 * z.heads_w), pair_q=bf(2, S, z.cut_pad, z.keys_w), relay_f=bf(2, 2, z.cut_pad, z.units), relay_a=bf(2, 2, z.cut_pad, 2 * z.heads_w), relay_q=bf(2, 2, z.cut_pad, z.keys_w),
        far_p=bf(S, z.cut_pad, z.units), far_c=bf(S, z.cut_pad, z.units), far_qk=bf(S, z.cut_pad, 2 * z.heads_w),
        far_vo=bf(S, z.cut_pad, 2 * z.heads_w), far_q=bf(S, z.cut_pad, z.keys_w), dqk=bf(R, 2 * z.heads_w),
        mem_k=fl(2, D, z.keys_w), mem_v=fl(2, D, z.val_w), pair_k=fl(z.cut, z.keys_w), pair_v=fl(z.cut, z.val_w),
        small=fl(2, 16, D), pair_small=fl(16, D), part_small=fl(T, 8, D), sum_small=fl(16, D), seg_small=bf(S, 16, D),
        send=pltpu.SemaphoreType.DMA((z.sems,)), recv=pltpu.SemaphoreType.DMA((z.sems,)), load=pltpu.SemaphoreType.DMA((14, 2)),
        shard=pltpu.SemaphoreType.DMA((2, 2, T)),
    )


class Outer(NamedTuple):
    inputs: Any
    out_grad: Any
    item_lengths: Any
    norm_gains: Any
    norm_biases: Any
    w_attn_in: Any
    attn_bias_in: Any
    w_out_in: Any
    out_biases_in: Any
    w_fc_in: Any
    fc_bias_in: Any
    w_proj_in: Any
    w_keys_in: Any
    w_value_in: Any
    input_grad: Any
    gain_grads: Any
    shift_grads: Any
    attn_grads: Any
    abias_grads: Any
    out_grads: Any
    obias_grads: Any
    fc_grads: Any
    fcb_grads: Any
    proj_grads: Any
    mkey_grads: Any
    mvalue_grads: Any


def kernel(z, held_names, *refs):
    outer = len(Outer._fields)
    r = SimpleNamespace(**Outer(*refs[:outer])._asdict(), **dict(zip(held_names, refs[outer:])))
    S, T, R, D, C, M = z.segs, z.parts, z.rows, z.width, z.chunk, z.mems
    c, s, t = (lax.axis_index(a) for a in ("section", "seg", "tensor"))
    other = 1 - c
    tpeers = [xor_peer(t, i, T) for i in range(T)]
    to_seg = [lax.rem(s + i, S) for i in range(S)]
    own = pl.ds(pl.multiple_of(t * C, C), C)
    seg_rows = pl.ds(pl.multiple_of(s * MEM, MEM), MEM)
    used = [0]
    sent = []
    owed = {}

    def alloc(count):
        used[0] += count
        assert used[0] <= z.sems
        return used[0] - count

    def owe(copies):
        def wait():
            for copy in copies:
                copy.wait_recv()

        owed[id(copies)] = wait
        return id(copies)

    def wait_bytes(ref, semaphore):
        pltpu.make_async_copy(ref, ref, semaphore).wait()

    def remote(src, dst, index, device, recv=None):
        copy = pltpu.make_async_remote_copy(
            src_ref=src, dst_ref=dst, send_sem=r.send.at[index],
            recv_sem=r.recv.at[index] if recv is None else recv, device_id=device, device_id_type=MESH,
        )
        return copy

    def to_parts(src_of, dst):
        base = alloc(T - 1)
        copies = []
        for i in range(T - 1, 0, -1):
            copy = remote(src_of(tpeers[i]), dst(i), base + i - 1, (c, s, tpeers[i]))
            copy.start()
            copies.append(copy)
        sent.extend((copy, None) for copy in copies)
        return owe(copies)

    def to_segs(src_of, dst):
        base = alloc(S - 1)
        copies = [
            remote(src_of(to_seg[i]), dst(i), base + i - 1, (c, to_seg[i], t)) for i in range(1, S)
        ]
        for copy in copies:
            copy.start()
        sent.extend((copy, None) for copy in copies)
        return owe(copies)

    def arrive(key):
        owed.pop(key)()

    def wait_load(ref, layer):
        arrive((id(ref), layer))

    barrier = pltpu.get_barrier_semaphore()
    greeted = [(other, to_seg[i], t) for i in range(S)] + [(c, to_seg[i], tpeers[j]) for i in range(S) for j in range(T) if i or j]
    for device in greeted:
        pl.semaphore_signal(barrier, inc=1, device_id=device, device_id_type=MESH)

    loads = [
        (r.w_value, r.w_value_in.at[0]), (r.gains, r.norm_gains.at[0]), (r.shifts, r.norm_biases.at[0]),
        (r.attn_bias, r.attn_bias_in.at[0]), (r.out_biases, r.out_biases_in.at[0]), (r.w_attn, r.w_attn_in.at[0]), (r.w_out, r.w_out_in.at[0]), (r.w_fc, r.w_fc_in.at[0]),
        (r.w_proj, r.w_proj_in.at[0]), (r.fc_bias, r.fc_bias_in),
    ]
    input_copy = pltpu.make_async_copy(r.inputs.at[c], r.xfull.at[0], r.load.at[10, 0])
    input_copy.start()
    owed[0] = input_copy.wait
    def shard_rows(part):
        return pl.ds(pl.multiple_of(part * z.keys_w, 16), z.keys_w)

    for which in (0, 1):
        pltpu.make_async_copy(
            r.w_keys_in.at[0, which], r.w_keys.at[c, which, shard_rows(t)], r.shard.at[c, which, 0]
        ).start()
    def load_own(kinds):
        for kind in kinds:
            held, source = loads[kind]
            pltpu.make_async_copy(source, held.at[c], r.load.at[kind, c]).start()

    def load_other(kinds):
        for kind in kinds:
            held, source = loads[kind]
            copy = remote(source, held.at[c], pair_base + kind, (other, s, t), r.load.at[kind, c])
            copy.start()
            sent.append((copy, None))
            for layer in range(LAYERS):
                owed[id(held), layer] = functools.partial(wait_bytes, held.at[layer], r.load.at[kind, layer])

    early, middle = range(0, 5), range(5, 7)
    load_own(range(len(loads)))
    grad_copy = pltpu.make_async_copy(r.out_grad.at[c], r.gfull.at[1], r.load.at[11, 0])
    grad_copy.start()
    owed[1] = grad_copy.wait

    pl.semaphore_wait(barrier, len(greeted))

    first_rows = to_segs(
        lambda _: r.inputs.at[c, pl.ds(R - MEM, MEM)], lambda i: r.mem_rows.at[0, seg_rows]
    )

    def shard_wait(layer, which, i):
        wait_bytes(r.w_keys.at[layer, which, pl.ds(0, z.keys_w)], r.shard.at[layer, which, i])

    def peer_shards(core, layer, which):
        @pl.when(c == core)
        def _():
            for i in range(1, T):
                shard_wait(layer, which, i)

    def spread_shard(layer, which):
        base = alloc(T - 1)
        place = r.w_keys.at[layer, which, shard_rows(t)]
        copies = [
            remote(r.w_keys_in.at[0, which], place, base + i - 1, (c, s, tpeers[i]), r.shard.at[layer, which, i])
            for i in range(T - 1, 0, -1)
        ]

        @pl.when(c == layer)
        def _():
            for copy in copies:
                copy.start()

        sent.extend((copy, c == layer) for copy in copies)
        owed[11, layer, which] = functools.partial(peer_shards, layer, layer, which)

    def forward_shard(layer, which):
        arrive((11, layer, which))
        base = alloc(T - 1)
        copies = []
        for i in range(1, T):
            place = r.w_keys.at[layer, which, shard_rows(tpeers[i])]
            copies.append(remote(place, place, base + i - 1, (other, s, t), r.shard.at[layer, which, i]))

        @pl.when(c == layer)
        def _():
            for copy in copies:
                copy.start()

        sent.extend((copy, c == layer) for copy in copies)
        owed[12, layer, which] = functools.partial(peer_shards, 1 - layer, layer, which)

    base = alloc(2)
    for which in (0, 1):
        copy = remote(
            r.w_keys_in.at[0, which], r.w_keys.at[c, which, shard_rows(t)], base + which, (other, s, t), r.shard.at[c, which, 0]
        )
        copy.start()
        sent.append((copy, None))
        for layer in range(LAYERS):
            owed[10, layer, which] = functools.partial(shard_wait, layer, which, 0)
    pair_base = alloc(len(loads))
    load_other(early)

    spread_shard(1, 1)
    row_seg = lax.broadcasted_iota(jnp.int32, (M, 1), 0) // MEM
    col_seg = lax.broadcasted_iota(jnp.int32, (1, M), 1) // MEM
    row_item, col_item, own_item = jnp.zeros((M, 1), jnp.int32), jnp.zeros((1, M), jnp.int32), 0
    begin = 0
    for i in range(r.item_lengths.shape[1]):
        length = r.item_lengths[c, i]
        there = jnp.where(length > 0, begin, S)
        row_item = row_item + (row_seg >= there).astype(jnp.int32)
        col_item = col_item + (col_seg >= there).astype(jnp.int32)
        own_item = own_item + jnp.where(s >= there, 1, 0)
        begin = begin + length
    key_mask = jnp.where((row_item == col_item) & (row_seg > col_seg), 1.0, 0.0)
    row_mask = jnp.where((col_item == own_item) & (col_seg < s), 1.0, 0.0)
    lane_head = lax.broadcasted_iota(jnp.int32, (1, z.heads_w), 1) // HEAD_DIM
    head_rows = [(lane_head == h).astype(F32).astype(BF16) for h in range(z.heads)]
    rs_count = [0]

    def reduce_rows(partial):
        k = rs_count[0]
        rs_count[0] += 1
        r.rs_own[...] = partial
        r.rs_src[k] = partial.astype(BF16)
        copies = to_parts(
            lambda peer: r.rs_src.at[k, pl.ds(pl.multiple_of(peer * C, C), C)], lambda i: r.rs_dst.at[k, i - 1]
        )

        def finish():
            arrive(copies)
            total = r.rs_own[own, :]
            for i in range(T - 1):
                total = total + r.rs_dst[k, i].astype(F32)
            return total

        return finish

    def share_rows(ref, layer):
        return to_parts(lambda _: ref.at[layer, own], lambda i: ref.at[layer, own])

    def forward(l):
        own_shard = shard_rows(t)
        if l == 0:
            arrive(0)
            arrive((10, 0, 0))
            r.q_src[...] = dot_nt(r.xfull[0], r.w_keys[0, 0, own_shard, :]).astype(BF16)
            r.q_parts[t] = r.q_src[own, :]
            query_step = to_parts(
                lambda peer: r.q_src.at[pl.ds(pl.multiple_of(peer * C, C), C)], lambda i: r.q_parts.at[t]
            )
            r.mem_rows[0, seg_rows, :] = r.xfull[0, R - MEM :, :]
            arrive((10, 0, 1))
            arrive(first_rows)
            mems = r.mem_rows[0]
            r.k_parts[t] = dot_nt(mems, r.w_keys[0, 1, own_shard, :]).astype(BF16)
            key_step = to_parts(lambda _: r.k_parts.at[t], lambda i: r.k_parts.at[t])
            load_other(middle)
            arrive(query_step)
            queries_mem = jnp.concatenate([r.q_parts[u] for u in range(T)], axis=1)
        else:
            for which in (0, 1):
                arrive((10, 1, which))
                arrive((12, 1, which))
            queries_mem = dot_nt(r.xfull[1, own, :], r.w_keys[1, 0]).astype(BF16)
        x = r.xfull[l, own, :]
        r.qmem[l] = queries_mem
        phi_query = feature_map(queries_mem.astype(F32)).astype(BF16)
        r.phiq[l] = phi_query
        wait_load(r.w_value, l)
        if l == 1:
            arrive(4)
            mems = r.mem_rows[1]
        value_part = dot_nt(mems, r.w_value[l])
        r.vpart[l] = value_part
        r.upart[l] = value_part
        if l == 0:
            arrive(key_step)
            keys = jnp.concatenate([r.k_parts[u] for u in range(T)], axis=1)
        else:
            keys = dot_nt(mems, r.w_keys[1, 1]).astype(BF16)
        r.keyb[l] = keys
        phi_key = feature_map(keys.astype(F32)).astype(BF16)
        r.phik[l] = phi_key
        key_dots = dot_nt(phi_key, phi_key) * key_mask
        r.kdots[l] = key_dots
        key_den = 1.0 + jnp.sum(key_dots, axis=1, keepdims=True)
        for k in range(1, S):
            rows = slice(k * MEM, (k + 1) * MEM)
            read = dot_nn(key_dots[rows].astype(BF16), r.upart[l].astype(BF16)) / key_den[rows]
            r.upart[l, rows, :] = value_part[rows] - read
        r.uall[l, t] = r.upart[l].astype(BF16)
        solved = to_parts(lambda _: r.uall.at[l, t], lambda i: r.uall.at[l, t])
        if l == 0:
            spread_shard(1, 0)
        query_dots = dot_nt(phi_query, phi_key) * row_mask
        r.qdots[l] = query_dots
        query_den = 1.0 + jnp.sum(query_dots, axis=1, keepdims=True)
        for ref in (r.gains, r.shifts, r.attn_bias, r.out_biases):
            wait_load(ref, l)
        arrive(solved)
        high, low = split(query_dots)
        recall = [dot_nn(high, r.uall[l, u]) + dot_nn(low, r.uall[l, u]) for u in range(T)]
        recall = jnp.concatenate(recall, axis=1) / query_den
        r.recall[l] = recall
        hidden = x.astype(F32) + recall.astype(BF16).astype(F32)
        r.hidden[l] = hidden
        unit, _ = norm_rows(hidden)
        r.normed[l, own, :] = (unit * r.gains[l, 0:1] + r.shifts[l, 0:1]).astype(BF16)
        shared = share_rows(r.normed, l)
        if l == 0:
            load_other([9, 7])
        wait_load(r.w_attn, l)
        wait_load(r.w_out, l)
        arrive(shared)
        normed = r.normed[l]
        queries = (dot_nt(normed, r.w_attn[l, 0]) + r.attn_bias[l, 0:1]).astype(BF16)
        key_heads = dot_nt(normed, r.w_attn[l, 1]).astype(BF16)
        values = (dot_nt(normed, r.w_attn[l, 2]) + r.attn_bias[l, 1:2]).astype(BF16)
        r.qkv[l, 0] = queries
        r.qkv[l, 1] = key_heads
        r.qkv[l, 2] = values
        causal = lax.broadcasted_iota(jnp.int32, (R, R), 0) >= lax.broadcasted_iota(jnp.int32, (R, R), 1)
        mixed = jnp.zeros((R, z.heads_w), F32)
        for h in range(z.heads):
            scores = dot_nt(queries, key_heads * head_rows[h]) * HEAD_DIM ** (-0.5)
            scores = jnp.where(causal, scores, -jnp.inf)
            heights = jnp.exp(scores - jnp.max(scores, axis=1, keepdims=True))
            probs = heights * (1.0 / jnp.sum(heights, axis=1, keepdims=True))
            r.probs[l, h] = probs
            mixed = mixed + dot_nn(probs.astype(BF16), values * head_rows[h])
        mixed = mixed.astype(BF16)
        r.mixed[l] = mixed
        finish = reduce_rows(dot_nn(mixed, r.w_out[l]))
        if l == 0:
            load_other([8])
        after = r.hidden[l] + finish() + r.out_biases[l, 0:1]
        r.after[l] = after
        unit, _ = norm_rows(after)
        r.normed_mlp[l, own, :] = (unit * r.gains[l, 1:2] + r.shifts[l, 1:2]).astype(BF16)
        shared = share_rows(r.normed_mlp, l)
        wait_load(r.w_fc, l)
        wait_load(r.fc_bias, l)
        wait_load(r.w_proj, l)
        if l == 0:
            forward_shard(1, 1)
            forward_shard(1, 0)
        arrive(shared)
        pre = dot_nn(r.normed_mlp[l], r.w_fc[l]) + r.fc_bias[l]
        activation, slope = gelu_and_slope(pre)
        activation = activation.astype(BF16)
        r.act[l] = activation
        r.slope[l] = slope
        if l == 0:
            finish = reduce_rows(dot_nn(activation, r.w_proj[l]))
            output = r.after[l] + finish() + r.out_biases[l, 1:2]
            r.xfull[1, own, :] = output.astype(BF16)
            base, places = alloc(S), alloc(S * T)
            last = r.xfull.at[1, pl.ds(R - MEM, MEM)]

            @pl.when(t == T - 1)
            def _():
                r.mem_rows[1, seg_rows, :] = r.xfull[1, R - MEM :, :]
                for i in range(S - 1, -1, -1):
                    for j in range(1 if i == 0 else 0, T):
                        copy = pltpu.make_async_remote_copy(
                            src_ref=last, dst_ref=r.mem_rows.at[1, seg_rows], send_sem=r.send.at[places + i * T + j],
                            recv_sem=r.recv.at[base + i], device_id=(c, to_seg[i], tpeers[j]), device_id_type=MESH,
                        )
                        copy.start()

            def wait_rows(i):
                wait_bytes(r.mem_rows.at[1, pl.ds(0, MEM)], r.recv.at[base + i])

            def wait_all():
                pl.when(t != T - 1)(functools.partial(wait_rows, 0))
                for i in range(1, S):
                    wait_rows(i)

            owed[4] = wait_all

            def drain():
                @pl.when(t == T - 1)
                def _():
                    for i in range(S):
                        for j in range(1 if i == 0 else 0, T):
                            wait_bytes(last, r.send.at[places + i * T + j])

            sent.append((drain, drain))

    fam_p, fam_c = (r.grad_p, r.pair_f, r.far_p, 0, r.relay_f), (r.grad_c, r.pair_f, r.far_c, 1, r.relay_f)
    fam_qk, fam_vo = (r.grad_qk, r.pair_a, r.far_qk, 0, r.relay_a), (r.grad_vo, r.pair_a, r.far_vo, 1, r.relay_a)
    fam_q = (r.grad_q, r.pair_q, r.far_q, None, r.relay_q)
    on_line = S == 4
    partner = s + 1 - 2 * lax.rem(s, 2)
    across = 2 - 2 * lax.div(s, 2)
    outer = jnp.logical_or(s == 0, s == 3)
    relays = {}

    def blocks_of(first_row, count):
        row, pieces = first_row, []
        while row < first_row + count:
            block, inside = row // z.cut, row % z.cut
            size = min(z.cut - inside, first_row + count - row)
            pieces.append((block, inside, row - first_row, size))
            row += size
        return pieces

    def weight_grad(l, family, *pairs):
        stripe = min(256, D)
        for k in range(0, D, stripe):
            parts = [dot_tn(left[:, k : k + stripe], right).astype(BF16) for left, right in pairs]
            grad = parts[0] if len(parts) == 1 else jnp.concatenate(parts, axis=1)
            for block, inside, row, size in blocks_of(k, stripe):
                family[0][l, block, inside : inside + size, :] = grad[row : row + size]

    def pair_send(src, dst):
        index = alloc(1)
        return remote(src, dst, index, (other, s, t))

    def adder_of(l, family):
        return l if family[3] is None else family[3]

    def hand_over(l, family):
        grad, pair, _, _, _ = family
        adder = adder_of(l, family)
        copy = pair_send(grad.at[l], pair.at[l])
        pl.when(c != adder)(copy.start)
        sent.append((copy, c != adder))
        return owe_owner(adder, [copy])

    def owe_owner(l, copies):
        def wait():
            @pl.when(c == l)
            def _():
                for copy in copies:
                    copy.wait_recv()

        owed[id(copies)] = wait
        return id(copies)

    def add_pair(l, family, key):
        grad, pair, _, _, _ = family
        arrive(key)

        @pl.when(c == adder_of(l, family))
        def _():
            @pl.loop(0, S)
            def _(j):
                grad[l, j] = (grad[l, j].astype(F32) + pair[l, j].astype(F32)).astype(BF16)

    def spread(l, family, direct):
        grad, _, far, _, relay = family
        adder = adder_of(l, family)
        near = adder == l
        direct = direct or not on_line
        base = alloc(S if direct else 5)
        steps = range(1, S) if direct else (1, 2)

        @pl.when(c == adder)
        def _():
            if direct:
                for i in range(S - 1, 0, -1):
                    remote(grad.at[l, to_seg[i]], far.at[i], base + i, (l, to_seg[i], t)).start()
            else:

                @pl.when(outer)
                def _():
                    for k in range(2):
                        remote(grad.at[l, across + k], relay.at[l, k], base + 3 + k, (c, partner, t)).start()

                remote(grad.at[l, partner], far.at[1], base + 1, (l, partner, t)).start()
            if near:
                far[0] = grad[l, s]
            else:
                remote(grad.at[l, s], far.at[0], base, (other, s, t)).start()

        if not direct:

            @pl.when(c == l)
            def _():
                for i in range(3, S):
                    far[i] = jnp.zeros(far.shape[1:], BF16)

            def pass_on():
                @pl.when(jnp.logical_and(c == adder, jnp.logical_not(outer)))
                def _():
                    for k in range(2):
                        wait_bytes(relay.at[l, k], r.recv.at[base + 3 + k])
                        place = across + k
                        grad[l, place] = (grad[l, place].astype(F32) + relay[l, k].astype(F32)).astype(BF16)
                        remote(grad.at[l, place], far.at[2], base + 3 + k, (l, place, t), r.recv.at[base + 2]).start()

            relays[id(far), l] = pass_on

        def wait():
            @pl.when(c == l)
            def _():
                for i in steps if near else (0, *steps):
                    wait_bytes(far.at[i], r.recv.at[base + i])

        def drain():
            @pl.when(c == adder)
            def _():
                ends = tuple(steps) if direct else (1, 3, 4)
                for i in ends if near else (0, *ends):
                    wait_bytes(far.at[0], r.send.at[base + i])

        owed[id(far), l] = wait
        sent.append((drain, drain))

    def pass_on(l, family):
        if (id(family[2]), l) in relays:
            relays.pop((id(family[2]), l))()

    def owe_small(l):
        copy = pair_send(r.small.at[l], r.pair_small)
        pl.when(c != l)(copy.start)
        sent.append((copy, c != l))
        return owe_owner(l, [copy])

    def owner_copies(l, copies):
        @pl.when(c == l)
        def _():
            for copy in copies:
                copy.start()

        sent.extend((copy, c == l) for copy in copies)
        return owe_owner(l, copies)

    def small_parts(l, key):
        arrive(key)

        @pl.when(c == l)
        def _():
            r.sum_small[...] = r.small[l] + r.pair_small[...]
            r.part_small[0] = r.sum_small[0:8, :]

        base = alloc(T - 1)
        return owner_copies(
            l, [remote(r.part_small.at[0], r.part_small.at[i], base + i - 1, (c, s, tpeers[i])) for i in range(1, T)]
        )

    def small_segs(l, key):
        arrive(key)

        @pl.when(c == l)
        def _():
            total = r.part_small[0]
            for i in range(1, T):
                total = total + r.part_small[i]
            r.sum_small[0:8, :] = total
            r.seg_small[0] = r.sum_small[...].astype(BF16)

        base = alloc(S - 1)
        return owner_copies(
            l, [remote(r.seg_small.at[0], r.seg_small.at[i], base + i - 1, (c, to_seg[i], t)) for i in range(1, S)]
        )

    def backward(l):
        if l == 1:
            arrive(1)
        grad_low = r.gfull[l]
        pre_grad = (r.slope[l] * dot_nt(grad_low, r.w_proj[l])).astype(BF16)
        r.dpre[...] = pre_grad
        finish = reduce_rows(dot_nt(pre_grad, r.w_fc[l]))
        own_grad = r.gfull[l, own, :].astype(F32)

        weight_grad(l, fam_p, (r.gfull.at[l], r.act[l]))
        pair_p = hand_over(l, fam_p)
        weight_grad(l, fam_c, (r.normed_mlp.at[l], r.dpre[...]))
        pair_c = hand_over(l, fam_c)
        r.small[l, 8:9, :] = jnp.sum(r.dpre[...].astype(F32), axis=0, keepdims=True)
        if l == 0:
            pass_on(1, fam_c)
            pass_on(1, fam_qk)
        add_pair(l, fam_p, pair_p)
        spread(l, fam_p, False)
        after_part, gain_mlp, shift_mlp = norm_back(r.after[l], r.gains[l, 1:2], finish())
        after_grad = own_grad + after_part
        r.tmp[...] = after_grad
        r.low2[l, own, :] = after_grad.astype(BF16)
        shared = share_rows(r.low2, l)
        r.small[l, 1:2, :] = gain_mlp
        r.small[l, 3:4, :] = shift_mlp
        r.small[l, 4:5, :] = jnp.sum(after_grad, axis=0, keepdims=True)
        r.small[l, 5:6, :] = jnp.sum(own_grad, axis=0, keepdims=True)
        add_pair(l, fam_c, pair_c)
        spread(l, fam_c, False)
        if l == 0:
            pass_on(1, fam_vo)
            pass_on(1, fam_q)
        arrive(shared)
        if l == 0:
            forward_shard(0, 0)
            forward_shard(0, 1)
        after_low = r.low2[l]
        mixed_grad = dot_nt(after_low, r.w_out[l]).astype(BF16)
        queries, key_heads, values = r.qkv[l, 0], r.qkv[l, 1], r.qkv[l, 2]
        q_grad = k_grad = v_grad = jnp.zeros((R, z.heads_w), F32)
        for h in range(z.heads):
            probs = r.probs[l, h]
            mixed_here = mixed_grad * head_rows[h]
            probs_grad = dot_nt(mixed_here, values)
            delta = jnp.sum(probs_grad * probs, axis=1, keepdims=True)
            score_grad = (probs * (probs_grad - delta)).astype(BF16)
            q_grad = q_grad + dot_nn(score_grad, key_heads * head_rows[h])
            k_grad = k_grad + dot_tn(score_grad, queries * head_rows[h])
            v_grad = v_grad + dot_tn(probs.astype(BF16), mixed_here)
        scale = HEAD_DIM ** (-0.5)
        r.dqkv[0] = (q_grad * scale).astype(BF16)
        r.dqkv[1] = (k_grad * scale).astype(BF16)
        r.dqkv[2] = v_grad.astype(BF16)
        r.dqk[...] = jnp.concatenate([r.dqkv[0], r.dqkv[1]], axis=1)
        finish = reduce_rows(sum(dot_nn(r.dqkv[i], r.w_attn[l, i]) for i in range(3)))

        weight_grad(l, fam_qk, (r.normed.at[l], r.dqk[...]))
        pair_qk = hand_over(l, fam_qk)
        weight_grad(l, fam_vo, (r.normed.at[l], r.dqkv[2]), (r.low2.at[l], r.mixed[l]))
        pair_vo = hand_over(l, fam_vo)
        for row, i in ((9, 0), (10, 2)):
            r.small[l, row : row + 1, : z.heads_w] = jnp.sum(r.dqkv[i].astype(F32), axis=0, keepdims=True)
        pass_on(l, fam_p)
        hidden_part, gain_attn, shift_attn = norm_back(r.hidden[l], r.gains[l, 0:1], finish())
        hidden_grad = r.tmp[...] + hidden_part
        r.tmp[...] = hidden_grad
        r.small[l, 0:1, :] = gain_attn
        r.small[l, 2:3, :] = shift_attn
        small_key = owe_small(l)
        query_den = 1.0 + jnp.sum(r.qdots[l], axis=1, keepdims=True)
        high, low = split(hidden_grad / query_den)
        den_grad = -jnp.sum((hidden_grad / query_den) * r.recall[l], axis=1, keepdims=True)
        highs = [high[:, u * z.val_w : (u + 1) * z.val_w] for u in range(T)]
        lows = [low[:, u * z.val_w : (u + 1) * z.val_w] for u in range(T)]
        dots_high, dots_low = split(r.qdots[l])
        for u in range(T):
            grad = dot_tn(dots_high, highs[u]) + dot_tn(dots_high, lows[u]) + dot_tn(dots_low, highs[u])
            r.x1_src[l, u] = grad[: M - MEM].astype(BF16)
        value_step = to_parts(lambda peer: r.x1_src.at[l, peer], lambda i: r.x1_dst.at[l, i - 1])
        dots_grad = sum(dot_nt(highs[u], r.uall[l, u]) + dot_nt(lows[u], r.uall[l, u]) for u in range(T)) + den_grad
        dots_grad = (dots_grad * row_mask).astype(BF16)
        key_direct = feature_map_back(r.keyb[l].astype(F32), dot_tn(dots_grad, r.phiq[l]))
        for u in range(T):
            r.x2_src[l, u] = key_direct[: M - MEM, u * z.keys_w : (u + 1) * z.keys_w].astype(BF16)
        key_step = to_parts(lambda peer: r.x2_src.at[l, peer], lambda i: r.x2_dst.at[l, i - 1])
        if l == 1:
            row_step = share_rows(r.xfull, 1)
        add_pair(l, fam_qk, pair_qk)
        add_pair(l, fam_vo, pair_vo)
        arrive(value_step)
        value_part = plus(r.x1_src[l, t], r.x1_dst.at[l], T - 1)
        r.x1_mid[l] = value_part.astype(BF16)
        value_step = to_segs(lambda _: r.x1_mid.at[l], lambda i: r.x1_far.at[l, i - 1])
        arrive(key_step)
        key_part = plus(r.x2_src[l, t], r.x2_dst.at[l], T - 1)
        r.x2_mid[l] = key_part.astype(BF16)
        key_step = to_segs(lambda _: r.x2_mid.at[l], lambda i: r.x2_far.at[l, i - 1])
        for family in (fam_qk, fam_vo):
            spread(l, family, False)
        query_grad = feature_map_back(r.qmem[l].astype(F32), dot_nn(dots_grad, r.phik[l])).astype(BF16)
        for u in range(T):
            r.dq_src[l, u] = query_grad[:, u * z.keys_w : (u + 1) * z.keys_w]
        r.dq_all[l, own, :] = r.dq_src[l, t]
        query_step = to_parts(lambda peer: r.dq_src.at[l, peer], lambda i: r.dq_all.at[l, own])
        if l == 0:
            arrive((12, 0, 0))
            arrive((12, 0, 1))
        r.tmp[...] += dot_nn(query_grad, r.w_keys[l, 0])
        target = r.gfull.at[0] if l == 1 else r.final
        first = pl.ds(pl.multiple_of(t * C, 16), C - MEM)
        rest = pl.ds(pl.multiple_of(t * C + C - MEM, 16), MEM)
        target[first, :] = r.tmp[: C - MEM, :].astype(BF16)
        first_step = to_parts(lambda _: target.at[first], lambda i: target.at[first])
        if l == 1:
            spread_shard(0, 0)
        if l == 1:
            pass_on(l, fam_c)
        arrive(value_step)
        direct = jnp.concatenate([plus(value_part, r.x1_far.at[l], S - 1), jnp.zeros((MEM, z.val_w), F32)], axis=0)
        arrive(key_step)
        small_key = small_parts(l, small_key)
        key_dots = r.kdots[l]
        key_den = 1.0 + jnp.sum(key_dots, axis=1, keepdims=True)
        r.vgrad[...] = direct
        for k in range(S - 1, 0, -1):
            rows = slice(k * MEM, (k + 1) * MEM)
            back = -r.vgrad[rows, :] / key_den[rows]
            r.vgrad[...] += dot_tn(key_dots[rows].astype(BF16), back.astype(BF16))
        value_grad = r.vgrad[...]
        read = r.vpart[l] - r.upart[l]
        back = (-value_grad / key_den).astype(BF16)
        key_den_grad = -jnp.sum(back.astype(F32) * read, axis=1, keepdims=True)
        key_dots_grad = (dot_nt(back, r.upart[l].astype(BF16)) + key_den_grad) * key_mask
        both = (key_dots_grad + key_dots_grad.T).astype(BF16)
        key_solve = feature_map_back(r.keyb[l].astype(F32), dot_nn(both, r.phik[l]))
        r.ksolve[...] = key_solve
        r.dv[...] = value_grad.astype(BF16)
        r.dk_direct[: M - MEM, :] = plus(key_part, r.x2_far.at[l], S - 1)
        r.dk_direct[M - MEM :, :] = jnp.zeros((MEM, z.keys_w), F32)
        tail = dot_nn(r.dv[seg_rows, :], r.w_value[l])
        tail = tail + dot_nn(r.dk_direct[seg_rows, :].astype(BF16), r.w_keys[l, 1, shard_rows(t), :])
        tail = tail + dot_nn(r.ksolve[seg_rows, :].astype(BF16), r.w_keys[l, 1])
        r.x3_src[l] = tail.astype(BF16)
        base, place = alloc(T - 1), alloc(1)

        for i in range(1, T):

            @pl.when(tpeers[i] == T - 1)
            def _():
                copy = pltpu.make_async_remote_copy(
                    src_ref=r.x3_src.at[l], dst_ref=r.x3_dst.at[l, i - 1], send_sem=r.send.at[place],
                    recv_sem=r.recv.at[base + i - 1], device_id=(c, s, tpeers[i]), device_id_type=MESH,
                )
                copy.start()

        def drain():
            @pl.when(t != T - 1)
            def _():
                wait_bytes(r.x3_src.at[l], r.send.at[place])

        sent.append((drain, drain))
        for u in range(T):
            r.x4_src[l, u] = key_solve[:, u * z.keys_w : (u + 1) * z.keys_w].astype(BF16)
        solve_step = to_parts(lambda peer: r.x4_src.at[l, peer], lambda i: r.x4_dst.at[l, i - 1])

        @pl.when(t == T - 1)
        def _():
            total = r.x3_src[l].astype(F32)
            for i in range(T - 1):
                wait_bytes(r.x3_dst.at[l, i], r.recv.at[base + i])
                total = total + r.x3_dst[l, i].astype(F32)
            r.tmp[C - MEM :, :] += total

        target[rest, :] = r.tmp[C - MEM :, :].astype(BF16)
        rest_step = to_parts(lambda _: target.at[rest], lambda i: target.at[rest])
        small_key = small_segs(l, small_key)
        if l == 1:
            spread_shard(0, 1)
        arrive(query_step)
        if l == 1:
            arrive(row_step)
        weight_grad(l, fam_q, (r.xfull.at[l], r.dq_all[l]))
        pair_q = hand_over(l, fam_q)
        r.mem_v[l] = dot_tn(r.mem_rows[l], r.dv[...])
        arrive(solve_step)
        key_grad = plus(r.dk_direct[...] + r.x4_src[l, t].astype(F32), r.x4_dst.at[l], T - 1)
        r.mem_k[l] = dot_tn(r.mem_rows[l], key_grad.astype(BF16))
        rows = pl.ds(pl.multiple_of(s * z.cut, 8), z.cut)
        mem_copies = [pair_send(r.mem_k.at[l, rows], r.pair_k), pair_send(r.mem_v.at[l, rows], r.pair_v)]

        @pl.when(c != l)
        def _():
            for copy in mem_copies:
                copy.start()

        sent.extend((copy, c != l) for copy in mem_copies)
        mem_key = owe_owner(l, mem_copies)
        add_pair(l, fam_q, pair_q)
        spread(l, fam_q, False)
        if l == 0:
            pass_on(l, fam_c)
            pass_on(l, fam_qk)
            pass_on(l, fam_vo)
            pass_on(l, fam_q)
        arrive(first_step)
        arrive(rest_step)
        return mem_key, small_key

    forward(0)
    forward(1)
    for l in range(LAYERS):
        r.small[l] = jnp.zeros((16, D), F32)
    mem_key1, small_key1 = backward(1)
    mem_key0, small_key0 = backward(0)

    r.input_grad[0] = r.final[...]
    l = c

    arrive(mem_key1)
    arrive(mem_key0)
    rows = pl.ds(pl.multiple_of(s * z.cut, 8), z.cut)
    r.mkey_grads[0, 1] = r.mem_k[l, rows, :] + r.pair_k[...]
    r.mvalue_grads[0] = r.mem_v[l, rows, :] + r.pair_v[...]

    def far_sum(far):
        arrive((id(far), 1))
        arrive((id(far), 0))
        return sum(far[i, : z.cut, :].astype(F32) for i in range(S))

    r.proj_grads[0] = far_sum(r.far_p)
    r.fc_grads[0] = far_sum(r.far_c)
    both = far_sum(r.far_qk)
    r.attn_grads[0, 0] = both[:, : z.heads_w]
    r.attn_grads[0, 1] = both[:, z.heads_w :]
    both = far_sum(r.far_vo)
    r.attn_grads[0, 2] = both[:, : z.heads_w]
    r.out_grads[0] = both[:, z.heads_w :].T
    r.mkey_grads[0, 0] = far_sum(r.far_q)
    arrive(small_key1)
    arrive(small_key0)
    total = r.sum_small[...]
    for i in range(1, S):
        total = total + r.seg_small[i].astype(F32)
    r.gain_grads[0] = total[0:2]
    r.shift_grads[0] = total[2:4]
    r.obias_grads[0] = total[4:6]
    r.fcb_grads[...] = total[8:9, : z.units]
    r.abias_grads[0] = total[9:11, : z.heads_w]

    assert not owed and not relays
    for copy, when in sent:
        if when is copy:
            copy()
        elif when is None:
            copy.wait_send()
        else:
            pl.when(when)(copy.wait_send)


def hand_out(*refs):
    count = len(refs) // 2
    for source, target in zip(refs[:count], refs[count:]):
        target[...] = source[...]


def item_ids(lengths):
    item_ends = jnp.cumsum(lengths, axis=-1)
    item_begins = item_ends - lengths
    places = jnp.arange(lengths.shape[-1], dtype=jnp.int32)
    matches = (item_begins[:, :, None] == places[None, None, :]) & (lengths[:, :, None] > 0)
    return jnp.cumsum(jnp.sum(matches.astype(jnp.int32), axis=1), axis=-1)


def reach_mask(lengths):
    ids = item_ids(lengths)
    places = jnp.arange(lengths.shape[-1])
    earlier = places[:, None] > places[None, :]
    same = (ids[:, :, None] == ids[:, None, :]) & earlier[None]
    return jnp.repeat(jnp.repeat(same.astype(F32), MEM, axis=1), MEM, axis=2)


def gather_rows(values, axis):
    return lax.all_gather(values, axis, axis=0, tiled=True)


def scatter_rows(values, axis):
    peers = lax.axis_size(axis)
    pieces = values.astype(BF16).reshape(peers, values.shape[0] // peers, values.shape[1])
    got = lax.all_to_all(pieces, axis, 0, 0, tiled=True)
    return jnp.sum(got.astype(F32), axis=0)


def scatter_columns(values, axis):
    peers = lax.axis_size(axis)
    rows = values.shape[0]
    pieces = values.reshape(rows, peers, -1).transpose(1, 0, 2)
    got = lax.all_to_all(pieces.astype(BF16), axis, 0, 0, tiled=True)
    return jnp.sum(got.astype(F32), axis=0)


def solve_forward(key_dots, key_den, value_mem):
    segments = key_dots.shape[0] // MEM
    solved = value_mem
    for s in range(1, segments):
        rows = slice(s * MEM, (s + 1) * MEM)
        read = dot_nn(key_dots[rows].astype(BF16), solved.astype(BF16)) / key_den[rows]
        solved = solved.at[rows].add(-read)
    return solved


def solve_backward(key_dots, key_den, direct):
    segments = key_dots.shape[0] // MEM
    total = direct
    for s in range(segments - 1, 0, -1):
        rows = slice(s * MEM, (s + 1) * MEM)
        back = -total[rows] / key_den[rows]
        total = total + dot_tn(key_dots[rows].astype(BF16), back.astype(BF16))
    return total


def layer_forward(own_rows, mem_rows, mask, place, params):
    gains, shifts, w_attn, attn_bias, w_out, out_biases, w_fc, fc_bias, w_proj, w_q, w_k, w_v = params
    seg, _ = place
    own_mask = lax.dynamic_slice_in_dim(mask, seg * MEM, 1, 0)
    key_mem = dot_nn(mem_rows, w_k).astype(BF16)
    phi_key = feature_map(key_mem.astype(F32), jnp.roll).astype(BF16)
    key_dots = dot_nt(phi_key, phi_key) * mask
    key_den = 1.0 + jnp.sum(key_dots, axis=1, keepdims=True)
    value_part = dot_nn(mem_rows, w_v)
    solved_part = solve_forward(key_dots, key_den, value_part)
    solved = lax.all_gather(solved_part.astype(BF16), "tensor", axis=1, tiled=True)
    query_mem = dot_nn(own_rows, w_q).astype(BF16)
    phi_query = feature_map(query_mem.astype(F32), jnp.roll).astype(BF16)
    query_dots = dot_nt(phi_query, phi_key) * own_mask
    query_den = 1.0 + jnp.sum(query_dots, axis=1, keepdims=True)
    recall = dot_nn(query_dots.astype(BF16), solved) / query_den
    hidden = own_rows.astype(F32) + recall.astype(BF16).astype(F32)
    unit, _ = norm_rows(hidden)
    normed = gather_rows((unit * gains[0] + shifts[0]).astype(BF16), "tensor")
    queries = (dot_nn(normed, w_attn[0]) + attn_bias[0]).astype(BF16)
    key_heads = dot_nn(normed, w_attn[1]).astype(BF16)
    values = (dot_nn(normed, w_attn[2]) + attn_bias[1]).astype(BF16)
    rows = normed.shape[0]
    causal = jnp.arange(rows)[:, None] >= jnp.arange(rows)[None, :]
    probs, mixed = [], []
    for h in range(queries.shape[1] // HEAD_DIM):
        cols = slice(h * HEAD_DIM, (h + 1) * HEAD_DIM)
        scores = dot_nt(queries[:, cols], key_heads[:, cols]) * HEAD_DIM ** (-0.5)
        scores = jnp.where(causal, scores, -jnp.inf)
        heights = jnp.exp(scores - jnp.max(scores, axis=1, keepdims=True))
        probs.append(heights / jnp.sum(heights, axis=1, keepdims=True))
        mixed.append(dot_nn(probs[-1].astype(BF16), values[:, cols]).astype(BF16))
    mixed = jnp.concatenate(mixed, axis=1)
    after = hidden + scatter_rows(dot_nn(mixed, w_out), "tensor") + out_biases[0]
    unit, _ = norm_rows(after)
    normed_mlp = gather_rows((unit * gains[1] + shifts[1]).astype(BF16), "tensor")
    pre = dot_nn(normed_mlp, w_fc) + fc_bias
    activation, slope = gelu_and_slope(pre)
    activation = activation.astype(BF16)
    output = after + scatter_rows(dot_nn(activation, w_proj), "tensor") + out_biases[1]
    kept = (
        own_rows, mem_rows, key_mem, phi_key, key_dots, key_den, value_part, solved_part, solved, query_mem,
        phi_query, query_dots, query_den, recall, hidden, normed, queries, key_heads, values, probs, mixed,
        after, normed_mlp, slope, activation,
    )
    return output, kept


def layer_backward(own_grad, kept, mask, place, params):
    gains, shifts, w_attn, attn_bias, w_out, out_biases, w_fc, fc_bias, w_proj, w_q, w_k, w_v = params
    (
        own_rows, mem_rows, key_mem, phi_key, key_dots, key_den, value_part, solved_part, solved, query_mem,
        phi_query, query_dots, query_den, recall, hidden, normed, queries, key_heads, values, probs, mixed,
        after, normed_mlp, slope, activation,
    ) = kept
    seg, part = place
    own_mask = lax.dynamic_slice_in_dim(mask, seg * MEM, 1, 0)
    grad_low = gather_rows(own_grad.astype(BF16), "tensor")
    pre_grad = (slope * dot_nt(grad_low, w_proj)).astype(BF16)
    proj_grad = dot_tn(activation, grad_low)
    fc_bias_grad = jnp.sum(pre_grad.astype(F32), axis=0)
    fc_grad = dot_tn(normed_mlp, pre_grad)
    after_part, gain_mlp, shift_mlp = norm_back(
        after, gains[1:2], scatter_rows(dot_nt(pre_grad, w_fc), "tensor")
    )
    after_grad = own_grad + after_part
    after_low = gather_rows(after_grad.astype(BF16), "tensor")
    out_grad = dot_tn(mixed, after_low)
    mixed_grad = dot_nt(after_low, w_out).astype(BF16)
    q_grads, k_grads, v_grads = [], [], []
    for h in range(queries.shape[1] // HEAD_DIM):
        cols = slice(h * HEAD_DIM, (h + 1) * HEAD_DIM)
        probs_grad = dot_nt(mixed_grad[:, cols], values[:, cols])
        delta = jnp.sum(probs_grad * probs[h], axis=1, keepdims=True)
        score_grad = (probs[h] * (probs_grad - delta)).astype(BF16)
        q_grads.append((dot_nn(score_grad, key_heads[:, cols]) * HEAD_DIM ** (-0.5)).astype(BF16))
        k_grads.append((dot_tn(score_grad, queries[:, cols]) * HEAD_DIM ** (-0.5)).astype(BF16))
        v_grads.append(dot_tn(probs[h].astype(BF16), mixed_grad[:, cols]).astype(BF16))
    three = [jnp.concatenate(g, axis=1) for g in (q_grads, k_grads, v_grads)]
    attn_bias_grad = jnp.stack([jnp.sum(three[i].astype(F32), axis=0) for i in (0, 2)])
    attn_grad = jnp.stack([dot_tn(normed, g) for g in three])
    normed_part = sum(dot_nt(g, w_attn[i]) for i, g in enumerate(three))
    hidden_part, gain_attn, shift_attn = norm_back(
        hidden, gains[0:1], scatter_rows(normed_part, "tensor")
    )
    hidden_grad = after_grad + hidden_part
    num_grad = (hidden_grad / query_den).astype(BF16)
    den_grad = -jnp.sum(hidden_grad * recall, axis=1, keepdims=True) / query_den
    dots_grad = ((dot_nt(num_grad, solved) + den_grad) * own_mask).astype(BF16)
    query_grad = feature_map_back(query_mem.astype(F32), dot_nn(dots_grad, phi_key), jnp.roll).astype(BF16)
    solved_direct = dot_tn(query_dots.astype(BF16), num_grad)
    key_direct = feature_map_back(key_mem.astype(F32), dot_tn(dots_grad, phi_query), jnp.roll)
    solved_direct = scatter_columns(solved_direct, "tensor")
    solved_direct = jnp.sum(lax.all_gather(solved_direct.astype(BF16), "seg").astype(F32), axis=0)
    value_grad = solve_backward(key_dots, key_den, solved_direct)
    read = value_part - solved_part
    key_den_grad = jnp.sum(value_grad * read, axis=1, keepdims=True) / key_den
    back = (-value_grad / key_den).astype(BF16)
    key_dots_grad = (dot_nt(back, solved_part.astype(BF16)) + key_den_grad) * mask
    both = (key_dots_grad + key_dots_grad.T).astype(BF16)
    key_solve = feature_map_back(key_mem.astype(F32), dot_nn(both, phi_key), jnp.roll)
    mine = (jnp.arange(key_solve.shape[0]) // MEM == seg)[:, None]
    key_direct = key_direct + jnp.where(mine, key_solve, 0.0)
    key_direct = scatter_columns(key_direct, "tensor")
    key_grad = jnp.sum(lax.all_gather(key_direct.astype(BF16), "seg").astype(F32), axis=0).astype(BF16)
    value_low = value_grad.astype(BF16)
    mem_width = mem_rows.shape[1] // lax.axis_size("seg")
    mem_cols = lax.dynamic_slice_in_dim(mem_rows, seg * mem_width, mem_width, 1)
    mem_key_grad = dot_tn(mem_cols, key_grad)
    mem_value_grad = dot_tn(mem_cols, value_low)
    return (
        hidden_grad, query_grad, key_grad, value_low,
        (gain_attn, gain_mlp, shift_attn, shift_mlp, jnp.sum(after_grad, axis=0, keepdims=True), jnp.sum(own_grad, axis=0, keepdims=True)),
        (attn_grad, attn_bias_grad, out_grad, fc_grad, fc_bias_grad, proj_grad, mem_key_grad, mem_value_grad),
    )


def general_device(
    inputs, out_grad, item_lengths, norm_gains, norm_biases, w_attn, attn_bias, w_out, out_biases, w_fc, fc_bias,
    w_proj, w_mem_keys, w_mem_value,
):
    section, seg, part = (lax.axis_index(name) for name in ("section", "seg", "tensor"))
    segments, parts = lax.axis_size("seg"), lax.axis_size("tensor")
    layers = lax.axis_size("section")
    mask = reach_mask(item_lengths)[section]
    weights = (norm_gains, norm_biases, w_attn, attn_bias, w_out, out_biases, w_fc, fc_bias, w_proj, w_mem_keys, w_mem_value)
    weights = [lax.all_gather(w, "section", axis=0, tiled=True) for w in weights]
    full_keys = lax.all_gather(weights[9], "tensor", axis=3, tiled=True)
    rows_all, grad_all = inputs[section], out_grad[section]
    chunk = rows_all.shape[0] // parts
    own_rows = lax.dynamic_slice_in_dim(rows_all, part * chunk, chunk, 0)
    place = (seg, part)
    saved, layer_params = [], []
    for layer in range(layers):
        mems = lax.all_gather(own_rows[-MEM:], ("seg", "tensor"), axis=0)
        mem_rows = mems[parts - 1 :: parts].reshape(segments * MEM, -1)
        params = tuple(w[layer] for w in weights[:9]) + (full_keys[layer, 0], full_keys[layer, 1], weights[10][layer])
        output, kept = layer_forward(own_rows, mem_rows, mask, place, params)
        saved.append(kept)
        layer_params.append(params)
        own_rows = output.astype(BF16)
    own_grad = lax.dynamic_slice_in_dim(grad_all, part * chunk, chunk, 0).astype(F32)
    rows_grads, matrix_grads = [None] * layers, [None] * layers
    for layer in reversed(range(layers)):
        params, kept = layer_params[layer], saved[layer]
        hidden_grad, query_grad, key_grad, value_low, rows_grads[layer], grads = layer_backward(own_grad, kept, mask, place, params)
        w_q = params[9]
        keys_here = lax.dynamic_slice_in_dim(key_grad, seg * MEM, MEM, 0)
        values_here = lax.dynamic_slice_in_dim(value_low, seg * MEM, MEM, 0)
        tail = dot_nt(keys_here, weights[9][layer, 1]) + dot_nt(values_here, params[11])
        tail = jnp.sum(lax.all_gather(tail.astype(BF16), "tensor").astype(F32), axis=0)
        tail = jnp.concatenate([jnp.zeros((chunk - MEM, tail.shape[1]), F32), tail], axis=0)
        rows_grad = hidden_grad + dot_nt(query_grad, w_q) + jnp.where(part == parts - 1, tail, 0.0)
        own_grad = rows_grad.astype(BF16).astype(F32)
        rows_full = gather_rows(kept[0], "tensor")
        query_cols = lax.all_to_all(query_grad.reshape(chunk, parts, -1).transpose(1, 0, 2), "tensor", 0, 0, tiled=True)
        query_cols = query_cols.reshape(chunk * parts, -1)
        matrix_grads[layer] = grads + (dot_tn(rows_full, query_cols),)
    input_grad = gather_rows(own_grad.astype(BF16), "tensor")[None]

    def over_layers(values):
        return lax.psum_scatter(jnp.stack(values), "section", scatter_dimension=0, tiled=True)

    rows_sums = lax.psum(over_layers([jnp.concatenate(r, axis=0) for r in rows_grads]), ("seg", "tensor"))

    def spread(index, axis):
        stacked = jnp.stack([g[index] for g in matrix_grads]).astype(BF16)
        pair = lax.all_to_all(stacked, "section", 0, 0, tiled=True)
        both = jnp.sum(pair.astype(F32), axis=0)
        cut = both.astype(BF16).reshape(both.shape[:axis] + (segments, -1) + both.shape[axis + 1 :])
        got = lax.all_to_all(cut, "seg", axis, axis, tiled=True)
        return jnp.sum(got.astype(F32), axis=axis)[None]

    biases = lax.psum(
        (over_layers([g[1] for g in matrix_grads]), over_layers([g[4] for g in matrix_grads])), "seg"
    )
    query_w = spread(8, 0)
    key_w = over_layers([g[6] for g in matrix_grads])
    return (
        input_grad,
        rows_sums[:, 0:2],
        rows_sums[:, 2:4],
        spread(0, 1),
        biases[0],
        spread(2, 1),
        rows_sums[:, 4:6],
        spread(3, 0),
        biases[1],
        spread(5, 1),
        jnp.stack([query_w, key_w], axis=1),
        over_layers([g[7] for g in matrix_grads]),
    )


def solution(mesh):
    def per_device(*args):
        inputs, out_grad, item_lengths = args[:3]
        S, T = mesh.shape["seg"], mesh.shape["tensor"]
        w_attn, w_fc, w_keys = args[5], args[9], args[12]
        z = Sizes(
            mesh,
            (
                (0, inputs.shape[1] * S, inputs.shape[2]), (0, 0, 0, w_attn.shape[3] * T), (0, 0, w_fc.shape[2] * T),
                (0, 0, 0, w_keys.shape[3] * T),
            ),
        )
        scratch = scratch_of(z)
        D = z.width
        outs = dict(
            input_grad=((1, z.rows, D), BF16), gain_grads=((1, 2, D), F32), shift_grads=((1, 2, D), F32),
            attn_grads=((1, 3, z.cut, z.heads_w), F32), abias_grads=((1, 2, z.heads_w), F32),
            out_grads=((1, z.heads_w, z.cut), F32), obias_grads=((1, 2, D), F32), fc_grads=((1, z.cut, z.units), F32),
            fcb_grads=((1, z.units), F32), proj_grads=((1, z.cut, z.units), F32),
            mkey_grads=((1, 2, z.cut, z.keys_w), F32), mvalue_grads=((1, z.cut, z.val_w), F32),
        )
        names = tuple(scratch)
        vmem, anywhere = pl.BlockSpec(memory_space=pltpu.VMEM), pl.BlockSpec(memory_space=pl.ANY)
        shapes = [jax.ShapeDtypeStruct(*shape) for shape in outs.values()]
        flip = lambda w: jnp.swapaxes(w, -1, -2)
        results = pl.pallas_call(
            functools.partial(kernel, z, names),
            out_shape=shapes,
            in_specs=[anywhere, anywhere, pl.BlockSpec(memory_space=pltpu.SMEM)] + [anywhere] * 11,
            out_specs=[vmem] * len(outs),
            scratch_shapes=list(scratch.values()),
            compiler_params=pltpu.CompilerParams(
                collective_id=0, has_side_effects=True, vmem_limit_bytes=63 * 2**20
            ),
            name="two_layers",
        )(*args[:5], flip(w_attn), *args[6:12], flip(w_keys), flip(args[13]))
        results = list(pl.pallas_call(
            hand_out, out_shape=shapes, in_specs=[vmem] * len(outs), out_specs=[vmem] * len(outs), name="hand_out"
        )(*results))
        results[9] = flip(results[9])
        return tuple(results)

    return jax.shard_map(
        per_device if mesh.shape["seg"] * MEM <= 128 else general_device,
        mesh=mesh,
        in_specs=(
            P(None, "seg", None),
            P(None, "seg", None),
            P(),
            P("section", None, None),
            P("section", None, None),
            P("section", None, None, "tensor"),
            P("section", None, "tensor"),
            P("section", "tensor", None),
            P("section", None, None),
            P("section", None, "tensor"),
            P("section", "tensor"),
            P("section", "tensor", None),
            P("section", None, None, "tensor"),
            P("section", None, "tensor"),
        ),
        out_specs=(
            P("section", "seg", None),
            P("section", None, None),
            P("section", None, None),
            P("section", None, "seg", "tensor"),
            P("section", None, "tensor"),
            P("section", "tensor", "seg"),
            P("section", None, None),
            P("section", "seg", "tensor"),
            P("section", "tensor"),
            P("section", "tensor", "seg"),
            P("section", None, "seg", "tensor"),
            P("section", "seg", "tensor"),
        ),
        check_vma=False,
    )
```
